32 devices in a mesh: job: 2 (over y), rollout: 4 (over z), tensor: 4 (over x, core).
Axes of the slice: x: 2, y: 2, z: 4, core: 2. Of those that a mesh axis runs over, the one named last changes fastest.
Arguments:
- normed_tokens: bfloat16 [4, 64, 5120], P(None, ('job', 'rollout'), 'tensor'), parts along dimension 1, may hold values from -6 to 6
- key_value_weight: bfloat16 [5120, 2048], P('tensor'), may hold values from -0.078125 to 0.078125
- adapter_down: bfloat16 [10240, 64], P(('job', 'rollout', 'tensor')), parts along dimension 0, may hold values from -0.078125 to 0.078125
- adapter_up: bfloat16 [64, 4096], P(None, ('job', 'rollout')), parts along dimension 1, may hold values from -0.47851562 to 0.47851562
- key_gain: float32 [128], replicated, may hold values from 0.25 to 1.75
- queries: bfloat16 [4, 64, 8192], P(None, ('job', 'rollout'), 'tensor'), parts along dimension 1, may hold values from -100 to 100
- cache_keys: bfloat16 [64, 512, 1024], P(('job', 'rollout'), None, 'tensor'), parts along dimension 0, may hold values from -6 to 6
- stored_values: bfloat16 [64, 512, 1024], P(('job', 'rollout'), None, 'tensor'), parts along dimension 0, may hold values from -6 to 6
- lengths: int32 [64], P(('job', 'rollout')), parts along dimension 0, may hold values from 1 to 512, 6553 in all
- owners: int32 [8], P('job'), parts along dimension 0, may hold values from 0 to 3, each once
Outputs:
- attention: bfloat16 [4, 64, 8192], P(None, ('job', 'rollout'), 'tensor'), parts along dimension 1
- incoming_keys: bfloat16 [4, 64, 1024], P(None, ('job', 'rollout'), 'tensor'), parts along dimension 1
- incoming_values: bfloat16 [4, 64, 1024], P(None, ('job', 'rollout'), 'tensor'), parts along dimension 1
The draws below stay inside these ranges and needn't reach their ends.
There are 2 independent parts, one for each index of `job`. The reference program is written for one: setup_inputs(seed, part) draws one part's arguments, and reference() takes and returns one part's arrays. A program takes and returns all parts, laid end to end along the dimension named above; an argument that names none is the same for every part. Nothing has to cross between parts.
All inputs are finite; a program needn't handle non-finite values. No bound on the sum of `lengths` on one device may be relied on, other than what follows from the above.
Results may differ from the reference program's by a relative error of at most 0.0055.
Values may be sent and summed in bfloat16 or wider, within the bound.
No kernel may reach another device: no remote copies, remote signals or barrier semaphores. Data moves between devices by JAX's collectives and lax.ppermute only.
A program may use at most 64 MiB of HBM per device.

```python
import math
import jax
import jax.numpy as jnp
import numpy as np
from jax import lax

D = 5120
QUERY_HEAD_COUNT = 64
KEY_VALUE_HEADS = 8
HEAD_WIDTH = 128
RANK = 64
DECODE_STEPS = 4
CACHE_SLOT_COUNT = 512
DECODED_ROWS = 32
KVW = 2048
N_ROLLOUT = 4
N_TENSOR = 4


def shared_keys(key):
    return jax.random.normal(key, (DECODED_ROWS, 2, KEY_VALUE_HEADS * HEAD_WIDTH), jnp.float32)


def draw_cache_keys(key, part):
    front_part = shared_keys(key)
    key = jax.random.fold_in(key, 5)
    leftover_part = jax.random.normal(key, (DECODED_ROWS, CACHE_SLOT_COUNT - 2, KEY_VALUE_HEADS * HEAD_WIDTH), jnp.float32)
    whole = jnp.clip(jnp.concatenate([front_part, leftover_part], axis=1), -6.0, 6.0)
    return whole.astype(jnp.bfloat16)


def draw_queries(key, part):
    key = jax.random.fold_in(key, 9)
    drawn = jnp.clip(jax.random.normal(key, (DECODE_STEPS, DECODED_ROWS, QUERY_HEAD_COUNT * HEAD_WIDTH), jnp.float32), -6.0, 6.0)
    return drawn.astype(jnp.bfloat16)


def shard_levels(own_key, dims, pieces, low, top_value):
    factor_of = 1.0
    for position, blocks in pieces:
        steps = jax.random.uniform(jax.random.fold_in(jax.random.fold_in(own_key, 6), position), (blocks,), jnp.float32, low / len(pieces), top_value / len(pieces))
        factor_of = factor_of * jnp.repeat(jnp.exp(steps), dims[position] // blocks).reshape((-1,) + (1,) * (len(dims) - 1 - position))
    return factor_of


def profile(count, total, most, lean):
    weights = [(1 << 20) // math.isqrt(standing ** lean) + 1 for standing in range(2, count + 1)]
    surplus, given = total - most - (count - 1), [1] * (count - 1)
    while surplus > 0:
        candidates = [i for i in range(count - 1) if given[i] < most]
        pool, left = sum([weights[i] for i in candidates]), surplus
        for i in candidates:
            more = min(most - given[i], max(1, left * weights[i] // pool), surplus)
            given[i] = given[i] + more
            surplus = surplus - more
    return np.array([most] + given)


def ragged(stream_key, count, total, bound, slope):
    if count == 2:
        one = jax.random.randint(stream_key, (), max(1, total - bound), min(bound, total - 1) + 1)
        return jnp.stack([one, total - one])
    sizes = jnp.asarray(profile(count, total, bound, slope), jnp.int32)
    twos = (count - 1) // 2
    giver, taker = sizes[1:1 + 2 * twos:2], sizes[2:2 + 2 * twos:2]
    margin = jnp.minimum(giver - 1, bound - taker)
    shifted = jax.random.randint(jax.random.fold_in(stream_key, 1), (twos,), 0, 1 << 20) % (margin + 1)
    sizes = sizes.at[1:1 + 2 * twos:2].set(giver - shifted).at[2:2 + 2 * twos:2].set(taker + shifted)
    return sizes[jax.random.permutation(jax.random.fold_in(stream_key, 2), count)]


def noise(rng, dims, scale, bound, pieces=(), kind=jnp.bfloat16):
    result = scale * jax.random.normal(rng, dims, jnp.float32)
    if pieces:
        result = result * shard_levels(rng, dims, pieces, -0.22, 0.18)
    return jnp.clip(result, -bound, bound).astype(kind)


def setup_inputs(seed: int = 0, part: int = 0) -> dict:
    key_of = jax.random.split(jax.random.key(seed), 11)
    part_keys = jax.random.split(jax.random.fold_in(key_of[10], part), 11)
    normed_tokens = noise(part_keys[0], (DECODE_STEPS, DECODED_ROWS, D), 1.0, 6.0, ((1, 4), (2, 4)))
    key_value_weight = noise(key_of[1], (D, KVW), D ** -0.5, 0.078125, ((0, 4),))
    adapter_down = noise(part_keys[2], (D, RANK), D ** -0.5, 0.078125, ((0, 16),))
    adapter_up = noise(part_keys[3], (RANK, KVW), 0.08, 0.47851562, ((1, 4),))
    key_gain = jnp.clip(1.0 + 0.15 * jax.random.normal(key_of[4], (HEAD_WIDTH,), jnp.float32), 0.25, 1.75)
    queries = draw_queries(jax.random.fold_in(jax.random.fold_in(key_of[10], part), 71), part)
    cache_keys = draw_cache_keys(jax.random.fold_in(jax.random.fold_in(key_of[10], part), 71), part)
    stored_values = noise(part_keys[7], (DECODED_ROWS, CACHE_SLOT_COUNT, KEY_VALUE_HEADS * HEAD_WIDTH), 1.0, 6.0, ((0, 4), (2, 4)))
    lengths = ragged(part_keys[8], DECODED_ROWS, DECODED_ROWS * CACHE_SLOT_COUNT * 2 // 5, CACHE_SLOT_COUNT, 2).astype(jnp.int32)
    owners = jax.random.permutation(part_keys[9], N_ROLLOUT).astype(jnp.int32)
    return dict(normed_tokens=normed_tokens, key_value_weight=key_value_weight, adapter_down=adapter_down, adapter_up=adapter_up, key_gain=key_gain, queries=queries, cache_keys=cache_keys, stored_values=stored_values, lengths=lengths, owners=owners)


norm_eps = 1e-06
rope_base = 1000000.0
adapter_scale = 2.0
masked_score = -1e+30

def rotate(vectors, positions):
    middle = vectors.shape[-1] // 2
    spacing = jnp.arange(middle, dtype=jnp.float32) * (-2.0 / vectors.shape[-1])
    inverse = jnp.power(jnp.float32(rope_base), spacing)
    angles = positions.astype(jnp.float32)[..., None, None] * inverse
    cosine = jnp.cos(angles)
    sine_part = jnp.sin(angles)
    leading = vectors[..., :middle]
    trailing = vectors[..., middle:]
    return jnp.concatenate([leading * cosine - trailing * sine_part, trailing * cosine + leading * sine_part], axis=-1)

def key_norm(raw_keys, key_gain):
    mean_square = lax.optimization_barrier(jnp.mean(raw_keys * raw_keys, axis=-1, keepdims=True))
    return raw_keys * lax.rsqrt(mean_square + norm_eps) * key_gain

def attend_row(row_inputs):
    row_query, row_keys, row_values, fresh_keys, fresh_values, row_length = row_inputs
    step_count, head_count, head_size = fresh_keys.shape
    cache_slots = row_keys.shape[0]
    query_full = row_query.reshape(step_count, head_count, -1, head_size).astype(jnp.float32)
    keys_full = row_keys.reshape(cache_slots, head_count, head_size).astype(jnp.float32)
    values_full = row_values.reshape(cache_slots, head_count, head_size).astype(jnp.float32)
    scale_factor = head_size ** (-0.5)
    cached = jnp.einsum('thge,phe->thgp', query_full, keys_full) * scale_factor
    live_mask = jnp.arange(cache_slots) < row_length
    cached = jnp.where(live_mask, cached, masked_score)
    recent = jnp.einsum('thge,she->thgs', query_full, fresh_keys.astype(jnp.float32)) * scale_factor
    causal = jnp.arange(step_count)[None, :] <= jnp.arange(step_count)[:, None]
    recent = jnp.where(causal[:, None, None, :], recent, masked_score)
    scores = jnp.concatenate([cached, recent], axis=-1)
    row_peak = lax.optimization_barrier(jnp.max(scores, axis=-1, keepdims=True))
    raised = jnp.exp(scores - row_peak)
    weights = (raised / lax.optimization_barrier(jnp.sum(raised, axis=-1, keepdims=True))).astype(jnp.bfloat16)
    values_all = jnp.concatenate([values_full, fresh_values.astype(jnp.float32)], axis=0)
    combined = jnp.einsum('thgp,phe->thge', weights.astype(jnp.float32), values_all)
    return combined.reshape(step_count, -1).astype(jnp.bfloat16)

def reference(normed_tokens, key_value_weight, adapter_down, adapter_up, key_gain, queries, cache_keys, stored_values, lengths, owners):
    rank_size = adapter_down.shape[1]
    blocks = adapter_down.reshape(N_ROLLOUT, N_TENSOR, -1, rank_size)
    down_matrix = jnp.transpose(jnp.take(blocks, owners, axis=0), (1, 0, 2, 3)).reshape(D, rank_size)
    up_matrix = jnp.take(adapter_up.reshape(rank_size, N_ROLLOUT, -1), owners, axis=1).reshape(rank_size, KVW)
    merged_weight = (key_value_weight.astype(jnp.float32) + adapter_scale * jnp.dot(down_matrix, up_matrix, preferred_element_type=jnp.float32)).astype(jnp.bfloat16)
    key_list = []
    value_list = []
    for decode_step_index in range(DECODE_STEPS):
        joined_matrix = jnp.dot(normed_tokens[decode_step_index], merged_weight, preferred_element_type=jnp.float32).reshape(DECODED_ROWS, KEY_VALUE_HEADS, 2, HEAD_WIDTH)
        value_list.append(joined_matrix[:, :, 1].astype(jnp.bfloat16))
        normed = key_norm(joined_matrix[:, :, 0], key_gain)
        key_list.append(rotate(normed, lengths + decode_step_index).astype(jnp.bfloat16))
    incoming_keys = jnp.stack(key_list)
    incoming_values = jnp.stack(value_list)
    row_inputs = (jnp.moveaxis(queries, 1, 0), cache_keys, stored_values, jnp.moveaxis(incoming_keys, 1, 0), jnp.moveaxis(incoming_values, 1, 0), lengths)
    attention = jnp.moveaxis(lax.map(attend_row, row_inputs), 0, 1)
    return (attention, incoming_keys.reshape(DECODE_STEPS, DECODED_ROWS, KEY_VALUE_HEADS * HEAD_WIDTH), incoming_values.reshape(DECODE_STEPS, DECODED_ROWS, KEY_VALUE_HEADS * HEAD_WIDTH))
```

```python
import jax
import jax.numpy as jnp
from jax import lax
from jax.sharding import PartitionSpec as P

norm_eps = 1e-06
rope_base = 1000000.0
adapter_scale = 2.0
masked_score = -1e30


def rotate(vectors, positions):
    middle = vectors.shape[-1] // 2
    spacing = jnp.arange(middle, dtype=jnp.float32) * (-2.0 / vectors.shape[-1])
    inverse = jnp.power(jnp.float32(rope_base), spacing)
    angles = positions.astype(jnp.float32)[..., None, None] * inverse
    cosine = jnp.cos(angles)
    sine_part = jnp.sin(angles)
    leading = vectors[..., :middle]
    trailing = vectors[..., middle:]
    return jnp.concatenate(
        [leading * cosine - trailing * sine_part, trailing * cosine + leading * sine_part], axis=-1
    )


def key_norm(raw_keys, key_gain):
    mean_square = jnp.mean(raw_keys * raw_keys, axis=-1, keepdims=True)
    return raw_keys * lax.rsqrt(mean_square + norm_eps) * key_gain


def swap(block, axis, offset):
    count = lax.axis_size(axis)
    return lax.ppermute(block, axis, [(s, s ^ offset) for s in range(count)])


def gather_by_offset(block, axis):
    count = lax.axis_size(axis)
    if count <= 8:
        return jnp.stack([block] + [swap(block, axis, i) for i in range(1, count)])
    whole = lax.all_gather(block, axis, axis=0, tiled=False)
    return jnp.take(whole, jnp.arange(count) ^ lax.axis_index(axis), axis=0, mode="clip")


def per_device(
    normed_tokens,
    key_value_weight,
    adapter_down,
    adapter_up,
    key_gain,
    queries,
    cache_keys,
    stored_values,
    lengths,
    owners,
):
    replicas = lax.axis_size("rollout")
    shards = lax.axis_size("tensor")
    replica = lax.axis_index("rollout")
    shard = lax.axis_index("tensor")
    down_rows, rank_size = adapter_down.shape
    up_columns = adapter_up.shape[1]
    step_count, row_count, depth = normed_tokens.shape
    head_size = key_gain.shape[0]
    columns = key_value_weight.shape[1]
    own_columns = columns // shards

    rank_part = rank_size // shards
    up_part = lax.dynamic_slice_in_dim(adapter_up, shard * rank_part, rank_part, axis=0)
    half = down_rows // 2
    down_packed = jnp.concatenate([adapter_down[:half], adapter_down[half:]], axis=1)
    packed = jnp.concatenate([down_packed, up_part.reshape(-1, 2 * rank_size)], axis=0)
    pieces = gather_by_offset(packed, "rollout")

    tokens = normed_tokens.reshape(step_count * row_count, depth)
    base = jnp.dot(tokens, key_value_weight, preferred_element_type=jnp.float32)
    joined = lax.dynamic_slice_in_dim(base, shard * own_columns, own_columns, axis=1)
    for i in range(1, shards):
        block = lax.dynamic_slice_in_dim(base, (shard ^ i) * own_columns, own_columns, axis=1)
        joined = joined + swap(block, "tensor", i)

    ordered = jnp.take(pieces, owners ^ replica, axis=0, mode="clip")
    down_ordered = ordered[:, :half]
    down_matrix = jnp.concatenate(
        [down_ordered[:, :, :rank_size], down_ordered[:, :, rank_size:]], axis=1
    ).reshape(-1, rank_size)
    up_matrix = (
        ordered[:, half:]
        .reshape(replicas, rank_part, up_columns)
        .transpose(1, 0, 2)
        .reshape(rank_part, columns)
    )
    lowered = jnp.dot(tokens, down_matrix, preferred_element_type=jnp.float32)
    high = lowered.astype(jnp.bfloat16)
    low = (lowered - high.astype(jnp.float32)).astype(jnp.bfloat16)
    lowered_packed = jnp.concatenate([high, low], axis=1)

    sums = []
    ups = []
    for i in range(shards):
        up_block = lax.dynamic_slice_in_dim(
            up_matrix, (shard ^ i) * own_columns, own_columns, axis=1
        )
        block = jnp.concatenate([lowered_packed, up_block.reshape(-1, 2 * rank_size)], axis=0)
        if i:
            block = swap(block, "tensor", i)
        sums.append(block[: step_count * row_count])
        ups.append(block[step_count * row_count :].reshape(rank_part, own_columns))
    total = sum(s.astype(jnp.float32) for s in sums)
    total = total[:, :rank_size] + total[:, rank_size:]
    total_high = total.astype(jnp.bfloat16)
    total_low = (total - total_high.astype(jnp.float32)).astype(jnp.bfloat16)
    up_own = jnp.take(jnp.stack(ups), jnp.arange(shards) ^ shard, axis=0, mode="clip").reshape(
        rank_size, own_columns
    )
    raised_up = jnp.dot(total_high, up_own, preferred_element_type=jnp.float32) + jnp.dot(
        total_low, up_own, preferred_element_type=jnp.float32
    )
    joined = joined + adapter_scale * raised_up

    joined_matrix = joined.reshape(step_count, row_count, -1, 2, head_size)
    incoming_values = joined_matrix[:, :, :, 1].astype(jnp.bfloat16)
    positions = lengths[None, :] + jnp.arange(step_count, dtype=jnp.int32)[:, None]
    incoming_keys = rotate(key_norm(joined_matrix[:, :, :, 0], key_gain), positions).astype(
        jnp.bfloat16
    )
    head_count = incoming_keys.shape[2]
    query_heads = queries.reshape(step_count, row_count, head_count, -1, head_size)
    keys_local = cache_keys.reshape(row_count, -1, head_count, head_size)
    values_local = stored_values.reshape(row_count, -1, head_count, head_size)
    scale_factor = head_size ** (-0.5)
    cached = (
        jnp.einsum("tbhge,bphe->tbhgp", query_heads, keys_local, preferred_element_type=jnp.float32)
        * scale_factor
    )
    live_mask = jnp.arange(keys_local.shape[1])[None, :] < lengths[:, None]
    cached = jnp.where(live_mask[None, :, None, None, :], cached, masked_score)
    recent = (
        jnp.einsum(
            "tbhge,sbhe->tbhgs", query_heads, incoming_keys, preferred_element_type=jnp.float32
        )
        * scale_factor
    )
    causal = jnp.arange(step_count)[None, :] <= jnp.arange(step_count)[:, None]
    recent = jnp.where(causal[:, None, None, None, :], recent, masked_score)
    row_peak = jnp.maximum(
        jnp.max(cached, axis=-1, keepdims=True), jnp.max(recent, axis=-1, keepdims=True)
    )
    raised_cached = jnp.exp(cached - row_peak)
    raised_recent = jnp.exp(recent - row_peak)
    denominator = jnp.sum(raised_cached, axis=-1, keepdims=True) + jnp.sum(
        raised_recent, axis=-1, keepdims=True
    )
    weights_cached = (raised_cached / denominator).astype(jnp.bfloat16)
    weights_recent = (raised_recent / denominator).astype(jnp.bfloat16)
    combined = jnp.einsum(
        "tbhgp,bphe->tbhge", weights_cached, values_local, preferred_element_type=jnp.float32
    )
    combined = combined + jnp.einsum(
        "tbhgs,sbhe->tbhge", weights_recent, incoming_values, preferred_element_type=jnp.float32
    )
    attention = combined.reshape(step_count, row_count, -1).astype(jnp.bfloat16)
    return (
        attention,
        incoming_keys.reshape(step_count, row_count, -1),
        incoming_values.reshape(step_count, row_count, -1),
    )


def solution(mesh):
    placed = (
        P(None, ("job", "rollout"), "tensor"),
        P("tensor", None),
        P(("job", "rollout", "tensor"), None),
        P(None, ("job", "rollout")),
        P(),
        P(None, ("job", "rollout"), "tensor"),
        P(("job", "rollout"), None, "tensor"),
        P(("job", "rollout"), None, "tensor"),
        P(("job", "rollout")),
        P("job"),
    )
    return jax.shard_map(
        per_device,
        mesh=mesh,
        in_specs=placed,
        out_specs=(
            P(None, ("job", "rollout"), "tensor"),
            P(None, ("job", "rollout"), "tensor"),
            P(None, ("job", "rollout"), "tensor"),
        ),
        check_vma=False,
    )
```

```python
import jax
import jax.numpy as jnp
from jax import lax
from jax.sharding import PartitionSpec as P

norm_eps = 1e-06
rope_base = 1000000.0
adapter_scale = 2.0
masked_score = -1e30


def rotate(vectors, positions):
    middle = vectors.shape[-1] // 2
    spacing = jnp.arange(middle, dtype=jnp.float32) * (-2.0 / vectors.shape[-1])
    inverse = jnp.power(jnp.float32(rope_base), spacing)
    angles = positions.astype(jnp.float32)[..., None, None] * inverse
    cosine = jnp.cos(angles)
    sine_part = jnp.sin(angles)
    leading = vectors[..., :middle]
    trailing = vectors[..., middle:]
    return jnp.concatenate(
        [leading * cosine - trailing * sine_part, trailing * cosine + leading * sine_part], axis=-1
    )


def key_norm(raw_keys, key_gain):
    mean_square = jnp.mean(raw_keys * raw_keys, axis=-1, keepdims=True)
    return raw_keys * lax.rsqrt(mean_square + norm_eps) * key_gain


def exchange(blocks, axis):
    return lax.all_to_all(blocks, axis, split_axis=0, concat_axis=0)


def per_device(
    normed_tokens,
    key_value_weight,
    adapter_down,
    adapter_up,
    key_gain,
    queries,
    cache_keys,
    stored_values,
    lengths,
    owners,
):
    replicas = lax.axis_size("rollout")
    shards = lax.axis_size("tensor")
    shard = lax.axis_index("tensor")
    down_rows, rank_size = adapter_down.shape
    up_columns = adapter_up.shape[1]
    step_count, row_count, depth = normed_tokens.shape
    head_size = key_gain.shape[0]
    columns = key_value_weight.shape[1]
    own_columns = columns // shards

    rank_part = rank_size // shards
    up_part = lax.dynamic_slice_in_dim(adapter_up, shard * rank_part, rank_part, axis=0)
    half = down_rows // 2
    down_packed = jnp.concatenate([adapter_down[:half], adapter_down[half:]], axis=1)
    packed = jnp.concatenate([down_packed, up_part.reshape(-1, 2 * rank_size)], axis=0)
    pieces = exchange(jnp.broadcast_to(packed, (replicas,) + packed.shape), "rollout")

    tokens = normed_tokens.reshape(step_count * row_count, depth)
    base = jnp.dot(tokens, key_value_weight, preferred_element_type=jnp.float32)
    blocks = base.reshape(-1, shards, own_columns).transpose(1, 0, 2)
    joined = jnp.sum(exchange(blocks, "tensor"), axis=0)

    ordered = jnp.take(pieces, owners, axis=0, mode="clip")
    down_ordered = ordered[:, :half]
    down_matrix = jnp.concatenate(
        [down_ordered[:, :, :rank_size], down_ordered[:, :, rank_size:]], axis=1
    ).reshape(-1, rank_size)
    up_matrix = (
        ordered[:, half:]
        .reshape(replicas, rank_part, up_columns)
        .transpose(1, 0, 2)
        .reshape(rank_part, columns)
    )
    lowered = jnp.dot(tokens, down_matrix, preferred_element_type=jnp.float32)
    high = lowered.astype(jnp.bfloat16)
    low = (lowered - high.astype(jnp.float32)).astype(jnp.bfloat16)
    lowered_packed = jnp.concatenate([high, low], axis=1)

    row_total = step_count * row_count
    up_blocks = up_matrix.reshape(rank_part, shards, own_columns).transpose(1, 0, 2)
    up_blocks = up_blocks.reshape(shards, -1, 2 * rank_size)
    blocks = jnp.concatenate(
        [jnp.broadcast_to(lowered_packed, (shards,) + lowered_packed.shape), up_blocks], axis=1
    )
    blocks = exchange(blocks, "tensor")
    total = jnp.sum(blocks[:, :row_total].astype(jnp.float32), axis=0)
    total = total[:, :rank_size] + total[:, rank_size:]
    total_high = total.astype(jnp.bfloat16)
    total_low = (total - total_high.astype(jnp.float32)).astype(jnp.bfloat16)
    up_own = blocks[:, row_total:].reshape(rank_size, own_columns)
    raised_up = jnp.dot(total_high, up_own, preferred_element_type=jnp.float32) + jnp.dot(
        total_low, up_own, preferred_element_type=jnp.float32
    )
    joined = joined + adapter_scale * raised_up

    joined_matrix = joined.reshape(step_count, row_count, -1, 2, head_size)
    incoming_values = joined_matrix[:, :, :, 1].astype(jnp.bfloat16)
    positions = lengths[None, :] + jnp.arange(step_count, dtype=jnp.int32)[:, None]
    incoming_keys = rotate(key_norm(joined_matrix[:, :, :, 0], key_gain), positions).astype(
        jnp.bfloat16
    )
    head_count = incoming_keys.shape[2]
    query_heads = queries.reshape(step_count, row_count, head_count, -1, head_size)
    keys_local = cache_keys.reshape(row_count, -1, head_count, head_size)
    values_local = stored_values.reshape(row_count, -1, head_count, head_size)
    scale_factor = head_size ** (-0.5)
    cached = (
        jnp.einsum("tbhge,bphe->tbhgp", query_heads, keys_local, preferred_element_type=jnp.float32)
        * scale_factor
    )
    live_mask = jnp.arange(keys_local.shape[1])[None, :] < lengths[:, None]
    cached = jnp.where(live_mask[None, :, None, None, :], cached, masked_score)
    recent = (
        jnp.einsum(
            "tbhge,sbhe->tbhgs", query_heads, incoming_keys, preferred_element_type=jnp.float32
        )
        * scale_factor
    )
    causal = jnp.arange(step_count)[None, :] <= jnp.arange(step_count)[:, None]
    recent = jnp.where(causal[:, None, None, None, :], recent, masked_score)
    row_peak = jnp.maximum(
        jnp.max(cached, axis=-1, keepdims=True), jnp.max(recent, axis=-1, keepdims=True)
    )
    raised_cached = jnp.exp(cached - row_peak)
    raised_recent = jnp.exp(recent - row_peak)
    denominator = jnp.sum(raised_cached, axis=-1, keepdims=True) + jnp.sum(
        raised_recent, axis=-1, keepdims=True
    )
    weights_cached = (raised_cached / denominator).astype(jnp.bfloat16)
    weights_recent = (raised_recent / denominator).astype(jnp.bfloat16)
    combined = jnp.einsum(
        "tbhgp,bphe->tbhge", weights_cached, values_local, preferred_element_type=jnp.float32
    )
    combined = combined + jnp.einsum(
        "tbhgs,sbhe->tbhge", weights_recent, incoming_values, preferred_element_type=jnp.float32
    )
    attention = combined.reshape(step_count, row_count, -1).astype(jnp.bfloat16)
    return (
        attention,
        incoming_keys.reshape(step_count, row_count, -1),
        incoming_values.reshape(step_count, row_count, -1),
    )


def solution(mesh):
    placed = (
        P(None, ("job", "rollout"), "tensor"),
        P("tensor", None),
        P(("job", "rollout", "tensor"), None),
        P(None, ("job", "rollout")),
        P(),
        P(None, ("job", "rollout"), "tensor"),
        P(("job", "rollout"), None, "tensor"),
        P(("job", "rollout"), None, "tensor"),
        P(("job", "rollout")),
        P("job"),
    )
    return jax.shard_map(
        per_device,
        mesh=mesh,
        in_specs=placed,
        out_specs=(
            P(None, ("job", "rollout"), "tensor"),
            P(None, ("job", "rollout"), "tensor"),
            P(None, ("job", "rollout"), "tensor"),
        ),
        check_vma=False,
    )
```

```python
import functools
import math

import jax
import jax.numpy as jnp
from jax import lax
from jax.experimental import pallas as pl
from jax.experimental.pallas import tpu as pltpu
from jax.sharding import PartitionSpec as P

norm_eps = 1e-06
rope_base = 1000000.0
adapter_scale = 2.0
masked_score = -1e30
lanes = 128
f32 = jnp.float32
bf16 = jnp.bfloat16

whole_in_vmem = pl.BlockSpec(memory_space=pltpu.VMEM)
whole_in_smem = pl.BlockSpec(memory_space=pltpu.SMEM)
left_in_place = pl.BlockSpec(memory_space=pl.ANY)


def swap(block, axis, offset):
    count = lax.axis_size(axis)
    return lax.ppermute(block, axis, [(s, s ^ offset) for s in range(count)])


def side_by_side(rows_of_blocks):
    r, c = rows_of_blocks.shape
    return rows_of_blocks.reshape(r, c // lanes, lanes).transpose(1, 0, 2).reshape(-1, lanes)


def split_halves(total):
    high = total.astype(bf16)
    return high, (total - high.astype(f32)).astype(bf16)


def pack_kernel(down_ref, up_ref, out_ref):
    half = down_ref.shape[0] // 2
    rank_part = (out_ref.shape[0] - half) * lanes // up_ref.shape[1]
    out_ref[:half, :] = jnp.concatenate([down_ref[:half, :], down_ref[half:, :]], axis=1)
    first = pl.multiple_of(lax.axis_index("tensor") * rank_part, rank_part)
    for c in range(up_ref.shape[1] // lanes):
        out_ref[half + c * rank_part : half + (c + 1) * rank_part, :] = up_ref[
            pl.ds(first, rank_part), c * lanes : (c + 1) * lanes
        ]


def pack(down, up, rank_part):
    rows = down.shape[0] // 2 + rank_part * up.shape[1] // lanes
    return pl.pallas_call(
        pack_kernel,
        out_shape=jax.ShapeDtypeStruct((rows, lanes), bf16),
        in_specs=[whole_in_vmem] * 2,
        out_specs=whole_in_vmem,
        name="pack",
        cost_estimate=pl.CostEstimate(flops=0, bytes_accessed=200000, transcendentals=0),
    )(down, up)


def front_kernel(
    step_count,
    row_count,
    head_count,
    shards,
    lengths_ref,
    tokens_ref,
    queries_ref,
    weight_ref,
    keys_ref,
    values_ref,
    base_ref,
    grouped_ref,
    total_ref,
    peak_ref,
    sum_ref,
    cosine_ref,
    sine_ref,
    weight_buf,
    keys_buf,
    values_buf,
    regroup,
    scores,
    raised,
    key_sems,
    value_sems,
    weight_sems,
):
    shard = lax.axis_index("tensor")
    own = base_ref.shape[2]
    slots = keys_buf.shape[1]
    group = queries_ref.shape[1] // (head_count * lanes)
    seen = step_count * group
    scale = lanes**-0.5

    key_copies = [
        pltpu.make_async_copy(keys_ref.at[b], keys_buf.at[b], key_sems.at[b])
        for b in range(row_count)
    ]
    value_copies = [
        pltpu.make_async_copy(values_ref.at[b], values_buf.at[b], value_sems.at[b])
        for b in range(row_count)
    ]
    weight_copies = [
        pltpu.make_async_copy(
            weight_ref.at[:, pl.ds(pl.multiple_of((shard ^ i) * own, lanes), own)],
            weight_buf.at[i],
            weight_sems.at[i],
        )
        for i in range(shards)
    ]
    for copy in key_copies + value_copies + weight_copies:
        copy.start()

    for pair in range(step_count // 2):
        for q in range(head_count * group):
            h, g = q // group, q % group
            both = queries_ref[
                pair * 2 * row_count : (pair + 1) * 2 * row_count, q * lanes : (q + 1) * lanes
            ].astype(f32)
            for side in range(2):
                first = h * row_count * seen + (pair * 2 + side) * group + g
                regroup[pl.ds(first, row_count, stride=seen), :] = both[
                    side * row_count : (side + 1) * row_count, :
                ]
    grouped_ref[...] = regroup[...].astype(bf16)

    rows = step_count * row_count
    row = lax.broadcasted_iota(jnp.int32, (rows, lanes), 0)
    lane = lax.broadcasted_iota(jnp.int32, (rows, lanes), 1)
    position = row // row_count
    for b in range(row_count):
        position = position + jnp.where(row % row_count == b, lengths_ref[b], 0)
    middle = lanes // 2
    spacing = (lane % middle).astype(f32) * (-2.0 / lanes * math.log(rope_base))
    angles = position.astype(f32) * jnp.exp(spacing)
    cosine_ref[...] = jnp.cos(angles)
    sine = jnp.sin(angles)
    sine_ref[...] = jnp.where(lane < middle, -sine, sine)

    for b in range(row_count):
        key_copies[b].wait()
        for h in range(head_count):
            at = (h * row_count + b) * seen
            scores[at : at + seen, :] = lax.dot_general(
                grouped_ref[at : at + seen, :],
                keys_buf[b, :, h * lanes : (h + 1) * lanes],
                (((1,), (1,)), ((), ())),
                preferred_element_type=f32,
            )
    slot = lax.broadcasted_iota(jnp.int32, (seen, slots), 1)
    for b in range(row_count):
        live = slot < lengths_ref[b]
        for h in range(head_count):
            at = (h * row_count + b) * seen
            score = jnp.where(live, scores[at : at + seen, :] * scale, masked_score)
            peak = jnp.max(score, axis=1, keepdims=True)
            lifted = jnp.exp(score - peak)
            raised[at : at + seen, :] = lifted.astype(bf16)
            peak_ref[at : at + seen, :] = jnp.broadcast_to(peak, (seen, lanes))
            sum_ref[at : at + seen, :] = jnp.broadcast_to(
                jnp.sum(lifted, axis=1, keepdims=True), (seen, lanes)
            )
    for b in range(row_count):
        value_copies[b].wait()
        for h in range(head_count):
            at = (h * row_count + b) * seen
            total_ref[at : at + seen, :] = jnp.dot(
                raised[at : at + seen, :],
                values_buf[b, :, h * lanes : (h + 1) * lanes],
                preferred_element_type=f32,
            )
    for i in range(shards):
        weight_copies[i].wait()
        base_ref[i] = jnp.dot(tokens_ref[...], weight_buf[i], preferred_element_type=f32)


def front(lengths, tokens, queries, weight, keys, values, step_count, shards):
    row_count, slots, width = keys.shape
    head_count = width // lanes
    depth, columns = weight.shape
    own = columns // shards
    rows = step_count * row_count
    seen_rows = rows * queries.shape[1] // lanes
    table = jax.ShapeDtypeStruct((rows, lanes), f32)
    seen_table = jax.ShapeDtypeStruct((seen_rows, lanes), f32)
    return pl.pallas_call(
        functools.partial(front_kernel, step_count, row_count, head_count, shards),
        out_shape=(
            jax.ShapeDtypeStruct((shards, rows, own), f32),
            jax.ShapeDtypeStruct((seen_rows, lanes), bf16),
            seen_table,
            seen_table,
            seen_table,
            table,
            table,
        ),
        in_specs=[whole_in_smem, whole_in_vmem, whole_in_vmem] + [left_in_place] * 3,
        out_specs=(whole_in_vmem,) * 7,
        scratch_shapes=[
            pltpu.VMEM((shards, depth, own), bf16),
            pltpu.VMEM(keys.shape, bf16),
            pltpu.VMEM(values.shape, bf16),
            pltpu.VMEM((seen_rows, lanes), f32),
            pltpu.VMEM((seen_rows, slots), f32),
            pltpu.VMEM((seen_rows, slots), bf16),
            pltpu.SemaphoreType.DMA((row_count,)),
            pltpu.SemaphoreType.DMA((row_count,)),
            pltpu.SemaphoreType.DMA((shards,)),
        ],
        compiler_params=pltpu.CompilerParams(vmem_limit_bytes=32 * 2**20),
        name="front",
        cost_estimate=pl.CostEstimate(
            flops=2 * rows * depth * columns + 4 * seen_rows * slots * lanes,
            bytes_accessed=2 * (weight.size + keys.size + values.size),
            transcendentals=seen_rows * slots,
        ),
    )(lengths, tokens, queries, weight, keys, values)


def route_kernel(replicas, shards, *refs):
    owners_ref, tokens_ref, base_ref = refs[:3]
    piece_refs = refs[3 : 3 + replicas]
    out_refs = refs[3 + replicas : 3 + replicas + shards]
    down_buf, up_buf = refs[3 + replicas + shards :]
    replica = lax.axis_index("rollout")
    shard = lax.axis_index("tensor")
    down_rows = down_buf.shape[0] // replicas
    rank = down_buf.shape[1]
    half = down_rows // 2
    for i in range(replicas):
        source = replica ^ i
        place = jnp.int32(0)
        for k in range(1, replicas):
            place = place + jnp.where(owners_ref[k] == source, k, 0)
        first = pl.multiple_of(place * down_rows, half)
        down_buf[pl.ds(first, half), :] = piece_refs[i][:half, :rank]
        second = pl.multiple_of(place * down_rows + half, half)
        down_buf[pl.ds(second, half), :] = piece_refs[i][:half, rank:]
        up_buf[i] = piece_refs[i][half:, :]
    lowered = jnp.dot(tokens_ref[...], down_buf[...], preferred_element_type=f32)
    both = jnp.concatenate(split_halves(lowered), axis=1)
    rows = tokens_ref.shape[0]
    for i in range(shards):
        first = 0
        if i:
            for c in range(base_ref.shape[2] // lanes):
                out_refs[i][first : first + rows, :] = base_ref[
                    i, :, c * lanes : (c + 1) * lanes
                ].astype(bf16)
                first += rows
        out_refs[i][first : first + rows, :] = both
        out_refs[i][first + rows :, :] = up_buf[owners_ref[shard ^ i] ^ replica]


def route(owners, tokens, base, pieces, down_rows, rank):
    shards, rows, own = base.shape
    replicas = len(pieces)
    up_rows = pieces[0].shape[0] - down_rows // 2
    sent = rows * own // lanes
    return pl.pallas_call(
        functools.partial(route_kernel, replicas, shards),
        out_shape=[
            jax.ShapeDtypeStruct(((sent if i else 0) + rows + up_rows, lanes), bf16)
            for i in range(shards)
        ],
        in_specs=[whole_in_smem] + [whole_in_vmem] * (2 + replicas),
        out_specs=[whole_in_vmem] * shards,
        scratch_shapes=[
            pltpu.VMEM((replicas * down_rows, rank), bf16),
            pltpu.VMEM((replicas, up_rows, lanes), bf16),
        ],
        name="route",
        cost_estimate=pl.CostEstimate(flops=0, bytes_accessed=800000, transcendentals=0),
    )(owners, tokens, base, *pieces)


def route_plain(owners, tokens, base, down, up, rank_part):
    shards, rows, own = base.shape
    rank = down.shape[1]
    shard = lax.axis_index("tensor")
    first = shard * rank_part
    up_part = lax.dynamic_slice_in_dim(up, first, rank_part, axis=0)
    downs = lax.all_gather(down, "rollout", axis=0, tiled=False)
    ups = lax.all_gather(up_part, "rollout", axis=0, tiled=False)
    down_matrix = jnp.take(downs, owners, axis=0, mode="clip").reshape(-1, rank)
    up_matrix = jnp.take(ups, owners, axis=0, mode="clip").transpose(1, 0, 2)
    up_matrix = up_matrix.reshape(rank_part, -1)
    lowered = jnp.dot(tokens, down_matrix, preferred_element_type=f32)
    both = jnp.concatenate(split_halves(lowered), axis=1)
    packets = []
    for i in range(shards):
        up_block = lax.dynamic_slice_in_dim(up_matrix, (shard ^ i) * own, own, axis=1)
        parts = [both, side_by_side(up_block)]
        if i:
            parts = [side_by_side(base[i].astype(bf16))] + parts
        packets.append(jnp.concatenate(parts, axis=0))
    return packets


def finish_kernel(step_count, row_count, head_count, shards, *refs):
    base_ref, gain_ref, grouped_ref, total_ref, peak_ref, sum_ref, cosine_ref, sine_ref = refs[:8]
    packet_refs = refs[8 : 8 + shards]
    attention_ref, keys_ref, values_ref = refs[8 + shards : 11 + shards]
    up_buf, ordered = refs[11 + shards :]
    shard = lax.axis_index("tensor")
    rows = step_count * row_count
    own = base_ref.shape[2]
    blocks = own // lanes
    rank = up_buf.shape[0]
    rank_part = rank // shards
    group = grouped_ref.shape[0] // (head_count * rows)
    seen = step_count * group
    scale = lanes**-0.5

    lowered = jnp.zeros((rows, lanes), f32)
    for i in range(shards):
        first = rows * blocks if i else 0
        lowered = lowered + packet_refs[i][first : first + rows, :].astype(f32)
        ups = packet_refs[i][first + rows :, :].astype(f32)
        at = pl.multiple_of((shard ^ i) * rank_part, rank_part)
        for c in range(blocks):
            up_buf[pl.ds(at, rank_part), c * lanes : (c + 1) * lanes] = ups[
                c * rank_part : (c + 1) * rank_part, :
            ]
    lane = lax.broadcasted_iota(jnp.int32, (rows, lanes), 1)
    lowered = lowered + pltpu.roll(lowered, rank, 1)
    high, low = split_halves(lowered)
    left = jnp.where(lane < rank, high.astype(f32), low.astype(f32)).astype(bf16)
    up = up_buf[...].astype(bf16)
    raised_up = jnp.dot(left, jnp.concatenate([up, up], axis=0), preferred_element_type=f32)
    joined = []
    for c in range(blocks):
        block = base_ref[0, :, c * lanes : (c + 1) * lanes]
        for i in range(1, shards):
            block = block + packet_refs[i][c * rows : (c + 1) * rows, :].astype(f32)
        joined.append(block + adapter_scale * raised_up[:, c * lanes : (c + 1) * lanes])

    all_rows = row_count * seen
    seen_by = lax.broadcasted_iota(jnp.int32, (all_rows, rows), 0)
    made_by = lax.broadcasted_iota(jnp.int32, (all_rows, rows), 1)
    visible = (seen_by // seen == made_by % row_count) & (
        made_by // row_count <= seen_by % seen // group
    )
    for h in range(head_count):
        raw_key = joined[2 * h]
        mean_square = jnp.mean(raw_key * raw_key, axis=1, keepdims=True)
        normed = raw_key * lax.rsqrt(mean_square + norm_eps) * gain_ref[...]
        key = normed * cosine_ref[...] + pltpu.roll(normed, lanes // 2, 1) * sine_ref[...]
        key = key.astype(bf16)
        value = joined[2 * h + 1].astype(bf16)
        keys_ref[:, h * lanes : (h + 1) * lanes] = key
        values_ref[:, h * lanes : (h + 1) * lanes] = value
        mine = slice(h * all_rows, (h + 1) * all_rows)
        score = lax.dot_general(
            grouped_ref[mine, :], key, (((1,), (1,)), ((), ())), preferred_element_type=f32
        )
        score = jnp.where(visible, score * scale, masked_score)
        old_peak = peak_ref[mine, :]
        peak = jnp.maximum(old_peak, jnp.max(score, axis=1, keepdims=True))
        fade = jnp.exp(old_peak - peak)
        lifted = jnp.exp(score - peak[:, :rows])
        denominator = fade * sum_ref[mine, :] + jnp.sum(lifted, axis=1, keepdims=True)
        total = fade * total_ref[mine, :] + jnp.dot(
            lifted.astype(bf16), value, preferred_element_type=f32
        )
        ordered[mine, :] = total / denominator
    for pair in range(step_count // 2):
        for q in range(head_count * group):
            h, g = q // group, q % group
            both = [
                ordered[
                    pl.ds(
                        h * all_rows + (pair * 2 + side) * group + g, row_count, stride=seen
                    ),
                    :,
                ]
                for side in range(2)
            ]
            attention_ref[
                pair * 2 * row_count : (pair + 1) * 2 * row_count, q * lanes : (q + 1) * lanes
            ] = jnp.concatenate(both, axis=0).astype(bf16)


def finish(partials, gain, packets, rank, step_count, row_count, query_width):
    base, grouped, total, peak, denominator, cosine, sine = partials
    shards, rows, own = base.shape
    head_count = own // (2 * lanes)
    return pl.pallas_call(
        functools.partial(finish_kernel, step_count, row_count, head_count, shards),
        out_shape=(
            jax.ShapeDtypeStruct((rows, query_width), bf16),
            jax.ShapeDtypeStruct((rows, head_count * lanes), bf16),
            jax.ShapeDtypeStruct((rows, head_count * lanes), bf16),
        ),
        in_specs=[whole_in_vmem] * (8 + shards),
        out_specs=(whole_in_vmem,) * 3,
        scratch_shapes=[
            pltpu.VMEM((rank, own), f32),
            pltpu.VMEM(total.shape, f32),
        ],
        name="finish",
        cost_estimate=pl.CostEstimate(flops=0, bytes_accessed=1000000, transcendentals=0),
    )(base, gain, grouped, total, peak, denominator, cosine, sine, *packets)


def per_device(
    normed_tokens,
    key_value_weight,
    adapter_down,
    adapter_up,
    key_gain,
    queries,
    cache_keys,
    stored_values,
    lengths,
    owners,
):
    replicas = lax.axis_size("rollout")
    shards = lax.axis_size("tensor")
    down_rows, rank = adapter_down.shape
    step_count, row_count, depth = normed_tokens.shape
    own = key_value_weight.shape[1] // shards
    rank_part = rank // shards
    rows = step_count * row_count
    tokens = normed_tokens.reshape(rows, depth)
    query_rows = queries.reshape(rows, -1)

    fits = (
        replicas <= 4 and adapter_up.shape[1] == own and down_rows % 32 == 0 and rank_part % 16 == 0
    )
    if fits:
        packed = pack(adapter_down, adapter_up, rank_part)
        pieces = [packed] + [swap(packed, "rollout", i) for i in range(1, replicas)]
    partials = front(
        lengths, tokens, query_rows, key_value_weight, cache_keys, stored_values, step_count, shards
    )
    base = partials[0]
    if fits:
        packets = route(owners, tokens, base, pieces, down_rows, rank)
    else:
        packets = route_plain(owners, tokens, base, adapter_down, adapter_up, rank_part)
    packets = [packets[0]] + [swap(packets[i], "tensor", i) for i in range(1, shards)]
    attention, keys, values = finish(
        partials, key_gain.reshape(1, -1), packets, rank, step_count, row_count, query_rows.shape[1]
    )
    return tuple(a.reshape(step_count, row_count, -1) for a in (attention, keys, values))


def solution(mesh):
    placed = (
        P(None, ("job", "rollout"), "tensor"),
        P("tensor", None),
        P(("job", "rollout", "tensor"), None),
        P(None, ("job", "rollout")),
        P(),
        P(None, ("job", "rollout"), "tensor"),
        P(("job", "rollout"), None, "tensor"),
        P(("job", "rollout"), None, "tensor"),
        P(("job", "rollout")),
        P("job"),
    )
    return jax.shard_map(
        per_device,
        mesh=mesh,
        in_specs=placed,
        out_specs=(
            P(None, ("job", "rollout"), "tensor"),
            P(None, ("job", "rollout"), "tensor"),
            P(None, ("job", "rollout"), "tensor"),
        ),
        check_vma=False,
    )
```

```python
import functools
import math

import jax
import jax.numpy as jnp
from jax import lax
from jax.experimental import pallas as pl
from jax.experimental.pallas import tpu as pltpu
from jax.sharding import PartitionSpec as P

norm_eps = 1e-06
rope_base = 1000000.0
adapter_scale = 2.0
masked_score = -1e30
lanes = 128
f32 = jnp.float32
bf16 = jnp.bfloat16

whole_in_vmem = pl.BlockSpec(memory_space=pltpu.VMEM)
whole_in_smem = pl.BlockSpec(memory_space=pltpu.SMEM)
stays_in_hbm = pl.BlockSpec(memory_space=pltpu.HBM)


def swap(block, axis, offset):
    count = lax.axis_size(axis)
    return lax.ppermute(block, axis, [(s, s ^ offset) for s in range(count)])


def in_hbm(*arrays):
    return tuple(pltpu.with_memory_space_constraint(a, pltpu.HBM) for a in arrays)


def side_by_side(rows_of_blocks):
    r, c = rows_of_blocks.shape
    return rows_of_blocks.reshape(r, c // lanes, lanes).transpose(1, 0, 2).reshape(-1, lanes)


def split_halves(total):
    high = total.astype(bf16)
    return high, (total - high.astype(f32)).astype(bf16)


def pack_kernel(down_hbm, up_hbm, out_ref, down_ref, up_ref, sems):
    rank, down_rows = down_ref.shape
    rank_part = up_ref.shape[0]
    start = pl.multiple_of(lax.axis_index("tensor") * rank_part, rank_part)
    copies = [
        pltpu.make_async_copy(down_hbm, down_ref, sems.at[0]),
        pltpu.make_async_copy(up_hbm.at[pl.ds(start, rank_part), :], up_ref, sems.at[1]),
    ]
    for copy in copies:
        copy.start()
    for copy in copies:
        copy.wait()
    first = 0
    for c in range(down_rows // lanes):
        out_ref[first : first + rank, :] = down_ref[:, c * lanes : (c + 1) * lanes]
        first += rank
    rest = down_rows % lanes
    if rest:
        half = rank // 2
        tail = down_ref[:, down_rows - rest :]
        out_ref[first : first + half, :] = jnp.concatenate([tail[:half], tail[half:]], axis=1)
        first += half
    for c in range(up_ref.shape[1] // lanes):
        out_ref[first : first + rank_part, :] = up_ref[:, c * lanes : (c + 1) * lanes]
        first += rank_part


def pack(down, up, rank_part):
    rows = (down.size + rank_part * up.shape[1]) // lanes
    return pl.pallas_call(
        pack_kernel,
        out_shape=jax.ShapeDtypeStruct((rows, lanes), bf16),
        in_specs=[stays_in_hbm] * 2,
        out_specs=whole_in_vmem,
        scratch_shapes=[
            pltpu.VMEM(down.shape, bf16),
            pltpu.VMEM((rank_part, up.shape[1]), bf16),
            pltpu.SemaphoreType.DMA((2,)),
        ],
        compiler_params=pltpu.CompilerParams(vmem_limit_bytes=2 * 2**20),
        name="pack",
        cost_estimate=pl.CostEstimate(flops=0, bytes_accessed=200000, transcendentals=0),
    )(*in_hbm(down, up))


def project_kernel(
    step_count,
    row_count,
    head_count,
    shards,
    lengths_hbm,
    tokens_hbm,
    queries_hbm,
    weight_hbm,
    own_ref,
    base_ref,
    grouped_ref,
    cosine_ref,
    sine_ref,
    lengths_ref,
    tokens_ref,
    queries_ref,
    weight_ref,
    regroup,
    sems,
    weight_sems,
):
    shard = lax.axis_index("tensor")
    rows, own = own_ref.shape
    group = queries_ref.shape[1] // (head_count * lanes)
    seen = step_count * group
    lengths_copy = pltpu.make_async_copy(lengths_hbm, lengths_ref, sems.at[0])
    queries_copy = pltpu.make_async_copy(queries_hbm, queries_ref, sems.at[1])
    tokens_copy = pltpu.make_async_copy(tokens_hbm, tokens_ref, sems.at[2])
    weight_copies = [
        pltpu.make_async_copy(
            weight_hbm.at[:, pl.ds(pl.multiple_of((shard ^ i) * own, lanes), own)],
            weight_ref.at[i],
            weight_sems.at[i],
        )
        for i in range(shards)
    ]
    for copy in [lengths_copy, queries_copy, tokens_copy] + weight_copies:
        copy.start()

    lengths_copy.wait()
    row = lax.broadcasted_iota(jnp.int32, (rows, lanes), 0)
    lane = lax.broadcasted_iota(jnp.int32, (rows, lanes), 1)
    position = row // row_count
    for b in range(row_count):
        position = position + jnp.where(row % row_count == b, lengths_ref[b], 0)
    middle = lanes // 2
    spacing = (lane % middle).astype(f32) * (-2.0 / lanes * math.log(rope_base))
    angles = position.astype(f32) * jnp.exp(spacing)
    cosine_ref[...] = jnp.cos(angles)
    sine = jnp.sin(angles)
    sine_ref[...] = jnp.where(lane < middle, -sine, sine)

    queries_copy.wait()
    for pair in range(step_count // 2):
        for q in range(head_count * group):
            h, g = q // group, q % group
            both = queries_ref[
                pair * 2 * row_count : (pair + 1) * 2 * row_count, q * lanes : (q + 1) * lanes
            ].astype(f32)
            for side in range(2):
                first = h * row_count * seen + (pair * 2 + side) * group + g
                regroup[pl.ds(first, row_count, stride=seen), :] = both[
                    side * row_count : (side + 1) * row_count, :
                ]
    grouped_ref[...] = regroup[...].astype(bf16)

    tokens_copy.wait()
    for i in range(shards):
        weight_copies[i].wait()
        block = jnp.dot(tokens_ref[...], weight_ref[i], preferred_element_type=f32)
        if i == 0:
            own_ref[...] = block
            continue
        for c in range(own // lanes):
            base_ref[i - 1, c * rows : (c + 1) * rows, :] = block[
                :, c * lanes : (c + 1) * lanes
            ].astype(bf16)


def project(lengths, tokens, queries, weight, step_count, head_count, shards):
    rows, depth = tokens.shape
    columns = weight.shape[1]
    own = columns // shards
    seen_rows = rows * queries.shape[1] // lanes
    table = jax.ShapeDtypeStruct((rows, lanes), f32)
    return pl.pallas_call(
        functools.partial(project_kernel, step_count, rows // step_count, head_count, shards),
        out_shape=(
            jax.ShapeDtypeStruct((rows, own), f32),
            jax.ShapeDtypeStruct((shards - 1, rows * own // lanes, lanes), bf16),
            jax.ShapeDtypeStruct((seen_rows, lanes), bf16),
            table,
            table,
        ),
        in_specs=[stays_in_hbm] * 4,
        out_specs=(whole_in_vmem,) * 5,
        scratch_shapes=[
            pltpu.SMEM(lengths.shape, jnp.int32),
            pltpu.VMEM(tokens.shape, bf16),
            pltpu.VMEM(queries.shape, bf16),
            pltpu.VMEM((shards, depth, own), bf16),
            pltpu.VMEM((seen_rows, lanes), f32),
            pltpu.SemaphoreType.DMA((3,)),
            pltpu.SemaphoreType.DMA((shards,)),
        ],
        compiler_params=pltpu.CompilerParams(vmem_limit_bytes=12 * 2**20),
        name="project",
        cost_estimate=pl.CostEstimate(
            flops=2 * rows * weight.size, bytes_accessed=2 * weight.size, transcendentals=0
        ),
    )(*in_hbm(lengths, tokens, queries, weight))


def attend_kernel(
    head_count,
    lengths_hbm,
    grouped_ref,
    keys_hbm,
    values_hbm,
    total_ref,
    peak_ref,
    sum_ref,
    lengths_ref,
    keys_ref,
    values_ref,
    scores,
    raised,
    length_sem,
    key_sems,
    value_sems,
):
    row_count, slots, _ = keys_ref.shape
    seen = grouped_ref.shape[0] // (head_count * row_count)
    scale = lanes**-0.5
    lengths_copy = pltpu.make_async_copy(lengths_hbm, lengths_ref, length_sem)
    key_copies = [
        pltpu.make_async_copy(keys_hbm.at[b], keys_ref.at[b], key_sems.at[b])
        for b in range(row_count)
    ]
    value_copies = [
        pltpu.make_async_copy(values_hbm.at[b], values_ref.at[b], value_sems.at[b])
        for b in range(row_count)
    ]
    for copy in [lengths_copy] + key_copies + value_copies:
        copy.start()
    lengths_copy.wait()

    def place(h, b):
        at = (h * row_count + b) * seen
        return slice(at, at + seen)

    for b in range(row_count):
        key_copies[b].wait()
        for h in range(head_count):
            scores[place(h, b), :] = lax.dot_general(
                grouped_ref[place(h, b), :],
                keys_ref[b, :, h * lanes : (h + 1) * lanes],
                (((1,), (1,)), ((), ())),
                preferred_element_type=f32,
            )
    for copy in value_copies:
        copy.wait()
    slot = lax.broadcasted_iota(jnp.int32, (seen, slots), 1)
    for b in range(row_count):
        live = slot < lengths_ref[b]
        for h in range(head_count):
            score = jnp.where(live, scores[place(h, b), :] * scale, masked_score)
            peak = jnp.max(score, axis=1, keepdims=True)
            lifted = jnp.exp(score - peak)
            raised[place(h, b), :] = lifted.astype(bf16)
            peak_ref[place(h, b), :] = jnp.broadcast_to(peak, (seen, lanes))
            sum_ref[place(h, b), :] = jnp.broadcast_to(
                jnp.sum(lifted, axis=1, keepdims=True), (seen, lanes)
            )
    for b in range(row_count):
        for h in range(head_count):
            total_ref[place(h, b), :] = jnp.dot(
                raised[place(h, b), :],
                values_ref[b, :, h * lanes : (h + 1) * lanes],
                preferred_element_type=f32,
            )


def attend(lengths, grouped, keys, values):
    row_count, slots, width = keys.shape
    seen_rows = grouped.shape[0]
    seen_table = jax.ShapeDtypeStruct((seen_rows, lanes), f32)
    lengths, keys, values = in_hbm(lengths, keys, values)
    return pl.pallas_call(
        functools.partial(attend_kernel, width // lanes),
        out_shape=(seen_table,) * 3,
        in_specs=[stays_in_hbm, whole_in_vmem, stays_in_hbm, stays_in_hbm],
        out_specs=(whole_in_vmem,) * 3,
        scratch_shapes=[
            pltpu.SMEM(lengths.shape, jnp.int32),
            pltpu.VMEM(keys.shape, bf16),
            pltpu.VMEM(values.shape, bf16),
            pltpu.VMEM((seen_rows, slots), f32),
            pltpu.VMEM((seen_rows, slots), bf16),
            pltpu.SemaphoreType.DMA,
            pltpu.SemaphoreType.DMA((row_count,)),
            pltpu.SemaphoreType.DMA((row_count,)),
        ],
        compiler_params=pltpu.CompilerParams(vmem_limit_bytes=12 * 2**20),
        name="attend",
        cost_estimate=pl.CostEstimate(
            flops=4 * seen_rows * slots * lanes,
            bytes_accessed=2 * (keys.size + values.size),
            transcendentals=seen_rows * slots,
        ),
    )(lengths, grouped, keys, values)


def route_kernel(replicas, shards, *refs):
    owners_ref, tokens_ref, base_ref = refs[:3]
    piece_refs = refs[3 : 3 + replicas]
    out_refs = refs[3 + replicas : 3 + replicas + shards]
    token_buf, left, right, up_buf = refs[3 + replicas + shards :]
    replica = lax.axis_index("rollout")
    shard = lax.axis_index("tensor")
    rows, depth = tokens_ref.shape
    rank = right.shape[0]
    down_rows = depth // replicas
    width = token_buf.shape[2]
    rest = down_rows % lanes
    for k in range(replicas):
        token_buf[k, :, :down_rows] = tokens_ref[:, k * down_rows : (k + 1) * down_rows]
        if rest:
            token_buf[k, :, down_rows:] = jnp.zeros((rows, width - down_rows), bf16)
    for i in range(replicas):
        source = replica ^ i
        place = jnp.int32(0)
        for k in range(1, replicas):
            place = place + jnp.where(owners_ref[k] == source, k, 0)
        left[:, i * width : (i + 1) * width] = token_buf[place]
        first = 0
        for c in range(down_rows // lanes):
            right[:, i * width + c * lanes : i * width + (c + 1) * lanes] = piece_refs[i][
                first : first + rank, :
            ]
            first += rank
        if rest:
            both = piece_refs[i][first : first + rank // 2, :]
            tail = jnp.concatenate([both[:, :rest], both[:, rest:]], axis=0)
            right[:, (i + 1) * width - lanes : (i + 1) * width] = jnp.concatenate(
                [tail, jnp.zeros((rank, lanes - rest), bf16)], axis=1
            )
            first += rank // 2
        up_buf[i] = piece_refs[i][first:, :]
    lowered = lax.dot_general(
        left[...], right[...], (((1,), (1,)), ((), ())), preferred_element_type=f32
    )
    both = jnp.concatenate(split_halves(lowered), axis=1)
    for i in range(shards):
        first = 0
        if i:
            first = base_ref.shape[1]
            out_refs[i][:first, :] = base_ref[i - 1]
        out_refs[i][first : first + rows, :] = both
        out_refs[i][first + rows :, :] = up_buf[owners_ref[shard ^ i] ^ replica]


def route(owners, tokens, base, pieces, rank, up_rows):
    rows, depth = tokens.shape
    shards = base.shape[0] + 1
    replicas = len(pieces)
    sent = base.shape[1]
    width = -(-depth // replicas // lanes) * lanes
    return pl.pallas_call(
        functools.partial(route_kernel, replicas, shards),
        out_shape=[
            jax.ShapeDtypeStruct(((sent if i else 0) + rows + up_rows, lanes), bf16)
            for i in range(shards)
        ],
        in_specs=[whole_in_smem] + [whole_in_vmem] * (2 + replicas),
        out_specs=[whole_in_vmem] * shards,
        scratch_shapes=[
            pltpu.VMEM((replicas, rows, width), bf16),
            pltpu.VMEM((rows, replicas * width), bf16),
            pltpu.VMEM((rank, replicas * width), bf16),
            pltpu.VMEM((replicas, up_rows, lanes), bf16),
        ],
        compiler_params=pltpu.CompilerParams(vmem_limit_bytes=4 * 2**20),
        name="route",
        cost_estimate=pl.CostEstimate(flops=0, bytes_accessed=800000, transcendentals=0),
    )(owners, tokens, base, *pieces)


def route_plain(owners, tokens, base, down, up, rank_part, own):
    shards = base.shape[0] + 1
    rank = down.shape[1]
    shard = lax.axis_index("tensor")
    first = shard * rank_part
    up_part = lax.dynamic_slice_in_dim(up, first, rank_part, axis=0)
    downs = lax.all_gather(down, "rollout", axis=0, tiled=False)
    ups = lax.all_gather(up_part, "rollout", axis=0, tiled=False)
    down_matrix = jnp.take(downs, owners, axis=0, mode="clip").reshape(-1, rank)
    up_matrix = jnp.take(ups, owners, axis=0, mode="clip").transpose(1, 0, 2)
    up_matrix = up_matrix.reshape(rank_part, -1)
    lowered = jnp.dot(tokens, down_matrix, preferred_element_type=f32)
    both = jnp.concatenate(split_halves(lowered), axis=1)
    packets = []
    for i in range(shards):
        up_block = lax.dynamic_slice_in_dim(up_matrix, (shard ^ i) * own, own, axis=1)
        parts = [both, side_by_side(up_block)]
        if i:
            parts = [base[i - 1]] + parts
        packets.append(jnp.concatenate(parts, axis=0))
    return packets


def finish_kernel(step_count, row_count, head_count, shards, *refs):
    own_ref, gain_ref, grouped_ref, total_ref, peak_ref, sum_ref, cosine_ref, sine_ref = refs[:8]
    packet_refs = refs[8 : 8 + shards]
    attention_ref, keys_ref, values_ref = refs[8 + shards : 11 + shards]
    up_buf, ordered = refs[11 + shards :]
    shard = lax.axis_index("tensor")
    rows = step_count * row_count
    own = own_ref.shape[1]
    blocks = own // lanes
    rank = up_buf.shape[0]
    rank_part = rank // shards
    group = grouped_ref.shape[0] // (head_count * rows)
    seen = step_count * group
    scale = lanes**-0.5

    lowered = jnp.zeros((rows, lanes), f32)
    for i in range(shards):
        first = rows * blocks if i else 0
        lowered = lowered + packet_refs[i][first : first + rows, :].astype(f32)
        ups = packet_refs[i][first + rows :, :].astype(f32)
        at = pl.multiple_of((shard ^ i) * rank_part, rank_part)
        for c in range(blocks):
            up_buf[pl.ds(at, rank_part), c * lanes : (c + 1) * lanes] = ups[
                c * rank_part : (c + 1) * rank_part, :
            ]
    lane = lax.broadcasted_iota(jnp.int32, (rows, lanes), 1)
    lowered = lowered + pltpu.roll(lowered, rank, 1)
    high, low = split_halves(lowered)
    left = jnp.where(lane < rank, high.astype(f32), low.astype(f32)).astype(bf16)
    up = up_buf[...].astype(bf16)
    raised_up = jnp.dot(left, jnp.concatenate([up, up], axis=0), preferred_element_type=f32)
    joined = []
    for c in range(blocks):
        block = own_ref[:, c * lanes : (c + 1) * lanes]
        for i in range(1, shards):
            block = block + packet_refs[i][c * rows : (c + 1) * rows, :].astype(f32)
        joined.append(block + adapter_scale * raised_up[:, c * lanes : (c + 1) * lanes])

    all_rows = row_count * seen
    seen_by = lax.broadcasted_iota(jnp.int32, (all_rows, rows), 0)
    made_by = lax.broadcasted_iota(jnp.int32, (all_rows, rows), 1)
    visible = (seen_by // seen == made_by % row_count) & (
        made_by // row_count <= seen_by % seen // group
    )
    for h in range(head_count):
        raw_key = joined[2 * h]
        mean_square = jnp.mean(raw_key * raw_key, axis=1, keepdims=True)
        normed = raw_key * lax.rsqrt(mean_square + norm_eps) * gain_ref[...]
        key = normed * cosine_ref[...] + pltpu.roll(normed, lanes // 2, 1) * sine_ref[...]
        key = key.astype(bf16)
        value = joined[2 * h + 1].astype(bf16)
        keys_ref[:, h * lanes : (h + 1) * lanes] = key
        values_ref[:, h * lanes : (h + 1) * lanes] = value
        mine = slice(h * all_rows, (h + 1) * all_rows)
        score = lax.dot_general(
            grouped_ref[mine, :], key, (((1,), (1,)), ((), ())), preferred_element_type=f32
        )
        score = jnp.where(visible, score * scale, masked_score)
        old_peak = peak_ref[mine, :]
        peak = jnp.maximum(old_peak, jnp.max(score, axis=1, keepdims=True))
        fade = jnp.exp(old_peak - peak)
        lifted = jnp.exp(score - peak[:, :rows])
        denominator = fade * sum_ref[mine, :] + jnp.sum(lifted, axis=1, keepdims=True)
        total = fade * total_ref[mine, :] + jnp.dot(
            lifted.astype(bf16), value, preferred_element_type=f32
        )
        ordered[mine, :] = total / denominator
    for pair in range(step_count // 2):
        for q in range(head_count * group):
            h, g = q // group, q % group
            both = [
                ordered[
                    pl.ds(
                        h * all_rows + (pair * 2 + side) * group + g, row_count, stride=seen
                    ),
                    :,
                ]
                for side in range(2)
            ]
            attention_ref[
                pair * 2 * row_count : (pair + 1) * 2 * row_count, q * lanes : (q + 1) * lanes
            ] = jnp.concatenate(both, axis=0).astype(bf16)


def finish(partials, gain, packets, rank, step_count, row_count, query_width):
    mine, grouped, total, peak, denominator, cosine, sine = partials
    rows, own = mine.shape
    shards = len(packets)
    head_count = own // (2 * lanes)
    return pl.pallas_call(
        functools.partial(finish_kernel, step_count, row_count, head_count, shards),
        out_shape=(
            jax.ShapeDtypeStruct((rows, query_width), bf16),
            jax.ShapeDtypeStruct((rows, head_count * lanes), bf16),
            jax.ShapeDtypeStruct((rows, head_count * lanes), bf16),
        ),
        in_specs=[whole_in_vmem] * (8 + shards),
        out_specs=(whole_in_vmem,) * 3,
        scratch_shapes=[
            pltpu.VMEM((rank, own), f32),
            pltpu.VMEM(total.shape, f32),
        ],
        compiler_params=pltpu.CompilerParams(vmem_limit_bytes=6 * 2**20),
        name="finish",
        cost_estimate=pl.CostEstimate(flops=0, bytes_accessed=1000000, transcendentals=0),
    )(mine, gain, grouped, total, peak, denominator, cosine, sine, *packets)


def per_device(
    normed_tokens,
    key_value_weight,
    adapter_down,
    adapter_up,
    key_gain,
    queries,
    cache_keys,
    stored_values,
    lengths,
    owners,
):
    replicas = lax.axis_size("rollout")
    shards = lax.axis_size("tensor")
    down_rows, rank = adapter_down.shape
    step_count, row_count, depth = normed_tokens.shape
    own = key_value_weight.shape[1] // shards
    rank_part = rank // shards
    rows = step_count * row_count
    tokens = normed_tokens.reshape(rows, depth)
    query_rows = queries.reshape(rows, -1)

    fits = (
        replicas <= 4
        and adapter_up.shape[1] == own
        and down_rows % lanes in (0, lanes // 2)
        and rank == lanes // 2
        and rank_part % 16 == 0
    )
    if fits:
        packed = pack(adapter_down.T, adapter_up, rank_part)
        arrived = {i: swap(packed, "rollout", i) for i in reversed(range(1, replicas))}
        pieces = [packed] + [arrived[i] for i in range(1, replicas)]
    head_count = cache_keys.shape[2] // lanes
    mine, base, grouped, cosine, sine = project(
        lengths, tokens, query_rows, key_value_weight, step_count, head_count, shards
    )
    if fits:
        packets = route(owners, tokens, base, pieces, rank, rank_part * own // lanes)
    else:
        packets = route_plain(owners, tokens, base, adapter_down, adapter_up, rank_part, own)
    arrived = {i: swap(packets[i], "tensor", i) for i in reversed(range(1, shards))}
    packets = [packets[0]] + [arrived[i] for i in range(1, shards)]
    total, peak, denominator = attend(lengths, grouped, cache_keys, stored_values)
    attention, keys, values = finish(
        (mine, grouped, total, peak, denominator, cosine, sine),
        key_gain.reshape(1, -1),
        packets,
        rank,
        step_count,
        row_count,
        query_rows.shape[1],
    )
    return tuple(a.reshape(step_count, row_count, -1) for a in (attention, keys, values))


def solution(mesh):
    placed = (
        P(None, ("job", "rollout"), "tensor"),
        P("tensor", None),
        P(("job", "rollout", "tensor"), None),
        P(None, ("job", "rollout")),
        P(),
        P(None, ("job", "rollout"), "tensor"),
        P(("job", "rollout"), None, "tensor"),
        P(("job", "rollout"), None, "tensor"),
        P(("job", "rollout")),
        P("job"),
    )
    return jax.shard_map(
        per_device,
        mesh=mesh,
        in_specs=placed,
        out_specs=(
            P(None, ("job", "rollout"), "tensor"),
            P(None, ("job", "rollout"), "tensor"),
            P(None, ("job", "rollout"), "tensor"),
        ),
        check_vma=False,
    )
```

```python
import functools
import math

import jax
import jax.numpy as jnp
from jax import lax
from jax.experimental import pallas as pl
from jax.experimental.pallas import tpu as pltpu
from jax.sharding import PartitionSpec as P

norm_eps = 1e-06
rope_base = 1000000.0
adapter_scale = 2.0
masked_score = -1e30
lanes = 128
f32 = jnp.float32
bf16 = jnp.bfloat16

whole_in_vmem = pl.BlockSpec(memory_space=pltpu.VMEM)
whole_in_smem = pl.BlockSpec(memory_space=pltpu.SMEM)
stays_in_hbm = pl.BlockSpec(memory_space=pltpu.HBM)


def swap(block, axis, offset):
    count = lax.axis_size(axis)
    return lax.ppermute(block, axis, [(s, s ^ offset) for s in range(count)])


def in_hbm(*arrays):
    return tuple(pltpu.with_memory_space_constraint(a, pltpu.HBM) for a in arrays)


def side_by_side(rows_of_blocks):
    r, c = rows_of_blocks.shape
    return rows_of_blocks.reshape(r, c // lanes, lanes).transpose(1, 0, 2).reshape(-1, lanes)


def split_halves(total):
    high = total.astype(bf16)
    return high, (total - high.astype(f32)).astype(bf16)


def pack_kernel(down_hbm, up_hbm, out_ref, down_ref, up_ref, sems):
    rank, down_rows = down_ref.shape
    rank_part = up_ref.shape[0]
    start = pl.multiple_of(lax.axis_index("tensor") * rank_part, rank_part)
    copies = [
        pltpu.make_async_copy(down_hbm, down_ref, sems.at[0]),
        pltpu.make_async_copy(up_hbm.at[pl.ds(start, rank_part), :], up_ref, sems.at[1]),
    ]
    for copy in copies:
        copy.start()
    for copy in copies:
        copy.wait()
    first = 0
    for c in range(down_rows // lanes):
        out_ref[first : first + rank, :] = down_ref[:, c * lanes : (c + 1) * lanes]
        first += rank
    rest = down_rows % lanes
    if rest:
        half = rank // 2
        tail = down_ref[:, down_rows - rest :]
        out_ref[first : first + half, :] = jnp.concatenate([tail[:half], tail[half:]], axis=1)
        first += half
    for c in range(up_ref.shape[1] // lanes):
        out_ref[first : first + rank_part, :] = up_ref[:, c * lanes : (c + 1) * lanes]
        first += rank_part


def pack(down, up, rank_part, beside):
    rows = (down.size + rank_part * up.shape[1]) // lanes
    return pl.pallas_call(
        pack_kernel,
        out_shape=jax.ShapeDtypeStruct((rows, lanes), bf16),
        in_specs=[stays_in_hbm] * 2,
        out_specs=whole_in_vmem,
        scratch_shapes=[
            pltpu.VMEM(down.shape, bf16),
            pltpu.VMEM((rank_part, up.shape[1]), bf16),
            pltpu.SemaphoreType.DMA((2,)),
        ],
        compiler_params=pltpu.CompilerParams(vmem_limit_bytes=2 * 2**20),
        name="pack",
        cost_estimate=beside,
    )(*in_hbm(down, up))


def front_kernel(
    step_count,
    row_count,
    head_count,
    shards,
    lengths_hbm,
    tokens_ref,
    queries_ref,
    weight_ref,
    keys_ref,
    values_ref,
    own_ref,
    base_ref,
    grouped_ref,
    total_ref,
    peak_ref,
    sum_ref,
    cosine_ref,
    sine_ref,
    lengths_ref,
    regroup,
    scores,
    raised,
    length_sem,
):
    lengths_copy = pltpu.make_async_copy(lengths_hbm, lengths_ref, length_sem)
    lengths_copy.start()
    shard = lax.axis_index("tensor")
    rows, own = own_ref.shape
    slots = keys_ref.shape[1]
    group = queries_ref.shape[1] // (head_count * lanes)
    seen = step_count * group
    scale = lanes**-0.5

    def product(i):
        first = pl.multiple_of((shard ^ i) * own, lanes)
        block = jnp.dot(
            tokens_ref[...], weight_ref[:, pl.ds(first, own)], preferred_element_type=f32
        )
        if i == 0:
            own_ref[...] = block
            return
        for c in range(own // lanes):
            base_ref[i - 1, c * rows : (c + 1) * rows, :] = block[
                :, c * lanes : (c + 1) * lanes
            ].astype(bf16)

    for pair in range(step_count // 2):
        for q in range(head_count * group):
            h, g = q // group, q % group
            both = queries_ref[
                pair * 2 * row_count : (pair + 1) * 2 * row_count, q * lanes : (q + 1) * lanes
            ].astype(f32)
            for side in range(2):
                first = h * row_count * seen + (pair * 2 + side) * group + g
                regroup[pl.ds(first, row_count, stride=seen), :] = both[
                    side * row_count : (side + 1) * row_count, :
                ]
    grouped_ref[...] = regroup[...].astype(bf16)

    def place(h, b):
        at = (h * row_count + b) * seen
        return slice(at, at + seen)

    def score_row(b):
        for h in range(head_count):
            scores[place(h, b), :] = lax.dot_general(
                grouped_ref[place(h, b), :],
                keys_ref[b, :, h * lanes : (h + 1) * lanes],
                (((1,), (1,)), ((), ())),
                preferred_element_type=f32,
            )

    slot = lax.broadcasted_iota(jnp.int32, (seen, slots), 1)

    def lift_row(b):
        live = slot < lengths_ref[b]
        for h in range(head_count):
            score = jnp.where(live, scores[place(h, b), :] * scale, masked_score)
            peak = jnp.max(score, axis=1, keepdims=True)
            lifted = jnp.exp(score - peak)
            raised[place(h, b), :] = lifted.astype(bf16)
            peak_ref[place(h, b), :] = jnp.broadcast_to(peak, (seen, lanes))
            sum_ref[place(h, b), :] = jnp.broadcast_to(
                jnp.sum(lifted, axis=1, keepdims=True), (seen, lanes)
            )

    def weigh_row(b):
        for h in range(head_count):
            total_ref[place(h, b), :] = jnp.dot(
                raised[place(h, b), :],
                values_ref[b, :, h * lanes : (h + 1) * lanes],
                preferred_element_type=f32,
            )

    for b in range(row_count):
        score_row(b)
    lengths_copy.wait()
    for b in range(row_count):
        lift_row(b)
        if b < shards:
            product(b)
    for i in range(row_count, shards):
        product(i)
    for b in range(row_count):
        weigh_row(b)

    row = lax.broadcasted_iota(jnp.int32, (rows, lanes), 0)
    lane = lax.broadcasted_iota(jnp.int32, (rows, lanes), 1)
    position = row // row_count
    for b in range(row_count):
        position = position + jnp.where(row % row_count == b, lengths_ref[b], 0)
    middle = lanes // 2
    spacing = (lane % middle).astype(f32) * (-2.0 / lanes * math.log(rope_base))
    angles = position.astype(f32) * jnp.exp(spacing)
    cosine_ref[...] = jnp.cos(angles)
    sine = jnp.sin(angles)
    sine_ref[...] = jnp.where(lane < middle, -sine, sine)

def front(lengths, tokens, queries, weight, keys, values, step_count, shards):
    row_count, slots, width = keys.shape
    head_count = width // lanes
    depth, columns = weight.shape
    own = columns // shards
    rows = step_count * row_count
    seen_rows = rows * queries.shape[1] // lanes
    table = jax.ShapeDtypeStruct((rows, lanes), f32)
    seen_table = jax.ShapeDtypeStruct((seen_rows, lanes), f32)
    return pl.pallas_call(
        functools.partial(front_kernel, step_count, row_count, head_count, shards),
        out_shape=(
            jax.ShapeDtypeStruct((rows, own), f32),
            jax.ShapeDtypeStruct((shards - 1, rows * own // lanes, lanes), bf16),
            jax.ShapeDtypeStruct((seen_rows, lanes), bf16),
            seen_table,
            seen_table,
            seen_table,
            table,
            table,
        ),
        in_specs=[stays_in_hbm] + [whole_in_vmem] * 5,
        out_specs=(whole_in_vmem,) * 8,
        scratch_shapes=[
            pltpu.SMEM(lengths.shape, jnp.int32),
            pltpu.VMEM((seen_rows, lanes), f32),
            pltpu.VMEM((seen_rows, slots), f32),
            pltpu.VMEM((seen_rows, slots), bf16),
            pltpu.SemaphoreType.DMA,
        ],
        compiler_params=pltpu.CompilerParams(vmem_limit_bytes=8 * 2**20),
        name="front",
        cost_estimate=pl.CostEstimate(
            flops=2 * rows * depth * columns + 4 * seen_rows * slots * lanes,
            bytes_accessed=2 * (weight.size + keys.size + values.size),
            transcendentals=seen_rows * slots,
        ),
    )(*in_hbm(lengths), tokens, queries, weight, keys, values)


def route_kernel(replicas, shards, *refs):
    owners_ref, tokens_ref, base_ref = refs[:3]
    piece_refs = refs[3 : 3 + replicas][::-1]
    out_refs = refs[3 + replicas : 3 + replicas + shards]
    token_buf, left, right, up_buf = refs[3 + replicas + shards :]
    replica = lax.axis_index("rollout")
    shard = lax.axis_index("tensor")
    rows, depth = tokens_ref.shape
    rank = right.shape[0]
    down_rows = depth // replicas
    width = token_buf.shape[2]
    rest = down_rows % lanes
    for k in range(replicas):
        token_buf[k, :, :down_rows] = tokens_ref[:, k * down_rows : (k + 1) * down_rows]
        if rest:
            token_buf[k, :, down_rows:] = jnp.zeros((rows, width - down_rows), bf16)
    for i in range(replicas):
        source = replica ^ i
        place = jnp.int32(0)
        for k in range(1, replicas):
            place = place + jnp.where(owners_ref[k] == source, k, 0)
        left[:, i * width : (i + 1) * width] = token_buf[place]
        first = 0
        for c in range(down_rows // lanes):
            right[:, i * width + c * lanes : i * width + (c + 1) * lanes] = piece_refs[i][
                first : first + rank, :
            ]
            first += rank
        if rest:
            both = piece_refs[i][first : first + rank // 2, :]
            tail = jnp.concatenate([both[:, :rest], both[:, rest:]], axis=0)
            right[:, (i + 1) * width - lanes : (i + 1) * width] = jnp.concatenate(
                [tail, jnp.zeros((rank, lanes - rest), bf16)], axis=1
            )
            first += rank // 2
        up_buf[i] = piece_refs[i][first:, :]
    lowered = lax.dot_general(
        left[...], right[...], (((1,), (1,)), ((), ())), preferred_element_type=f32
    )
    both = jnp.concatenate(split_halves(lowered), axis=1)
    for i in range(shards):
        first = 0
        if i:
            first = base_ref.shape[1]
            out_refs[i][:first, :] = base_ref[i - 1]
        out_refs[i][first : first + rows, :] = both
        out_refs[i][first + rows :, :] = up_buf[owners_ref[shard ^ i] ^ replica]


def route(owners, tokens, base, pieces, rank, up_rows):
    rows, depth = tokens.shape
    shards = base.shape[0] + 1
    replicas = len(pieces)
    sent = base.shape[1]
    width = -(-depth // replicas // lanes) * lanes
    return pl.pallas_call(
        functools.partial(route_kernel, replicas, shards),
        out_shape=[
            jax.ShapeDtypeStruct(((sent if i else 0) + rows + up_rows, lanes), bf16)
            for i in range(shards)
        ],
        in_specs=[whole_in_smem] + [whole_in_vmem] * (2 + replicas),
        out_specs=[whole_in_vmem] * shards,
        scratch_shapes=[
            pltpu.VMEM((replicas, rows, width), bf16),
            pltpu.VMEM((rows, replicas * width), bf16),
            pltpu.VMEM((rank, replicas * width), bf16),
            pltpu.VMEM((replicas, up_rows, lanes), bf16),
        ],
        compiler_params=pltpu.CompilerParams(vmem_limit_bytes=4 * 2**20),
        name="route",
        cost_estimate=pl.CostEstimate(flops=0, bytes_accessed=800000, transcendentals=0),
    )(owners, tokens, base, *pieces[::-1])


def route_plain(owners, tokens, base, down, up, rank_part, own):
    shards = base.shape[0] + 1
    rank = down.shape[1]
    shard = lax.axis_index("tensor")
    first = shard * rank_part
    up_part = lax.dynamic_slice_in_dim(up, first, rank_part, axis=0)
    downs = lax.all_gather(down, "rollout", axis=0, tiled=False)
    ups = lax.all_gather(up_part, "rollout", axis=0, tiled=False)
    down_matrix = jnp.take(downs, owners, axis=0, mode="clip").reshape(-1, rank)
    up_matrix = jnp.take(ups, owners, axis=0, mode="clip").transpose(1, 0, 2)
    up_matrix = up_matrix.reshape(rank_part, -1)
    lowered = jnp.dot(tokens, down_matrix, preferred_element_type=f32)
    both = jnp.concatenate(split_halves(lowered), axis=1)
    packets = []
    for i in range(shards):
        up_block = lax.dynamic_slice_in_dim(up_matrix, (shard ^ i) * own, own, axis=1)
        parts = [both, side_by_side(up_block)]
        if i:
            parts = [base[i - 1]] + parts
        packets.append(jnp.concatenate(parts, axis=0))
    return packets


def finish_kernel(step_count, row_count, head_count, shards, *refs):
    own_ref, gain_ref, grouped_ref, total_ref, peak_ref, sum_ref, cosine_ref, sine_ref = refs[:8]
    packet_refs = refs[8 : 8 + shards][::-1]
    attention_ref, keys_ref, values_ref = refs[8 + shards : 11 + shards]
    up_buf, ordered = refs[11 + shards :]
    shard = lax.axis_index("tensor")
    rows = step_count * row_count
    own = own_ref.shape[1]
    blocks = own // lanes
    rank = up_buf.shape[0]
    rank_part = rank // shards
    group = grouped_ref.shape[0] // (head_count * rows)
    seen = step_count * group
    scale = lanes**-0.5

    lowered = jnp.zeros((rows, lanes), f32)
    for i in range(shards):
        first = rows * blocks if i else 0
        lowered = lowered + packet_refs[i][first : first + rows, :].astype(f32)
        ups = packet_refs[i][first + rows :, :].astype(f32)
        at = pl.multiple_of((shard ^ i) * rank_part, rank_part)
        for c in range(blocks):
            up_buf[pl.ds(at, rank_part), c * lanes : (c + 1) * lanes] = ups[
                c * rank_part : (c + 1) * rank_part, :
            ]
    lane = lax.broadcasted_iota(jnp.int32, (rows, lanes), 1)
    lowered = lowered + pltpu.roll(lowered, rank, 1)
    high, low = split_halves(lowered)
    left = jnp.where(lane < rank, high.astype(f32), low.astype(f32)).astype(bf16)
    up = up_buf[...].astype(bf16)
    raised_up = jnp.dot(left, jnp.concatenate([up, up], axis=0), preferred_element_type=f32)
    joined = []
    for c in range(blocks):
        block = own_ref[:, c * lanes : (c + 1) * lanes]
        for i in range(1, shards):
            block = block + packet_refs[i][c * rows : (c + 1) * rows, :].astype(f32)
        joined.append(block + adapter_scale * raised_up[:, c * lanes : (c + 1) * lanes])

    all_rows = row_count * seen
    seen_by = lax.broadcasted_iota(jnp.int32, (all_rows, rows), 0)
    made_by = lax.broadcasted_iota(jnp.int32, (all_rows, rows), 1)
    visible = (seen_by // seen == made_by % row_count) & (
        made_by // row_count <= seen_by % seen // group
    )
    for h in range(head_count):
        raw_key = joined[2 * h]
        mean_square = jnp.mean(raw_key * raw_key, axis=1, keepdims=True)
        normed = raw_key * lax.rsqrt(mean_square + norm_eps) * gain_ref[...]
        key = normed * cosine_ref[...] + pltpu.roll(normed, lanes // 2, 1) * sine_ref[...]
        key = key.astype(bf16)
        value = joined[2 * h + 1].astype(bf16)
        keys_ref[:, h * lanes : (h + 1) * lanes] = key
        values_ref[:, h * lanes : (h + 1) * lanes] = value
        mine = slice(h * all_rows, (h + 1) * all_rows)
        score = lax.dot_general(
            grouped_ref[mine, :], key, (((1,), (1,)), ((), ())), preferred_element_type=f32
        )
        score = jnp.where(visible, score * scale, masked_score)
        old_peak = peak_ref[mine, :]
        peak = jnp.maximum(old_peak, jnp.max(score, axis=1, keepdims=True))
        fade = jnp.exp(old_peak - peak)
        lifted = jnp.exp(score - peak[:, :rows])
        denominator = fade * sum_ref[mine, :] + jnp.sum(lifted, axis=1, keepdims=True)
        total = fade * total_ref[mine, :] + jnp.dot(
            lifted.astype(bf16), value, preferred_element_type=f32
        )
        ordered[mine, :] = total / denominator
    for pair in range(step_count // 2):
        for q in range(head_count * group):
            h, g = q // group, q % group
            both = [
                ordered[
                    pl.ds(
                        h * all_rows + (pair * 2 + side) * group + g, row_count, stride=seen
                    ),
                    :,
                ]
                for side in range(2)
            ]
            attention_ref[
                pair * 2 * row_count : (pair + 1) * 2 * row_count, q * lanes : (q + 1) * lanes
            ] = jnp.concatenate(both, axis=0).astype(bf16)


def finish(partials, gain, packets, rank, step_count, row_count, query_width):
    mine, grouped, total, peak, denominator, cosine, sine = partials
    rows, own = mine.shape
    shards = len(packets)
    head_count = own // (2 * lanes)
    return pl.pallas_call(
        functools.partial(finish_kernel, step_count, row_count, head_count, shards),
        out_shape=(
            jax.ShapeDtypeStruct((rows, query_width), bf16),
            jax.ShapeDtypeStruct((rows, head_count * lanes), bf16),
            jax.ShapeDtypeStruct((rows, head_count * lanes), bf16),
        ),
        in_specs=[whole_in_vmem] * (8 + shards),
        out_specs=(whole_in_vmem,) * 3,
        scratch_shapes=[
            pltpu.VMEM((rank, own), f32),
            pltpu.VMEM(total.shape, f32),
        ],
        compiler_params=pltpu.CompilerParams(vmem_limit_bytes=6 * 2**20),
        name="finish",
        cost_estimate=pl.CostEstimate(flops=0, bytes_accessed=1000000, transcendentals=0),
    )(mine, gain, grouped, total, peak, denominator, cosine, sine, *packets[::-1])


def per_device(
    normed_tokens,
    key_value_weight,
    adapter_down,
    adapter_up,
    key_gain,
    queries,
    cache_keys,
    stored_values,
    lengths,
    owners,
):
    replicas = lax.axis_size("rollout")
    shards = lax.axis_size("tensor")
    down_rows, rank = adapter_down.shape
    step_count, row_count, depth = normed_tokens.shape
    own = key_value_weight.shape[1] // shards
    rank_part = rank // shards
    rows = step_count * row_count
    tokens = normed_tokens.reshape(rows, depth)
    query_rows = queries.reshape(rows, -1)

    fits = (
        replicas <= 4
        and adapter_up.shape[1] == own
        and down_rows % lanes in (0, lanes // 2)
        and rank == lanes // 2
        and rank_part % 16 == 0
    )
    if fits:
        fetched = 2 * (key_value_weight.size + cache_keys.size + stored_values.size)
        beside = pl.CostEstimate(flops=1000 * fetched, bytes_accessed=fetched, transcendentals=0)
        packed = pack(adapter_down.T, adapter_up, rank_part, beside)
        arrived = {i: swap(packed, "rollout", i) for i in reversed(range(1, replicas))}
        pieces = [packed] + [arrived[i] for i in range(1, replicas)]
    mine, base, *partials = front(
        lengths, tokens, query_rows, key_value_weight, cache_keys, stored_values, step_count, shards
    )
    if fits:
        packets = route(owners, tokens, base, pieces, rank, rank_part * own // lanes)
    else:
        packets = route_plain(owners, tokens, base, adapter_down, adapter_up, rank_part, own)
    arrived = {i: swap(packets[i], "tensor", i) for i in reversed(range(1, shards))}
    packets = [packets[0]] + [arrived[i] for i in range(1, shards)]
    attention, keys, values = finish(
        [mine] + partials,
        key_gain.reshape(1, -1),
        packets,
        rank,
        step_count,
        row_count,
        query_rows.shape[1],
    )
    return tuple(a.reshape(step_count, row_count, -1) for a in (attention, keys, values))


def solution(mesh):
    placed = (
        P(None, ("job", "rollout"), "tensor"),
        P("tensor", None),
        P(("job", "rollout", "tensor"), None),
        P(None, ("job", "rollout")),
        P(),
        P(None, ("job", "rollout"), "tensor"),
        P(("job", "rollout"), None, "tensor"),
        P(("job", "rollout"), None, "tensor"),
        P(("job", "rollout")),
        P("job"),
    )
    return jax.shard_map(
        per_device,
        mesh=mesh,
        in_specs=placed,
        out_specs=(
            P(None, ("job", "rollout"), "tensor"),
            P(None, ("job", "rollout"), "tensor"),
            P(None, ("job", "rollout"), "tensor"),
        ),
        check_vma=False,
    )
```

```python
import functools
import math

import jax
import jax.numpy as jnp
from jax import lax
from jax.experimental import pallas as pl
from jax.experimental.pallas import tpu as pltpu
from jax.sharding import PartitionSpec as P

norm_eps = 1e-06
rope_base = 1000000.0
adapter_scale = 2.0
masked_score = -1e30
lanes = 128
f32 = jnp.float32
bf16 = jnp.bfloat16

whole_in_vmem = pl.BlockSpec(memory_space=pltpu.VMEM)
whole_in_smem = pl.BlockSpec(memory_space=pltpu.SMEM)
stays_in_hbm = pl.BlockSpec(memory_space=pltpu.HBM)


def swap(block, axis, offset):
    count = lax.axis_size(axis)
    return lax.ppermute(block, axis, [(s, s ^ offset) for s in range(count)])


def in_hbm(*arrays):
    return tuple(pltpu.with_memory_space_constraint(a, pltpu.HBM) for a in arrays)


def side_by_side(rows_of_blocks):
    r, c = rows_of_blocks.shape
    return rows_of_blocks.reshape(r, c // lanes, lanes).transpose(1, 0, 2).reshape(-1, lanes)


def split_halves(total):
    high = total.astype(bf16)
    return high, (total - high.astype(f32)).astype(bf16)


def pack_kernel(down_hbm, up_hbm, out_ref, down_ref, up_ref, sems):
    rank, down_rows = down_ref.shape
    rank_part = up_ref.shape[0]
    start = pl.multiple_of(lax.axis_index("tensor") * rank_part, rank_part)
    copies = [
        pltpu.make_async_copy(down_hbm, down_ref, sems.at[0]),
        pltpu.make_async_copy(up_hbm.at[pl.ds(start, rank_part), :], up_ref, sems.at[1]),
    ]
    for copy in copies:
        copy.start()
    for copy in copies:
        copy.wait()
    first = 0
    for c in range(down_rows // lanes):
        out_ref[first : first + rank, :] = down_ref[:, c * lanes : (c + 1) * lanes]
        first += rank
    rest = down_rows % lanes
    if rest:
        half = rank // 2
        tail = down_ref[:, down_rows - rest :]
        out_ref[first : first + half, :] = jnp.concatenate([tail[:half], tail[half:]], axis=1)
        first += half
    for c in range(up_ref.shape[1] // lanes):
        out_ref[first : first + rank_part, :] = up_ref[:, c * lanes : (c + 1) * lanes]
        first += rank_part


def pack(down, up, rank_part, beside):
    rows = (down.size + rank_part * up.shape[1]) // lanes
    return pl.pallas_call(
        pack_kernel,
        out_shape=jax.ShapeDtypeStruct((rows, lanes), bf16),
        in_specs=[stays_in_hbm] * 2,
        out_specs=whole_in_vmem,
        scratch_shapes=[
            pltpu.VMEM(down.shape, bf16),
            pltpu.VMEM((rank_part, up.shape[1]), bf16),
            pltpu.SemaphoreType.DMA((2,)),
        ],
        compiler_params=pltpu.CompilerParams(vmem_limit_bytes=2 * 2**20),
        name="pack",
        cost_estimate=beside,
    )(*in_hbm(down, up))


def project_kernel(tokens_ref, weight_ref, own_ref, *base_refs):
    shard = lax.axis_index("tensor")
    rows, own = own_ref.shape
    for i in reversed(range(1 + len(base_refs))):
        first = pl.multiple_of((shard ^ i) * own, lanes)
        block = jnp.dot(
            tokens_ref[...], weight_ref[:, pl.ds(first, own)], preferred_element_type=f32
        )
        if i == 0:
            own_ref[...] = block
            continue
        for c in range(own // lanes):
            base_refs[i - 1][c * rows : (c + 1) * rows, :] = block[
                :, c * lanes : (c + 1) * lanes
            ].astype(bf16)


def project(tokens, weight, shards):
    rows, depth = tokens.shape
    own = weight.shape[1] // shards
    mine, *base = pl.pallas_call(
        project_kernel,
        out_shape=[jax.ShapeDtypeStruct((rows, own), f32)]
        + [jax.ShapeDtypeStruct((rows * own // lanes, lanes), bf16)] * (shards - 1),
        in_specs=[whole_in_vmem] * 2,
        out_specs=[whole_in_vmem] * shards,
        compiler_params=pltpu.CompilerParams(vmem_limit_bytes=4 * 2**20),
        name="project",
        cost_estimate=pl.CostEstimate(
            flops=2 * rows * weight.size, bytes_accessed=2 * weight.size, transcendentals=0
        ),
    )(tokens, weight)
    return mine, base


def attend_kernel(
    step_count,
    head_count,
    lengths_hbm,
    queries_ref,
    keys_ref,
    values_ref,
    _,
    grouped_ref,
    total_ref,
    peak_ref,
    sum_ref,
    cosine_ref,
    sine_ref,
    lengths_ref,
    regroup,
    scores,
    raised,
    length_sem,
):
    lengths_copy = pltpu.make_async_copy(lengths_hbm, lengths_ref, length_sem)
    lengths_copy.start()
    row_count, slots, _ = keys_ref.shape
    rows = step_count * row_count
    group = queries_ref.shape[1] // (head_count * lanes)
    seen = step_count * group
    scale = lanes**-0.5

    for pair in range(step_count // 2):
        for q in range(head_count * group):
            h, g = q // group, q % group
            both = queries_ref[
                pair * 2 * row_count : (pair + 1) * 2 * row_count, q * lanes : (q + 1) * lanes
            ].astype(f32)
            for side in range(2):
                first = h * row_count * seen + (pair * 2 + side) * group + g
                regroup[pl.ds(first, row_count, stride=seen), :] = both[
                    side * row_count : (side + 1) * row_count, :
                ]
    grouped_ref[...] = regroup[...].astype(bf16)

    def place(h, b):
        at = (h * row_count + b) * seen
        return slice(at, at + seen)

    for b in range(row_count):
        for h in range(head_count):
            scores[place(h, b), :] = lax.dot_general(
                grouped_ref[place(h, b), :],
                keys_ref[b, :, h * lanes : (h + 1) * lanes],
                (((1,), (1,)), ((), ())),
                preferred_element_type=f32,
            )
    lengths_copy.wait()
    slot = lax.broadcasted_iota(jnp.int32, (seen, slots), 1)
    for b in range(row_count):
        live = slot < lengths_ref[b]
        for h in range(head_count):
            score = jnp.where(live, scores[place(h, b), :] * scale, masked_score)
            peak = jnp.max(score, axis=1, keepdims=True)
            lifted = jnp.exp(score - peak)
            raised[place(h, b), :] = lifted.astype(bf16)
            peak_ref[place(h, b), :] = jnp.broadcast_to(peak, (seen, lanes))
            sum_ref[place(h, b), :] = jnp.broadcast_to(
                jnp.sum(lifted, axis=1, keepdims=True), (seen, lanes)
            )
    for b in range(row_count):
        for h in range(head_count):
            total_ref[place(h, b), :] = jnp.dot(
                raised[place(h, b), :],
                values_ref[b, :, h * lanes : (h + 1) * lanes],
                preferred_element_type=f32,
            )

    row = lax.broadcasted_iota(jnp.int32, (rows, lanes), 0)
    lane = lax.broadcasted_iota(jnp.int32, (rows, lanes), 1)
    position = row // row_count
    for b in range(row_count):
        position = position + jnp.where(row % row_count == b, lengths_ref[b], 0)
    middle = lanes // 2
    spacing = (lane % middle).astype(f32) * (-2.0 / lanes * math.log(rope_base))
    angles = position.astype(f32) * jnp.exp(spacing)
    cosine_ref[...] = jnp.cos(angles)
    sine = jnp.sin(angles)
    sine_ref[...] = jnp.where(lane < middle, -sine, sine)


def attend(lengths, queries, keys, values, after, step_count):
    row_count, slots, width = keys.shape
    rows = step_count * row_count
    seen_rows = rows * queries.shape[1] // lanes
    table = jax.ShapeDtypeStruct((rows, lanes), f32)
    seen_table = jax.ShapeDtypeStruct((seen_rows, lanes), f32)
    return pl.pallas_call(
        functools.partial(attend_kernel, step_count, width // lanes),
        out_shape=(
            jax.ShapeDtypeStruct((seen_rows, lanes), bf16),
            seen_table,
            seen_table,
            seen_table,
            table,
            table,
        ),
        in_specs=[stays_in_hbm] + [whole_in_vmem] * 4,
        out_specs=(whole_in_vmem,) * 6,
        scratch_shapes=[
            pltpu.SMEM(lengths.shape, jnp.int32),
            pltpu.VMEM((seen_rows, lanes), f32),
            pltpu.VMEM((seen_rows, slots), f32),
            pltpu.VMEM((seen_rows, slots), bf16),
            pltpu.SemaphoreType.DMA,
        ],
        compiler_params=pltpu.CompilerParams(vmem_limit_bytes=8 * 2**20),
        name="attend",
        cost_estimate=pl.CostEstimate(
            flops=4 * seen_rows * slots * lanes,
            bytes_accessed=2 * (keys.size + values.size),
            transcendentals=seen_rows * slots,
        ),
    )(*in_hbm(lengths), queries, keys, values, after)


def add_far(mine, far):
    rows = mine.shape[0]
    blocks = []
    for c in range(mine.shape[1] // lanes):
        block = mine[:, c * lanes : (c + 1) * lanes]
        for sent in far:
            block = block + sent[c * rows : (c + 1) * rows, :].astype(f32)
        blocks.append(block)
    return jnp.concatenate(blocks, axis=1)


def route_kernel(replicas, shards, *refs):
    owners_ref, tokens_ref, mine_ref, base_ref = refs[:4]
    piece_refs = refs[4 : 4 + replicas]
    far_refs = refs[4 + replicas : 2 + replicas + shards][::-1]
    sum_ref = refs[2 + replicas + shards]
    out_refs = refs[3 + replicas + shards : 3 + replicas + 2 * shards]
    token_buf, left, right, up_buf = refs[3 + replicas + 2 * shards :]
    sum_ref[...] = add_far(mine_ref[...], far_refs)
    replica = lax.axis_index("rollout")
    shard = lax.axis_index("tensor")
    rows, depth = tokens_ref.shape
    rank = right.shape[0]
    down_rows = depth // replicas
    width = token_buf.shape[2]
    rest = down_rows % lanes
    for k in range(replicas):
        token_buf[k, :, :down_rows] = tokens_ref[:, k * down_rows : (k + 1) * down_rows]
        if rest:
            token_buf[k, :, down_rows:] = jnp.zeros((rows, width - down_rows), bf16)
    for i in range(replicas):
        source = replica ^ i
        place = jnp.int32(0)
        for k in range(1, replicas):
            place = place + jnp.where(owners_ref[k] == source, k, 0)
        left[:, i * width : (i + 1) * width] = token_buf[place]
        first = 0
        for c in range(down_rows // lanes):
            right[:, i * width + c * lanes : i * width + (c + 1) * lanes] = piece_refs[i][
                first : first + rank, :
            ]
            first += rank
        if rest:
            both = piece_refs[i][first : first + rank // 2, :]
            tail = jnp.concatenate([both[:, :rest], both[:, rest:]], axis=0)
            right[:, (i + 1) * width - lanes : (i + 1) * width] = jnp.concatenate(
                [tail, jnp.zeros((rank, lanes - rest), bf16)], axis=1
            )
            first += rank // 2
        up_buf[i] = piece_refs[i][first:, :]
    lowered = lax.dot_general(
        left[...], right[...], (((1,), (1,)), ((), ())), preferred_element_type=f32
    )
    both = jnp.concatenate(split_halves(lowered), axis=1)
    for i in range(shards):
        first = 0
        if i == 1:
            first = base_ref.shape[0]
            out_refs[i][:first, :] = base_ref[...]
        out_refs[i][first : first + rows, :] = both
        out_refs[i][first + rows :, :] = up_buf[owners_ref[shard ^ i] ^ replica]


def route(owners, tokens, mine, near, far, pieces, rank, up_rows, shards):
    rows, depth = tokens.shape
    replicas = len(pieces)
    sent = near.shape[0]
    width = -(-depth // replicas // lanes) * lanes
    mine, *packets = pl.pallas_call(
        functools.partial(route_kernel, replicas, shards),
        out_shape=[jax.ShapeDtypeStruct(mine.shape, f32)]
        + [
            jax.ShapeDtypeStruct(((sent if i == 1 else 0) + rows + up_rows, lanes), bf16)
            for i in range(shards)
        ],
        in_specs=[whole_in_smem] + [whole_in_vmem] * (1 + replicas + shards),
        out_specs=[whole_in_vmem] * (1 + shards),
        scratch_shapes=[
            pltpu.VMEM((replicas, rows, width), bf16),
            pltpu.VMEM((rows, replicas * width), bf16),
            pltpu.VMEM((rank, replicas * width), bf16),
            pltpu.VMEM((replicas, up_rows, lanes), bf16),
        ],
        compiler_params=pltpu.CompilerParams(vmem_limit_bytes=4 * 2**20),
        name="route",
        cost_estimate=pl.CostEstimate(flops=0, bytes_accessed=800000, transcendentals=0),
    )(owners, tokens, mine, near, *pieces, *far[::-1])
    return mine, packets


def route_plain(owners, tokens, near, down, up, rank_part, own, shards):
    rank = down.shape[1]
    shard = lax.axis_index("tensor")
    first = shard * rank_part
    up_part = lax.dynamic_slice_in_dim(up, first, rank_part, axis=0)
    downs = lax.all_gather(down, "rollout", axis=0, tiled=False)
    ups = lax.all_gather(up_part, "rollout", axis=0, tiled=False)
    down_matrix = jnp.take(downs, owners, axis=0, mode="clip").reshape(-1, rank)
    up_matrix = jnp.take(ups, owners, axis=0, mode="clip").transpose(1, 0, 2)
    up_matrix = up_matrix.reshape(rank_part, -1)
    lowered = jnp.dot(tokens, down_matrix, preferred_element_type=f32)
    both = jnp.concatenate(split_halves(lowered), axis=1)
    packets = []
    for i in range(shards):
        up_block = lax.dynamic_slice_in_dim(up_matrix, (shard ^ i) * own, own, axis=1)
        parts = [both, side_by_side(up_block)]
        if i == 1:
            parts = [near] + parts
        packets.append(jnp.concatenate(parts, axis=0))
    return packets


def finish_kernel(step_count, row_count, head_count, shards, *refs):
    own_ref, gain_ref, grouped_ref, total_ref, peak_ref, sum_ref, cosine_ref, sine_ref = refs[:8]
    packet_refs = refs[8 : 8 + shards][::-1]
    attention_ref, keys_ref, values_ref = refs[8 + shards : 11 + shards]
    up_buf, ordered = refs[11 + shards :]
    shard = lax.axis_index("tensor")
    rows = step_count * row_count
    own = own_ref.shape[1]
    blocks = own // lanes
    rank = up_buf.shape[0]
    rank_part = rank // shards
    group = grouped_ref.shape[0] // (head_count * rows)
    seen = step_count * group
    scale = lanes**-0.5

    lowered = jnp.zeros((rows, lanes), f32)
    for i in range(shards):
        first = rows * blocks if i == 1 else 0
        lowered = lowered + packet_refs[i][first : first + rows, :].astype(f32)
        ups = packet_refs[i][first + rows :, :].astype(f32)
        at = pl.multiple_of((shard ^ i) * rank_part, rank_part)
        for c in range(blocks):
            up_buf[pl.ds(at, rank_part), c * lanes : (c + 1) * lanes] = ups[
                c * rank_part : (c + 1) * rank_part, :
            ]
    lane = lax.broadcasted_iota(jnp.int32, (rows, lanes), 1)
    lowered = lowered + pltpu.roll(lowered, rank, 1)
    high, low = split_halves(lowered)
    left = jnp.where(lane < rank, high.astype(f32), low.astype(f32)).astype(bf16)
    up = up_buf[...].astype(bf16)
    raised_up = jnp.dot(left, jnp.concatenate([up, up], axis=0), preferred_element_type=f32)
    joined = []
    for c in range(blocks):
        block = own_ref[:, c * lanes : (c + 1) * lanes]
        block = block + packet_refs[1][c * rows : (c + 1) * rows, :].astype(f32)
        joined.append(block + adapter_scale * raised_up[:, c * lanes : (c + 1) * lanes])

    all_rows = row_count * seen
    seen_by = lax.broadcasted_iota(jnp.int32, (all_rows, rows), 0)
    made_by = lax.broadcasted_iota(jnp.int32, (all_rows, rows), 1)
    visible = (seen_by // seen == made_by % row_count) & (
        made_by // row_count <= seen_by % seen // group
    )
    for h in range(head_count):
        raw_key = joined[2 * h]
        mean_square = jnp.mean(raw_key * raw_key, axis=1, keepdims=True)
        normed = raw_key * lax.rsqrt(mean_square + norm_eps) * gain_ref[...]
        key = normed * cosine_ref[...] + pltpu.roll(normed, lanes // 2, 1) * sine_ref[...]
        key = key.astype(bf16)
        value = joined[2 * h + 1].astype(bf16)
        keys_ref[:, h * lanes : (h + 1) * lanes] = key
        values_ref[:, h * lanes : (h + 1) * lanes] = value
        mine = slice(h * all_rows, (h + 1) * all_rows)
        score = lax.dot_general(
            grouped_ref[mine, :], key, (((1,), (1,)), ((), ())), preferred_element_type=f32
        )
        score = jnp.where(visible, score * scale, masked_score)
        old_peak = peak_ref[mine, :]
        peak = jnp.maximum(old_peak, jnp.max(score, axis=1, keepdims=True))
        fade = jnp.exp(old_peak - peak)
        lifted = jnp.exp(score - peak[:, :rows])
        denominator = fade * sum_ref[mine, :] + jnp.sum(lifted, axis=1, keepdims=True)
        total = fade * total_ref[mine, :] + jnp.dot(
            lifted.astype(bf16), value, preferred_element_type=f32
        )
        ordered[mine, :] = total / denominator
    for pair in range(step_count // 2):
        for q in range(head_count * group):
            h, g = q // group, q % group
            both = [
                ordered[
                    pl.ds(
                        h * all_rows + (pair * 2 + side) * group + g, row_count, stride=seen
                    ),
                    :,
                ]
                for side in range(2)
            ]
            attention_ref[
                pair * 2 * row_count : (pair + 1) * 2 * row_count, q * lanes : (q + 1) * lanes
            ] = jnp.concatenate(both, axis=0).astype(bf16)


def finish(partials, gain, packets, rank, step_count, row_count, query_width):
    mine, grouped, total, peak, denominator, cosine, sine = partials
    rows, own = mine.shape
    shards = len(packets)
    head_count = own // (2 * lanes)
    return pl.pallas_call(
        functools.partial(finish_kernel, step_count, row_count, head_count, shards),
        out_shape=(
            jax.ShapeDtypeStruct((rows, query_width), bf16),
            jax.ShapeDtypeStruct((rows, head_count * lanes), bf16),
            jax.ShapeDtypeStruct((rows, head_count * lanes), bf16),
        ),
        in_specs=[whole_in_vmem] * (8 + shards),
        out_specs=(whole_in_vmem,) * 3,
        scratch_shapes=[
            pltpu.VMEM((rank, own), f32),
            pltpu.VMEM(total.shape, f32),
        ],
        compiler_params=pltpu.CompilerParams(vmem_limit_bytes=6 * 2**20),
        name="finish",
        cost_estimate=pl.CostEstimate(flops=0, bytes_accessed=1000000, transcendentals=0),
    )(mine, gain, grouped, total, peak, denominator, cosine, sine, *packets[::-1])


def per_device(
    normed_tokens,
    key_value_weight,
    adapter_down,
    adapter_up,
    key_gain,
    queries,
    cache_keys,
    stored_values,
    lengths,
    owners,
):
    replicas = lax.axis_size("rollout")
    shards = lax.axis_size("tensor")
    down_rows, rank = adapter_down.shape
    step_count, row_count, depth = normed_tokens.shape
    own = key_value_weight.shape[1] // shards
    rank_part = rank // shards
    rows = step_count * row_count
    tokens = normed_tokens.reshape(rows, depth)
    query_rows = queries.reshape(rows, -1)

    fits = (
        replicas <= 4
        and adapter_up.shape[1] == own
        and down_rows % lanes in (0, lanes // 2)
        and rank == lanes // 2
        and rank_part % 16 == 0
    )
    if fits:
        fetched = 2 * (key_value_weight.size + cache_keys.size + stored_values.size)
        beside = pl.CostEstimate(flops=1000 * fetched, bytes_accessed=fetched, transcendentals=0)
        packed = pack(adapter_down.T, adapter_up, rank_part, beside)
        arrived = {i: swap(packed, "rollout", i) for i in reversed(range(1, replicas))}
        pieces = [packed] + [arrived[i] for i in range(1, replicas)]
    mine, base = project(tokens, key_value_weight, shards)
    far = [swap(base[i - 1], "tensor", i) for i in range(2, shards)]
    if fits:
        mine, packets = route(
            owners, tokens, mine, base[0], far, pieces, rank, rank_part * own // lanes, shards
        )
    else:
        packets = route_plain(
            owners, tokens, base[0], adapter_down, adapter_up, rank_part, own, shards
        )
        mine = add_far(mine, far)
    partials = attend(lengths, query_rows, cache_keys, stored_values, packets[0], step_count)
    packets = [packets[0]] + [swap(packets[i], "tensor", i) for i in range(1, shards)]
    attention, keys, values = finish(
        [mine] + list(partials),
        key_gain.reshape(1, -1),
        packets,
        rank,
        step_count,
        row_count,
        query_rows.shape[1],
    )
    return tuple(a.reshape(step_count, row_count, -1) for a in (attention, keys, values))


def solution(mesh):
    placed = (
        P(None, ("job", "rollout"), "tensor"),
        P("tensor", None),
        P(("job", "rollout", "tensor"), None),
        P(None, ("job", "rollout")),
        P(),
        P(None, ("job", "rollout"), "tensor"),
        P(("job", "rollout"), None, "tensor"),
        P(("job", "rollout"), None, "tensor"),
        P(("job", "rollout")),
        P("job"),
    )
    return jax.shard_map(
        per_device,
        mesh=mesh,
        in_specs=placed,
        out_specs=(
            P(None, ("job", "rollout"), "tensor"),
            P(None, ("job", "rollout"), "tensor"),
            P(None, ("job", "rollout"), "tensor"),
        ),
        check_vma=False,
    )
```

```python
import functools
import math

import jax
import jax.numpy as jnp
from jax import lax
from jax.experimental import pallas as pl
from jax.experimental.pallas import tpu as pltpu
from jax.sharding import PartitionSpec as P

norm_eps = 1e-06
rope_base = 1000000.0
adapter_scale = 2.0
masked_score = -1e30
lanes = 128
f32 = jnp.float32
bf16 = jnp.bfloat16

whole_in_vmem = pl.BlockSpec(memory_space=pltpu.VMEM)
whole_in_smem = pl.BlockSpec(memory_space=pltpu.SMEM)
stays_in_hbm = pl.BlockSpec(memory_space=pltpu.HBM)


def swap(block, axis, offset):
    count = lax.axis_size(axis)
    return lax.ppermute(block, axis, [(s, s ^ offset) for s in range(count)])


def in_hbm(*arrays):
    return tuple(pltpu.with_memory_space_constraint(a, pltpu.HBM) for a in arrays)


def side_by_side(rows_of_blocks):
    r, c = rows_of_blocks.shape
    return rows_of_blocks.reshape(r, c // lanes, lanes).transpose(1, 0, 2).reshape(-1, lanes)


def split_halves(total):
    high = total.astype(bf16)
    return high, (total - high.astype(f32)).astype(bf16)


def pack_kernel(down_hbm, up_hbm, out_ref, down_ref, up_ref, sems):
    rank, down_rows = down_ref.shape
    rank_part = up_ref.shape[0]
    start = pl.multiple_of(lax.axis_index("tensor") * rank_part, rank_part)
    copies = [
        pltpu.make_async_copy(down_hbm, down_ref, sems.at[0]),
        pltpu.make_async_copy(up_hbm.at[pl.ds(start, rank_part), :], up_ref, sems.at[1]),
    ]
    for copy in copies:
        copy.start()
    for copy in copies:
        copy.wait()
    first = 0
    for c in range(down_rows // lanes):
        out_ref[first : first + rank, :] = down_ref[:, c * lanes : (c + 1) * lanes]
        first += rank
    rest = down_rows % lanes
    if rest:
        half = rank // 2
        tail = down_ref[:, down_rows - rest :]
        out_ref[first : first + half, :] = jnp.concatenate([tail[:half], tail[half:]], axis=1)
        first += half
    for c in range(up_ref.shape[1] // lanes):
        out_ref[first : first + rank_part, :] = up_ref[:, c * lanes : (c + 1) * lanes]
        first += rank_part


def pack(down, up, rank_part, beside):
    rows = (down.size + rank_part * up.shape[1]) // lanes
    return pl.pallas_call(
        pack_kernel,
        out_shape=jax.ShapeDtypeStruct((rows, lanes), bf16),
        in_specs=[stays_in_hbm] * 2,
        out_specs=whole_in_vmem,
        scratch_shapes=[
            pltpu.VMEM(down.shape, bf16),
            pltpu.VMEM((rank_part, up.shape[1]), bf16),
            pltpu.SemaphoreType.DMA((2,)),
        ],
        compiler_params=pltpu.CompilerParams(vmem_limit_bytes=2 * 2**20),
        name="pack",
        cost_estimate=beside,
    )(*in_hbm(down, up))


def project_kernel(tokens_ref, weight_ref, _, own_ref, first_ref, near_ref, kept_ref):
    shard = lax.axis_index("tensor")
    pairs, rows, own = kept_ref.shape

    def product(i):
        first = pl.multiple_of((shard ^ i) * own, lanes)
        return jnp.dot(
            tokens_ref[...], weight_ref[:, pl.ds(first, own)], preferred_element_type=f32
        )

    def put(block, ref):
        for c in range(own // lanes):
            ref[c * rows : (c + 1) * rows, :] = block[:, c * lanes : (c + 1) * lanes].astype(bf16)

    for m in range(pairs):
        put(product(2 * m + 3), near_ref.at[m])
        kept_ref[m] = product(2 * m + 2)
    put(product(1), first_ref)
    own_ref[...] = product(0)


def project(tokens, weight, after, shards):
    rows, depth = tokens.shape
    own = weight.shape[1] // shards
    pairs = shards // 2 - 1
    sent = rows * own // lanes
    return pl.pallas_call(
        project_kernel,
        out_shape=(
            jax.ShapeDtypeStruct((rows, own), f32),
            jax.ShapeDtypeStruct((sent, lanes), bf16),
            jax.ShapeDtypeStruct((pairs, sent, lanes), bf16),
            jax.ShapeDtypeStruct((pairs, rows, own), f32),
        ),
        in_specs=[whole_in_vmem] * 3,
        out_specs=(whole_in_vmem,) * 4,
        compiler_params=pltpu.CompilerParams(vmem_limit_bytes=4 * 2**20),
        name="project",
        cost_estimate=pl.CostEstimate(
            flops=2 * rows * weight.size, bytes_accessed=2 * weight.size, transcendentals=0
        ),
    )(tokens, weight, after)


def attend_kernel(
    step_count,
    head_count,
    lengths_hbm,
    queries_ref,
    keys_ref,
    values_ref,
    _,
    grouped_ref,
    total_ref,
    peak_ref,
    sum_ref,
    cosine_ref,
    sine_ref,
    lengths_ref,
    regroup,
    scores,
    raised,
    length_sem,
):
    lengths_copy = pltpu.make_async_copy(lengths_hbm, lengths_ref, length_sem)
    lengths_copy.start()
    row_count, slots, _ = keys_ref.shape
    rows = step_count * row_count
    group = queries_ref.shape[1] // (head_count * lanes)
    seen = step_count * group
    scale = lanes**-0.5

    for pair in range(step_count // 2):
        for q in range(head_count * group):
            h, g = q // group, q % group
            both = queries_ref[
                pair * 2 * row_count : (pair + 1) * 2 * row_count, q * lanes : (q + 1) * lanes
            ].astype(f32)
            for side in range(2):
                first = h * row_count * seen + (pair * 2 + side) * group + g
                regroup[pl.ds(first, row_count, stride=seen), :] = both[
                    side * row_count : (side + 1) * row_count, :
                ]
    grouped_ref[...] = regroup[...].astype(bf16)

    def place(h, b):
        at = (h * row_count + b) * seen
        return slice(at, at + seen)

    for b in range(row_count):
        for h in range(head_count):
            scores[place(h, b), :] = lax.dot_general(
                grouped_ref[place(h, b), :],
                keys_ref[b, :, h * lanes : (h + 1) * lanes],
                (((1,), (1,)), ((), ())),
                preferred_element_type=f32,
            )
    lengths_copy.wait()
    slot = lax.broadcasted_iota(jnp.int32, (seen, slots), 1)
    for b in range(row_count):
        live = slot < lengths_ref[b]
        for h in range(head_count):
            score = jnp.where(live, scores[place(h, b), :] * scale, masked_score)
            peak = jnp.max(score, axis=1, keepdims=True)
            lifted = jnp.exp(score - peak)
            raised[place(h, b), :] = lifted.astype(bf16)
            peak_ref[place(h, b), :] = jnp.broadcast_to(peak, (seen, lanes))
            sum_ref[place(h, b), :] = jnp.broadcast_to(
                jnp.sum(lifted, axis=1, keepdims=True), (seen, lanes)
            )
    for b in range(row_count):
        for h in range(head_count):
            total_ref[place(h, b), :] = jnp.dot(
                raised[place(h, b), :],
                values_ref[b, :, h * lanes : (h + 1) * lanes],
                preferred_element_type=f32,
            )

    row = lax.broadcasted_iota(jnp.int32, (rows, lanes), 0)
    lane = lax.broadcasted_iota(jnp.int32, (rows, lanes), 1)
    position = row // row_count
    for b in range(row_count):
        position = position + jnp.where(row % row_count == b, lengths_ref[b], 0)
    middle = lanes // 2
    spacing = (lane % middle).astype(f32) * (-2.0 / lanes * math.log(rope_base))
    angles = position.astype(f32) * jnp.exp(spacing)
    cosine_ref[...] = jnp.cos(angles)
    sine = jnp.sin(angles)
    sine_ref[...] = jnp.where(lane < middle, -sine, sine)


def attend(lengths, queries, keys, values, after, step_count):
    row_count, slots, width = keys.shape
    rows = step_count * row_count
    seen_rows = rows * queries.shape[1] // lanes
    table = jax.ShapeDtypeStruct((rows, lanes), f32)
    seen_table = jax.ShapeDtypeStruct((seen_rows, lanes), f32)
    return pl.pallas_call(
        functools.partial(attend_kernel, step_count, width // lanes),
        out_shape=(
            jax.ShapeDtypeStruct((seen_rows, lanes), bf16),
            seen_table,
            seen_table,
            seen_table,
            table,
            table,
        ),
        in_specs=[stays_in_hbm] + [whole_in_vmem] * 4,
        out_specs=(whole_in_vmem,) * 6,
        scratch_shapes=[
            pltpu.SMEM(lengths.shape, jnp.int32),
            pltpu.VMEM((seen_rows, lanes), f32),
            pltpu.VMEM((seen_rows, slots), f32),
            pltpu.VMEM((seen_rows, slots), bf16),
            pltpu.SemaphoreType.DMA,
        ],
        compiler_params=pltpu.CompilerParams(vmem_limit_bytes=8 * 2**20),
        name="attend",
        cost_estimate=pl.CostEstimate(
            flops=4 * seen_rows * slots * lanes,
            bytes_accessed=2 * (keys.size + values.size),
            transcendentals=seen_rows * slots,
        ),
    )(*in_hbm(lengths), queries, keys, values, after)


def add_near(kept, near):
    rows, own = kept.shape
    return [
        kept[:, c * lanes : (c + 1) * lanes] + near[c * rows : (c + 1) * rows, :].astype(f32)
        for c in range(own // lanes)
    ]


def carries_sums(i):
    return i == 1 or (i > 0 and i % 2 == 0)


def route_kernel(replicas, shards, *refs):
    owners_ref, tokens_ref, first_ref, kept_ref = refs[:4]
    piece_refs = refs[4 : 4 + replicas]
    near_ref = refs[4 + replicas]
    out_refs = refs[5 + replicas : 5 + replicas + shards]
    token_buf, left, right, up_buf = refs[5 + replicas + shards :]
    replica = lax.axis_index("rollout")
    shard = lax.axis_index("tensor")
    rows, depth = tokens_ref.shape
    rank = right.shape[0]
    down_rows = depth // replicas
    width = token_buf.shape[2]
    rest = down_rows % lanes
    for k in range(replicas):
        token_buf[k, :, :down_rows] = tokens_ref[:, k * down_rows : (k + 1) * down_rows]
        if rest:
            token_buf[k, :, down_rows:] = jnp.zeros((rows, width - down_rows), bf16)
    for i in range(replicas):
        source = replica ^ i
        place = jnp.int32(0)
        for k in range(1, replicas):
            place = place + jnp.where(owners_ref[k] == source, k, 0)
        left[:, i * width : (i + 1) * width] = token_buf[place]
        first = 0
        for c in range(down_rows // lanes):
            right[:, i * width + c * lanes : i * width + (c + 1) * lanes] = piece_refs[i][
                first : first + rank, :
            ]
            first += rank
        if rest:
            both = piece_refs[i][first : first + rank // 2, :]
            tail = jnp.concatenate([both[:, :rest], both[:, rest:]], axis=0)
            right[:, (i + 1) * width - lanes : (i + 1) * width] = jnp.concatenate(
                [tail, jnp.zeros((rank, lanes - rest), bf16)], axis=1
            )
            first += rank // 2
        up_buf[i] = piece_refs[i][first:, :]
    lowered = lax.dot_general(
        left[...], right[...], (((1,), (1,)), ((), ())), preferred_element_type=f32
    )
    both = jnp.concatenate(split_halves(lowered), axis=1)
    for i in range(shards):
        first = 0
        if i == 1:
            first = first_ref.shape[0]
            out_refs[i][:first, :] = first_ref[...]
        elif carries_sums(i):
            for block in add_near(kept_ref[i // 2 - 1], near_ref[i // 2 - 1]):
                out_refs[i][first : first + rows, :] = block.astype(bf16)
                first += rows
        out_refs[i][first : first + rows, :] = both
        out_refs[i][first + rows :, :] = up_buf[owners_ref[shard ^ i] ^ replica]


def route(owners, tokens, sums, pieces, rank, up_rows, shards):
    rows, depth = tokens.shape
    replicas = len(pieces)
    first, kept, near = sums
    sent = first.shape[0]
    width = -(-depth // replicas // lanes) * lanes
    return pl.pallas_call(
        functools.partial(route_kernel, replicas, shards),
        out_shape=[
            jax.ShapeDtypeStruct(((sent if carries_sums(i) else 0) + rows + up_rows, lanes), bf16)
            for i in range(shards)
        ],
        in_specs=[whole_in_smem] + [whole_in_vmem] * (4 + replicas),
        out_specs=[whole_in_vmem] * shards,
        scratch_shapes=[
            pltpu.VMEM((replicas, rows, width), bf16),
            pltpu.VMEM((rows, replicas * width), bf16),
            pltpu.VMEM((rank, replicas * width), bf16),
            pltpu.VMEM((replicas, up_rows, lanes), bf16),
        ],
        compiler_params=pltpu.CompilerParams(vmem_limit_bytes=4 * 2**20),
        name="route",
        cost_estimate=pl.CostEstimate(flops=0, bytes_accessed=800000, transcendentals=0),
    )(owners, tokens, first, kept, *pieces, near)


def route_plain(owners, tokens, sums, down, up, rank_part, own, shards):
    first_sent, kept, near = sums
    rank = down.shape[1]
    shard = lax.axis_index("tensor")
    first = shard * rank_part
    up_part = lax.dynamic_slice_in_dim(up, first, rank_part, axis=0)
    downs = lax.all_gather(down, "rollout", axis=0, tiled=False)
    ups = lax.all_gather(up_part, "rollout", axis=0, tiled=False)
    down_matrix = jnp.take(downs, owners, axis=0, mode="clip").reshape(-1, rank)
    up_matrix = jnp.take(ups, owners, axis=0, mode="clip").transpose(1, 0, 2)
    up_matrix = up_matrix.reshape(rank_part, -1)
    lowered = jnp.dot(tokens, down_matrix, preferred_element_type=f32)
    both = jnp.concatenate(split_halves(lowered), axis=1)
    packets = []
    for i in range(shards):
        up_block = lax.dynamic_slice_in_dim(up_matrix, (shard ^ i) * own, own, axis=1)
        parts = [both, side_by_side(up_block)]
        if i == 1:
            parts = [first_sent] + parts
        elif carries_sums(i):
            sums = add_near(kept[i // 2 - 1], near[i // 2 - 1])
            parts = [jnp.concatenate(sums, axis=0).astype(bf16)] + parts
        packets.append(jnp.concatenate(parts, axis=0))
    return packets


def finish_kernel(step_count, row_count, head_count, shards, *refs):
    own_ref, gain_ref, grouped_ref, total_ref, peak_ref, sum_ref, cosine_ref, sine_ref = refs[:8]
    packet_refs = refs[8 : 8 + shards][::-1]
    attention_ref, keys_ref, values_ref = refs[8 + shards : 11 + shards]
    up_buf, ordered = refs[11 + shards :]
    shard = lax.axis_index("tensor")
    rows = step_count * row_count
    own = own_ref.shape[1]
    blocks = own // lanes
    rank = up_buf.shape[0]
    rank_part = rank // shards
    group = grouped_ref.shape[0] // (head_count * rows)
    seen = step_count * group
    scale = lanes**-0.5

    lowered = jnp.zeros((rows, lanes), f32)
    for i in range(shards):
        first = rows * blocks if carries_sums(i) else 0
        lowered = lowered + packet_refs[i][first : first + rows, :].astype(f32)
        ups = packet_refs[i][first + rows :, :].astype(f32)
        at = pl.multiple_of((shard ^ i) * rank_part, rank_part)
        for c in range(blocks):
            up_buf[pl.ds(at, rank_part), c * lanes : (c + 1) * lanes] = ups[
                c * rank_part : (c + 1) * rank_part, :
            ]
    lane = lax.broadcasted_iota(jnp.int32, (rows, lanes), 1)
    lowered = lowered + pltpu.roll(lowered, rank, 1)
    high, low = split_halves(lowered)
    left = jnp.where(lane < rank, high.astype(f32), low.astype(f32)).astype(bf16)
    up = up_buf[...].astype(bf16)
    raised_up = jnp.dot(left, jnp.concatenate([up, up], axis=0), preferred_element_type=f32)
    joined = []
    for c in range(blocks):
        block = own_ref[:, c * lanes : (c + 1) * lanes]
        for i in filter(carries_sums, range(shards)):
            block = block + packet_refs[i][c * rows : (c + 1) * rows, :].astype(f32)
        joined.append(block + adapter_scale * raised_up[:, c * lanes : (c + 1) * lanes])

    all_rows = row_count * seen
    seen_by = lax.broadcasted_iota(jnp.int32, (all_rows, rows), 0)
    made_by = lax.broadcasted_iota(jnp.int32, (all_rows, rows), 1)
    visible = (seen_by // seen == made_by % row_count) & (
        made_by // row_count <= seen_by % seen // group
    )
    for h in range(head_count):
        raw_key = joined[2 * h]
        mean_square = jnp.mean(raw_key * raw_key, axis=1, keepdims=True)
        normed = raw_key * lax.rsqrt(mean_square + norm_eps) * gain_ref[...]
        key = normed * cosine_ref[...] + pltpu.roll(normed, lanes // 2, 1) * sine_ref[...]
        key = key.astype(bf16)
        value = joined[2 * h + 1].astype(bf16)
        keys_ref[:, h * lanes : (h + 1) * lanes] = key
        values_ref[:, h * lanes : (h + 1) * lanes] = value
        mine = slice(h * all_rows, (h + 1) * all_rows)
        score = lax.dot_general(
            grouped_ref[mine, :], key, (((1,), (1,)), ((), ())), preferred_element_type=f32
        )
        score = jnp.where(visible, score * scale, masked_score)
        old_peak = peak_ref[mine, :]
        peak = jnp.maximum(old_peak, jnp.max(score, axis=1, keepdims=True))
        fade = jnp.exp(old_peak - peak)
        lifted = jnp.exp(score - peak[:, :rows])
        denominator = fade * sum_ref[mine, :] + jnp.sum(lifted, axis=1, keepdims=True)
        total = fade * total_ref[mine, :] + jnp.dot(
            lifted.astype(bf16), value, preferred_element_type=f32
        )
        ordered[mine, :] = total / denominator
    for pair in range(step_count // 2):
        for q in range(head_count * group):
            h, g = q // group, q % group
            both = [
                ordered[
                    pl.ds(
                        h * all_rows + (pair * 2 + side) * group + g, row_count, stride=seen
                    ),
                    :,
                ]
                for side in range(2)
            ]
            attention_ref[
                pair * 2 * row_count : (pair + 1) * 2 * row_count, q * lanes : (q + 1) * lanes
            ] = jnp.concatenate(both, axis=0).astype(bf16)


def finish(partials, gain, packets, rank, step_count, row_count, query_width):
    mine, grouped, total, peak, denominator, cosine, sine = partials
    rows, own = mine.shape
    shards = len(packets)
    head_count = own // (2 * lanes)
    return pl.pallas_call(
        functools.partial(finish_kernel, step_count, row_count, head_count, shards),
        out_shape=(
            jax.ShapeDtypeStruct((rows, query_width), bf16),
            jax.ShapeDtypeStruct((rows, head_count * lanes), bf16),
            jax.ShapeDtypeStruct((rows, head_count * lanes), bf16),
        ),
        in_specs=[whole_in_vmem] * (8 + shards),
        out_specs=(whole_in_vmem,) * 3,
        scratch_shapes=[
            pltpu.VMEM((rank, own), f32),
            pltpu.VMEM(total.shape, f32),
        ],
        compiler_params=pltpu.CompilerParams(vmem_limit_bytes=6 * 2**20),
        name="finish",
        cost_estimate=pl.CostEstimate(flops=0, bytes_accessed=1000000, transcendentals=0),
    )(mine, gain, grouped, total, peak, denominator, cosine, sine, *packets[::-1])


def per_device(
    normed_tokens,
    key_value_weight,
    adapter_down,
    adapter_up,
    key_gain,
    queries,
    cache_keys,
    stored_values,
    lengths,
    owners,
):
    replicas = lax.axis_size("rollout")
    shards = lax.axis_size("tensor")
    down_rows, rank = adapter_down.shape
    step_count, row_count, depth = normed_tokens.shape
    own = key_value_weight.shape[1] // shards
    rank_part = rank // shards
    rows = step_count * row_count
    tokens = normed_tokens.reshape(rows, depth)
    query_rows = queries.reshape(rows, -1)

    fits = (
        replicas <= 4
        and adapter_up.shape[1] == own
        and down_rows % lanes in (0, lanes // 2)
        and rank == lanes // 2
        and rank_part % 16 == 0
    )
    if fits:
        fetched = 2 * (key_value_weight.size + cache_keys.size + stored_values.size)
        beside = pl.CostEstimate(flops=1000 * fetched, bytes_accessed=fetched, transcendentals=0)
        packed = pack(adapter_down.T, adapter_up, rank_part, beside)
        arrived = {i: swap(packed, "rollout", i) for i in reversed(range(1, replicas))}
        pieces = [packed] + [arrived[i] for i in range(1, replicas)]
    mine, first, near, kept = project(
        tokens, key_value_weight, packed if fits else adapter_up, shards
    )
    sums = (first, kept, swap(near, "tensor", 1))
    if fits:
        packets = route(owners, tokens, sums, pieces, rank, rank_part * own // lanes, shards)
    else:
        packets = route_plain(
            owners, tokens, sums, adapter_down, adapter_up, rank_part, own, shards
        )
    partials = attend(lengths, query_rows, cache_keys, stored_values, packets[0], step_count)
    packets = [packets[0]] + [swap(packets[i], "tensor", i) for i in range(1, shards)]
    attention, keys, values = finish(
        [mine] + list(partials),
        key_gain.reshape(1, -1),
        packets,
        rank,
        step_count,
        row_count,
        query_rows.shape[1],
    )
    return tuple(a.reshape(step_count, row_count, -1) for a in (attention, keys, values))


def solution(mesh):
    placed = (
        P(None, ("job", "rollout"), "tensor"),
        P("tensor", None),
        P(("job", "rollout", "tensor"), None),
        P(None, ("job", "rollout")),
        P(),
        P(None, ("job", "rollout"), "tensor"),
        P(("job", "rollout"), None, "tensor"),
        P(("job", "rollout"), None, "tensor"),
        P(("job", "rollout")),
        P("job"),
    )
    return jax.shard_map(
        per_device,
        mesh=mesh,
        in_specs=placed,
        out_specs=(
            P(None, ("job", "rollout"), "tensor"),
            P(None, ("job", "rollout"), "tensor"),
            P(None, ("job", "rollout"), "tensor"),
        ),
        check_vma=False,
    )
```

```python
import functools
import math

import jax
import jax.numpy as jnp
from jax import lax
from jax.experimental import pallas as pl
from jax.experimental.pallas import tpu as pltpu
from jax.sharding import PartitionSpec as P

norm_eps = 1e-06
rope_base = 1000000.0
adapter_scale = 2.0
masked_score = -1e30
lanes = 128
exponent_scale = lanes**-0.5 / math.log(2.0)
f32 = jnp.float32
bf16 = jnp.bfloat16

whole_in_vmem = pl.BlockSpec(memory_space=pltpu.VMEM)
whole_in_smem = pl.BlockSpec(memory_space=pltpu.SMEM)
stays_in_hbm = pl.BlockSpec(memory_space=pltpu.HBM)


def swap(block, axis, offset):
    count = lax.axis_size(axis)
    return lax.ppermute(block, axis, [(s, s ^ offset) for s in range(count)])


def in_hbm(*arrays):
    return tuple(pltpu.with_memory_space_constraint(a, pltpu.HBM) for a in arrays)


def side_by_side(rows_of_blocks):
    r, c = rows_of_blocks.shape
    return rows_of_blocks.reshape(r, c // lanes, lanes).transpose(1, 0, 2).reshape(-1, lanes)


def split_halves(total):
    high = total.astype(bf16)
    return high, (total - high.astype(f32)).astype(bf16)


def pack_kernel(down_hbm, up_hbm, out_ref, down_ref, up_ref, sems):
    rank, down_rows = down_ref.shape
    rank_part = up_ref.shape[0]
    start = pl.multiple_of(lax.axis_index("tensor") * rank_part, rank_part)
    copies = [
        pltpu.make_async_copy(down_hbm, down_ref, sems.at[0]),
        pltpu.make_async_copy(up_hbm.at[pl.ds(start, rank_part), :], up_ref, sems.at[1]),
    ]
    for copy in copies:
        copy.start()
    for copy in copies:
        copy.wait()
    first = 0
    for c in range(down_rows // lanes):
        out_ref[first : first + rank, :] = down_ref[:, c * lanes : (c + 1) * lanes]
        first += rank
    rest = down_rows % lanes
    if rest:
        half = rank // 2
        tail = down_ref[:, down_rows - rest :]
        out_ref[first : first + half, :] = jnp.concatenate([tail[:half], tail[half:]], axis=1)
        first += half
    for c in range(up_ref.shape[1] // lanes):
        out_ref[first : first + rank_part, :] = up_ref[:, c * lanes : (c + 1) * lanes]
        first += rank_part


def pack(down, up, rank_part, beside):
    rows = (down.size + rank_part * up.shape[1]) // lanes
    return pl.pallas_call(
        pack_kernel,
        out_shape=jax.ShapeDtypeStruct((rows, lanes), bf16),
        in_specs=[stays_in_hbm] * 2,
        out_specs=whole_in_vmem,
        scratch_shapes=[
            pltpu.VMEM(down.shape, bf16),
            pltpu.VMEM((rank_part, up.shape[1]), bf16),
            pltpu.SemaphoreType.DMA((2,)),
        ],
        compiler_params=pltpu.CompilerParams(vmem_limit_bytes=2 * 2**20),
        name="pack",
        cost_estimate=beside,
    )(*in_hbm(down, up))


def project_kernel(step_count, head_count, shards, *refs):
    lengths_hbm, tokens_ref, weight_ref, queries_ref, keys_ref, _ = refs[:6]
    pairs = shards // 2
    near_refs = refs[6 : 6 + pairs]
    kept_ref, grouped_ref, scores_ref, cosine_ref, sine_ref = refs[6 + pairs : 11 + pairs]
    lengths_ref, regroup, length_sem = refs[11 + pairs :]
    lengths_copy = pltpu.make_async_copy(lengths_hbm, lengths_ref, length_sem)
    lengths_copy.start()

    row_count = keys_ref.shape[0]
    group = queries_ref.shape[1] // (head_count * lanes)
    seen = step_count * group
    for pair in range(step_count // 2):
        for q in range(head_count * group):
            h, g = q // group, q % group
            both = queries_ref[
                pair * 2 * row_count : (pair + 1) * 2 * row_count, q * lanes : (q + 1) * lanes
            ].astype(f32)
            for side in range(2):
                first = h * row_count * seen + (pair * 2 + side) * group + g
                regroup[pl.ds(first, row_count, stride=seen), :] = both[
                    side * row_count : (side + 1) * row_count, :
                ]
    grouped_ref[...] = regroup[...].astype(bf16)

    shard = lax.axis_index("tensor")
    _, rows, own = kept_ref.shape
    for i in range(shards):
        first = pl.multiple_of((shard ^ i) * own, lanes)
        block = jnp.dot(
            tokens_ref[...], weight_ref[:, pl.ds(first, own)], preferred_element_type=f32
        )
        if i % 2 == 0:
            kept_ref[i // 2] = block
            continue
        for c in range(own // lanes):
            near_refs[i // 2][c * rows : (c + 1) * rows, :] = block[
                :, c * lanes : (c + 1) * lanes
            ].astype(bf16)

    for b in range(row_count):
        for h in range(head_count):
            at = (h * row_count + b) * seen
            scores_ref[at : at + seen, :] = lax.dot_general(
                grouped_ref[at : at + seen, :],
                keys_ref[b, :, h * lanes : (h + 1) * lanes],
                (((1,), (1,)), ((), ())),
                preferred_element_type=f32,
            )

    lengths_copy.wait()
    row = lax.broadcasted_iota(jnp.int32, (rows, lanes), 0)
    lane = lax.broadcasted_iota(jnp.int32, (rows, lanes), 1)
    position = row // row_count
    for b in range(row_count):
        position = position + jnp.where(row % row_count == b, lengths_ref[b], 0)
    middle = lanes // 2
    spacing = (lane % middle).astype(f32) * (-2.0 / lanes * math.log(rope_base))
    angles = position.astype(f32) * jnp.exp(spacing)
    cosine_ref[...] = jnp.cos(angles)
    sine = jnp.sin(angles)
    sine_ref[...] = jnp.where(lane < middle, -sine, sine)


def project(lengths, tokens, weight, queries, keys, after, step_count, shards):
    rows, depth = tokens.shape
    own = weight.shape[1] // shards
    pairs = shards // 2
    row_count, slots, width = keys.shape
    seen_rows = rows * queries.shape[1] // lanes
    table = jax.ShapeDtypeStruct((rows, lanes), f32)
    outs = pl.pallas_call(
        functools.partial(project_kernel, step_count, width // lanes, shards),
        out_shape=[jax.ShapeDtypeStruct((rows * own // lanes, lanes), bf16)] * pairs
        + [
            jax.ShapeDtypeStruct((pairs, rows, own), f32),
            jax.ShapeDtypeStruct((seen_rows, lanes), bf16),
            jax.ShapeDtypeStruct((seen_rows, slots), f32),
            table,
            table,
        ],
        in_specs=[stays_in_hbm] + [whole_in_vmem] * 5,
        out_specs=[whole_in_vmem] * (pairs + 5),
        scratch_shapes=[
            pltpu.SMEM(lengths.shape, jnp.int32),
            pltpu.VMEM((seen_rows, lanes), f32),
            pltpu.SemaphoreType.DMA,
        ],
        compiler_params=pltpu.CompilerParams(vmem_limit_bytes=6 * 2**20),
        name="project",
        cost_estimate=pl.CostEstimate(
            flops=2 * rows * weight.size + 2 * seen_rows * slots * lanes,
            bytes_accessed=2 * (weight.size + keys.size),
            transcendentals=0,
        ),
    )(*in_hbm(lengths), tokens, weight, queries, keys, after)
    return outs[:pairs], *outs[pairs:]


def attend_kernel(
    head_count,
    lengths_hbm,
    scores_ref,
    values_ref,
    _,
    total_ref,
    peak_ref,
    sum_ref,
    lengths_ref,
    raised,
    length_sem,
):
    lengths_copy = pltpu.make_async_copy(lengths_hbm, lengths_ref, length_sem)
    lengths_copy.start()
    row_count, slots, _ = values_ref.shape
    seen = scores_ref.shape[0] // (head_count * row_count)
    places = [
        (b, h, slice((h * row_count + b) * seen, (h * row_count + b + 1) * seen))
        for b in range(row_count)
        for h in range(head_count)
    ]
    lengths_copy.wait()
    slot = lax.broadcasted_iota(jnp.int32, (seen, slots), 1)
    for b, h, place in places:
        score = jnp.where(slot < lengths_ref[b], scores_ref[place, :], masked_score)
        peak = jnp.max(score, axis=1, keepdims=True)
        lifted = jnp.exp2((score - peak) * exponent_scale)
        raised[place, :] = lifted.astype(bf16)
        peak_ref[place, :] = jnp.broadcast_to(peak, (seen, lanes))
        sum_ref[place, :] = jnp.broadcast_to(
            jnp.sum(lifted, axis=1, keepdims=True), (seen, lanes)
        )
    for b, h, place in places:
        total_ref[place, :] = jnp.dot(
            raised[place, :],
            values_ref[b, :, h * lanes : (h + 1) * lanes],
            preferred_element_type=f32,
        )


def attend(lengths, scores, values, after):
    row_count, slots, width = values.shape
    seen_rows = scores.shape[0]
    seen_table = jax.ShapeDtypeStruct((seen_rows, lanes), f32)
    return pl.pallas_call(
        functools.partial(attend_kernel, width // lanes),
        out_shape=(seen_table,) * 3,
        in_specs=[stays_in_hbm] + [whole_in_vmem] * 3,
        out_specs=(whole_in_vmem,) * 3,
        scratch_shapes=[
            pltpu.SMEM(lengths.shape, jnp.int32),
            pltpu.VMEM((seen_rows, slots), bf16),
            pltpu.SemaphoreType.DMA,
        ],
        compiler_params=pltpu.CompilerParams(vmem_limit_bytes=6 * 2**20),
        name="attend",
        cost_estimate=pl.CostEstimate(
            flops=2 * seen_rows * slots * lanes,
            bytes_accessed=2 * values.size,
            transcendentals=seen_rows * slots,
        ),
    )(*in_hbm(lengths), scores, values, after)


def add_near(kept, near):
    rows, own = kept.shape
    return [
        kept[:, c * lanes : (c + 1) * lanes] + near[c * rows : (c + 1) * rows, :].astype(f32)
        for c in range(own // lanes)
    ]


def carries_sums(i):
    return i > 0 and i % 2 == 0


def route_kernel(replicas, shards, *refs):
    owners_ref, tokens_ref, kept_ref = refs[:3]
    piece_refs = refs[3 : 3 + replicas]
    near_refs = refs[3 + replicas : 3 + replicas + shards // 2]
    out_refs = refs[3 + replicas + shards // 2 : 3 + replicas + shards // 2 + shards]
    token_buf, left, right, up_buf = refs[3 + replicas + shards // 2 + shards :]
    replica = lax.axis_index("rollout")
    shard = lax.axis_index("tensor")
    rows, depth = tokens_ref.shape
    rank = right.shape[0]
    down_rows = depth // replicas
    width = token_buf.shape[2]
    rest = down_rows % lanes
    for k in range(replicas):
        token_buf[k, :, :down_rows] = tokens_ref[:, k * down_rows : (k + 1) * down_rows]
        if rest:
            token_buf[k, :, down_rows:] = jnp.zeros((rows, width - down_rows), bf16)
    for i in range(replicas):
        source = replica ^ i
        place = jnp.int32(0)
        for k in range(1, replicas):
            place = place + jnp.where(owners_ref[k] == source, k, 0)
        left[:, i * width : (i + 1) * width] = token_buf[place]
        first = 0
        for c in range(down_rows // lanes):
            right[:, i * width + c * lanes : i * width + (c + 1) * lanes] = piece_refs[i][
                first : first + rank, :
            ]
            first += rank
        if rest:
            both = piece_refs[i][first : first + rank // 2, :]
            tail = jnp.concatenate([both[:, :rest], both[:, rest:]], axis=0)
            right[:, (i + 1) * width - lanes : (i + 1) * width] = jnp.concatenate(
                [tail, jnp.zeros((rank, lanes - rest), bf16)], axis=1
            )
            first += rank // 2
        up_buf[i] = piece_refs[i][first:, :]
    lowered = lax.dot_general(
        left[...], right[...], (((1,), (1,)), ((), ())), preferred_element_type=f32
    )
    both = jnp.concatenate(split_halves(lowered), axis=1)
    for i in range(shards):
        first = 0
        if carries_sums(i):
            for block in add_near(kept_ref[i // 2], near_refs[i // 2]):
                out_refs[i][first : first + rows, :] = block.astype(bf16)
                first += rows
        out_refs[i][first : first + rows, :] = both
        out_refs[i][first + rows :, :] = up_buf[owners_ref[shard ^ i] ^ replica]


def route(owners, tokens, sums, pieces, rank, up_rows, shards):
    rows, depth = tokens.shape
    replicas = len(pieces)
    kept, near = sums
    sent = near[0].shape[0]
    width = -(-depth // replicas // lanes) * lanes
    return pl.pallas_call(
        functools.partial(route_kernel, replicas, shards),
        out_shape=[
            jax.ShapeDtypeStruct(((sent if carries_sums(i) else 0) + rows + up_rows, lanes), bf16)
            for i in range(shards)
        ],
        in_specs=[whole_in_smem] + [whole_in_vmem] * (2 + replicas + len(near)),
        out_specs=[whole_in_vmem] * shards,
        scratch_shapes=[
            pltpu.VMEM((replicas, rows, width), bf16),
            pltpu.VMEM((rows, replicas * width), bf16),
            pltpu.VMEM((rank, replicas * width), bf16),
            pltpu.VMEM((replicas, up_rows, lanes), bf16),
        ],
        compiler_params=pltpu.CompilerParams(vmem_limit_bytes=4 * 2**20),
        name="route",
        cost_estimate=pl.CostEstimate(flops=0, bytes_accessed=800000, transcendentals=0),
    )(owners, tokens, kept, *pieces, *near)


def route_plain(owners, tokens, sums, down, up, rank_part, own, shards):
    kept, near = sums
    rank = down.shape[1]
    shard = lax.axis_index("tensor")
    first = shard * rank_part
    up_part = lax.dynamic_slice_in_dim(up, first, rank_part, axis=0)
    downs = lax.all_gather(down, "rollout", axis=0, tiled=False)
    ups = lax.all_gather(up_part, "rollout", axis=0, tiled=False)
    down_matrix = jnp.take(downs, owners, axis=0, mode="clip").reshape(-1, rank)
    up_matrix = jnp.take(ups, owners, axis=0, mode="clip").transpose(1, 0, 2)
    up_matrix = up_matrix.reshape(rank_part, -1)
    lowered = jnp.dot(tokens, down_matrix, preferred_element_type=f32)
    both = jnp.concatenate(split_halves(lowered), axis=1)
    packets = []
    for i in range(shards):
        up_block = lax.dynamic_slice_in_dim(up_matrix, (shard ^ i) * own, own, axis=1)
        parts = [both, side_by_side(up_block)]
        if carries_sums(i):
            sums = add_near(kept[i // 2], near[i // 2])
            parts = [jnp.concatenate(sums, axis=0).astype(bf16)] + parts
        packets.append(jnp.concatenate(parts, axis=0))
    return packets


def finish_kernel(step_count, row_count, head_count, shards, *refs):
    kept_ref, near_ref, gain_ref, grouped_ref, total_ref, peak_ref, sum_ref = refs[:7]
    cosine_ref, sine_ref = refs[7:9]
    packet_refs = refs[9 : 9 + shards][::-1]
    attention_ref, keys_ref, values_ref = refs[9 + shards : 12 + shards]
    up_buf, ordered = refs[12 + shards :]
    shard = lax.axis_index("tensor")
    rows = step_count * row_count
    own = kept_ref.shape[2]
    blocks = own // lanes
    rank = up_buf.shape[0]
    rank_part = rank // shards
    group = grouped_ref.shape[0] // (head_count * rows)
    seen = step_count * group

    lowered = jnp.zeros((rows, lanes), f32)
    for i in range(shards):
        first = rows * blocks if carries_sums(i) else 0
        lowered = lowered + packet_refs[i][first : first + rows, :].astype(f32)
        ups = packet_refs[i][first + rows :, :].astype(f32)
        at = pl.multiple_of((shard ^ i) * rank_part, rank_part)
        for c in range(blocks):
            up_buf[pl.ds(at, rank_part), c * lanes : (c + 1) * lanes] = ups[
                c * rank_part : (c + 1) * rank_part, :
            ]
    lane = lax.broadcasted_iota(jnp.int32, (rows, lanes), 1)
    lowered = lowered + pltpu.roll(lowered, rank, 1)
    high, low = split_halves(lowered)
    left = jnp.where(lane < rank, high.astype(f32), low.astype(f32)).astype(bf16)
    up = up_buf[...].astype(bf16)
    raised_up = jnp.dot(left, jnp.concatenate([up, up], axis=0), preferred_element_type=f32)
    joined = []
    for c, block in enumerate(add_near(kept_ref[0], near_ref)):
        for i in filter(carries_sums, range(shards)):
            block = block + packet_refs[i][c * rows : (c + 1) * rows, :].astype(f32)
        joined.append(block + adapter_scale * raised_up[:, c * lanes : (c + 1) * lanes])

    all_rows = row_count * seen
    seen_by = lax.broadcasted_iota(jnp.int32, (all_rows, rows), 0)
    made_by = lax.broadcasted_iota(jnp.int32, (all_rows, rows), 1)
    visible = (seen_by // seen == made_by % row_count) & (
        made_by // row_count <= seen_by % seen // group
    )
    for h in range(head_count):
        raw_key = joined[2 * h]
        mean_square = jnp.mean(raw_key * raw_key, axis=1, keepdims=True)
        normed = raw_key * lax.rsqrt(mean_square + norm_eps) * gain_ref[...]
        key = normed * cosine_ref[...] + pltpu.roll(normed, lanes // 2, 1) * sine_ref[...]
        key = key.astype(bf16)
        value = joined[2 * h + 1].astype(bf16)
        keys_ref[:, h * lanes : (h + 1) * lanes] = key
        values_ref[:, h * lanes : (h + 1) * lanes] = value
        mine = slice(h * all_rows, (h + 1) * all_rows)
        score = lax.dot_general(
            grouped_ref[mine, :], key, (((1,), (1,)), ((), ())), preferred_element_type=f32
        )
        score = jnp.where(visible, score, masked_score)
        old_peak = peak_ref[mine, :]
        peak = jnp.maximum(old_peak, jnp.max(score, axis=1, keepdims=True))
        fade = jnp.exp2((old_peak - peak) * exponent_scale)
        lifted = jnp.exp2((score - peak[:, :rows]) * exponent_scale)
        denominator = fade * sum_ref[mine, :] + jnp.sum(lifted, axis=1, keepdims=True)
        total = fade * total_ref[mine, :] + jnp.dot(
            lifted.astype(bf16), value, preferred_element_type=f32
        )
        ordered[mine, :] = total / denominator
    for pair in range(step_count // 2):
        for q in range(head_count * group):
            h, g = q // group, q % group
            both = [
                ordered[
                    pl.ds(
                        h * all_rows + (pair * 2 + side) * group + g, row_count, stride=seen
                    ),
                    :,
                ]
                for side in range(2)
            ]
            attention_ref[
                pair * 2 * row_count : (pair + 1) * 2 * row_count, q * lanes : (q + 1) * lanes
            ] = jnp.concatenate(both, axis=0).astype(bf16)


def finish(kept, near, partials, gain, packets, rank, step_count, row_count, query_width):
    grouped, total, peak, denominator, cosine, sine = partials
    _, rows, own = kept.shape
    shards = len(packets)
    head_count = own // (2 * lanes)
    return pl.pallas_call(
        functools.partial(finish_kernel, step_count, row_count, head_count, shards),
        out_shape=(
            jax.ShapeDtypeStruct((rows, query_width), bf16),
            jax.ShapeDtypeStruct((rows, head_count * lanes), bf16),
            jax.ShapeDtypeStruct((rows, head_count * lanes), bf16),
        ),
        in_specs=[whole_in_vmem] * (9 + shards),
        out_specs=(whole_in_vmem,) * 3,
        scratch_shapes=[
            pltpu.VMEM((rank, own), f32),
            pltpu.VMEM(total.shape, f32),
        ],
        compiler_params=pltpu.CompilerParams(vmem_limit_bytes=6 * 2**20),
        name="finish",
        cost_estimate=pl.CostEstimate(flops=0, bytes_accessed=1000000, transcendentals=0),
    )(kept, near, gain, grouped, total, peak, denominator, cosine, sine, *packets[::-1])


def per_device(
    normed_tokens,
    key_value_weight,
    adapter_down,
    adapter_up,
    key_gain,
    queries,
    cache_keys,
    stored_values,
    lengths,
    owners,
):
    replicas = lax.axis_size("rollout")
    shards = lax.axis_size("tensor")
    down_rows, rank = adapter_down.shape
    step_count, row_count, depth = normed_tokens.shape
    own = key_value_weight.shape[1] // shards
    rank_part = rank // shards
    rows = step_count * row_count
    tokens = normed_tokens.reshape(rows, depth)
    query_rows = queries.reshape(rows, -1)

    fits = (
        replicas <= 4
        and adapter_up.shape[1] == own
        and down_rows % lanes in (0, lanes // 2)
        and rank == lanes // 2
        and rank_part % 16 == 0
    )
    if fits:
        fetched = 2 * (key_value_weight.size + cache_keys.size + stored_values.size)
        beside = pl.CostEstimate(flops=1000 * fetched, bytes_accessed=fetched, transcendentals=0)
        packed = pack(adapter_down.T, adapter_up, rank_part, beside)
        arrived = {i: swap(packed, "rollout", i) for i in reversed(range(1, replicas))}
        pieces = [packed] + [arrived[i] for i in range(1, replicas)]
    near, kept, grouped, scores, cosine, sine = project(
        lengths,
        tokens,
        key_value_weight,
        query_rows,
        cache_keys,
        packed if fits else adapter_up,
        step_count,
        shards,
    )
    near = [swap(block, "tensor", 1) for block in near]
    if fits:
        packets = route(
            owners, tokens, (kept, near), pieces, rank, rank_part * own // lanes, shards
        )
    else:
        packets = route_plain(
            owners, tokens, (kept, near), adapter_down, adapter_up, rank_part, own, shards
        )
    total, peak, denominator = attend(lengths, scores, stored_values, packets[0])
    packets = [packets[0]] + [swap(packets[i], "tensor", i) for i in range(1, shards)]
    attention, keys, values = finish(
        kept,
        near[0],
        (grouped, total, peak, denominator, cosine, sine),
        key_gain.reshape(1, -1),
        packets,
        rank,
        step_count,
        row_count,
        query_rows.shape[1],
    )
    return tuple(a.reshape(step_count, row_count, -1) for a in (attention, keys, values))


def solution(mesh):
    placed = (
        P(None, ("job", "rollout"), "tensor"),
        P("tensor", None),
        P(("job", "rollout", "tensor"), None),
        P(None, ("job", "rollout")),
        P(),
        P(None, ("job", "rollout"), "tensor"),
        P(("job", "rollout"), None, "tensor"),
        P(("job", "rollout"), None, "tensor"),
        P(("job", "rollout")),
        P("job"),
    )
    return jax.shard_map(
        per_device,
        mesh=mesh,
        in_specs=placed,
        out_specs=(
            P(None, ("job", "rollout"), "tensor"),
            P(None, ("job", "rollout"), "tensor"),
            P(None, ("job", "rollout"), "tensor"),
        ),
        check_vma=False,
    )
```

```python
import functools
import math

import jax
import jax.numpy as jnp
from jax import lax
from jax.experimental import pallas as pl
from jax.experimental.pallas import tpu as pltpu
from jax.sharding import PartitionSpec as P

norm_eps = 1e-06
rope_base = 1000000.0
adapter_scale = 2.0
masked_score = -1e30
lanes = 128
exponent_scale = lanes**-0.5 / math.log(2.0)
f32 = jnp.float32
bf16 = jnp.bfloat16

whole_in_vmem = pl.BlockSpec(memory_space=pltpu.VMEM)
whole_in_smem = pl.BlockSpec(memory_space=pltpu.SMEM)
stays_in_hbm = pl.BlockSpec(memory_space=pltpu.HBM)


def swap(block, axis, offset):
    count = lax.axis_size(axis)
    return lax.ppermute(block, axis, [(s, s ^ offset) for s in range(count)])


def shift(block, axis, offset):
    count = lax.axis_size(axis)
    return lax.ppermute(block, axis, [((s + offset) % count, s) for s in range(count)])


def in_hbm(*arrays):
    return tuple(pltpu.with_memory_space_constraint(a, pltpu.HBM) for a in arrays)


def side_by_side(rows_of_blocks):
    r, c = rows_of_blocks.shape
    return rows_of_blocks.reshape(r, c // lanes, lanes).transpose(1, 0, 2).reshape(-1, lanes)


def split_halves(total):
    high = total.astype(bf16)
    return high, (total - high.astype(f32)).astype(bf16)


def pack_kernel(down_hbm, up_hbm, out_ref, down_ref, up_ref, sems):
    rank, down_rows = down_ref.shape
    rank_part = up_ref.shape[0]
    start = pl.multiple_of(lax.axis_index("tensor") * rank_part, rank_part)
    copies = [
        pltpu.make_async_copy(down_hbm, down_ref, sems.at[0]),
        pltpu.make_async_copy(up_hbm.at[pl.ds(start, rank_part), :], up_ref, sems.at[1]),
    ]
    for copy in copies:
        copy.start()
    for copy in copies:
        copy.wait()
    first = 0
    for c in range(down_rows // lanes):
        out_ref[first : first + rank, :] = down_ref[:, c * lanes : (c + 1) * lanes]
        first += rank
    rest = down_rows % lanes
    if rest:
        half = rank // 2
        tail = down_ref[:, down_rows - rest :]
        out_ref[first : first + half, :] = jnp.concatenate([tail[:half], tail[half:]], axis=1)
        first += half
    for c in range(up_ref.shape[1] // lanes):
        out_ref[first : first + rank_part, :] = up_ref[:, c * lanes : (c + 1) * lanes]
        first += rank_part


def pack(down, up, rank_part, beside):
    rows = (down.size + rank_part * up.shape[1]) // lanes
    return pl.pallas_call(
        pack_kernel,
        out_shape=jax.ShapeDtypeStruct((rows, lanes), bf16),
        in_specs=[stays_in_hbm] * 2,
        out_specs=whole_in_vmem,
        scratch_shapes=[
            pltpu.VMEM(down.shape, bf16),
            pltpu.VMEM((rank_part, up.shape[1]), bf16),
            pltpu.SemaphoreType.DMA((2,)),
        ],
        compiler_params=pltpu.CompilerParams(vmem_limit_bytes=2 * 2**20),
        name="pack",
        cost_estimate=beside,
    )(*in_hbm(down, up))


def project_kernel(step_count, head_count, shards, replicas, *refs):
    lengths_hbm, owners_hbm, tokens_ref, weight_ref, queries_ref, keys_ref, _ = refs[:7]
    pairs = shards // 2
    near_refs = refs[7 : 7 + pairs]
    kept_ref, grouped_ref, scores_ref, cosine_ref, sine_ref, left_ref = refs[7 + pairs : 13 + pairs]
    lengths_ref, owners_ref, regroup, token_buf, sems = refs[13 + pairs :]
    lengths_copy = pltpu.make_async_copy(lengths_hbm, lengths_ref, sems.at[0])
    owners_copy = pltpu.make_async_copy(owners_hbm, owners_ref, sems.at[1])
    lengths_copy.start()
    owners_copy.start()

    row_count = keys_ref.shape[0]
    group = queries_ref.shape[1] // (head_count * lanes)
    seen = step_count * group
    for pair in range(step_count // 2):
        for q in range(head_count * group):
            h, g = q // group, q % group
            both = queries_ref[
                pair * 2 * row_count : (pair + 1) * 2 * row_count, q * lanes : (q + 1) * lanes
            ].astype(f32)
            for side in range(2):
                first = h * row_count * seen + (pair * 2 + side) * group + g
                regroup[pl.ds(first, row_count, stride=seen), :] = both[
                    side * row_count : (side + 1) * row_count, :
                ]
            if g % 2:
                for side in range(2):
                    half = slice(side * row_count, (side + 1) * row_count)
                    last = (h * seen + (pair * 2 + side) * group + g + 1) * row_count
                    grouped_ref[last - 2 * row_count : last, :] = jnp.concatenate(
                        [before[half], both[half]], axis=0
                    ).astype(bf16)
            before = both

    shard = lax.axis_index("tensor")
    _, rows, own = kept_ref.shape
    for i in range(shards):
        first = pl.multiple_of((shard ^ i) * own, lanes)
        block = jnp.dot(
            tokens_ref[...], weight_ref[:, pl.ds(first, own)], preferred_element_type=f32
        )
        if i % 2 == 0:
            kept_ref[i // 2] = block
            continue
        for c in range(own // lanes):
            near_refs[i // 2][c * rows : (c + 1) * rows, :] = block[
                :, c * lanes : (c + 1) * lanes
            ].astype(bf16)

    for b in range(row_count):
        for h in range(head_count):
            at = (h * row_count + b) * seen
            scores_ref[at : at + seen, :] = lax.dot_general(
                regroup[at : at + seen, :].astype(bf16),
                keys_ref[b, :, h * lanes : (h + 1) * lanes],
                (((1,), (1,)), ((), ())),
                preferred_element_type=f32,
            )

    lengths_copy.wait()
    row = lax.broadcasted_iota(jnp.int32, (rows, lanes), 0)
    lane = lax.broadcasted_iota(jnp.int32, (rows, lanes), 1)
    position = row // row_count
    for b in range(row_count):
        position = position + jnp.where(row % row_count == b, lengths_ref[b], 0)
    middle = lanes // 2
    spacing = (lane % middle).astype(f32) * (-2.0 / lanes * math.log(rope_base))
    angles = position.astype(f32) * jnp.exp(spacing)
    cosine_ref[...] = jnp.cos(angles)
    sine = jnp.sin(angles)
    sine_ref[...] = jnp.where(lane < middle, -sine, sine)

    owners_copy.wait()
    width = token_buf.shape[2]
    down_rows = tokens_ref.shape[1] // replicas
    for k in range(replicas):
        token_buf[k, :, :down_rows] = tokens_ref[:, k * down_rows : (k + 1) * down_rows]
        if down_rows < width:
            token_buf[k, :, down_rows:] = jnp.zeros((rows, width - down_rows), bf16)
    for i in range(replicas):
        source = lax.rem(lax.axis_index("rollout") + i, replicas)
        place = jnp.int32(0)
        for k in range(1, replicas):
            place = place + jnp.where(owners_ref[k] == source, k, 0)
        left_ref[:, i * width : (i + 1) * width] = token_buf[place]


def project(
    lengths, owners, tokens, weight, queries, keys, after, step_count, shards, replicas
):
    rows, depth = tokens.shape
    own = weight.shape[1] // shards
    pairs = shards // 2
    row_count, slots, width = keys.shape
    seen_rows = rows * queries.shape[1] // lanes
    table = jax.ShapeDtypeStruct((rows, lanes), f32)
    piece_width = -(-depth // replicas // lanes) * lanes
    outs = pl.pallas_call(
        functools.partial(project_kernel, step_count, width // lanes, shards, replicas),
        out_shape=[jax.ShapeDtypeStruct((rows * own // lanes, lanes), bf16)] * pairs
        + [
            jax.ShapeDtypeStruct((pairs, rows, own), f32),
            jax.ShapeDtypeStruct((seen_rows, lanes), bf16),
            jax.ShapeDtypeStruct((seen_rows, slots), f32),
            table,
            table,
            jax.ShapeDtypeStruct((rows, replicas * piece_width), bf16),
        ],
        in_specs=[stays_in_hbm] * 2 + [whole_in_vmem] * 5,
        out_specs=[whole_in_vmem] * (pairs + 6),
        scratch_shapes=[
            pltpu.SMEM(lengths.shape, jnp.int32),
            pltpu.SMEM(owners.shape, jnp.int32),
            pltpu.VMEM((seen_rows, lanes), f32),
            pltpu.VMEM((replicas, rows, piece_width), bf16),
            pltpu.SemaphoreType.DMA((2,)),
        ],
        compiler_params=pltpu.CompilerParams(vmem_limit_bytes=6 * 2**20),
        name="project",
        cost_estimate=pl.CostEstimate(
            flops=2 * rows * weight.size + 2 * seen_rows * slots * lanes,
            bytes_accessed=2 * (weight.size + keys.size),
            transcendentals=0,
        ),
    )(*in_hbm(lengths, owners), tokens, weight, queries, keys, after)
    return outs[:pairs], *outs[pairs:]


def attend_kernel(
    head_count,
    lengths_hbm,
    scores_ref,
    values_ref,
    _,
    total_ref,
    peak_ref,
    sum_ref,
    lengths_ref,
    raised,
    length_sem,
):
    lengths_copy = pltpu.make_async_copy(lengths_hbm, lengths_ref, length_sem)
    lengths_copy.start()
    row_count, slots, _ = values_ref.shape
    seen = scores_ref.shape[0] // (head_count * row_count)
    places = [
        (
            b,
            h,
            slice((h * row_count + b) * seen, (h * row_count + b + 1) * seen),
            pl.ds(h * row_count * seen + b, seen, stride=row_count),
        )
        for b in range(row_count)
        for h in range(head_count)
    ]
    lengths_copy.wait()
    slot = lax.broadcasted_iota(jnp.int32, (seen, slots), 1)
    for b, h, place, out in places:
        score = jnp.where(slot < lengths_ref[b], scores_ref[place, :], masked_score)
        peak = jnp.max(score, axis=1, keepdims=True)
        lifted = jnp.exp2((score - peak) * exponent_scale)
        raised[place, :] = lifted.astype(bf16)
        peak_ref[out, :] = jnp.broadcast_to(peak, (seen, lanes))
        sum_ref[out, :] = jnp.broadcast_to(
            jnp.sum(lifted, axis=1, keepdims=True), (seen, lanes)
        )
    for b, h, place, out in places:
        total_ref[out, :] = jnp.dot(
            raised[place, :],
            values_ref[b, :, h * lanes : (h + 1) * lanes],
            preferred_element_type=f32,
        )


def attend(lengths, scores, values, after):
    row_count, slots, width = values.shape
    seen_rows = scores.shape[0]
    seen_table = jax.ShapeDtypeStruct((seen_rows, lanes), f32)
    return pl.pallas_call(
        functools.partial(attend_kernel, width // lanes),
        out_shape=(seen_table,) * 3,
        in_specs=[stays_in_hbm] + [whole_in_vmem] * 3,
        out_specs=(whole_in_vmem,) * 3,
        scratch_shapes=[
            pltpu.SMEM(lengths.shape, jnp.int32),
            pltpu.VMEM((seen_rows, slots), bf16),
            pltpu.SemaphoreType.DMA,
        ],
        compiler_params=pltpu.CompilerParams(vmem_limit_bytes=6 * 2**20),
        name="attend",
        cost_estimate=pl.CostEstimate(
            flops=2 * seen_rows * slots * lanes,
            bytes_accessed=2 * values.size,
            transcendentals=seen_rows * slots,
        ),
    )(*in_hbm(lengths), scores, values, after)


def add_near(kept, near):
    rows, own = kept.shape
    return [
        kept[:, c * lanes : (c + 1) * lanes] + near[c * rows : (c + 1) * rows, :].astype(f32)
        for c in range(own // lanes)
    ]


def carries_sums(i):
    return i > 0 and i % 2 == 0


def route_kernel(replicas, shards, *refs):
    owners_hbm, left_ref, kept_ref = refs[:3]
    piece_refs = refs[3 : 3 + replicas]
    near_refs = refs[3 + replicas : 3 + replicas + shards // 2]
    out_refs = refs[3 + replicas + shards // 2 : 3 + replicas + shards // 2 + shards]
    owners_ref, right, up_buf, owner_sem = refs[3 + replicas + shards // 2 + shards :]
    owners_copy = pltpu.make_async_copy(owners_hbm, owners_ref, owner_sem)
    owners_copy.start()
    rows = left_ref.shape[0]
    rank = right.shape[0]
    width = right.shape[1] // replicas
    half = rank // 2
    rest = (piece_refs[0].shape[0] - up_buf.shape[1]) % rank
    for i in range(replicas):
        first = 0
        for c in range(width // lanes - (1 if rest else 0)):
            right[:, i * width + c * lanes : i * width + (c + 1) * lanes] = piece_refs[i][
                first : first + rank, :
            ]
            first += rank
        if rest:
            both = piece_refs[i][first : first + half, :]
            tail = jnp.concatenate([both[:, : lanes // 2], both[:, lanes // 2 :]], axis=0)
            right[:, (i + 1) * width - lanes : (i + 1) * width] = jnp.concatenate(
                [tail, jnp.zeros((rank, lanes // 2), bf16)], axis=1
            )
            first += half
        up_buf[i] = piece_refs[i][first:, :]
    lowered = lax.dot_general(
        left_ref[...], right[...], (((1,), (1,)), ((), ())), preferred_element_type=f32
    )
    both = jnp.concatenate(split_halves(lowered), axis=1)
    replica = lax.axis_index("rollout")
    shard = lax.axis_index("tensor")
    owners_copy.wait()
    for i in range(shards):
        first = 0
        if carries_sums(i):
            for block in add_near(kept_ref[i // 2], near_refs[i // 2]):
                out_refs[i][first : first + rows, :] = block.astype(bf16)
                first += rows
        out_refs[i][first : first + rows, :] = both
        slot = lax.rem(owners_ref[shard ^ i] + replicas - replica, replicas)
        out_refs[i][first + rows :, :] = up_buf[slot]


def route(owners, left, sums, pieces, rank, up_rows, shards):
    rows, depth = left.shape
    replicas = len(pieces)
    kept, near = sums
    sent = near[0].shape[0]
    return pl.pallas_call(
        functools.partial(route_kernel, replicas, shards),
        out_shape=[
            jax.ShapeDtypeStruct(((sent if carries_sums(i) else 0) + rows + up_rows, lanes), bf16)
            for i in range(shards)
        ],
        in_specs=[stays_in_hbm] + [whole_in_vmem] * (2 + replicas + len(near)),
        out_specs=[whole_in_vmem] * shards,
        scratch_shapes=[
            pltpu.SMEM(owners.shape, jnp.int32),
            pltpu.VMEM((rank, depth), bf16),
            pltpu.VMEM((replicas, up_rows, lanes), bf16),
            pltpu.SemaphoreType.DMA,
        ],
        compiler_params=pltpu.CompilerParams(vmem_limit_bytes=4 * 2**20),
        name="route",
        cost_estimate=pl.CostEstimate(flops=0, bytes_accessed=800000, transcendentals=0),
    )(*in_hbm(owners), left, kept, *pieces, *near)


def route_plain(owners, tokens, sums, down, up, rank_part, own, shards):
    kept, near = sums
    rank = down.shape[1]
    shard = lax.axis_index("tensor")
    first = shard * rank_part
    up_part = lax.dynamic_slice_in_dim(up, first, rank_part, axis=0)
    downs = lax.all_gather(down, "rollout", axis=0, tiled=False)
    ups = lax.all_gather(up_part, "rollout", axis=0, tiled=False)
    down_matrix = jnp.take(downs, owners, axis=0, mode="clip").reshape(-1, rank)
    up_matrix = jnp.take(ups, owners, axis=0, mode="clip").transpose(1, 0, 2)
    up_matrix = up_matrix.reshape(rank_part, -1)
    lowered = jnp.dot(tokens, down_matrix, preferred_element_type=f32)
    both = jnp.concatenate(split_halves(lowered), axis=1)
    packets = []
    for i in range(shards):
        up_block = lax.dynamic_slice_in_dim(up_matrix, (shard ^ i) * own, own, axis=1)
        parts = [both, side_by_side(up_block)]
        if carries_sums(i):
            sums = add_near(kept[i // 2], near[i // 2])
            parts = [jnp.concatenate(sums, axis=0).astype(bf16)] + parts
        packets.append(jnp.concatenate(parts, axis=0))
    return packets


def finish_kernel(step_count, row_count, head_count, shards, *refs):
    kept_ref, near_ref, gain_ref, grouped_ref, total_ref, peak_ref, sum_ref = refs[:7]
    cosine_ref, sine_ref = refs[7:9]
    packet_refs = refs[9 : 9 + shards][::-1]
    attention_ref, keys_ref, values_ref = refs[9 + shards : 12 + shards]
    (up_buf,) = refs[12 + shards :]
    shard = lax.axis_index("tensor")
    rows = step_count * row_count
    own = kept_ref.shape[2]
    blocks = own // lanes
    rank = up_buf.shape[0]
    rank_part = rank // shards
    group = grouped_ref.shape[0] // (head_count * rows)
    seen = step_count * group

    lowered = jnp.zeros((rows, lanes), f32)
    for i in range(shards):
        first = rows * blocks if carries_sums(i) else 0
        lowered = lowered + packet_refs[i][first : first + rows, :].astype(f32)
        ups = packet_refs[i][first + rows :, :].astype(f32)
        at = pl.multiple_of((shard ^ i) * rank_part, rank_part)
        for c in range(blocks):
            up_buf[pl.ds(at, rank_part), c * lanes : (c + 1) * lanes] = ups[
                c * rank_part : (c + 1) * rank_part, :
            ]
    lane = lax.broadcasted_iota(jnp.int32, (rows, lanes), 1)
    lowered = lowered + pltpu.roll(lowered, rank, 1)
    high, low = split_halves(lowered)
    left = jnp.where(lane < rank, high.astype(f32), low.astype(f32)).astype(bf16)
    up = up_buf[...].astype(bf16)
    raised_up = jnp.dot(left, jnp.concatenate([up, up], axis=0), preferred_element_type=f32)
    joined = []
    for c, block in enumerate(add_near(kept_ref[0], near_ref)):
        for i in filter(carries_sums, range(shards)):
            block = block + packet_refs[i][c * rows : (c + 1) * rows, :].astype(f32)
        joined.append(block + adapter_scale * raised_up[:, c * lanes : (c + 1) * lanes])

    all_rows = row_count * seen
    seen_by = lax.broadcasted_iota(jnp.int32, (all_rows, rows), 0)
    made_by = lax.broadcasted_iota(jnp.int32, (all_rows, rows), 1)
    visible = (seen_by % row_count == made_by % row_count) & (
        made_by // row_count <= seen_by // (row_count * group)
    )
    heads = [(h, slice(h * all_rows, (h + 1) * all_rows)) for h in range(head_count)]
    keys, values, scores, results = [], [], [], []
    for h, _ in heads:
        raw_key = joined[2 * h]
        mean_square = jnp.mean(raw_key * raw_key, axis=1, keepdims=True)
        normed = raw_key * lax.rsqrt(mean_square + norm_eps) * gain_ref[...]
        key = normed * cosine_ref[...] + pltpu.roll(normed, lanes // 2, 1) * sine_ref[...]
        keys.append(key.astype(bf16))
        values.append(joined[2 * h + 1].astype(bf16))
        keys_ref[:, h * lanes : (h + 1) * lanes] = keys[h]
        values_ref[:, h * lanes : (h + 1) * lanes] = values[h]
    for h, mine in heads:
        score = lax.dot_general(
            grouped_ref[mine, :], keys[h], (((1,), (1,)), ((), ())), preferred_element_type=f32
        )
        scores.append(jnp.where(visible, score, masked_score))
    for h, mine in heads:
        old_peak = peak_ref[mine, :]
        peak = jnp.maximum(old_peak, jnp.max(scores[h], axis=1, keepdims=True))
        fade = jnp.exp2((old_peak - peak) * exponent_scale)
        lifted = jnp.exp2((scores[h] - peak[:, :rows]) * exponent_scale)
        denominator = fade * sum_ref[mine, :] + jnp.sum(lifted, axis=1, keepdims=True)
        total = fade * total_ref[mine, :] + jnp.dot(
            lifted.astype(bf16), values[h], preferred_element_type=f32
        )
        results.append(total / denominator)
    for pair in range(step_count // 2):
        for q in range(head_count * group):
            h, g = q // group, q % group
            both = []
            for side in range(2):
                first = ((pair * 2 + side) * group + g) * row_count
                both.append(results[h][first : first + row_count])
            attention_ref[
                pair * 2 * row_count : (pair + 1) * 2 * row_count, q * lanes : (q + 1) * lanes
            ] = jnp.concatenate(both, axis=0).astype(bf16)


def finish(kept, near, partials, gain, packets, rank, step_count, row_count, query_width):
    grouped, total, peak, denominator, cosine, sine = partials
    _, rows, own = kept.shape
    shards = len(packets)
    head_count = own // (2 * lanes)
    return pl.pallas_call(
        functools.partial(finish_kernel, step_count, row_count, head_count, shards),
        out_shape=(
            jax.ShapeDtypeStruct((rows, query_width), bf16),
            jax.ShapeDtypeStruct((rows, head_count * lanes), bf16),
            jax.ShapeDtypeStruct((rows, head_count * lanes), bf16),
        ),
        in_specs=[whole_in_vmem] * (9 + shards),
        out_specs=(whole_in_vmem,) * 3,
        scratch_shapes=[
            pltpu.VMEM((rank, own), f32),
        ],
        compiler_params=pltpu.CompilerParams(vmem_limit_bytes=6 * 2**20),
        name="finish",
        cost_estimate=pl.CostEstimate(flops=0, bytes_accessed=1000000, transcendentals=0),
    )(kept, near, gain, grouped, total, peak, denominator, cosine, sine, *packets[::-1])


def per_device(
    normed_tokens,
    key_value_weight,
    adapter_down,
    adapter_up,
    key_gain,
    queries,
    cache_keys,
    stored_values,
    lengths,
    owners,
):
    replicas = lax.axis_size("rollout")
    shards = lax.axis_size("tensor")
    down_rows, rank = adapter_down.shape
    step_count, row_count, depth = normed_tokens.shape
    own = key_value_weight.shape[1] // shards
    rank_part = rank // shards
    rows = step_count * row_count
    tokens = normed_tokens.reshape(rows, depth)
    query_rows = queries.reshape(rows, -1)

    fits = (
        replicas <= 4
        and adapter_up.shape[1] == own
        and down_rows % lanes in (0, lanes // 2)
        and rank == lanes // 2
        and rank_part % 16 == 0
    )
    if fits:
        fetched = 2 * (key_value_weight.size + cache_keys.size + stored_values.size)
        beside = pl.CostEstimate(flops=1000 * fetched, bytes_accessed=fetched, transcendentals=0)
        packed = pack(adapter_down.T, adapter_up, rank_part, beside)
        pieces = [packed] + [shift(packed, "rollout", i) for i in range(1, replicas)]
    near, kept, grouped, scores, cosine, sine, left = project(
        lengths,
        owners,
        tokens,
        key_value_weight,
        query_rows,
        cache_keys,
        packed if fits else adapter_up,
        step_count,
        shards,
        replicas if fits else 1,
    )
    near = [swap(block, "tensor", 1) for block in near]
    if fits:
        packets = route(
            owners, left, (kept, near), pieces, rank, rank_part * own // lanes, shards
        )
    else:
        packets = route_plain(
            owners, tokens, (kept, near), adapter_down, adapter_up, rank_part, own, shards
        )
    total, peak, denominator = attend(lengths, scores, stored_values, packets[0])
    packets = [packets[0]] + [swap(packets[i], "tensor", i) for i in range(1, shards)]
    attention, keys, values = finish(
        kept,
        near[0],
        (grouped, total, peak, denominator, cosine, sine),
        key_gain.reshape(1, -1),
        packets,
        rank,
        step_count,
        row_count,
        query_rows.shape[1],
    )
    return tuple(a.reshape(step_count, row_count, -1) for a in (attention, keys, values))


def solution(mesh):
    placed = (
        P(None, ("job", "rollout"), "tensor"),
        P("tensor", None),
        P(("job", "rollout", "tensor"), None),
        P(None, ("job", "rollout")),
        P(),
        P(None, ("job", "rollout"), "tensor"),
        P(("job", "rollout"), None, "tensor"),
        P(("job", "rollout"), None, "tensor"),
        P(("job", "rollout")),
        P("job"),
    )
    return jax.shard_map(
        per_device,
        mesh=mesh,
        in_specs=placed,
        out_specs=(
            P(None, ("job", "rollout"), "tensor"),
            P(None, ("job", "rollout"), "tensor"),
            P(None, ("job", "rollout"), "tensor"),
        ),
        check_vma=False,
    )
```

```python
import functools
import math

import jax
import jax.numpy as jnp
from jax import lax
from jax.experimental import pallas as pl
from jax.experimental.pallas import tpu as pltpu
from jax.sharding import PartitionSpec as P

norm_eps = 1e-06
rope_base = 1000000.0
adapter_scale = 2.0
masked_score = -1e30
lanes = 128
exponent_scale = lanes**-0.5 / math.log(2.0)
f32 = jnp.float32
bf16 = jnp.bfloat16

whole_in_vmem = pl.BlockSpec(memory_space=pltpu.VMEM)
whole_in_smem = pl.BlockSpec(memory_space=pltpu.SMEM)
stays_in_hbm = pl.BlockSpec(memory_space=pltpu.HBM)


def swap(block, axis, offset):
    count = lax.axis_size(axis)
    return lax.ppermute(block, axis, [(s, s ^ offset) for s in range(count)])


def shift(block, axis, offset):
    count = lax.axis_size(axis)
    return lax.ppermute(block, axis, [((s + offset) % count, s) for s in range(count)])


def in_hbm(*arrays):
    return tuple(pltpu.with_memory_space_constraint(a, pltpu.HBM) for a in arrays)


def side_by_side(rows_of_blocks):
    r, c = rows_of_blocks.shape
    return rows_of_blocks.reshape(r, c // lanes, lanes).transpose(1, 0, 2).reshape(-1, lanes)


def split_halves(total):
    high = total.astype(bf16)
    return high, (total - high.astype(f32)).astype(bf16)


def pack_kernel(down_hbm, up_hbm, out_ref, down_ref, up_ref, sems):
    rank, down_rows = down_ref.shape
    rank_part = up_ref.shape[0]
    start = pl.multiple_of(lax.axis_index("tensor") * rank_part, rank_part)
    copies = [
        pltpu.make_async_copy(down_hbm, down_ref, sems.at[0]),
        pltpu.make_async_copy(up_hbm.at[pl.ds(start, rank_part), :], up_ref, sems.at[1]),
    ]
    for copy in copies:
        copy.start()
    for copy in copies:
        copy.wait()
    first = 0
    for c in range(down_rows // lanes):
        out_ref[first : first + rank, :] = down_ref[:, c * lanes : (c + 1) * lanes]
        first += rank
    rest = down_rows % lanes
    if rest:
        half = rank // 2
        tail = down_ref[:, down_rows - rest :]
        out_ref[first : first + half, :] = jnp.concatenate([tail[:half], tail[half:]], axis=1)
        first += half
    for c in range(up_ref.shape[1] // lanes):
        out_ref[first : first + rank_part, :] = up_ref[:, c * lanes : (c + 1) * lanes]
        first += rank_part


def pack(down, up, rank_part, beside):
    rows = (down.size + rank_part * up.shape[1]) // lanes
    return pl.pallas_call(
        pack_kernel,
        out_shape=jax.ShapeDtypeStruct((rows, lanes), bf16),
        in_specs=[stays_in_hbm] * 2,
        out_specs=whole_in_vmem,
        scratch_shapes=[
            pltpu.VMEM(down.shape, bf16),
            pltpu.VMEM((rank_part, up.shape[1]), bf16),
            pltpu.SemaphoreType.DMA((2,)),
        ],
        compiler_params=pltpu.CompilerParams(vmem_limit_bytes=2 * 2**20),
        name="pack",
        cost_estimate=beside,
    )(*in_hbm(down, up))


def project_kernel(shards, replicas, *refs):
    owners_hbm, tokens_ref, weight_ref, _ = refs[:4]
    pairs = shards // 2
    near_refs = refs[4 : 4 + pairs]
    kept_ref, left_ref, owners_ref, token_buf, owner_sem = refs[4 + pairs :]
    owners_copy = pltpu.make_async_copy(owners_hbm, owners_ref, owner_sem)
    owners_copy.start()

    shard = lax.axis_index("tensor")
    _, rows, own = kept_ref.shape
    for i in range(shards):
        first = pl.multiple_of((shard ^ i) * own, lanes)
        block = jnp.dot(
            tokens_ref[...], weight_ref[:, pl.ds(first, own)], preferred_element_type=f32
        )
        if i % 2 == 0:
            kept_ref[i // 2] = block
            continue
        for c in range(own // lanes):
            near_refs[i // 2][c * rows : (c + 1) * rows, :] = block[
                :, c * lanes : (c + 1) * lanes
            ].astype(bf16)

    owners_copy.wait()
    width = token_buf.shape[2]
    down_rows = tokens_ref.shape[1] // replicas
    for k in range(replicas):
        token_buf[k, :, :down_rows] = tokens_ref[:, k * down_rows : (k + 1) * down_rows]
        if down_rows < width:
            token_buf[k, :, down_rows:] = jnp.zeros((rows, width - down_rows), bf16)
    for i in range(replicas):
        source = lax.rem(lax.axis_index("rollout") + i, replicas)
        place = jnp.int32(0)
        for k in range(1, replicas):
            place = place + jnp.where(owners_ref[k] == source, k, 0)
        left_ref[:, i * width : (i + 1) * width] = token_buf[place]


def project(owners, tokens, weight, after, shards, replicas):
    rows, depth = tokens.shape
    own = weight.shape[1] // shards
    pairs = shards // 2
    piece_width = -(-depth // replicas // lanes) * lanes
    outs = pl.pallas_call(
        functools.partial(project_kernel, shards, replicas),
        out_shape=[jax.ShapeDtypeStruct((rows * own // lanes, lanes), bf16)] * pairs
        + [
            jax.ShapeDtypeStruct((pairs, rows, own), f32),
            jax.ShapeDtypeStruct((rows, replicas * piece_width), bf16),
        ],
        in_specs=[stays_in_hbm] + [whole_in_vmem] * 3,
        out_specs=[whole_in_vmem] * (pairs + 2),
        scratch_shapes=[
            pltpu.SMEM(owners.shape, jnp.int32),
            pltpu.VMEM((replicas, rows, piece_width), bf16),
            pltpu.SemaphoreType.DMA,
        ],
        compiler_params=pltpu.CompilerParams(vmem_limit_bytes=4 * 2**20),
        name="project",
        cost_estimate=pl.CostEstimate(
            flops=2 * rows * weight.size, bytes_accessed=2 * weight.size, transcendentals=0
        ),
    )(*in_hbm(owners), tokens, weight, after)
    return outs[:pairs], *outs[pairs:]


def attend_kernel(
    step_count,
    head_count,
    lengths_hbm,
    queries_ref,
    keys_ref,
    values_ref,
    _,
    grouped_ref,
    total_ref,
    peak_ref,
    sum_ref,
    cosine_ref,
    sine_ref,
    lengths_ref,
    regroup,
    scores_ref,
    raised,
    length_sem,
):
    lengths_copy = pltpu.make_async_copy(lengths_hbm, lengths_ref, length_sem)
    lengths_copy.start()
    rows = cosine_ref.shape[0]

    row_count, slots, _ = keys_ref.shape
    group = queries_ref.shape[1] // (head_count * lanes)
    seen = step_count * group
    for pair in range(step_count // 2):
        for q in range(head_count * group):
            h, g = q // group, q % group
            both = queries_ref[
                pair * 2 * row_count : (pair + 1) * 2 * row_count, q * lanes : (q + 1) * lanes
            ].astype(f32)
            for side in range(2):
                first = h * row_count * seen + (pair * 2 + side) * group + g
                regroup[pl.ds(first, row_count, stride=seen), :] = both[
                    side * row_count : (side + 1) * row_count, :
                ]
            if g % 2:
                for side in range(2):
                    half = slice(side * row_count, (side + 1) * row_count)
                    last = (h * seen + (pair * 2 + side) * group + g + 1) * row_count
                    grouped_ref[last - 2 * row_count : last, :] = jnp.concatenate(
                        [before[half], both[half]], axis=0
                    ).astype(bf16)
            before = both

    for b in range(row_count):
        for h in range(head_count):
            at = (h * row_count + b) * seen
            scores_ref[at : at + seen, :] = lax.dot_general(
                regroup[at : at + seen, :].astype(bf16),
                keys_ref[b, :, h * lanes : (h + 1) * lanes],
                (((1,), (1,)), ((), ())),
                preferred_element_type=f32,
            )

    places = [
        (
            b,
            h,
            slice((h * row_count + b) * seen, (h * row_count + b + 1) * seen),
            pl.ds(h * row_count * seen + b, seen, stride=row_count),
        )
        for b in range(row_count)
        for h in range(head_count)
    ]
    lengths_copy.wait()
    slot = lax.broadcasted_iota(jnp.int32, (seen, slots), 1)
    for b, h, place, out in places:
        score = jnp.where(slot < lengths_ref[b], scores_ref[place, :], masked_score)
        peak = jnp.max(score, axis=1, keepdims=True)
        lifted = jnp.exp2((score - peak) * exponent_scale)
        raised[place, :] = lifted.astype(bf16)
        peak_ref[out, :] = jnp.broadcast_to(peak, (seen, lanes))
        sum_ref[out, :] = jnp.broadcast_to(
            jnp.sum(lifted, axis=1, keepdims=True), (seen, lanes)
        )
    for b, h, place, out in places:
        total_ref[out, :] = jnp.dot(
            raised[place, :],
            values_ref[b, :, h * lanes : (h + 1) * lanes],
            preferred_element_type=f32,
        )

    row = lax.broadcasted_iota(jnp.int32, (rows, lanes), 0)
    lane = lax.broadcasted_iota(jnp.int32, (rows, lanes), 1)
    position = row // row_count
    for b in range(row_count):
        position = position + jnp.where(row % row_count == b, lengths_ref[b], 0)
    middle = lanes // 2
    spacing = (lane % middle).astype(f32) * (-2.0 / lanes * math.log(rope_base))
    angles = position.astype(f32) * jnp.exp(spacing)
    cosine_ref[...] = jnp.cos(angles)
    sine = jnp.sin(angles)
    sine_ref[...] = jnp.where(lane < middle, -sine, sine)


def attend(lengths, queries, keys, values, after, step_count):
    row_count, slots, width = keys.shape
    rows = step_count * row_count
    seen_rows = rows * queries.shape[1] // lanes
    table = jax.ShapeDtypeStruct((rows, lanes), f32)
    seen_table = jax.ShapeDtypeStruct((seen_rows, lanes), f32)
    return pl.pallas_call(
        functools.partial(attend_kernel, step_count, width // lanes),
        out_shape=(
            jax.ShapeDtypeStruct((seen_rows, lanes), bf16),
            seen_table,
            seen_table,
            seen_table,
            table,
            table,
        ),
        in_specs=[stays_in_hbm] + [whole_in_vmem] * 4,
        out_specs=(whole_in_vmem,) * 6,
        scratch_shapes=[
            pltpu.SMEM(lengths.shape, jnp.int32),
            pltpu.VMEM((seen_rows, lanes), f32),
            pltpu.VMEM((seen_rows, slots), f32),
            pltpu.VMEM((seen_rows, slots), bf16),
            pltpu.SemaphoreType.DMA,
        ],
        compiler_params=pltpu.CompilerParams(vmem_limit_bytes=8 * 2**20),
        name="attend",
        cost_estimate=pl.CostEstimate(
            flops=4 * seen_rows * slots * lanes,
            bytes_accessed=2 * (keys.size + values.size),
            transcendentals=seen_rows * slots,
        ),
    )(*in_hbm(lengths), queries, keys, values, after)


def add_near(kept, near):
    rows, own = kept.shape
    return [
        kept[:, c * lanes : (c + 1) * lanes] + near[c * rows : (c + 1) * rows, :].astype(f32)
        for c in range(own // lanes)
    ]


def carries_sums(i):
    return i > 0 and i % 2 == 0


def route_kernel(replicas, shards, *refs):
    owners_hbm, left_ref, kept_ref = refs[:3]
    piece_refs = refs[3 : 3 + replicas]
    near_refs = refs[3 + replicas : 3 + replicas + shards // 2]
    out_refs = refs[3 + replicas + shards // 2 : 3 + replicas + shards // 2 + shards]
    owners_ref, right, up_buf, owner_sem = refs[3 + replicas + shards // 2 + shards :]
    owners_copy = pltpu.make_async_copy(owners_hbm, owners_ref, owner_sem)
    owners_copy.start()
    rows = left_ref.shape[0]
    rank = right.shape[0]
    width = right.shape[1] // replicas
    half = rank // 2
    rest = (piece_refs[0].shape[0] - up_buf.shape[1]) % rank
    for i in range(replicas):
        first = 0
        for c in range(width // lanes - (1 if rest else 0)):
            right[:, i * width + c * lanes : i * width + (c + 1) * lanes] = piece_refs[i][
                first : first + rank, :
            ]
            first += rank
        if rest:
            both = piece_refs[i][first : first + half, :]
            tail = jnp.concatenate([both[:, : lanes // 2], both[:, lanes // 2 :]], axis=0)
            right[:, (i + 1) * width - lanes : (i + 1) * width] = jnp.concatenate(
                [tail, jnp.zeros((rank, lanes // 2), bf16)], axis=1
            )
            first += half
        up_buf[i] = piece_refs[i][first:, :]
    lowered = lax.dot_general(
        left_ref[...], right[...], (((1,), (1,)), ((), ())), preferred_element_type=f32
    )
    both = jnp.concatenate(split_halves(lowered), axis=1)
    replica = lax.axis_index("rollout")
    shard = lax.axis_index("tensor")
    owners_copy.wait()
    for i in range(shards):
        first = 0
        if carries_sums(i):
            for block in add_near(kept_ref[i // 2], near_refs[i // 2]):
                out_refs[i][first : first + rows, :] = block.astype(bf16)
                first += rows
        out_refs[i][first : first + rows, :] = both
        slot = lax.rem(owners_ref[shard ^ i] + replicas - replica, replicas)
        out_refs[i][first + rows :, :] = up_buf[slot]


def route(owners, left, sums, pieces, rank, up_rows, shards):
    rows, depth = left.shape
    replicas = len(pieces)
    kept, near = sums
    sent = near[0].shape[0]
    return pl.pallas_call(
        functools.partial(route_kernel, replicas, shards),
        out_shape=[
            jax.ShapeDtypeStruct(((sent if carries_sums(i) else 0) + rows + up_rows, lanes), bf16)
            for i in range(shards)
        ],
        in_specs=[stays_in_hbm] + [whole_in_vmem] * (2 + replicas + len(near)),
        out_specs=[whole_in_vmem] * shards,
        scratch_shapes=[
            pltpu.SMEM(owners.shape, jnp.int32),
            pltpu.VMEM((rank, depth), bf16),
            pltpu.VMEM((replicas, up_rows, lanes), bf16),
            pltpu.SemaphoreType.DMA,
        ],
        compiler_params=pltpu.CompilerParams(vmem_limit_bytes=4 * 2**20),
        name="route",
        cost_estimate=pl.CostEstimate(flops=0, bytes_accessed=800000, transcendentals=0),
    )(*in_hbm(owners), left, kept, *pieces, *near)


def route_plain(owners, tokens, sums, down, up, rank_part, own, shards):
    kept, near = sums
    rank = down.shape[1]
    shard = lax.axis_index("tensor")
    first = shard * rank_part
    up_part = lax.dynamic_slice_in_dim(up, first, rank_part, axis=0)
    downs = lax.all_gather(down, "rollout", axis=0, tiled=False)
    ups = lax.all_gather(up_part, "rollout", axis=0, tiled=False)
    down_matrix = jnp.take(downs, owners, axis=0, mode="clip").reshape(-1, rank)
    up_matrix = jnp.take(ups, owners, axis=0, mode="clip").transpose(1, 0, 2)
    up_matrix = up_matrix.reshape(rank_part, -1)
    lowered = jnp.dot(tokens, down_matrix, preferred_element_type=f32)
    both = jnp.concatenate(split_halves(lowered), axis=1)
    packets = []
    for i in range(shards):
        up_block = lax.dynamic_slice_in_dim(up_matrix, (shard ^ i) * own, own, axis=1)
        parts = [both, side_by_side(up_block)]
        if carries_sums(i):
            sums = add_near(kept[i // 2], near[i // 2])
            parts = [jnp.concatenate(sums, axis=0).astype(bf16)] + parts
        packets.append(jnp.concatenate(parts, axis=0))
    return packets


def finish_kernel(step_count, row_count, head_count, shards, *refs):
    kept_ref, near_ref, gain_ref, grouped_ref, total_ref, peak_ref, sum_ref = refs[:7]
    cosine_ref, sine_ref = refs[7:9]
    packet_refs = refs[9 : 9 + shards][::-1]
    attention_ref, keys_ref, values_ref = refs[9 + shards : 12 + shards]
    (up_buf,) = refs[12 + shards :]
    shard = lax.axis_index("tensor")
    rows = step_count * row_count
    own = kept_ref.shape[2]
    blocks = own // lanes
    rank = up_buf.shape[0]
    rank_part = rank // shards
    group = grouped_ref.shape[0] // (head_count * rows)
    seen = step_count * group

    lowered = jnp.zeros((rows, lanes), f32)
    for i in range(shards):
        first = rows * blocks if carries_sums(i) else 0
        lowered = lowered + packet_refs[i][first : first + rows, :].astype(f32)
        ups = packet_refs[i][first + rows :, :].astype(f32)
        at = pl.multiple_of((shard ^ i) * rank_part, rank_part)
        for c in range(blocks):
            up_buf[pl.ds(at, rank_part), c * lanes : (c + 1) * lanes] = ups[
                c * rank_part : (c + 1) * rank_part, :
            ]
    lane = lax.broadcasted_iota(jnp.int32, (rows, lanes), 1)
    lowered = lowered + pltpu.roll(lowered, rank, 1)
    high, low = split_halves(lowered)
    left = jnp.where(lane < rank, high.astype(f32), low.astype(f32)).astype(bf16)
    up = up_buf[...].astype(bf16)
    raised_up = jnp.dot(left, jnp.concatenate([up, up], axis=0), preferred_element_type=f32)
    joined = []
    for c, block in enumerate(add_near(kept_ref[0], near_ref)):
        for i in filter(carries_sums, range(shards)):
            block = block + packet_refs[i][c * rows : (c + 1) * rows, :].astype(f32)
        joined.append(block + adapter_scale * raised_up[:, c * lanes : (c + 1) * lanes])

    all_rows = row_count * seen
    seen_by = lax.broadcasted_iota(jnp.int32, (all_rows, rows), 0)
    made_by = lax.broadcasted_iota(jnp.int32, (all_rows, rows), 1)
    visible = (seen_by % row_count == made_by % row_count) & (
        made_by // row_count <= seen_by // (row_count * group)
    )
    heads = [(h, slice(h * all_rows, (h + 1) * all_rows)) for h in range(head_count)]
    keys, values, scores, results = [], [], [], []
    for h, _ in heads:
        raw_key = joined[2 * h]
        mean_square = jnp.mean(raw_key * raw_key, axis=1, keepdims=True)
        normed = raw_key * lax.rsqrt(mean_square + norm_eps) * gain_ref[...]
        key = normed * cosine_ref[...] + pltpu.roll(normed, lanes // 2, 1) * sine_ref[...]
        keys.append(key.astype(bf16))
        values.append(joined[2 * h + 1].astype(bf16))
        keys_ref[:, h * lanes : (h + 1) * lanes] = keys[h]
        values_ref[:, h * lanes : (h + 1) * lanes] = values[h]
    for h, mine in heads:
        score = lax.dot_general(
            grouped_ref[mine, :], keys[h], (((1,), (1,)), ((), ())), preferred_element_type=f32
        )
        scores.append(jnp.where(visible, score, masked_score))
    for h, mine in heads:
        old_peak = peak_ref[mine, :]
        peak = jnp.maximum(old_peak, jnp.max(scores[h], axis=1, keepdims=True))
        fade = jnp.exp2((old_peak - peak) * exponent_scale)
        lifted = jnp.exp2((scores[h] - peak[:, :rows]) * exponent_scale)
        denominator = fade * sum_ref[mine, :] + jnp.sum(lifted, axis=1, keepdims=True)
        total = fade * total_ref[mine, :] + jnp.dot(
            lifted.astype(bf16), values[h], preferred_element_type=f32
        )
        results.append(total / denominator)
    for pair in range(step_count // 2):
        for q in range(head_count * group):
            h, g = q // group, q % group
            both = []
            for side in range(2):
                first = ((pair * 2 + side) * group + g) * row_count
                both.append(results[h][first : first + row_count])
            attention_ref[
                pair * 2 * row_count : (pair + 1) * 2 * row_count, q * lanes : (q + 1) * lanes
            ] = jnp.concatenate(both, axis=0).astype(bf16)


def finish(kept, near, partials, gain, packets, rank, step_count, row_count, query_width):
    grouped, total, peak, denominator, cosine, sine = partials
    _, rows, own = kept.shape
    shards = len(packets)
    head_count = own // (2 * lanes)
    return pl.pallas_call(
        functools.partial(finish_kernel, step_count, row_count, head_count, shards),
        out_shape=(
            jax.ShapeDtypeStruct((rows, query_width), bf16),
            jax.ShapeDtypeStruct((rows, head_count * lanes), bf16),
            jax.ShapeDtypeStruct((rows, head_count * lanes), bf16),
        ),
        in_specs=[whole_in_vmem] * (9 + shards),
        out_specs=(whole_in_vmem,) * 3,
        scratch_shapes=[
            pltpu.VMEM((rank, own), f32),
        ],
        compiler_params=pltpu.CompilerParams(vmem_limit_bytes=6 * 2**20),
        name="finish",
        cost_estimate=pl.CostEstimate(flops=0, bytes_accessed=1000000, transcendentals=0),
    )(kept, near, gain, grouped, total, peak, denominator, cosine, sine, *packets[::-1])


def per_device(
    normed_tokens,
    key_value_weight,
    adapter_down,
    adapter_up,
    key_gain,
    queries,
    cache_keys,
    stored_values,
    lengths,
    owners,
):
    replicas = lax.axis_size("rollout")
    shards = lax.axis_size("tensor")
    down_rows, rank = adapter_down.shape
    step_count, row_count, depth = normed_tokens.shape
    own = key_value_weight.shape[1] // shards
    rank_part = rank // shards
    rows = step_count * row_count
    tokens = normed_tokens.reshape(rows, depth)
    query_rows = queries.reshape(rows, -1)

    fits = (
        replicas <= 4
        and adapter_up.shape[1] == own
        and down_rows % lanes in (0, lanes // 2)
        and rank == lanes // 2
        and rank_part % 16 == 0
    )
    if fits:
        fetched = 2 * (key_value_weight.size + cache_keys.size + stored_values.size)
        beside = pl.CostEstimate(flops=1000 * fetched, bytes_accessed=fetched, transcendentals=0)
        packed = pack(adapter_down.T, adapter_up, rank_part, beside)
        pieces = [packed] + [shift(packed, "rollout", i) for i in range(1, replicas)]
    near, kept, left = project(
        owners,
        tokens,
        key_value_weight,
        packed if fits else adapter_up,
        shards,
        replicas if fits else 1,
    )
    near = [swap(block, "tensor", 1) for block in near]
    if fits:
        packets = route(
            owners, left, (kept, near), pieces, rank, rank_part * own // lanes, shards
        )
    else:
        packets = route_plain(
            owners, tokens, (kept, near), adapter_down, adapter_up, rank_part, own, shards
        )
    partials = attend(lengths, query_rows, cache_keys, stored_values, packets[0], step_count)
    packets = [packets[0]] + [swap(packets[i], "tensor", i) for i in range(1, shards)]
    attention, keys, values = finish(
        kept,
        near[0],
        partials,
        key_gain.reshape(1, -1),
        packets,
        rank,
        step_count,
        row_count,
        query_rows.shape[1],
    )
    return tuple(a.reshape(step_count, row_count, -1) for a in (attention, keys, values))


def solution(mesh):
    placed = (
        P(None, ("job", "rollout"), "tensor"),
        P("tensor", None),
        P(("job", "rollout", "tensor"), None),
        P(None, ("job", "rollout")),
        P(),
        P(None, ("job", "rollout"), "tensor"),
        P(("job", "rollout"), None, "tensor"),
        P(("job", "rollout"), None, "tensor"),
        P(("job", "rollout")),
        P("job"),
    )
    return jax.shard_map(
        per_device,
        mesh=mesh,
        in_specs=placed,
        out_specs=(
            P(None, ("job", "rollout"), "tensor"),
            P(None, ("job", "rollout"), "tensor"),
            P(None, ("job", "rollout"), "tensor"),
        ),
        check_vma=False,
    )
```

```python
import functools
import math

import jax
import jax.numpy as jnp
from jax import lax
from jax.experimental import pallas as pl
from jax.experimental.pallas import tpu as pltpu
from jax.sharding import PartitionSpec as P

norm_eps = 1e-06
rope_base = 1000000.0
adapter_scale = 2.0
masked_score = -1e30
lanes = 128
exponent_scale = lanes**-0.5 / math.log(2.0)
f32 = jnp.float32
bf16 = jnp.bfloat16

whole_in_vmem = pl.BlockSpec(memory_space=pltpu.VMEM)
whole_in_smem = pl.BlockSpec(memory_space=pltpu.SMEM)
stays_in_hbm = pl.BlockSpec(memory_space=pltpu.HBM)


def swap(block, axis, offset):
    count = lax.axis_size(axis)
    return lax.ppermute(block, axis, [(s, s ^ offset) for s in range(count)])


def in_hbm(*arrays):
    return tuple(pltpu.with_memory_space_constraint(a, pltpu.HBM) for a in arrays)


def side_by_side(rows_of_blocks):
    r, c = rows_of_blocks.shape
    return rows_of_blocks.reshape(r, c // lanes, lanes).transpose(1, 0, 2).reshape(-1, lanes)


def split_halves(total):
    high = total.astype(bf16)
    return high, (total - high.astype(f32)).astype(bf16)


def pack_kernel(down_hbm, up_hbm, out_ref, down_ref, up_ref, sems):
    rank, down_rows = down_ref.shape
    rank_part = up_ref.shape[0]
    start = pl.multiple_of(lax.axis_index("tensor") * rank_part, rank_part)
    copies = [
        pltpu.make_async_copy(down_hbm, down_ref, sems.at[0]),
        pltpu.make_async_copy(up_hbm.at[pl.ds(start, rank_part), :], up_ref, sems.at[1]),
    ]
    for copy in copies:
        copy.start()
    for copy in copies:
        copy.wait()
    first = 0
    for c in range(down_rows // lanes):
        out_ref[first : first + rank, :] = down_ref[:, c * lanes : (c + 1) * lanes]
        first += rank
    rest = down_rows % lanes
    if rest:
        half = rank // 2
        tail = down_ref[:, down_rows - rest :]
        out_ref[first : first + half, :] = jnp.concatenate([tail[:half], tail[half:]], axis=1)
        first += half
    for c in range(up_ref.shape[1] // lanes):
        out_ref[first : first + rank_part, :] = up_ref[:, c * lanes : (c + 1) * lanes]
        first += rank_part


def pack(down, up, rank_part, beside):
    rows = (down.size + rank_part * up.shape[1]) // lanes
    return pl.pallas_call(
        pack_kernel,
        out_shape=jax.ShapeDtypeStruct((rows, lanes), bf16),
        in_specs=[stays_in_hbm] * 2,
        out_specs=whole_in_vmem,
        scratch_shapes=[
            pltpu.VMEM(down.shape, bf16),
            pltpu.VMEM((rank_part, up.shape[1]), bf16),
            pltpu.SemaphoreType.DMA((2,)),
        ],
        compiler_params=pltpu.CompilerParams(vmem_limit_bytes=2 * 2**20),
        name="pack",
        cost_estimate=beside,
    )(*in_hbm(down, up))


def project_kernel(shards, replicas, *refs):
    owners_hbm, tokens_ref, weight_ref, _ = refs[:4]
    pairs = shards // 2
    near_refs = refs[4 : 4 + pairs]
    kept_ref, left_ref, owners_ref, token_buf, owner_sem = refs[4 + pairs :]
    owners_copy = pltpu.make_async_copy(owners_hbm, owners_ref, owner_sem)
    owners_copy.start()

    shard = lax.axis_index("tensor")
    _, rows, own = kept_ref.shape
    for i in range(shards):
        first = pl.multiple_of((shard ^ i) * own, lanes)
        block = jnp.dot(
            tokens_ref[...], weight_ref[:, pl.ds(first, own)], preferred_element_type=f32
        )
        if i % 2 == 0:
            kept_ref[i // 2] = block
            continue
        for c in range(own // lanes):
            near_refs[i // 2][c * rows : (c + 1) * rows, :] = block[
                :, c * lanes : (c + 1) * lanes
            ].astype(bf16)

    owners_copy.wait()
    width = token_buf.shape[2]
    down_rows = tokens_ref.shape[1] // replicas
    for k in range(replicas):
        token_buf[k, :, :down_rows] = tokens_ref[:, k * down_rows : (k + 1) * down_rows]
        if down_rows < width:
            token_buf[k, :, down_rows:] = jnp.zeros((rows, width - down_rows), bf16)
    for i in range(replicas):
        source = lax.axis_index("rollout") ^ i
        place = jnp.int32(0)
        for k in range(1, replicas):
            place = place + jnp.where(owners_ref[k] == source, k, 0)
        left_ref[:, i * width : (i + 1) * width] = token_buf[place]


def project(owners, tokens, weight, after, shards, replicas):
    rows, depth = tokens.shape
    own = weight.shape[1] // shards
    pairs = shards // 2
    piece_width = -(-depth // replicas // lanes) * lanes
    outs = pl.pallas_call(
        functools.partial(project_kernel, shards, replicas),
        out_shape=[jax.ShapeDtypeStruct((rows * own // lanes, lanes), bf16)] * pairs
        + [
            jax.ShapeDtypeStruct((pairs, rows, own), f32),
            jax.ShapeDtypeStruct((rows, replicas * piece_width), bf16),
        ],
        in_specs=[stays_in_hbm] + [whole_in_vmem] * 3,
        out_specs=[whole_in_vmem] * (pairs + 2),
        scratch_shapes=[
            pltpu.SMEM(owners.shape, jnp.int32),
            pltpu.VMEM((replicas, rows, piece_width), bf16),
            pltpu.SemaphoreType.DMA,
        ],
        compiler_params=pltpu.CompilerParams(vmem_limit_bytes=4 * 2**20),
        name="project",
        cost_estimate=pl.CostEstimate(
            flops=2 * rows * weight.size, bytes_accessed=2 * weight.size, transcendentals=0
        ),
    )(*in_hbm(owners), tokens, weight, after)
    return outs[:pairs], *outs[pairs:]


def chip_sums_kernel(kept_ref, *refs):
    pairs, rows, own = kept_ref.shape
    near_refs, own_ref, far_refs = refs[:pairs], refs[pairs], refs[pairs + 1 :]
    for c in range(own // lanes):
        for m in range(pairs):
            block = kept_ref[m, :, c * lanes : (c + 1) * lanes] + near_refs[m][
                c * rows : (c + 1) * rows, :
            ].astype(f32)
            if m == 0:
                own_ref[:, c * lanes : (c + 1) * lanes] = block
            else:
                far_refs[m - 1][c * rows : (c + 1) * rows, :] = block.astype(bf16)


def chip_sums(kept, near):
    pairs, rows, own = kept.shape
    mine, *far = pl.pallas_call(
        chip_sums_kernel,
        out_shape=[jax.ShapeDtypeStruct((rows, own), f32)]
        + [jax.ShapeDtypeStruct(near[0].shape, bf16)] * (pairs - 1),
        in_specs=[whole_in_vmem] * (1 + pairs),
        out_specs=[whole_in_vmem] * pairs,
        compiler_params=pltpu.CompilerParams(vmem_limit_bytes=2 * 2**20),
        name="chip_sums",
        cost_estimate=pl.CostEstimate(flops=0, bytes_accessed=400000, transcendentals=0),
    )(kept, *near)
    return mine, far


def attend_kernel(
    step_count,
    head_count,
    lengths_hbm,
    queries_ref,
    keys_ref,
    values_ref,
    _,
    own_ref,
    *refs,
):
    far_refs = refs[:-12]
    base_ref, grouped_ref, total_ref, peak_ref, sum_ref, cosine_ref, sine_ref = refs[-12:-5]
    lengths_ref, regroup, scores_ref, raised, length_sem = refs[-5:]
    lengths_copy = pltpu.make_async_copy(lengths_hbm, lengths_ref, length_sem)
    lengths_copy.start()
    rows, own = own_ref.shape
    for c in range(own // lanes):
        block = own_ref[:, c * lanes : (c + 1) * lanes]
        for far_ref in far_refs:
            block = block + far_ref[c * rows : (c + 1) * rows, :].astype(f32)
        base_ref[:, c * lanes : (c + 1) * lanes] = block

    row_count, slots, _ = keys_ref.shape
    group = queries_ref.shape[1] // (head_count * lanes)
    seen = step_count * group
    for pair in range(step_count // 2):
        for q in range(head_count * group):
            h, g = q // group, q % group
            both = queries_ref[
                pair * 2 * row_count : (pair + 1) * 2 * row_count, q * lanes : (q + 1) * lanes
            ].astype(f32)
            for side in range(2):
                first = h * row_count * seen + (pair * 2 + side) * group + g
                regroup[pl.ds(first, row_count, stride=seen), :] = both[
                    side * row_count : (side + 1) * row_count, :
                ]
            if g % 2:
                for side in range(2):
                    half = slice(side * row_count, (side + 1) * row_count)
                    last = (h * seen + (pair * 2 + side) * group + g + 1) * row_count
                    grouped_ref[last - 2 * row_count : last, :] = jnp.concatenate(
                        [before[half], both[half]], axis=0
                    ).astype(bf16)
            before = both

    for b in range(row_count):
        for h in range(head_count):
            at = (h * row_count + b) * seen
            scores_ref[at : at + seen, :] = lax.dot_general(
                regroup[at : at + seen, :].astype(bf16),
                keys_ref[b, :, h * lanes : (h + 1) * lanes],
                (((1,), (1,)), ((), ())),
                preferred_element_type=f32,
            )

    places = [
        (
            b,
            h,
            slice((h * row_count + b) * seen, (h * row_count + b + 1) * seen),
            pl.ds(h * row_count * seen + b, seen, stride=row_count),
        )
        for b in range(row_count)
        for h in range(head_count)
    ]
    lengths_copy.wait()
    slot = lax.broadcasted_iota(jnp.int32, (seen, slots), 1)
    for b, h, place, out in places:
        score = jnp.where(slot < lengths_ref[b], scores_ref[place, :], masked_score)
        peak = jnp.max(score, axis=1, keepdims=True)
        lifted = jnp.exp2((score - peak) * exponent_scale)
        raised[place, :] = lifted.astype(bf16)
        peak_ref[out, :] = jnp.broadcast_to(peak, (seen, lanes))
        sum_ref[out, :] = jnp.broadcast_to(
            jnp.sum(lifted, axis=1, keepdims=True), (seen, lanes)
        )
    for b, h, place, out in places:
        total_ref[out, :] = jnp.dot(
            raised[place, :],
            values_ref[b, :, h * lanes : (h + 1) * lanes],
            preferred_element_type=f32,
        )

    row = lax.broadcasted_iota(jnp.int32, (rows, lanes), 0)
    lane = lax.broadcasted_iota(jnp.int32, (rows, lanes), 1)
    position = row // row_count
    for b in range(row_count):
        position = position + jnp.where(row % row_count == b, lengths_ref[b], 0)
    middle = lanes // 2
    spacing = (lane % middle).astype(f32) * (-2.0 / lanes * math.log(rope_base))
    angles = position.astype(f32) * jnp.exp(spacing)
    cosine_ref[...] = jnp.cos(angles)
    sine = jnp.sin(angles)
    sine_ref[...] = jnp.where(lane < middle, -sine, sine)


def attend(lengths, queries, keys, values, after, mine, far, step_count):
    row_count, slots, width = keys.shape
    rows = step_count * row_count
    seen_rows = rows * queries.shape[1] // lanes
    table = jax.ShapeDtypeStruct((rows, lanes), f32)
    seen_table = jax.ShapeDtypeStruct((seen_rows, lanes), f32)
    return pl.pallas_call(
        functools.partial(attend_kernel, step_count, width // lanes),
        out_shape=(
            jax.ShapeDtypeStruct(mine.shape, f32),
            jax.ShapeDtypeStruct((seen_rows, lanes), bf16),
            seen_table,
            seen_table,
            seen_table,
            table,
            table,
        ),
        in_specs=[stays_in_hbm] + [whole_in_vmem] * (5 + len(far)),
        out_specs=(whole_in_vmem,) * 7,
        scratch_shapes=[
            pltpu.SMEM(lengths.shape, jnp.int32),
            pltpu.VMEM((seen_rows, lanes), f32),
            pltpu.VMEM((seen_rows, slots), f32),
            pltpu.VMEM((seen_rows, slots), bf16),
            pltpu.SemaphoreType.DMA,
        ],
        compiler_params=pltpu.CompilerParams(vmem_limit_bytes=8 * 2**20),
        name="attend",
        cost_estimate=pl.CostEstimate(
            flops=4 * seen_rows * slots * lanes,
            bytes_accessed=2 * (keys.size + values.size),
            transcendentals=seen_rows * slots,
        ),
    )(*in_hbm(lengths), queries, keys, values, after, mine, *far)


def route_kernel(replicas, shards, *refs):
    owners_hbm, left_ref = refs[:2]
    piece_refs = refs[2 : 2 + replicas]
    out_refs = refs[3 + replicas : 3 + replicas + shards]
    owners_ref, right, up_buf, owner_sem = refs[3 + replicas + shards :]
    owners_copy = pltpu.make_async_copy(owners_hbm, owners_ref, owner_sem)
    owners_copy.start()
    rows = left_ref.shape[0]
    rank = right.shape[0]
    width = right.shape[1] // replicas
    half = rank // 2
    rest = (piece_refs[0].shape[0] - up_buf.shape[1]) % rank
    for i in range(replicas):
        first = 0
        for c in range(width // lanes - (1 if rest else 0)):
            right[:, i * width + c * lanes : i * width + (c + 1) * lanes] = piece_refs[i][
                first : first + rank, :
            ]
            first += rank
        if rest:
            both = piece_refs[i][first : first + half, :]
            tail = jnp.concatenate([both[:, : lanes // 2], both[:, lanes // 2 :]], axis=0)
            right[:, (i + 1) * width - lanes : (i + 1) * width] = jnp.concatenate(
                [tail, jnp.zeros((rank, lanes // 2), bf16)], axis=1
            )
            first += half
        up_buf[i] = piece_refs[i][first:, :]
    lowered = lax.dot_general(
        left_ref[...], right[...], (((1,), (1,)), ((), ())), preferred_element_type=f32
    )
    both = jnp.concatenate(split_halves(lowered), axis=1)
    replica = lax.axis_index("rollout")
    shard = lax.axis_index("tensor")
    owners_copy.wait()
    for i in range(shards):
        out_refs[i][:rows, :] = both
        slot = owners_ref[shard ^ i] ^ replica
        out_refs[i][rows:, :] = up_buf[slot]


def route(owners, left, pieces, after, rank, up_rows, shards):
    rows, depth = left.shape
    replicas = len(pieces)
    return pl.pallas_call(
        functools.partial(route_kernel, replicas, shards),
        out_shape=[jax.ShapeDtypeStruct((rows + up_rows, lanes), bf16)] * shards,
        in_specs=[stays_in_hbm] + [whole_in_vmem] * (2 + replicas),
        out_specs=[whole_in_vmem] * shards,
        scratch_shapes=[
            pltpu.SMEM(owners.shape, jnp.int32),
            pltpu.VMEM((rank, depth), bf16),
            pltpu.VMEM((replicas, up_rows, lanes), bf16),
            pltpu.SemaphoreType.DMA,
        ],
        compiler_params=pltpu.CompilerParams(vmem_limit_bytes=4 * 2**20),
        name="route",
        cost_estimate=pl.CostEstimate(flops=0, bytes_accessed=800000, transcendentals=0),
    )(*in_hbm(owners), left, *pieces, after)


def route_plain(owners, tokens, down, up, rank_part, own, shards):
    rank = down.shape[1]
    shard = lax.axis_index("tensor")
    first = shard * rank_part
    up_part = lax.dynamic_slice_in_dim(up, first, rank_part, axis=0)
    downs = lax.all_gather(down, "rollout", axis=0, tiled=False)
    ups = lax.all_gather(up_part, "rollout", axis=0, tiled=False)
    down_matrix = jnp.take(downs, owners, axis=0, mode="clip").reshape(-1, rank)
    up_matrix = jnp.take(ups, owners, axis=0, mode="clip").transpose(1, 0, 2)
    up_matrix = up_matrix.reshape(rank_part, -1)
    lowered = jnp.dot(tokens, down_matrix, preferred_element_type=f32)
    both = jnp.concatenate(split_halves(lowered), axis=1)
    packets = []
    for i in range(shards):
        up_block = lax.dynamic_slice_in_dim(up_matrix, (shard ^ i) * own, own, axis=1)
        parts = [both, side_by_side(up_block)]
        packets.append(jnp.concatenate(parts, axis=0))
    return packets


def finish_kernel(step_count, row_count, head_count, shards, *refs):
    gain_ref, base_ref, grouped_ref, total_ref, peak_ref, sum_ref, cosine_ref, sine_ref = refs[:8]
    packet_refs = refs[8 : 8 + shards][::-1]
    attention_ref, keys_ref, values_ref = refs[8 + shards : 11 + shards]
    (up_buf,) = refs[11 + shards :]
    shard = lax.axis_index("tensor")
    rows = step_count * row_count
    own = base_ref.shape[1]
    blocks = own // lanes
    rank = up_buf.shape[0]
    rank_part = rank // shards
    group = grouped_ref.shape[0] // (head_count * rows)
    seen = step_count * group

    lowered = jnp.zeros((rows, lanes), f32)
    for i in range(shards):
        lowered = lowered + packet_refs[i][:rows, :].astype(f32)
        ups = packet_refs[i][rows:, :].astype(f32)
        at = pl.multiple_of((shard ^ i) * rank_part, rank_part)
        for c in range(blocks):
            up_buf[pl.ds(at, rank_part), c * lanes : (c + 1) * lanes] = ups[
                c * rank_part : (c + 1) * rank_part, :
            ]
    lane = lax.broadcasted_iota(jnp.int32, (rows, lanes), 1)
    lowered = lowered + pltpu.roll(lowered, rank, 1)
    high, low = split_halves(lowered)
    left = jnp.where(lane < rank, high.astype(f32), low.astype(f32)).astype(bf16)
    up = up_buf[...].astype(bf16)
    raised_up = jnp.dot(left, jnp.concatenate([up, up], axis=0), preferred_element_type=f32)
    joined = []
    for c in range(blocks):
        block = base_ref[:, c * lanes : (c + 1) * lanes]
        joined.append(block + adapter_scale * raised_up[:, c * lanes : (c + 1) * lanes])

    all_rows = row_count * seen
    seen_by = lax.broadcasted_iota(jnp.int32, (all_rows, rows), 0)
    made_by = lax.broadcasted_iota(jnp.int32, (all_rows, rows), 1)
    visible = (seen_by % row_count == made_by % row_count) & (
        made_by // row_count <= seen_by // (row_count * group)
    )
    heads = [(h, slice(h * all_rows, (h + 1) * all_rows)) for h in range(head_count)]
    keys, values, scores, results = [], [], [], []
    for h, _ in heads:
        raw_key = joined[2 * h]
        mean_square = jnp.mean(raw_key * raw_key, axis=1, keepdims=True)
        normed = raw_key * lax.rsqrt(mean_square + norm_eps) * gain_ref[...]
        key = normed * cosine_ref[...] + pltpu.roll(normed, lanes // 2, 1) * sine_ref[...]
        keys.append(key.astype(bf16))
        values.append(joined[2 * h + 1].astype(bf16))
        keys_ref[:, h * lanes : (h + 1) * lanes] = keys[h]
        values_ref[:, h * lanes : (h + 1) * lanes] = values[h]
    for h, mine in heads:
        score = lax.dot_general(
            grouped_ref[mine, :], keys[h], (((1,), (1,)), ((), ())), preferred_element_type=f32
        )
        scores.append(jnp.where(visible, score, masked_score))
    for h, mine in heads:
        old_peak = peak_ref[mine, :]
        peak = jnp.maximum(old_peak, jnp.max(scores[h], axis=1, keepdims=True))
        fade = jnp.exp2((old_peak - peak) * exponent_scale)
        lifted = jnp.exp2((scores[h] - peak[:, :rows]) * exponent_scale)
        denominator = fade * sum_ref[mine, :] + jnp.sum(lifted, axis=1, keepdims=True)
        total = fade * total_ref[mine, :] + jnp.dot(
            lifted.astype(bf16), values[h], preferred_element_type=f32
        )
        results.append(total / denominator)
    for pair in range(step_count // 2):
        for q in range(head_count * group):
            h, g = q // group, q % group
            both = []
            for side in range(2):
                first = ((pair * 2 + side) * group + g) * row_count
                both.append(results[h][first : first + row_count])
            attention_ref[
                pair * 2 * row_count : (pair + 1) * 2 * row_count, q * lanes : (q + 1) * lanes
            ] = jnp.concatenate(both, axis=0).astype(bf16)


def finish(partials, gain, packets, rank, step_count, row_count, query_width):
    rows, own = partials[0].shape
    total = partials[2]
    shards = len(packets)
    head_count = own // (2 * lanes)
    return pl.pallas_call(
        functools.partial(finish_kernel, step_count, row_count, head_count, shards),
        out_shape=(
            jax.ShapeDtypeStruct((rows, query_width), bf16),
            jax.ShapeDtypeStruct((rows, head_count * lanes), bf16),
            jax.ShapeDtypeStruct((rows, head_count * lanes), bf16),
        ),
        in_specs=[whole_in_vmem] * (8 + shards),
        out_specs=(whole_in_vmem,) * 3,
        scratch_shapes=[
            pltpu.VMEM((rank, own), f32),
        ],
        compiler_params=pltpu.CompilerParams(vmem_limit_bytes=6 * 2**20),
        name="finish",
        cost_estimate=pl.CostEstimate(flops=0, bytes_accessed=1000000, transcendentals=0),
    )(gain, *partials, *packets[::-1])


def per_device(
    normed_tokens,
    key_value_weight,
    adapter_down,
    adapter_up,
    key_gain,
    queries,
    cache_keys,
    stored_values,
    lengths,
    owners,
):
    replicas = lax.axis_size("rollout")
    shards = lax.axis_size("tensor")
    down_rows, rank = adapter_down.shape
    step_count, row_count, depth = normed_tokens.shape
    own = key_value_weight.shape[1] // shards
    rank_part = rank // shards
    rows = step_count * row_count
    tokens = normed_tokens.reshape(rows, depth)
    query_rows = queries.reshape(rows, -1)

    fits = (
        replicas <= 4
        and adapter_up.shape[1] == own
        and down_rows % lanes in (0, lanes // 2)
        and rank == lanes // 2
        and rank_part % 16 == 0
    )
    if fits:
        fetched = 2 * (key_value_weight.size + cache_keys.size + stored_values.size)
        beside = pl.CostEstimate(flops=1000 * fetched, bytes_accessed=fetched, transcendentals=0)
        packed = pack(adapter_down.T, adapter_up, rank_part, beside)
        pieces = [packed] + [swap(packed, "rollout", i) for i in range(1, replicas)]
    near, kept, left = project(
        owners,
        tokens,
        key_value_weight,
        packed if fits else adapter_up,
        shards,
        replicas if fits else 1,
    )
    mine, far = chip_sums(kept, [swap(block, "tensor", 1) for block in near])
    far = [swap(block, "tensor", 2 * m + 2) for m, block in enumerate(far)]
    if fits:
        packets = route(
            owners, left, pieces, mine, rank, rank_part * own // lanes, shards
        )
    else:
        packets = route_plain(owners, tokens, adapter_down, adapter_up, rank_part, own, shards)
    partials = attend(
        lengths, query_rows, cache_keys, stored_values, packets[0], mine, far, step_count
    )
    packets = [packets[0]] + [swap(packets[i], "tensor", i) for i in range(1, shards)]
    attention, keys, values = finish(
        partials,
        key_gain.reshape(1, -1),
        packets,
        rank,
        step_count,
        row_count,
        query_rows.shape[1],
    )
    return tuple(a.reshape(step_count, row_count, -1) for a in (attention, keys, values))


def solution(mesh):
    placed = (
        P(None, ("job", "rollout"), "tensor"),
        P("tensor", None),
        P(("job", "rollout", "tensor"), None),
        P(None, ("job", "rollout")),
        P(),
        P(None, ("job", "rollout"), "tensor"),
        P(("job", "rollout"), None, "tensor"),
        P(("job", "rollout"), None, "tensor"),
        P(("job", "rollout")),
        P("job"),
    )
    return jax.shard_map(
        per_device,
        mesh=mesh,
        in_specs=placed,
        out_specs=(
            P(None, ("job", "rollout"), "tensor"),
            P(None, ("job", "rollout"), "tensor"),
            P(None, ("job", "rollout"), "tensor"),
        ),
        check_vma=False,
    )
```

```python
import functools
import math

import jax
import jax.numpy as jnp
from jax import lax
from jax.experimental import pallas as pl
from jax.experimental.pallas import tpu as pltpu
from jax.sharding import PartitionSpec as P

norm_eps = 1e-06
rope_base = 1000000.0
adapter_scale = 2.0
masked_score = -1e30
lanes = 128
exponent_scale = lanes**-0.5 / math.log(2.0)
f32 = jnp.float32
bf16 = jnp.bfloat16

whole_in_vmem = pl.BlockSpec(memory_space=pltpu.VMEM)
whole_in_smem = pl.BlockSpec(memory_space=pltpu.SMEM)
stays_in_hbm = pl.BlockSpec(memory_space=pltpu.HBM)


def swap(block, axis, offset):
    count = lax.axis_size(axis)
    return lax.ppermute(block, axis, [(s, s ^ offset) for s in range(count)])


def in_hbm(*arrays):
    return tuple(pltpu.with_memory_space_constraint(a, pltpu.HBM) for a in arrays)


def side_by_side(rows_of_blocks):
    r, c = rows_of_blocks.shape
    return rows_of_blocks.reshape(r, c // lanes, lanes).transpose(1, 0, 2).reshape(-1, lanes)


def split_halves(total):
    high = total.astype(bf16)
    return high, (total - high.astype(f32)).astype(bf16)


def pack_kernel(down_hbm, up_hbm, out_ref, down_ref, up_ref, sems):
    rank, down_rows = down_ref.shape
    rank_part = up_ref.shape[0]
    start = pl.multiple_of(lax.axis_index("tensor") * rank_part, rank_part)
    copies = [
        pltpu.make_async_copy(down_hbm, down_ref, sems.at[0]),
        pltpu.make_async_copy(up_hbm.at[pl.ds(start, rank_part), :], up_ref, sems.at[1]),
    ]
    for copy in copies:
        copy.start(priority=1)
    for copy in copies:
        copy.wait()
    first = 0
    for c in range(down_rows // lanes):
        out_ref[first : first + rank, :] = down_ref[:, c * lanes : (c + 1) * lanes]
        first += rank
    rest = down_rows % lanes
    if rest:
        half = rank // 2
        tail = down_ref[:, down_rows - rest :]
        out_ref[first : first + half, :] = jnp.concatenate([tail[:half], tail[half:]], axis=1)
        first += half
    for c in range(up_ref.shape[1] // lanes):
        out_ref[first : first + rank_part, :] = up_ref[:, c * lanes : (c + 1) * lanes]
        first += rank_part


def pack(down, up, rank_part, beside):
    rows = (down.size + rank_part * up.shape[1]) // lanes
    return pl.pallas_call(
        pack_kernel,
        out_shape=jax.ShapeDtypeStruct((rows, lanes), bf16),
        in_specs=[stays_in_hbm] * 2,
        out_specs=whole_in_vmem,
        scratch_shapes=[
            pltpu.VMEM(down.shape, bf16),
            pltpu.VMEM((rank_part, up.shape[1]), bf16),
            pltpu.SemaphoreType.DMA((2,)),
        ],
        compiler_params=pltpu.CompilerParams(vmem_limit_bytes=2 * 2**20),
        name="pack",
        cost_estimate=beside,
    )(*in_hbm(down, up))


def project_kernel(shards, replicas, *refs):
    owners_hbm, tokens_ref, weight_ref, _ = refs[:4]
    pairs = shards // 2
    near_refs = refs[4 : 4 + pairs]
    kept_ref, left_ref, owners_ref, token_buf, owner_sem = refs[4 + pairs :]
    owners_copy = pltpu.make_async_copy(owners_hbm, owners_ref, owner_sem)
    owners_copy.start()

    shard = lax.axis_index("tensor")
    _, rows, own = kept_ref.shape
    for i in range(shards):
        first = pl.multiple_of((shard ^ i) * own, lanes)
        block = jnp.dot(
            tokens_ref[...], weight_ref[:, pl.ds(first, own)], preferred_element_type=f32
        )
        if i % 2 == 0:
            kept_ref[i // 2] = block
            continue
        for c in range(own // lanes):
            near_refs[i // 2][c * rows : (c + 1) * rows, :] = block[
                :, c * lanes : (c + 1) * lanes
            ].astype(bf16)

    owners_copy.wait()
    width = token_buf.shape[2]
    down_rows = tokens_ref.shape[1] // replicas
    for k in range(replicas):
        token_buf[k, :, :down_rows] = tokens_ref[:, k * down_rows : (k + 1) * down_rows]
        if down_rows < width:
            token_buf[k, :, down_rows:] = jnp.zeros((rows, width - down_rows), bf16)
    for i in range(replicas):
        source = lax.axis_index("rollout") ^ i
        place = jnp.int32(0)
        for k in range(1, replicas):
            place = place + jnp.where(owners_ref[k] == source, k, 0)
        left_ref[:, i * width : (i + 1) * width] = token_buf[place]


def project(owners, tokens, weight, after, shards, replicas):
    rows, depth = tokens.shape
    own = weight.shape[1] // shards
    pairs = shards // 2
    piece_width = -(-depth // replicas // lanes) * lanes
    outs = pl.pallas_call(
        functools.partial(project_kernel, shards, replicas),
        out_shape=[jax.ShapeDtypeStruct((rows * own // lanes, lanes), bf16)] * pairs
        + [
            jax.ShapeDtypeStruct((pairs, rows, own), f32),
            jax.ShapeDtypeStruct((rows, replicas * piece_width), bf16),
        ],
        in_specs=[stays_in_hbm] + [whole_in_vmem] * 3,
        out_specs=[whole_in_vmem] * (pairs + 2),
        scratch_shapes=[
            pltpu.SMEM(owners.shape, jnp.int32),
            pltpu.VMEM((replicas, rows, piece_width), bf16),
            pltpu.SemaphoreType.DMA,
        ],
        compiler_params=pltpu.CompilerParams(vmem_limit_bytes=4 * 2**20),
        name="project",
        cost_estimate=pl.CostEstimate(
            flops=2 * rows * weight.size, bytes_accessed=2 * weight.size, transcendentals=0
        ),
    )(*in_hbm(owners), tokens, weight, after)
    return outs[:pairs], *outs[pairs:]


def chip_sums_kernel(kept_ref, *refs):
    pairs, rows, own = kept_ref.shape
    near_refs, own_ref, far_refs = refs[:pairs], refs[pairs], refs[pairs + 1 :]
    for c in range(own // lanes):
        for m in range(pairs):
            block = kept_ref[m, :, c * lanes : (c + 1) * lanes] + near_refs[m][
                c * rows : (c + 1) * rows, :
            ].astype(f32)
            if m == 0:
                own_ref[:, c * lanes : (c + 1) * lanes] = block
            else:
                far_refs[m - 1][c * rows : (c + 1) * rows, :] = block.astype(bf16)


def chip_sums(kept, near):
    pairs, rows, own = kept.shape
    mine, *far = pl.pallas_call(
        chip_sums_kernel,
        out_shape=[jax.ShapeDtypeStruct((rows, own), f32)]
        + [jax.ShapeDtypeStruct(near[0].shape, bf16)] * (pairs - 1),
        in_specs=[whole_in_vmem] * (1 + pairs),
        out_specs=[whole_in_vmem] * pairs,
        compiler_params=pltpu.CompilerParams(vmem_limit_bytes=2 * 2**20),
        name="chip_sums",
        cost_estimate=pl.CostEstimate(flops=0, bytes_accessed=400000, transcendentals=0),
    )(kept, *near)
    return mine, far


def attend_kernel(
    step_count,
    head_count,
    lengths_hbm,
    queries_ref,
    keys_ref,
    values_ref,
    _,
    own_ref,
    *refs,
):
    far_refs = refs[:-12]
    base_ref, grouped_ref, total_ref, peak_ref, sum_ref, cosine_ref, sine_ref = refs[-12:-5]
    lengths_ref, regroup, scores_ref, raised, length_sem = refs[-5:]
    lengths_copy = pltpu.make_async_copy(lengths_hbm, lengths_ref, length_sem)
    lengths_copy.start()
    rows, own = own_ref.shape
    for c in range(own // lanes):
        block = own_ref[:, c * lanes : (c + 1) * lanes]
        for far_ref in far_refs:
            block = block + far_ref[c * rows : (c + 1) * rows, :].astype(f32)
        base_ref[:, c * lanes : (c + 1) * lanes] = block

    row_count, slots, _ = keys_ref.shape
    group = queries_ref.shape[1] // (head_count * lanes)
    seen = step_count * group
    for pair in range(step_count // 2):
        for q in range(head_count * group):
            h, g = q // group, q % group
            both = queries_ref[
                pair * 2 * row_count : (pair + 1) * 2 * row_count, q * lanes : (q + 1) * lanes
            ].astype(f32)
            for side in range(2):
                first = h * row_count * seen + (pair * 2 + side) * group + g
                regroup[pl.ds(first, row_count, stride=seen), :] = both[
                    side * row_count : (side + 1) * row_count, :
                ]
            if g % 2:
                for side in range(2):
                    half = slice(side * row_count, (side + 1) * row_count)
                    last = (h * seen + (pair * 2 + side) * group + g + 1) * row_count
                    grouped_ref[last - 2 * row_count : last, :] = jnp.concatenate(
                        [before[half], both[half]], axis=0
                    ).astype(bf16)
            before = both

    for b in range(row_count):
        for h in range(head_count):
            at = (h * row_count + b) * seen
            scores_ref[at : at + seen, :] = lax.dot_general(
                regroup[at : at + seen, :].astype(bf16),
                keys_ref[b, :, h * lanes : (h + 1) * lanes],
                (((1,), (1,)), ((), ())),
                preferred_element_type=f32,
            )

    places = [
        (
            b,
            h,
            slice((h * row_count + b) * seen, (h * row_count + b + 1) * seen),
            pl.ds(h * row_count * seen + b, seen, stride=row_count),
        )
        for b in range(row_count)
        for h in range(head_count)
    ]
    lengths_copy.wait()
    slot = lax.broadcasted_iota(jnp.int32, (seen, slots), 1)
    for b, h, place, out in places:
        score = jnp.where(slot < lengths_ref[b], scores_ref[place, :], masked_score)
        peak = jnp.max(score, axis=1, keepdims=True)
        lifted = jnp.exp2((score - peak) * exponent_scale)
        raised[place, :] = lifted.astype(bf16)
        peak_ref[out, :] = jnp.broadcast_to(peak, (seen, lanes))
        sum_ref[out, :] = jnp.broadcast_to(
            jnp.sum(lifted, axis=1, keepdims=True), (seen, lanes)
        )
    for b, h, place, out in places:
        total_ref[out, :] = jnp.dot(
            raised[place, :],
            values_ref[b, :, h * lanes : (h + 1) * lanes],
            preferred_element_type=f32,
        )

    row = lax.broadcasted_iota(jnp.int32, (rows, lanes), 0)
    lane = lax.broadcasted_iota(jnp.int32, (rows, lanes), 1)
    position = row // row_count
    for b in range(row_count):
        position = position + jnp.where(row % row_count == b, lengths_ref[b], 0)
    middle = lanes // 2
    spacing = (lane % middle).astype(f32) * (-2.0 / lanes * math.log(rope_base))
    angles = position.astype(f32) * jnp.exp(spacing)
    cosine_ref[...] = jnp.cos(angles)
    sine = jnp.sin(angles)
    sine_ref[...] = jnp.where(lane < middle, -sine, sine)


def attend(lengths, queries, keys, values, after, mine, far, step_count):
    row_count, slots, width = keys.shape
    rows = step_count * row_count
    seen_rows = rows * queries.shape[1] // lanes
    table = jax.ShapeDtypeStruct((rows, lanes), f32)
    seen_table = jax.ShapeDtypeStruct((seen_rows, lanes), f32)
    return pl.pallas_call(
        functools.partial(attend_kernel, step_count, width // lanes),
        out_shape=(
            jax.ShapeDtypeStruct(mine.shape, f32),
            jax.ShapeDtypeStruct((seen_rows, lanes), bf16),
            seen_table,
            seen_table,
            seen_table,
            table,
            table,
        ),
        in_specs=[stays_in_hbm] + [whole_in_vmem] * (5 + len(far)),
        out_specs=(whole_in_vmem,) * 7,
        scratch_shapes=[
            pltpu.SMEM(lengths.shape, jnp.int32),
            pltpu.VMEM((seen_rows, lanes), f32),
            pltpu.VMEM((seen_rows, slots), f32),
            pltpu.VMEM((seen_rows, slots), bf16),
            pltpu.SemaphoreType.DMA,
        ],
        compiler_params=pltpu.CompilerParams(vmem_limit_bytes=8 * 2**20),
        name="attend",
        cost_estimate=pl.CostEstimate(
            flops=4 * seen_rows * slots * lanes,
            bytes_accessed=2 * (keys.size + values.size),
            transcendentals=seen_rows * slots,
        ),
    )(*in_hbm(lengths), queries, keys, values, after, mine, *far)


def piece_places(replicas):
    order = [0, 1] + list(range(replicas - 1, 1, -1))
    return [order.index(i) for i in range(replicas)]


def route_kernel(replicas, shards, *refs):
    owners_hbm, left_ref = refs[:2]
    piece_refs = [refs[2 + place] for place in piece_places(replicas)]
    out_refs = refs[3 + replicas : 3 + replicas + shards]
    owners_ref, right, up_buf, owner_sem = refs[3 + replicas + shards :]
    owners_copy = pltpu.make_async_copy(owners_hbm, owners_ref, owner_sem)
    owners_copy.start()
    rows = left_ref.shape[0]
    rank = right.shape[0]
    width = right.shape[1] // replicas
    half = rank // 2
    rest = (piece_refs[0].shape[0] - up_buf.shape[1]) % rank
    for i in range(replicas):
        first = 0
        for c in range(width // lanes - (1 if rest else 0)):
            right[:, i * width + c * lanes : i * width + (c + 1) * lanes] = piece_refs[i][
                first : first + rank, :
            ]
            first += rank
        if rest:
            both = piece_refs[i][first : first + half, :]
            tail = jnp.concatenate([both[:, : lanes // 2], both[:, lanes // 2 :]], axis=0)
            right[:, (i + 1) * width - lanes : (i + 1) * width] = jnp.concatenate(
                [tail, jnp.zeros((rank, lanes // 2), bf16)], axis=1
            )
            first += half
        up_buf[i] = piece_refs[i][first:, :]
    lowered = lax.dot_general(
        left_ref[...], right[...], (((1,), (1,)), ((), ())), preferred_element_type=f32
    )
    both = jnp.concatenate(split_halves(lowered), axis=1)
    replica = lax.axis_index("rollout")
    shard = lax.axis_index("tensor")
    owners_copy.wait()
    for i in range(shards):
        out_refs[i][:rows, :] = both
        slot = owners_ref[shard ^ i] ^ replica
        out_refs[i][rows:, :] = up_buf[slot]


def route(owners, left, pieces, after, rank, up_rows, shards):
    rows, depth = left.shape
    replicas = len(pieces)
    return pl.pallas_call(
        functools.partial(route_kernel, replicas, shards),
        out_shape=[jax.ShapeDtypeStruct((rows + up_rows, lanes), bf16)] * shards,
        in_specs=[stays_in_hbm] + [whole_in_vmem] * (2 + replicas),
        out_specs=[whole_in_vmem] * shards,
        scratch_shapes=[
            pltpu.SMEM(owners.shape, jnp.int32),
            pltpu.VMEM((rank, depth), bf16),
            pltpu.VMEM((replicas, up_rows, lanes), bf16),
            pltpu.SemaphoreType.DMA,
        ],
        compiler_params=pltpu.CompilerParams(vmem_limit_bytes=4 * 2**20),
        name="route",
        cost_estimate=pl.CostEstimate(flops=0, bytes_accessed=800000, transcendentals=0),
    )(*in_hbm(owners), left, *[pieces[i] for i in piece_places(replicas)], after)


def route_plain(owners, tokens, down, up, rank_part, own, shards):
    rank = down.shape[1]
    shard = lax.axis_index("tensor")
    first = shard * rank_part
    up_part = lax.dynamic_slice_in_dim(up, first, rank_part, axis=0)
    downs = lax.all_gather(down, "rollout", axis=0, tiled=False)
    ups = lax.all_gather(up_part, "rollout", axis=0, tiled=False)
    down_matrix = jnp.take(downs, owners, axis=0, mode="clip").reshape(-1, rank)
    up_matrix = jnp.take(ups, owners, axis=0, mode="clip").transpose(1, 0, 2)
    up_matrix = up_matrix.reshape(rank_part, -1)
    lowered = jnp.dot(tokens, down_matrix, preferred_element_type=f32)
    both = jnp.concatenate(split_halves(lowered), axis=1)
    packets = []
    for i in range(shards):
        up_block = lax.dynamic_slice_in_dim(up_matrix, (shard ^ i) * own, own, axis=1)
        parts = [both, side_by_side(up_block)]
        packets.append(jnp.concatenate(parts, axis=0))
    return packets


def finish_kernel(step_count, row_count, head_count, shards, *refs):
    gain_ref, base_ref, grouped_ref, total_ref, peak_ref, sum_ref, cosine_ref, sine_ref = refs[:8]
    packet_refs = refs[8 : 8 + shards][::-1]
    attention_ref, keys_ref, values_ref = refs[8 + shards : 11 + shards]
    (up_buf,) = refs[11 + shards :]
    shard = lax.axis_index("tensor")
    rows = step_count * row_count
    own = base_ref.shape[1]
    blocks = own // lanes
    rank = up_buf.shape[0]
    rank_part = rank // shards
    group = grouped_ref.shape[0] // (head_count * rows)
    seen = step_count * group

    lowered = jnp.zeros((rows, lanes), f32)
    for i in range(shards):
        lowered = lowered + packet_refs[i][:rows, :].astype(f32)
        ups = packet_refs[i][rows:, :].astype(f32)
        at = pl.multiple_of((shard ^ i) * rank_part, rank_part)
        for c in range(blocks):
            up_buf[pl.ds(at, rank_part), c * lanes : (c + 1) * lanes] = ups[
                c * rank_part : (c + 1) * rank_part, :
            ]
    lane = lax.broadcasted_iota(jnp.int32, (rows, lanes), 1)
    lowered = lowered + pltpu.roll(lowered, rank, 1)
    high, low = split_halves(lowered)
    left = jnp.where(lane < rank, high.astype(f32), low.astype(f32)).astype(bf16)
    up = up_buf[...].astype(bf16)
    raised_up = jnp.dot(left, jnp.concatenate([up, up], axis=0), preferred_element_type=f32)
    joined = []
    for c in range(blocks):
        block = base_ref[:, c * lanes : (c + 1) * lanes]
        joined.append(block + adapter_scale * raised_up[:, c * lanes : (c + 1) * lanes])

    all_rows = row_count * seen
    seen_by = lax.broadcasted_iota(jnp.int32, (all_rows, rows), 0)
    made_by = lax.broadcasted_iota(jnp.int32, (all_rows, rows), 1)
    visible = (seen_by % row_count == made_by % row_count) & (
        made_by // row_count <= seen_by // (row_count * group)
    )
    heads = [(h, slice(h * all_rows, (h + 1) * all_rows)) for h in range(head_count)]
    keys, values, scores, results = [], [], [], []
    for h, _ in heads:
        raw_key = joined[2 * h]
        mean_square = jnp.mean(raw_key * raw_key, axis=1, keepdims=True)
        normed = raw_key * lax.rsqrt(mean_square + norm_eps) * gain_ref[...]
        key = normed * cosine_ref[...] + pltpu.roll(normed, lanes // 2, 1) * sine_ref[...]
        keys.append(key.astype(bf16))
        values.append(joined[2 * h + 1].astype(bf16))
        keys_ref[:, h * lanes : (h + 1) * lanes] = keys[h]
        values_ref[:, h * lanes : (h + 1) * lanes] = values[h]
    for h, mine in heads:
        score = lax.dot_general(
            grouped_ref[mine, :], keys[h], (((1,), (1,)), ((), ())), preferred_element_type=f32
        )
        scores.append(jnp.where(visible, score, masked_score))
    for h, mine in heads:
        old_peak = peak_ref[mine, :]
        peak = jnp.maximum(old_peak, jnp.max(scores[h], axis=1, keepdims=True))
        fade = jnp.exp2((old_peak - peak) * exponent_scale)
        lifted = jnp.exp2((scores[h] - peak[:, :rows]) * exponent_scale)
        denominator = fade * sum_ref[mine, :] + jnp.sum(lifted, axis=1, keepdims=True)
        total = fade * total_ref[mine, :] + jnp.dot(
            lifted.astype(bf16), values[h], preferred_element_type=f32
        )
        results.append(total / denominator)
    for pair in range(step_count // 2):
        for q in range(head_count * group):
            h, g = q // group, q % group
            both = []
            for side in range(2):
                first = ((pair * 2 + side) * group + g) * row_count
                both.append(results[h][first : first + row_count])
            attention_ref[
                pair * 2 * row_count : (pair + 1) * 2 * row_count, q * lanes : (q + 1) * lanes
            ] = jnp.concatenate(both, axis=0).astype(bf16)


def finish(partials, gain, packets, rank, step_count, row_count, query_width):
    rows, own = partials[0].shape
    total = partials[2]
    shards = len(packets)
    head_count = own // (2 * lanes)
    return pl.pallas_call(
        functools.partial(finish_kernel, step_count, row_count, head_count, shards),
        out_shape=(
            jax.ShapeDtypeStruct((rows, query_width), bf16),
            jax.ShapeDtypeStruct((rows, head_count * lanes), bf16),
            jax.ShapeDtypeStruct((rows, head_count * lanes), bf16),
        ),
        in_specs=[whole_in_vmem] * (8 + shards),
        out_specs=(whole_in_vmem,) * 3,
        scratch_shapes=[
            pltpu.VMEM((rank, own), f32),
        ],
        compiler_params=pltpu.CompilerParams(vmem_limit_bytes=6 * 2**20),
        name="finish",
        cost_estimate=pl.CostEstimate(flops=0, bytes_accessed=1000000, transcendentals=0),
    )(gain, *partials, *packets[::-1])


def per_device(
    normed_tokens,
    key_value_weight,
    adapter_down,
    adapter_up,
    key_gain,
    queries,
    cache_keys,
    stored_values,
    lengths,
    owners,
):
    replicas = lax.axis_size("rollout")
    shards = lax.axis_size("tensor")
    down_rows, rank = adapter_down.shape
    step_count, row_count, depth = normed_tokens.shape
    own = key_value_weight.shape[1] // shards
    rank_part = rank // shards
    rows = step_count * row_count
    tokens = normed_tokens.reshape(rows, depth)
    query_rows = queries.reshape(rows, -1)

    fits = (
        replicas <= 4
        and adapter_up.shape[1] == own
        and down_rows % lanes in (0, lanes // 2)
        and rank == lanes // 2
        and rank_part % 16 == 0
    )
    if fits:
        fetched = 2 * (key_value_weight.size + cache_keys.size + stored_values.size)
        beside = pl.CostEstimate(flops=1000 * fetched, bytes_accessed=fetched, transcendentals=0)
        packed = pack(adapter_down.T, adapter_up, rank_part, beside)
        pieces = [packed] + [swap(packed, "rollout", i) for i in range(1, replicas)]
    near, kept, left = project(
        owners,
        tokens,
        key_value_weight,
        packed if fits else adapter_up,
        shards,
        replicas if fits else 1,
    )
    mine, far = chip_sums(kept, [swap(block, "tensor", 1) for block in near])
    far = [swap(block, "tensor", 2 * m + 2) for m, block in enumerate(far)]
    if fits:
        packets = route(
            owners, left, pieces, mine, rank, rank_part * own // lanes, shards
        )
    else:
        packets = route_plain(owners, tokens, adapter_down, adapter_up, rank_part, own, shards)
    partials = attend(
        lengths, query_rows, cache_keys, stored_values, packets[0], mine, far, step_count
    )
    packets = [packets[0]] + [swap(packets[i], "tensor", i) for i in range(1, shards)]
    attention, keys, values = finish(
        partials,
        key_gain.reshape(1, -1),
        packets,
        rank,
        step_count,
        row_count,
        query_rows.shape[1],
    )
    return tuple(a.reshape(step_count, row_count, -1) for a in (attention, keys, values))


def solution(mesh):
    placed = (
        P(None, ("job", "rollout"), "tensor"),
        P("tensor", None),
        P(("job", "rollout", "tensor"), None),
        P(None, ("job", "rollout")),
        P(),
        P(None, ("job", "rollout"), "tensor"),
        P(("job", "rollout"), None, "tensor"),
        P(("job", "rollout"), None, "tensor"),
        P(("job", "rollout")),
        P("job"),
    )
    return jax.shard_map(
        per_device,
        mesh=mesh,
        in_specs=placed,
        out_specs=(
            P(None, ("job", "rollout"), "tensor"),
            P(None, ("job", "rollout"), "tensor"),
            P(None, ("job", "rollout"), "tensor"),
        ),
        check_vma=False,
    )
```

```python
import functools
import math

import jax
import jax.numpy as jnp
from jax import lax
from jax.experimental import pallas as pl
from jax.experimental.pallas import tpu as pltpu
from jax.sharding import PartitionSpec as P

norm_eps = 1e-06
rope_base = 1000000.0
adapter_scale = 2.0
masked_score = -1e30
lanes = 128
exponent_scale = lanes**-0.5 / math.log(2.0)
f32 = jnp.float32
bf16 = jnp.bfloat16

whole_in_vmem = pl.BlockSpec(memory_space=pltpu.VMEM)
whole_in_smem = pl.BlockSpec(memory_space=pltpu.SMEM)
stays_in_hbm = pl.BlockSpec(memory_space=pltpu.HBM)


def swap(block, axis, offset):
    count = lax.axis_size(axis)
    return lax.ppermute(block, axis, [(s, s ^ offset) for s in range(count)])


def in_hbm(*arrays):
    return tuple(pltpu.with_memory_space_constraint(a, pltpu.HBM) for a in arrays)


def side_by_side(rows_of_blocks):
    r, c = rows_of_blocks.shape
    return rows_of_blocks.reshape(r, c // lanes, lanes).transpose(1, 0, 2).reshape(-1, lanes)


def split_halves(total):
    high = total.astype(bf16)
    return high, (total - high.astype(f32)).astype(bf16)


def pack_kernel(down_hbm, up_hbm, out_ref, down_ref, up_ref, sems):
    rank, down_rows = down_ref.shape
    rank_part = up_ref.shape[0]
    start = pl.multiple_of(lax.axis_index("tensor") * rank_part, rank_part)
    copies = [
        pltpu.make_async_copy(down_hbm, down_ref, sems.at[0]),
        pltpu.make_async_copy(up_hbm.at[pl.ds(start, rank_part), :], up_ref, sems.at[1]),
    ]
    for copy in copies:
        copy.start(priority=1)
    for copy in copies:
        copy.wait()
    first = 0
    for c in range(down_rows // lanes):
        out_ref[first : first + rank, :] = down_ref[:, c * lanes : (c + 1) * lanes]
        first += rank
    rest = down_rows % lanes
    if rest:
        half = rank // 2
        tail = down_ref[:, down_rows - rest :]
        out_ref[first : first + half, :] = jnp.concatenate([tail[:half], tail[half:]], axis=1)
        first += half
    for c in range(up_ref.shape[1] // lanes):
        out_ref[first : first + rank_part, :] = up_ref[:, c * lanes : (c + 1) * lanes]
        first += rank_part


def pack(down, up, rank_part, beside):
    rows = (down.size + rank_part * up.shape[1]) // lanes
    return pl.pallas_call(
        pack_kernel,
        out_shape=jax.ShapeDtypeStruct((rows, lanes), bf16),
        in_specs=[stays_in_hbm] * 2,
        out_specs=whole_in_vmem,
        scratch_shapes=[
            pltpu.VMEM(down.shape, bf16),
            pltpu.VMEM((rank_part, up.shape[1]), bf16),
            pltpu.SemaphoreType.DMA((2,)),
        ],
        compiler_params=pltpu.CompilerParams(vmem_limit_bytes=2 * 2**20),
        name="pack",
        cost_estimate=beside,
    )(*in_hbm(down, up))


def project_kernel(shards, replicas, *refs):
    owners_hbm, tokens_ref, weight_ref, _ = refs[:4]
    own_ref, near_ref = refs[4:6]
    far_refs = refs[6 : 4 + shards]
    left_ref, pick_ref, owners_ref, token_buf, owner_sem = refs[4 + shards :]
    owners_copy = pltpu.make_async_copy(owners_hbm, owners_ref, owner_sem)
    owners_copy.start()

    shard = lax.axis_index("tensor")
    rows, own = own_ref.shape
    for i in range(shards):
        first = pl.multiple_of((shard ^ i) * own, lanes)
        block = jnp.dot(
            tokens_ref[...], weight_ref[:, pl.ds(first, own)], preferred_element_type=f32
        )
        if i == 0:
            own_ref[...] = block
        elif i > 1:
            far_refs[i - 2][...] = block
        else:
            for c in range(own // lanes):
                near_ref[c * rows : (c + 1) * rows, :] = block[
                    :, c * lanes : (c + 1) * lanes
                ].astype(bf16)

    owners_copy.wait()
    replica = lax.axis_index("rollout")
    width = token_buf.shape[2]
    down_rows = tokens_ref.shape[1] // replicas
    for k in range(replicas):
        token_buf[k, :, :down_rows] = tokens_ref[:, k * down_rows : (k + 1) * down_rows]
        if down_rows < width:
            token_buf[k, :, down_rows:] = jnp.zeros((rows, width - down_rows), bf16)
    for i in range(replicas):
        place = jnp.int32(0)
        for k in range(1, replicas):
            place = place + jnp.where(owners_ref[k] == replica ^ i, k, 0)
        left_ref[:, i * width : (i + 1) * width] = token_buf[place]
    if replicas > 1:
        for i in range(shards):
            for k in range(replicas):
                picked = jnp.where(owners_ref[shard ^ i] == replica ^ k, 1.0, 0.0)
                row = i * replicas + k
                pick_ref[row : row + 1, :] = jnp.full((1, lanes), picked, f32)


def project(owners, tokens, weight, after, shards, replicas):
    rows, depth = tokens.shape
    own = weight.shape[1] // shards
    piece_width = -(-depth // replicas // lanes) * lanes
    mine, near, *rest = pl.pallas_call(
        functools.partial(project_kernel, shards, replicas),
        out_shape=[
            jax.ShapeDtypeStruct((rows, own), f32),
            jax.ShapeDtypeStruct((rows * own // lanes, lanes), bf16),
        ]
        + [jax.ShapeDtypeStruct((rows, own), f32)] * (shards - 2)
        + [
            jax.ShapeDtypeStruct((rows, replicas * piece_width), bf16),
            jax.ShapeDtypeStruct((shards * replicas, lanes), f32),
        ],
        in_specs=[stays_in_hbm] + [whole_in_vmem] * 3,
        out_specs=[whole_in_vmem] * (shards + 2),
        scratch_shapes=[
            pltpu.SMEM(owners.shape, jnp.int32),
            pltpu.VMEM((replicas, rows, piece_width), bf16),
            pltpu.SemaphoreType.DMA,
        ],
        compiler_params=pltpu.CompilerParams(vmem_limit_bytes=4 * 2**20),
        name="project",
        cost_estimate=pl.CostEstimate(
            flops=2 * rows * weight.size, bytes_accessed=2 * weight.size, transcendentals=0
        ),
    )(*in_hbm(owners), tokens, weight, after)
    return mine, near, rest[:-2], *rest[-2:]


def attend_kernel(
    step_count,
    head_count,
    lengths_hbm,
    queries_ref,
    keys_ref,
    values_ref,
    _,
    grouped_ref,
    total_ref,
    peak_ref,
    sum_ref,
    cosine_ref,
    sine_ref,
    lengths_ref,
    regroup,
    scores_ref,
    raised,
    length_sem,
):
    lengths_copy = pltpu.make_async_copy(lengths_hbm, lengths_ref, length_sem)
    lengths_copy.start()
    rows = cosine_ref.shape[0]

    row_count, slots, _ = keys_ref.shape
    group = queries_ref.shape[1] // (head_count * lanes)
    seen = step_count * group
    for pair in range(step_count // 2):
        for q in range(head_count * group):
            h, g = q // group, q % group
            both = queries_ref[
                pair * 2 * row_count : (pair + 1) * 2 * row_count, q * lanes : (q + 1) * lanes
            ].astype(f32)
            for side in range(2):
                first = h * row_count * seen + (pair * 2 + side) * group + g
                regroup[pl.ds(first, row_count, stride=seen), :] = both[
                    side * row_count : (side + 1) * row_count, :
                ]
            if g % 2:
                for side in range(2):
                    half = slice(side * row_count, (side + 1) * row_count)
                    last = (h * seen + (pair * 2 + side) * group + g + 1) * row_count
                    grouped_ref[last - 2 * row_count : last, :] = jnp.concatenate(
                        [before[half], both[half]], axis=0
                    ).astype(bf16)
            before = both

    for b in range(row_count):
        for h in range(head_count):
            at = (h * row_count + b) * seen
            scores_ref[at : at + seen, :] = lax.dot_general(
                regroup[at : at + seen, :].astype(bf16),
                keys_ref[b, :, h * lanes : (h + 1) * lanes],
                (((1,), (1,)), ((), ())),
                preferred_element_type=f32,
            )

    places = [
        (
            b,
            h,
            slice((h * row_count + b) * seen, (h * row_count + b + 1) * seen),
            pl.ds(h * row_count * seen + b, seen, stride=row_count),
        )
        for b in range(row_count)
        for h in range(head_count)
    ]
    lengths_copy.wait()
    slot = lax.broadcasted_iota(jnp.int32, (seen, slots), 1)
    for b, h, place, out in places:
        score = jnp.where(slot < lengths_ref[b], scores_ref[place, :], masked_score)
        peak = jnp.max(score, axis=1, keepdims=True)
        lifted = jnp.exp2((score - peak) * exponent_scale)
        raised[place, :] = lifted.astype(bf16)
        peak_ref[out, :] = jnp.broadcast_to(peak, (seen, lanes))
        sum_ref[out, :] = jnp.broadcast_to(
            jnp.sum(lifted, axis=1, keepdims=True), (seen, lanes)
        )
    for b, h, place, out in places:
        total_ref[out, :] = jnp.dot(
            raised[place, :],
            values_ref[b, :, h * lanes : (h + 1) * lanes],
            preferred_element_type=f32,
        )

    row = lax.broadcasted_iota(jnp.int32, (rows, lanes), 0)
    lane = lax.broadcasted_iota(jnp.int32, (rows, lanes), 1)
    position = row // row_count
    for b in range(row_count):
        position = position + jnp.where(row % row_count == b, lengths_ref[b], 0)
    middle = lanes // 2
    spacing = (lane % middle).astype(f32) * (-2.0 / lanes * math.log(rope_base))
    angles = position.astype(f32) * jnp.exp(spacing)
    cosine_ref[...] = jnp.cos(angles)
    sine = jnp.sin(angles)
    sine_ref[...] = jnp.where(lane < middle, -sine, sine)


def attend(lengths, queries, keys, values, after, step_count):
    row_count, slots, width = keys.shape
    rows = step_count * row_count
    seen_rows = rows * queries.shape[1] // lanes
    table = jax.ShapeDtypeStruct((rows, lanes), f32)
    seen_table = jax.ShapeDtypeStruct((seen_rows, lanes), f32)
    return pl.pallas_call(
        functools.partial(attend_kernel, step_count, width // lanes),
        out_shape=(
            jax.ShapeDtypeStruct((seen_rows, lanes), bf16),
            seen_table,
            seen_table,
            seen_table,
            table,
            table,
        ),
        in_specs=[stays_in_hbm] + [whole_in_vmem] * 4,
        out_specs=(whole_in_vmem,) * 6,
        scratch_shapes=[
            pltpu.SMEM(lengths.shape, jnp.int32),
            pltpu.VMEM((seen_rows, lanes), f32),
            pltpu.VMEM((seen_rows, slots), f32),
            pltpu.VMEM((seen_rows, slots), bf16),
            pltpu.SemaphoreType.DMA,
        ],
        compiler_params=pltpu.CompilerParams(vmem_limit_bytes=8 * 2**20),
        name="attend",
        cost_estimate=pl.CostEstimate(
            flops=4 * seen_rows * slots * lanes,
            bytes_accessed=2 * (keys.size + values.size),
            transcendentals=seen_rows * slots,
        ),
    )(*in_hbm(lengths), queries, keys, values, after)


def piece_places(replicas):
    order = [0, 1] + list(range(replicas - 1, 1, -1))
    return [order.index(i) for i in range(replicas)]


def route_kernel(replicas, shards, *refs):
    left_ref, pick_ref, near_ref = refs[:3]
    piece_refs = [refs[3 + place] for place in piece_places(replicas)]
    out_refs = refs[3 + replicas : 3 + replicas + shards]
    (right,) = refs[3 + replicas + shards :]
    up_rows = out_refs[0].shape[0] - left_ref.shape[0]
    rows = left_ref.shape[0]
    rank = right.shape[0]
    width = right.shape[1] // replicas
    half = rank // 2
    rest = (piece_refs[0].shape[0] - up_rows) % rank
    for i in range(replicas):
        first = 0
        for c in range(width // lanes - (1 if rest else 0)):
            right[:, i * width + c * lanes : i * width + (c + 1) * lanes] = piece_refs[i][
                first : first + rank, :
            ]
            first += rank
        if rest:
            both = piece_refs[i][first : first + half, :]
            tail = jnp.concatenate([both[:, : lanes // 2], both[:, lanes // 2 :]], axis=0)
            right[:, (i + 1) * width - lanes : (i + 1) * width] = jnp.concatenate(
                [tail, jnp.zeros((rank, lanes // 2), bf16)], axis=1
            )
            first += half
    lowered = lax.dot_general(
        left_ref[...], right[...], (((1,), (1,)), ((), ())), preferred_element_type=f32
    )
    both = jnp.concatenate(split_halves(lowered), axis=1)
    ups = [piece[piece.shape[0] - up_rows :, :].astype(f32) for piece in piece_refs]
    for i in range(shards):
        first = 0
        if i == 1:
            first = near_ref.shape[0]
            out_refs[i][:first, :] = near_ref[...]
        out_refs[i][first : first + rows, :] = both
        picked = sum(up * pick_ref[i * replicas + k, :][None, :] for k, up in enumerate(ups))
        out_refs[i][first + rows :, :] = picked.astype(bf16)


def route(left, pick, near, pieces, rank, up_rows, shards):
    rows, depth = left.shape
    replicas = len(pieces)
    sent = near.shape[0]
    return pl.pallas_call(
        functools.partial(route_kernel, replicas, shards),
        out_shape=[
            jax.ShapeDtypeStruct(((sent if i == 1 else 0) + rows + up_rows, lanes), bf16)
            for i in range(shards)
        ],
        in_specs=[whole_in_vmem] * (3 + replicas),
        out_specs=[whole_in_vmem] * shards,
        scratch_shapes=[pltpu.VMEM((rank, depth), bf16)],
        compiler_params=pltpu.CompilerParams(vmem_limit_bytes=4 * 2**20),
        name="route",
        cost_estimate=pl.CostEstimate(flops=0, bytes_accessed=800000, transcendentals=0),
    )(left, pick, near, *[pieces[i] for i in piece_places(replicas)])


def route_plain(owners, tokens, near, down, up, rank_part, own, shards):
    rank = down.shape[1]
    shard = lax.axis_index("tensor")
    first = shard * rank_part
    up_part = lax.dynamic_slice_in_dim(up, first, rank_part, axis=0)
    downs = lax.all_gather(down, "rollout", axis=0, tiled=False)
    ups = lax.all_gather(up_part, "rollout", axis=0, tiled=False)
    down_matrix = jnp.take(downs, owners, axis=0, mode="clip").reshape(-1, rank)
    up_matrix = jnp.take(ups, owners, axis=0, mode="clip").transpose(1, 0, 2)
    up_matrix = up_matrix.reshape(rank_part, -1)
    lowered = jnp.dot(tokens, down_matrix, preferred_element_type=f32)
    both = jnp.concatenate(split_halves(lowered), axis=1)
    packets = []
    for i in range(shards):
        up_block = lax.dynamic_slice_in_dim(up_matrix, (shard ^ i) * own, own, axis=1)
        parts = [both, side_by_side(up_block)]
        if i == 1:
            parts = [near] + parts
        packets.append(jnp.concatenate(parts, axis=0))
    return packets


def finish_kernel(step_count, row_count, head_count, shards, *refs):
    gain_ref, base_ref, grouped_ref, total_ref, peak_ref, sum_ref, cosine_ref, sine_ref = refs[:8]
    packet_refs = refs[8 : 8 + shards][::-1]
    far_refs = refs[8 + shards : 6 + 2 * shards]
    attention_ref, keys_ref, values_ref = refs[6 + 2 * shards : 9 + 2 * shards]
    (up_buf,) = refs[9 + 2 * shards :]
    shard = lax.axis_index("tensor")
    rows = step_count * row_count
    own = base_ref.shape[1]
    blocks = own // lanes
    rank = up_buf.shape[0]
    rank_part = rank // shards
    group = grouped_ref.shape[0] // (head_count * rows)
    seen = step_count * group

    lowered = jnp.zeros((rows, lanes), f32)
    for i in range(shards):
        first = rows * blocks if i == 1 else 0
        lowered = lowered + packet_refs[i][first : first + rows, :].astype(f32)
        ups = packet_refs[i][first + rows :, :].astype(f32)
        at = pl.multiple_of((shard ^ i) * rank_part, rank_part)
        for c in range(blocks):
            up_buf[pl.ds(at, rank_part), c * lanes : (c + 1) * lanes] = ups[
                c * rank_part : (c + 1) * rank_part, :
            ]
    lane = lax.broadcasted_iota(jnp.int32, (rows, lanes), 1)
    lowered = lowered + pltpu.roll(lowered, rank, 1)
    high, low = split_halves(lowered)
    left = jnp.where(lane < rank, high.astype(f32), low.astype(f32)).astype(bf16)
    up = up_buf[...].astype(bf16)
    raised_up = jnp.dot(left, jnp.concatenate([up, up], axis=0), preferred_element_type=f32)
    joined = []
    for c in range(blocks):
        block = base_ref[:, c * lanes : (c + 1) * lanes]
        for far_ref in far_refs:
            block = block + far_ref[:, c * lanes : (c + 1) * lanes]
        block = block + packet_refs[1][c * rows : (c + 1) * rows, :].astype(f32)
        joined.append(block + adapter_scale * raised_up[:, c * lanes : (c + 1) * lanes])

    all_rows = row_count * seen
    seen_by = lax.broadcasted_iota(jnp.int32, (all_rows, rows), 0)
    made_by = lax.broadcasted_iota(jnp.int32, (all_rows, rows), 1)
    visible = (seen_by % row_count == made_by % row_count) & (
        made_by // row_count <= seen_by // (row_count * group)
    )
    heads = [(h, slice(h * all_rows, (h + 1) * all_rows)) for h in range(head_count)]
    keys, values, scores, results = [], [], [], []
    for h, _ in heads:
        raw_key = joined[2 * h]
        mean_square = jnp.mean(raw_key * raw_key, axis=1, keepdims=True)
        normed = raw_key * lax.rsqrt(mean_square + norm_eps) * gain_ref[...]
        key = normed * cosine_ref[...] + pltpu.roll(normed, lanes // 2, 1) * sine_ref[...]
        keys.append(key.astype(bf16))
        values.append(joined[2 * h + 1].astype(bf16))
        keys_ref[:, h * lanes : (h + 1) * lanes] = keys[h]
        values_ref[:, h * lanes : (h + 1) * lanes] = values[h]
    for h, mine in heads:
        score = lax.dot_general(
            grouped_ref[mine, :], keys[h], (((1,), (1,)), ((), ())), preferred_element_type=f32
        )
        scores.append(jnp.where(visible, score, masked_score))
    for h, mine in heads:
        old_peak = peak_ref[mine, :]
        peak = jnp.maximum(old_peak, jnp.max(scores[h], axis=1, keepdims=True))
        fade = jnp.exp2((old_peak - peak) * exponent_scale)
        lifted = jnp.exp2((scores[h] - peak[:, :rows]) * exponent_scale)
        denominator = fade * sum_ref[mine, :] + jnp.sum(lifted, axis=1, keepdims=True)
        total = fade * total_ref[mine, :] + jnp.dot(
            lifted.astype(bf16), values[h], preferred_element_type=f32
        )
        results.append(total / denominator)
    for pair in range(step_count // 2):
        for q in range(head_count * group):
            h, g = q // group, q % group
            both = []
            for side in range(2):
                first = ((pair * 2 + side) * group + g) * row_count
                both.append(results[h][first : first + row_count])
            attention_ref[
                pair * 2 * row_count : (pair + 1) * 2 * row_count, q * lanes : (q + 1) * lanes
            ] = jnp.concatenate(both, axis=0).astype(bf16)


def finish(mine, far, partials, gain, packets, rank, step_count, row_count, query_width):
    rows, own = mine.shape
    shards = len(packets)
    head_count = own // (2 * lanes)
    return pl.pallas_call(
        functools.partial(finish_kernel, step_count, row_count, head_count, shards),
        out_shape=(
            jax.ShapeDtypeStruct((rows, query_width), bf16),
            jax.ShapeDtypeStruct((rows, head_count * lanes), bf16),
            jax.ShapeDtypeStruct((rows, head_count * lanes), bf16),
        ),
        in_specs=[whole_in_vmem] * (6 + 2 * shards),
        out_specs=(whole_in_vmem,) * 3,
        scratch_shapes=[
            pltpu.VMEM((rank, own), f32),
        ],
        compiler_params=pltpu.CompilerParams(vmem_limit_bytes=6 * 2**20),
        name="finish",
        cost_estimate=pl.CostEstimate(flops=0, bytes_accessed=1000000, transcendentals=0),
    )(gain, mine, *partials, *packets[::-1], *far)


def per_device(
    normed_tokens,
    key_value_weight,
    adapter_down,
    adapter_up,
    key_gain,
    queries,
    cache_keys,
    stored_values,
    lengths,
    owners,
):
    replicas = lax.axis_size("rollout")
    shards = lax.axis_size("tensor")
    down_rows, rank = adapter_down.shape
    step_count, row_count, depth = normed_tokens.shape
    own = key_value_weight.shape[1] // shards
    rank_part = rank // shards
    rows = step_count * row_count
    tokens = normed_tokens.reshape(rows, depth)
    query_rows = queries.reshape(rows, -1)

    fits = (
        replicas <= 4
        and adapter_up.shape[1] == own
        and down_rows % lanes in (0, lanes // 2)
        and rank == lanes // 2
        and rank_part % 16 == 0
    )
    if fits:
        fetched = 2 * (key_value_weight.size + cache_keys.size + stored_values.size)
        beside = pl.CostEstimate(flops=1000 * fetched, bytes_accessed=fetched, transcendentals=0)
        packed = pack(adapter_down.T, adapter_up, rank_part, beside)
        pieces = [packed] + [swap(packed, "rollout", i) for i in range(1, replicas)]
    mine, near, far, left, pick = project(
        owners,
        tokens,
        key_value_weight,
        packed if fits else adapter_up,
        shards,
        replicas if fits else 1,
    )
    far = [swap(block, "tensor", i + 2) for i, block in enumerate(far)]
    if fits:
        packets = route(left, pick, near, pieces, rank, rank_part * own // lanes, shards)
    else:
        packets = route_plain(
            owners, tokens, near, adapter_down, adapter_up, rank_part, own, shards
        )
    partials = attend(lengths, query_rows, cache_keys, stored_values, packets[0], step_count)
    packets = [packets[0]] + [swap(packets[i], "tensor", i) for i in range(1, shards)]
    attention, keys, values = finish(
        mine,
        far,
        partials,
        key_gain.reshape(1, -1),
        packets,
        rank,
        step_count,
        row_count,
        query_rows.shape[1],
    )
    return tuple(a.reshape(step_count, row_count, -1) for a in (attention, keys, values))


def solution(mesh):
    placed = (
        P(None, ("job", "rollout"), "tensor"),
        P("tensor", None),
        P(("job", "rollout", "tensor"), None),
        P(None, ("job", "rollout")),
        P(),
        P(None, ("job", "rollout"), "tensor"),
        P(("job", "rollout"), None, "tensor"),
        P(("job", "rollout"), None, "tensor"),
        P(("job", "rollout")),
        P("job"),
    )
    return jax.shard_map(
        per_device,
        mesh=mesh,
        in_specs=placed,
        out_specs=(
            P(None, ("job", "rollout"), "tensor"),
            P(None, ("job", "rollout"), "tensor"),
            P(None, ("job", "rollout"), "tensor"),
        ),
        check_vma=False,
    )
```

```python
import functools
import math

import jax
import jax.numpy as jnp
from jax import lax
from jax.experimental import pallas as pl
from jax.experimental.pallas import tpu as pltpu
from jax.sharding import PartitionSpec as P

norm_eps = 1e-06
rope_base = 1000000.0
adapter_scale = 2.0
masked_score = -1e30
lanes = 128
exponent_scale = lanes**-0.5 / math.log(2.0)
f32 = jnp.float32
bf16 = jnp.bfloat16

whole_in_vmem = pl.BlockSpec(memory_space=pltpu.VMEM)
whole_in_smem = pl.BlockSpec(memory_space=pltpu.SMEM)
stays_in_hbm = pl.BlockSpec(memory_space=pltpu.HBM)


def swap(block, axis, offset):
    count = lax.axis_size(axis)
    return lax.ppermute(block, axis, [(s, s ^ offset) for s in range(count)])


def in_hbm(*arrays):
    return tuple(pltpu.with_memory_space_constraint(a, pltpu.HBM) for a in arrays)


def side_by_side(rows_of_blocks):
    r, c = rows_of_blocks.shape
    return rows_of_blocks.reshape(r, c // lanes, lanes).transpose(1, 0, 2).reshape(-1, lanes)


def split_halves(total):
    high = total.astype(bf16)
    return high, (total - high.astype(f32)).astype(bf16)


def pack_kernel(down_hbm, up_hbm, out_ref, down_ref, up_ref, sems):
    rank, down_rows = down_ref.shape
    rank_part = up_ref.shape[0]
    start = pl.multiple_of(lax.axis_index("tensor") * rank_part, rank_part)
    copies = [
        pltpu.make_async_copy(down_hbm, down_ref, sems.at[0]),
        pltpu.make_async_copy(up_hbm.at[pl.ds(start, rank_part), :], up_ref, sems.at[1]),
    ]
    for copy in copies:
        copy.start(priority=1)
    for copy in copies:
        copy.wait()
    first = 0
    for c in range(down_rows // lanes):
        out_ref[first : first + rank, :] = down_ref[:, c * lanes : (c + 1) * lanes]
        first += rank
    rest = down_rows % lanes
    if rest:
        half = rank // 2
        tail = down_ref[:, down_rows - rest :]
        out_ref[first : first + half, :] = jnp.concatenate([tail[:half], tail[half:]], axis=1)
        first += half
    for c in range(up_ref.shape[1] // lanes):
        out_ref[first : first + rank_part, :] = up_ref[:, c * lanes : (c + 1) * lanes]
        first += rank_part


def pack(down, up, rank_part, beside):
    rows = (down.size + rank_part * up.shape[1]) // lanes
    return pl.pallas_call(
        pack_kernel,
        out_shape=jax.ShapeDtypeStruct((rows, lanes), bf16),
        in_specs=[stays_in_hbm] * 2,
        out_specs=whole_in_vmem,
        scratch_shapes=[
            pltpu.VMEM(down.shape, bf16),
            pltpu.VMEM((rank_part, up.shape[1]), bf16),
            pltpu.SemaphoreType.DMA((2,)),
        ],
        compiler_params=pltpu.CompilerParams(vmem_limit_bytes=2 * 2**20),
        name="pack",
        cost_estimate=beside,
    )(*in_hbm(down, up))


def project_kernel(shards, replicas, *refs):
    owners_hbm, tokens_ref, weight_ref, _ = refs[:4]
    own_ref = refs[4]
    block_refs = refs[5 : 4 + shards]
    left_ref, pick_ref, owners_ref, token_buf, owner_sem = refs[4 + shards :]
    owners_copy = pltpu.make_async_copy(owners_hbm, owners_ref, owner_sem)
    owners_copy.start()

    shard = lax.axis_index("tensor")
    rows, own = own_ref.shape
    for i in range(shards):
        first = pl.multiple_of((shard ^ i) * own, lanes)
        block = jnp.dot(
            tokens_ref[...], weight_ref[:, pl.ds(first, own)], preferred_element_type=f32
        )
        if i == 0:
            own_ref[...] = block
        else:
            block_refs[i - 1][...] = block.astype(bf16)

    owners_copy.wait()
    replica = lax.axis_index("rollout")
    width = token_buf.shape[2]
    down_rows = tokens_ref.shape[1] // replicas
    for k in range(replicas):
        token_buf[k, :, :down_rows] = tokens_ref[:, k * down_rows : (k + 1) * down_rows]
        if down_rows < width:
            token_buf[k, :, down_rows:] = jnp.zeros((rows, width - down_rows), bf16)
    for i in range(replicas):
        place = jnp.int32(0)
        for k in range(1, replicas):
            place = place + jnp.where(owners_ref[k] == replica ^ i, k, 0)
        left_ref[:, i * width : (i + 1) * width] = token_buf[place]
    if replicas > 1:
        for i in range(shards):
            for k in range(replicas):
                picked = jnp.where(owners_ref[shard ^ i] == replica ^ k, 1.0, 0.0)
                row = i * replicas + k
                pick_ref[row : row + 1, :] = jnp.full((1, lanes), picked, f32)


def project(owners, tokens, weight, after, shards, replicas):
    rows, depth = tokens.shape
    own = weight.shape[1] // shards
    piece_width = -(-depth // replicas // lanes) * lanes
    mine, *rest = pl.pallas_call(
        functools.partial(project_kernel, shards, replicas),
        out_shape=[jax.ShapeDtypeStruct((rows, own), f32)]
        + [jax.ShapeDtypeStruct((rows, own), bf16)] * (shards - 1)
        + [
            jax.ShapeDtypeStruct((rows, replicas * piece_width), bf16),
            jax.ShapeDtypeStruct((shards * replicas, lanes), f32),
        ],
        in_specs=[stays_in_hbm] + [whole_in_vmem] * 3,
        out_specs=[whole_in_vmem] * (shards + 2),
        scratch_shapes=[
            pltpu.SMEM(owners.shape, jnp.int32),
            pltpu.VMEM((replicas, rows, piece_width), bf16),
            pltpu.SemaphoreType.DMA,
        ],
        compiler_params=pltpu.CompilerParams(vmem_limit_bytes=4 * 2**20),
        name="project",
        cost_estimate=pl.CostEstimate(
            flops=2 * rows * weight.size, bytes_accessed=2 * weight.size, transcendentals=0
        ),
    )(*in_hbm(owners), tokens, weight, after)
    return mine, rest[:-2], *rest[-2:]


def attend_kernel(
    step_count,
    head_count,
    lengths_hbm,
    queries_ref,
    keys_ref,
    values_ref,
    _,
    grouped_ref,
    total_ref,
    peak_ref,
    sum_ref,
    cosine_ref,
    sine_ref,
    lengths_ref,
    regroup,
    scores_ref,
    raised,
    length_sem,
):
    lengths_copy = pltpu.make_async_copy(lengths_hbm, lengths_ref, length_sem)
    lengths_copy.start()
    rows = cosine_ref.shape[0]

    row_count, slots, _ = keys_ref.shape
    group = queries_ref.shape[1] // (head_count * lanes)
    seen = step_count * group
    for pair in range(step_count // 2):
        for q in range(head_count * group):
            h, g = q // group, q % group
            both = queries_ref[
                pair * 2 * row_count : (pair + 1) * 2 * row_count, q * lanes : (q + 1) * lanes
            ].astype(f32)
            for side in range(2):
                first = h * row_count * seen + (pair * 2 + side) * group + g
                regroup[pl.ds(first, row_count, stride=seen), :] = both[
                    side * row_count : (side + 1) * row_count, :
                ]
            if g % 2:
                for side in range(2):
                    half = slice(side * row_count, (side + 1) * row_count)
                    last = (h * seen + (pair * 2 + side) * group + g + 1) * row_count
                    grouped_ref[last - 2 * row_count : last, :] = jnp.concatenate(
                        [before[half], both[half]], axis=0
                    ).astype(bf16)
            before = both

    for b in range(row_count):
        for h in range(head_count):
            at = (h * row_count + b) * seen
            scores_ref[at : at + seen, :] = lax.dot_general(
                regroup[at : at + seen, :].astype(bf16),
                keys_ref[b, :, h * lanes : (h + 1) * lanes],
                (((1,), (1,)), ((), ())),
                preferred_element_type=f32,
            )

    places = [
        (
            b,
            h,
            slice((h * row_count + b) * seen, (h * row_count + b + 1) * seen),
            pl.ds(h * row_count * seen + b, seen, stride=row_count),
        )
        for b in range(row_count)
        for h in range(head_count)
    ]
    lengths_copy.wait()
    slot = lax.broadcasted_iota(jnp.int32, (seen, slots), 1)
    for b, h, place, out in places:
        score = jnp.where(slot < lengths_ref[b], scores_ref[place, :], masked_score)
        peak = jnp.max(score, axis=1, keepdims=True)
        lifted = jnp.exp2((score - peak) * exponent_scale)
        raised[place, :] = lifted.astype(bf16)
        peak_ref[out, :] = jnp.broadcast_to(peak, (seen, lanes))
        sum_ref[out, :] = jnp.broadcast_to(
            jnp.sum(lifted, axis=1, keepdims=True), (seen, lanes)
        )
    for b, h, place, out in places:
        total_ref[out, :] = jnp.dot(
            raised[place, :],
            values_ref[b, :, h * lanes : (h + 1) * lanes],
            preferred_element_type=f32,
        )

    row = lax.broadcasted_iota(jnp.int32, (rows, lanes), 0)
    lane = lax.broadcasted_iota(jnp.int32, (rows, lanes), 1)
    position = row // row_count
    for b in range(row_count):
        position = position + jnp.where(row % row_count == b, lengths_ref[b], 0)
    middle = lanes // 2
    spacing = (lane % middle).astype(f32) * (-2.0 / lanes * math.log(rope_base))
    angles = position.astype(f32) * jnp.exp(spacing)
    cosine_ref[...] = jnp.cos(angles)
    sine = jnp.sin(angles)
    sine_ref[...] = jnp.where(lane < middle, -sine, sine)


def attend(lengths, queries, keys, values, after, step_count):
    row_count, slots, width = keys.shape
    rows = step_count * row_count
    seen_rows = rows * queries.shape[1] // lanes
    table = jax.ShapeDtypeStruct((rows, lanes), f32)
    seen_table = jax.ShapeDtypeStruct((seen_rows, lanes), f32)
    return pl.pallas_call(
        functools.partial(attend_kernel, step_count, width // lanes),
        out_shape=(
            jax.ShapeDtypeStruct((seen_rows, lanes), bf16),
            seen_table,
            seen_table,
            seen_table,
            table,
            table,
        ),
        in_specs=[stays_in_hbm] + [whole_in_vmem] * 4,
        out_specs=(whole_in_vmem,) * 6,
        scratch_shapes=[
            pltpu.SMEM(lengths.shape, jnp.int32),
            pltpu.VMEM((seen_rows, lanes), f32),
            pltpu.VMEM((seen_rows, slots), f32),
            pltpu.VMEM((seen_rows, slots), bf16),
            pltpu.SemaphoreType.DMA,
        ],
        compiler_params=pltpu.CompilerParams(vmem_limit_bytes=8 * 2**20),
        name="attend",
        cost_estimate=pl.CostEstimate(
            flops=4 * seen_rows * slots * lanes,
            bytes_accessed=2 * (keys.size + values.size),
            transcendentals=seen_rows * slots,
        ),
    )(*in_hbm(lengths), queries, keys, values, after)


def piece_places(replicas):
    order = [0, 1] + list(range(replicas - 1, 1, -1))
    return [order.index(i) for i in range(replicas)]


def route_kernel(replicas, shards, *refs):
    left_ref, pick_ref = refs[:2]
    piece_refs = [refs[2 + place] for place in piece_places(replicas)]
    out_refs = refs[2 + replicas : 2 + replicas + shards]
    (right,) = refs[2 + replicas + shards :]
    up_rows = out_refs[0].shape[0] - left_ref.shape[0]
    rows = left_ref.shape[0]
    rank = right.shape[0]
    width = right.shape[1] // replicas
    half = rank // 2
    rest = (piece_refs[0].shape[0] - up_rows) % rank
    for i in range(replicas):
        first = 0
        for c in range(width // lanes - (1 if rest else 0)):
            right[:, i * width + c * lanes : i * width + (c + 1) * lanes] = piece_refs[i][
                first : first + rank, :
            ]
            first += rank
        if rest:
            both = piece_refs[i][first : first + half, :]
            tail = jnp.concatenate([both[:, : lanes // 2], both[:, lanes // 2 :]], axis=0)
            right[:, (i + 1) * width - lanes : (i + 1) * width] = jnp.concatenate(
                [tail, jnp.zeros((rank, lanes // 2), bf16)], axis=1
            )
            first += half
    lowered = lax.dot_general(
        left_ref[...], right[...], (((1,), (1,)), ((), ())), preferred_element_type=f32
    )
    both = jnp.concatenate(split_halves(lowered), axis=1)
    ups = [piece[piece.shape[0] - up_rows :, :].astype(f32) for piece in piece_refs]
    for i in range(shards):
        out_refs[i][:rows, :] = both
        picked = sum(up * pick_ref[i * replicas + k, :][None, :] for k, up in enumerate(ups))
        out_refs[i][rows:, :] = picked.astype(bf16)


def route(left, pick, pieces, rank, up_rows, shards):
    rows, depth = left.shape
    replicas = len(pieces)
    return pl.pallas_call(
        functools.partial(route_kernel, replicas, shards),
        out_shape=[jax.ShapeDtypeStruct((rows + up_rows, lanes), bf16)] * shards,
        in_specs=[whole_in_vmem] * (2 + replicas),
        out_specs=[whole_in_vmem] * shards,
        scratch_shapes=[pltpu.VMEM((rank, depth), bf16)],
        compiler_params=pltpu.CompilerParams(vmem_limit_bytes=4 * 2**20),
        name="route",
        cost_estimate=pl.CostEstimate(flops=0, bytes_accessed=800000, transcendentals=0),
    )(left, pick, *[pieces[i] for i in piece_places(replicas)])


def route_plain(owners, tokens, down, up, rank_part, own, shards):
    rank = down.shape[1]
    shard = lax.axis_index("tensor")
    first = shard * rank_part
    up_part = lax.dynamic_slice_in_dim(up, first, rank_part, axis=0)
    downs = lax.all_gather(down, "rollout", axis=0, tiled=False)
    ups = lax.all_gather(up_part, "rollout", axis=0, tiled=False)
    down_matrix = jnp.take(downs, owners, axis=0, mode="clip").reshape(-1, rank)
    up_matrix = jnp.take(ups, owners, axis=0, mode="clip").transpose(1, 0, 2)
    up_matrix = up_matrix.reshape(rank_part, -1)
    lowered = jnp.dot(tokens, down_matrix, preferred_element_type=f32)
    both = jnp.concatenate(split_halves(lowered), axis=1)
    packets = []
    for i in range(shards):
        up_block = lax.dynamic_slice_in_dim(up_matrix, (shard ^ i) * own, own, axis=1)
        parts = [both, side_by_side(up_block)]
        packets.append(jnp.concatenate(parts, axis=0))
    return packets


def finish_kernel(step_count, row_count, head_count, shards, *refs):
    gain_ref, base_ref, grouped_ref, total_ref, peak_ref, sum_ref, cosine_ref, sine_ref = refs[:8]
    packet_refs = refs[8 : 8 + shards][::-1]
    sum_refs = refs[8 + shards : 7 + 2 * shards]
    attention_ref, keys_ref, values_ref = refs[7 + 2 * shards : 10 + 2 * shards]
    (up_buf,) = refs[10 + 2 * shards :]
    shard = lax.axis_index("tensor")
    rows = step_count * row_count
    own = base_ref.shape[1]
    blocks = own // lanes
    rank = up_buf.shape[0]
    rank_part = rank // shards
    group = grouped_ref.shape[0] // (head_count * rows)
    seen = step_count * group

    lowered = jnp.zeros((rows, lanes), f32)
    for i in range(shards):
        lowered = lowered + packet_refs[i][:rows, :].astype(f32)
        ups = packet_refs[i][rows:, :].astype(f32)
        at = pl.multiple_of((shard ^ i) * rank_part, rank_part)
        for c in range(blocks):
            up_buf[pl.ds(at, rank_part), c * lanes : (c + 1) * lanes] = ups[
                c * rank_part : (c + 1) * rank_part, :
            ]
    lane = lax.broadcasted_iota(jnp.int32, (rows, lanes), 1)
    lowered = lowered + pltpu.roll(lowered, rank, 1)
    high, low = split_halves(lowered)
    left = jnp.where(lane < rank, high.astype(f32), low.astype(f32)).astype(bf16)
    up = up_buf[...].astype(bf16)
    raised_up = jnp.dot(left, jnp.concatenate([up, up], axis=0), preferred_element_type=f32)
    joined = []
    for c in range(blocks):
        block = base_ref[:, c * lanes : (c + 1) * lanes]
        for partial_ref in sum_refs:
            block = block + partial_ref[:, c * lanes : (c + 1) * lanes].astype(f32)
        joined.append(block + adapter_scale * raised_up[:, c * lanes : (c + 1) * lanes])

    all_rows = row_count * seen
    seen_by = lax.broadcasted_iota(jnp.int32, (all_rows, rows), 0)
    made_by = lax.broadcasted_iota(jnp.int32, (all_rows, rows), 1)
    visible = (seen_by % row_count == made_by % row_count) & (
        made_by // row_count <= seen_by // (row_count * group)
    )
    heads = [(h, slice(h * all_rows, (h + 1) * all_rows)) for h in range(head_count)]
    keys, values, scores, results = [], [], [], []
    for h, _ in heads:
        raw_key = joined[2 * h]
        mean_square = jnp.mean(raw_key * raw_key, axis=1, keepdims=True)
        normed = raw_key * lax.rsqrt(mean_square + norm_eps) * gain_ref[...]
        key = normed * cosine_ref[...] + pltpu.roll(normed, lanes // 2, 1) * sine_ref[...]
        keys.append(key.astype(bf16))
        values.append(joined[2 * h + 1].astype(bf16))
        keys_ref[:, h * lanes : (h + 1) * lanes] = keys[h]
        values_ref[:, h * lanes : (h + 1) * lanes] = values[h]
    for h, mine in heads:
        score = lax.dot_general(
            grouped_ref[mine, :], keys[h], (((1,), (1,)), ((), ())), preferred_element_type=f32
        )
        scores.append(jnp.where(visible, score, masked_score))
    for h, mine in heads:
        old_peak = peak_ref[mine, :]
        peak = jnp.maximum(old_peak, jnp.max(scores[h], axis=1, keepdims=True))
        fade = jnp.exp2((old_peak - peak) * exponent_scale)
        lifted = jnp.exp2((scores[h] - peak[:, :rows]) * exponent_scale)
        denominator = fade * sum_ref[mine, :] + jnp.sum(lifted, axis=1, keepdims=True)
        total = fade * total_ref[mine, :] + jnp.dot(
            lifted.astype(bf16), values[h], preferred_element_type=f32
        )
        results.append(total / denominator)
    for pair in range(step_count // 2):
        for q in range(head_count * group):
            h, g = q // group, q % group
            both = []
            for side in range(2):
                first = ((pair * 2 + side) * group + g) * row_count
                both.append(results[h][first : first + row_count])
            attention_ref[
                pair * 2 * row_count : (pair + 1) * 2 * row_count, q * lanes : (q + 1) * lanes
            ] = jnp.concatenate(both, axis=0).astype(bf16)


def finish(mine, others, partials, gain, packets, rank, step_count, row_count, query_width):
    rows, own = mine.shape
    shards = len(packets)
    head_count = own // (2 * lanes)
    return pl.pallas_call(
        functools.partial(finish_kernel, step_count, row_count, head_count, shards),
        out_shape=(
            jax.ShapeDtypeStruct((rows, query_width), bf16),
            jax.ShapeDtypeStruct((rows, head_count * lanes), bf16),
            jax.ShapeDtypeStruct((rows, head_count * lanes), bf16),
        ),
        in_specs=[whole_in_vmem] * (7 + 2 * shards),
        out_specs=(whole_in_vmem,) * 3,
        scratch_shapes=[
            pltpu.VMEM((rank, own), f32),
        ],
        compiler_params=pltpu.CompilerParams(vmem_limit_bytes=6 * 2**20),
        name="finish",
        cost_estimate=pl.CostEstimate(flops=0, bytes_accessed=1000000, transcendentals=0),
    )(gain, mine, *partials, *packets[::-1], *others)


def per_device(
    normed_tokens,
    key_value_weight,
    adapter_down,
    adapter_up,
    key_gain,
    queries,
    cache_keys,
    stored_values,
    lengths,
    owners,
):
    replicas = lax.axis_size("rollout")
    shards = lax.axis_size("tensor")
    down_rows, rank = adapter_down.shape
    step_count, row_count, depth = normed_tokens.shape
    own = key_value_weight.shape[1] // shards
    rank_part = rank // shards
    rows = step_count * row_count
    tokens = normed_tokens.reshape(rows, depth)
    query_rows = queries.reshape(rows, -1)

    fits = (
        replicas <= 4
        and adapter_up.shape[1] == own
        and down_rows % lanes in (0, lanes // 2)
        and rank == lanes // 2
        and rank_part % 16 == 0
    )
    if fits:
        fetched = 2 * (key_value_weight.size + cache_keys.size + stored_values.size)
        beside = pl.CostEstimate(flops=1000 * fetched, bytes_accessed=fetched, transcendentals=0)
        packed = pack(adapter_down.T, adapter_up, rank_part, beside)
        pieces = [packed] + [swap(packed, "rollout", i) for i in range(1, replicas)]
    mine, blocks, left, pick = project(
        owners,
        tokens,
        key_value_weight,
        packed if fits else adapter_up,
        shards,
        replicas if fits else 1,
    )
    others = [swap(block, "tensor", i + 1) for i, block in enumerate(blocks)]
    if fits:
        packets = route(left, pick, pieces, rank, rank_part * own // lanes, shards)
    else:
        packets = route_plain(
            owners, tokens, adapter_down, adapter_up, rank_part, own, shards
        )
    partials = attend(lengths, query_rows, cache_keys, stored_values, packets[0], step_count)
    packets = [packets[0]] + [swap(packets[i], "tensor", i) for i in range(1, shards)]
    attention, keys, values = finish(
        mine,
        others,
        partials,
        key_gain.reshape(1, -1),
        packets,
        rank,
        step_count,
        row_count,
        query_rows.shape[1],
    )
    return tuple(a.reshape(step_count, row_count, -1) for a in (attention, keys, values))


def solution(mesh):
    placed = (
        P(None, ("job", "rollout"), "tensor"),
        P("tensor", None),
        P(("job", "rollout", "tensor"), None),
        P(None, ("job", "rollout")),
        P(),
        P(None, ("job", "rollout"), "tensor"),
        P(("job", "rollout"), None, "tensor"),
        P(("job", "rollout"), None, "tensor"),
        P(("job", "rollout")),
        P("job"),
    )
    return jax.shard_map(
        per_device,
        mesh=mesh,
        in_specs=placed,
        out_specs=(
            P(None, ("job", "rollout"), "tensor"),
            P(None, ("job", "rollout"), "tensor"),
            P(None, ("job", "rollout"), "tensor"),
        ),
        check_vma=False,
    )
```

```python
import functools
import math

import jax
import jax.numpy as jnp
from jax import lax
from jax.experimental import pallas as pl
from jax.experimental.pallas import tpu as pltpu
from jax.sharding import PartitionSpec as P

norm_eps = 1e-06
rope_base = 1000000.0
adapter_scale = 2.0
masked_score = -1e30
lanes = 128
exponent_scale = lanes**-0.5 / math.log(2.0)
f32 = jnp.float32
bf16 = jnp.bfloat16

whole_in_vmem = pl.BlockSpec(memory_space=pltpu.VMEM)
whole_in_smem = pl.BlockSpec(memory_space=pltpu.SMEM)
stays_in_hbm = pl.BlockSpec(memory_space=pltpu.HBM)


def swap(block, axis, offset):
    count = lax.axis_size(axis)
    return lax.ppermute(block, axis, [(s, s ^ offset) for s in range(count)])


def shift(block, axis, offset):
    count = lax.axis_size(axis)
    return lax.ppermute(block, axis, [((s + offset) % count, s) for s in range(count)])


def in_hbm(*arrays):
    return tuple(pltpu.with_memory_space_constraint(a, pltpu.HBM) for a in arrays)


def side_by_side(rows_of_blocks):
    r, c = rows_of_blocks.shape
    return rows_of_blocks.reshape(r, c // lanes, lanes).transpose(1, 0, 2).reshape(-1, lanes)


def split_halves(total):
    high = total.astype(bf16)
    return high, (total - high.astype(f32)).astype(bf16)


def pack_kernel(down_hbm, up_hbm, out_ref, down_ref, up_ref, sems):
    rank, down_rows = down_ref.shape
    rank_part = up_ref.shape[0]
    start = pl.multiple_of(lax.axis_index("tensor") * rank_part, rank_part)
    copies = [
        pltpu.make_async_copy(down_hbm, down_ref, sems.at[0]),
        pltpu.make_async_copy(up_hbm.at[pl.ds(start, rank_part), :], up_ref, sems.at[1]),
    ]
    for copy in copies:
        copy.start(priority=1)
    for copy in copies:
        copy.wait()
    first = 0
    for c in range(down_rows // lanes):
        out_ref[first : first + rank, :] = down_ref[:, c * lanes : (c + 1) * lanes]
        first += rank
    rest = down_rows % lanes
    if rest:
        half = rank // 2
        tail = down_ref[:, down_rows - rest :]
        out_ref[first : first + half, :] = jnp.concatenate([tail[:half], tail[half:]], axis=1)
        first += half
    for c in range(up_ref.shape[1] // lanes):
        out_ref[first : first + rank_part, :] = up_ref[:, c * lanes : (c + 1) * lanes]
        first += rank_part


def pack(down, up, rank_part, beside):
    rows = (down.size + rank_part * up.shape[1]) // lanes
    return pl.pallas_call(
        pack_kernel,
        out_shape=jax.ShapeDtypeStruct((rows, lanes), bf16),
        in_specs=[stays_in_hbm] * 2,
        out_specs=whole_in_vmem,
        scratch_shapes=[
            pltpu.VMEM(down.shape, bf16),
            pltpu.VMEM((rank_part, up.shape[1]), bf16),
            pltpu.SemaphoreType.DMA((2,)),
        ],
        compiler_params=pltpu.CompilerParams(vmem_limit_bytes=2 * 2**20),
        name="pack",
        cost_estimate=beside,
    )(*in_hbm(down, up))


def project_kernel(shards, replicas, *refs):
    owners_hbm, tokens_ref, weight_ref, _ = refs[:4]
    own_ref = refs[4]
    block_refs = refs[5 : 4 + shards]
    left_ref, pick_ref, owners_ref, token_buf, owner_sem = refs[4 + shards :]
    owners_copy = pltpu.make_async_copy(owners_hbm, owners_ref, owner_sem)
    owners_copy.start()

    shard = lax.axis_index("tensor")
    rows, own = own_ref.shape
    for i in range(shards):
        first = pl.multiple_of((shard ^ i) * own, lanes)
        block = jnp.dot(
            tokens_ref[...], weight_ref[:, pl.ds(first, own)], preferred_element_type=f32
        )
        if i == 0:
            own_ref[...] = block
        else:
            block_refs[i - 1][...] = block.astype(bf16)

    owners_copy.wait()
    replica = lax.axis_index("rollout")
    width = token_buf.shape[2]
    down_rows = tokens_ref.shape[1] // replicas
    for k in range(replicas):
        token_buf[k, :, :down_rows] = tokens_ref[:, k * down_rows : (k + 1) * down_rows]
        if down_rows < width:
            token_buf[k, :, down_rows:] = jnp.zeros((rows, width - down_rows), bf16)
    for i in range(replicas):
        place = jnp.int32(0)
        for k in range(1, replicas):
            place = place + jnp.where(owners_ref[k] == lax.rem(replica + i, replicas), k, 0)
        left_ref[:, i * width : (i + 1) * width] = token_buf[place]
    if replicas > 1:
        for i in range(shards):
            for k in range(replicas):
                source = lax.rem(replica + k, replicas)
                picked = jnp.where(owners_ref[shard ^ i] == source, 1.0, 0.0)
                row = i * replicas + k
                pick_ref[row : row + 1, :] = jnp.full((1, lanes), picked, f32)


def project(owners, tokens, weight, after, shards, replicas):
    rows, depth = tokens.shape
    own = weight.shape[1] // shards
    piece_width = -(-depth // replicas // lanes) * lanes
    mine, *rest = pl.pallas_call(
        functools.partial(project_kernel, shards, replicas),
        out_shape=[jax.ShapeDtypeStruct((rows, own), f32)]
        + [jax.ShapeDtypeStruct((rows, own), bf16)] * (shards - 1)
        + [
            jax.ShapeDtypeStruct((rows, replicas * piece_width), bf16),
            jax.ShapeDtypeStruct((shards * replicas, lanes), f32),
        ],
        in_specs=[stays_in_hbm] + [whole_in_vmem] * 3,
        out_specs=[whole_in_vmem] * (shards + 2),
        scratch_shapes=[
            pltpu.SMEM(owners.shape, jnp.int32),
            pltpu.VMEM((replicas, rows, piece_width), bf16),
            pltpu.SemaphoreType.DMA,
        ],
        compiler_params=pltpu.CompilerParams(vmem_limit_bytes=4 * 2**20),
        name="project",
        cost_estimate=pl.CostEstimate(
            flops=2 * rows * weight.size, bytes_accessed=2 * weight.size, transcendentals=0
        ),
    )(*in_hbm(owners), tokens, weight, after)
    return mine, rest[:-2], *rest[-2:]


def attend_kernel(
    step_count,
    head_count,
    lengths_hbm,
    queries_ref,
    keys_ref,
    values_ref,
    _,
    grouped_ref,
    total_ref,
    peak_ref,
    sum_ref,
    cosine_ref,
    sine_ref,
    lengths_ref,
    regroup,
    scores_ref,
    raised,
    length_sem,
):
    lengths_copy = pltpu.make_async_copy(lengths_hbm, lengths_ref, length_sem)
    lengths_copy.start()
    rows = cosine_ref.shape[0]

    row_count, slots, _ = keys_ref.shape
    group = queries_ref.shape[1] // (head_count * lanes)
    seen = step_count * group
    for pair in range(step_count // 2):
        for q in range(head_count * group):
            h, g = q // group, q % group
            both = queries_ref[
                pair * 2 * row_count : (pair + 1) * 2 * row_count, q * lanes : (q + 1) * lanes
            ].astype(f32)
            for side in range(2):
                first = h * row_count * seen + (pair * 2 + side) * group + g
                regroup[pl.ds(first, row_count, stride=seen), :] = both[
                    side * row_count : (side + 1) * row_count, :
                ]
            if g % 2:
                for side in range(2):
                    half = slice(side * row_count, (side + 1) * row_count)
                    last = (h * seen + (pair * 2 + side) * group + g + 1) * row_count
                    grouped_ref[last - 2 * row_count : last, :] = jnp.concatenate(
                        [before[half], both[half]], axis=0
                    ).astype(bf16)
            before = both

    for b in range(row_count):
        for h in range(head_count):
            at = (h * row_count + b) * seen
            scores_ref[at : at + seen, :] = lax.dot_general(
                regroup[at : at + seen, :].astype(bf16),
                keys_ref[b, :, h * lanes : (h + 1) * lanes],
                (((1,), (1,)), ((), ())),
                preferred_element_type=f32,
            )

    places = [
        (
            b,
            h,
            slice((h * row_count + b) * seen, (h * row_count + b + 1) * seen),
            pl.ds(h * row_count * seen + b, seen, stride=row_count),
        )
        for b in range(row_count)
        for h in range(head_count)
    ]
    lengths_copy.wait()
    slot = lax.broadcasted_iota(jnp.int32, (seen, slots), 1)
    for b, h, place, out in places:
        score = jnp.where(slot < lengths_ref[b], scores_ref[place, :], masked_score)
        peak = jnp.max(score, axis=1, keepdims=True)
        lifted = jnp.exp2((score - peak) * exponent_scale)
        raised[place, :] = lifted.astype(bf16)
        peak_ref[out, :] = jnp.broadcast_to(peak, (seen, lanes))
        sum_ref[out, :] = jnp.broadcast_to(
            jnp.sum(lifted, axis=1, keepdims=True), (seen, lanes)
        )
    for b, h, place, out in places:
        total_ref[out, :] = jnp.dot(
            raised[place, :],
            values_ref[b, :, h * lanes : (h + 1) * lanes],
            preferred_element_type=f32,
        )

    row = lax.broadcasted_iota(jnp.int32, (rows, lanes), 0)
    lane = lax.broadcasted_iota(jnp.int32, (rows, lanes), 1)
    position = row // row_count
    for b in range(row_count):
        position = position + jnp.where(row % row_count == b, lengths_ref[b], 0)
    middle = lanes // 2
    spacing = (lane % middle).astype(f32) * (-2.0 / lanes * math.log(rope_base))
    angles = position.astype(f32) * jnp.exp(spacing)
    cosine_ref[...] = jnp.cos(angles)
    sine = jnp.sin(angles)
    sine_ref[...] = jnp.where(lane < middle, -sine, sine)


def attend(lengths, queries, keys, values, after, step_count):
    row_count, slots, width = keys.shape
    rows = step_count * row_count
    seen_rows = rows * queries.shape[1] // lanes
    table = jax.ShapeDtypeStruct((rows, lanes), f32)
    seen_table = jax.ShapeDtypeStruct((seen_rows, lanes), f32)
    return pl.pallas_call(
        functools.partial(attend_kernel, step_count, width // lanes),
        out_shape=(
            jax.ShapeDtypeStruct((seen_rows, lanes), bf16),
            seen_table,
            seen_table,
            seen_table,
            table,
            table,
        ),
        in_specs=[stays_in_hbm] + [whole_in_vmem] * 4,
        out_specs=(whole_in_vmem,) * 6,
        scratch_shapes=[
            pltpu.SMEM(lengths.shape, jnp.int32),
            pltpu.VMEM((seen_rows, lanes), f32),
            pltpu.VMEM((seen_rows, slots), f32),
            pltpu.VMEM((seen_rows, slots), bf16),
            pltpu.SemaphoreType.DMA,
        ],
        compiler_params=pltpu.CompilerParams(vmem_limit_bytes=8 * 2**20),
        name="attend",
        cost_estimate=pl.CostEstimate(
            flops=4 * seen_rows * slots * lanes,
            bytes_accessed=2 * (keys.size + values.size),
            transcendentals=seen_rows * slots,
        ),
    )(*in_hbm(lengths), queries, keys, values, after)


def piece_places(replicas):
    order = [0, 1] + list(range(replicas - 1, 1, -1))
    return [order.index(i) for i in range(replicas)]


def route_kernel(replicas, shards, *refs):
    left_ref, pick_ref = refs[:2]
    piece_refs = [refs[2 + place] for place in piece_places(replicas)]
    out_refs = refs[2 + replicas : 2 + replicas + shards]
    (right,) = refs[2 + replicas + shards :]
    up_rows = out_refs[0].shape[0] - left_ref.shape[0]
    rows = left_ref.shape[0]
    rank = right.shape[0]
    width = right.shape[1] // replicas
    half = rank // 2
    rest = (piece_refs[0].shape[0] - up_rows) % rank
    for i in range(replicas):
        first = 0
        for c in range(width // lanes - (1 if rest else 0)):
            right[:, i * width + c * lanes : i * width + (c + 1) * lanes] = piece_refs[i][
                first : first + rank, :
            ]
            first += rank
        if rest:
            both = piece_refs[i][first : first + half, :]
            tail = jnp.concatenate([both[:, : lanes // 2], both[:, lanes // 2 :]], axis=0)
            right[:, (i + 1) * width - lanes : (i + 1) * width] = jnp.concatenate(
                [tail, jnp.zeros((rank, lanes // 2), bf16)], axis=1
            )
            first += half
    lowered = lax.dot_general(
        left_ref[...], right[...], (((1,), (1,)), ((), ())), preferred_element_type=f32
    )
    both = jnp.concatenate(split_halves(lowered), axis=1)
    ups = [piece[piece.shape[0] - up_rows :, :].astype(f32) for piece in piece_refs]
    for i in range(shards):
        out_refs[i][:rows, :] = both
        picked = sum(up * pick_ref[i * replicas + k, :][None, :] for k, up in enumerate(ups))
        out_refs[i][rows:, :] = picked.astype(bf16)


def route(left, pick, pieces, rank, up_rows, shards):
    rows, depth = left.shape
    replicas = len(pieces)
    return pl.pallas_call(
        functools.partial(route_kernel, replicas, shards),
        out_shape=[jax.ShapeDtypeStruct((rows + up_rows, lanes), bf16)] * shards,
        in_specs=[whole_in_vmem] * (2 + replicas),
        out_specs=[whole_in_vmem] * shards,
        scratch_shapes=[pltpu.VMEM((rank, depth), bf16)],
        compiler_params=pltpu.CompilerParams(vmem_limit_bytes=4 * 2**20),
        name="route",
        cost_estimate=pl.CostEstimate(flops=0, bytes_accessed=800000, transcendentals=0),
    )(left, pick, *[pieces[i] for i in piece_places(replicas)])


def route_plain(owners, tokens, down, up, rank_part, own, shards):
    rank = down.shape[1]
    shard = lax.axis_index("tensor")
    first = shard * rank_part
    up_part = lax.dynamic_slice_in_dim(up, first, rank_part, axis=0)
    downs = lax.all_gather(down, "rollout", axis=0, tiled=False)
    ups = lax.all_gather(up_part, "rollout", axis=0, tiled=False)
    down_matrix = jnp.take(downs, owners, axis=0, mode="clip").reshape(-1, rank)
    up_matrix = jnp.take(ups, owners, axis=0, mode="clip").transpose(1, 0, 2)
    up_matrix = up_matrix.reshape(rank_part, -1)
    lowered = jnp.dot(tokens, down_matrix, preferred_element_type=f32)
    both = jnp.concatenate(split_halves(lowered), axis=1)
    packets = []
    for i in range(shards):
        up_block = lax.dynamic_slice_in_dim(up_matrix, (shard ^ i) * own, own, axis=1)
        parts = [both, side_by_side(up_block)]
        packets.append(jnp.concatenate(parts, axis=0))
    return packets


def finish_kernel(step_count, row_count, head_count, shards, *refs):
    gain_ref, base_ref, grouped_ref, total_ref, peak_ref, sum_ref, cosine_ref, sine_ref = refs[:8]
    packet_refs = refs[8 : 8 + shards][::-1]
    sum_refs = refs[8 + shards : 7 + 2 * shards]
    attention_ref, keys_ref, values_ref = refs[7 + 2 * shards : 10 + 2 * shards]
    (up_buf,) = refs[10 + 2 * shards :]
    shard = lax.axis_index("tensor")
    rows = step_count * row_count
    own = base_ref.shape[1]
    blocks = own // lanes
    rank = up_buf.shape[0]
    rank_part = rank // shards
    group = grouped_ref.shape[0] // (head_count * rows)
    seen = step_count * group

    lowered = jnp.zeros((rows, lanes), f32)
    for i in range(shards):
        lowered = lowered + packet_refs[i][:rows, :].astype(f32)
        ups = packet_refs[i][rows:, :].astype(f32)
        at = pl.multiple_of((shard ^ i) * rank_part, rank_part)
        for c in range(blocks):
            up_buf[pl.ds(at, rank_part), c * lanes : (c + 1) * lanes] = ups[
                c * rank_part : (c + 1) * rank_part, :
            ]
    lane = lax.broadcasted_iota(jnp.int32, (rows, lanes), 1)
    lowered = lowered + pltpu.roll(lowered, rank, 1)
    high, low = split_halves(lowered)
    left = jnp.where(lane < rank, high.astype(f32), low.astype(f32)).astype(bf16)
    up = up_buf[...].astype(bf16)
    raised_up = jnp.dot(left, jnp.concatenate([up, up], axis=0), preferred_element_type=f32)
    joined = []
    for c in range(blocks):
        block = base_ref[:, c * lanes : (c + 1) * lanes]
        for partial_ref in sum_refs:
            block = block + partial_ref[:, c * lanes : (c + 1) * lanes].astype(f32)
        joined.append(block + adapter_scale * raised_up[:, c * lanes : (c + 1) * lanes])

    all_rows = row_count * seen
    seen_by = lax.broadcasted_iota(jnp.int32, (all_rows, rows), 0)
    made_by = lax.broadcasted_iota(jnp.int32, (all_rows, rows), 1)
    visible = (seen_by % row_count == made_by % row_count) & (
        made_by // row_count <= seen_by // (row_count * group)
    )
    heads = [(h, slice(h * all_rows, (h + 1) * all_rows)) for h in range(head_count)]
    keys, values, scores, results = [], [], [], []
    for h, _ in heads:
        raw_key = joined[2 * h]
        mean_square = jnp.mean(raw_key * raw_key, axis=1, keepdims=True)
        normed = raw_key * lax.rsqrt(mean_square + norm_eps) * gain_ref[...]
        key = normed * cosine_ref[...] + pltpu.roll(normed, lanes // 2, 1) * sine_ref[...]
        keys.append(key.astype(bf16))
        values.append(joined[2 * h + 1].astype(bf16))
        keys_ref[:, h * lanes : (h + 1) * lanes] = keys[h]
        values_ref[:, h * lanes : (h + 1) * lanes] = values[h]
    for h, mine in heads:
        score = lax.dot_general(
            grouped_ref[mine, :], keys[h], (((1,), (1,)), ((), ())), preferred_element_type=f32
        )
        scores.append(jnp.where(visible, score, masked_score))
    for h, mine in heads:
        old_peak = peak_ref[mine, :]
        peak = jnp.maximum(old_peak, jnp.max(scores[h], axis=1, keepdims=True))
        fade = jnp.exp2((old_peak - peak) * exponent_scale)
        lifted = jnp.exp2((scores[h] - peak[:, :rows]) * exponent_scale)
        denominator = fade * sum_ref[mine, :] + jnp.sum(lifted, axis=1, keepdims=True)
        total = fade * total_ref[mine, :] + jnp.dot(
            lifted.astype(bf16), values[h], preferred_element_type=f32
        )
        results.append(total / denominator)
    for pair in range(step_count // 2):
        for q in range(head_count * group):
            h, g = q // group, q % group
            both = []
            for side in range(2):
                first = ((pair * 2 + side) * group + g) * row_count
                both.append(results[h][first : first + row_count])
            attention_ref[
                pair * 2 * row_count : (pair + 1) * 2 * row_count, q * lanes : (q + 1) * lanes
            ] = jnp.concatenate(both, axis=0).astype(bf16)


def finish(mine, others, partials, gain, packets, rank, step_count, row_count, query_width):
    rows, own = mine.shape
    shards = len(packets)
    head_count = own // (2 * lanes)
    return pl.pallas_call(
        functools.partial(finish_kernel, step_count, row_count, head_count, shards),
        out_shape=(
            jax.ShapeDtypeStruct((rows, query_width), bf16),
            jax.ShapeDtypeStruct((rows, head_count * lanes), bf16),
            jax.ShapeDtypeStruct((rows, head_count * lanes), bf16),
        ),
        in_specs=[whole_in_vmem] * (7 + 2 * shards),
        out_specs=(whole_in_vmem,) * 3,
        scratch_shapes=[
            pltpu.VMEM((rank, own), f32),
        ],
        compiler_params=pltpu.CompilerParams(vmem_limit_bytes=6 * 2**20),
        name="finish",
        cost_estimate=pl.CostEstimate(flops=0, bytes_accessed=1000000, transcendentals=0),
    )(gain, mine, *partials, *packets[::-1], *others)


def per_device(
    normed_tokens,
    key_value_weight,
    adapter_down,
    adapter_up,
    key_gain,
    queries,
    cache_keys,
    stored_values,
    lengths,
    owners,
):
    replicas = lax.axis_size("rollout")
    shards = lax.axis_size("tensor")
    down_rows, rank = adapter_down.shape
    step_count, row_count, depth = normed_tokens.shape
    own = key_value_weight.shape[1] // shards
    rank_part = rank // shards
    rows = step_count * row_count
    tokens = normed_tokens.reshape(rows, depth)
    query_rows = queries.reshape(rows, -1)

    fits = (
        replicas <= 4
        and adapter_up.shape[1] == own
        and down_rows % lanes in (0, lanes // 2)
        and rank == lanes // 2
        and rank_part % 16 == 0
    )
    if fits:
        fetched = 2 * (key_value_weight.size + cache_keys.size + stored_values.size)
        beside = pl.CostEstimate(flops=1000 * fetched, bytes_accessed=fetched, transcendentals=0)
        packed = pack(adapter_down.T, adapter_up, rank_part, beside)
        pieces = [packed] + [shift(packed, "rollout", i) for i in range(1, replicas)]
    mine, blocks, left, pick = project(
        owners,
        tokens,
        key_value_weight,
        packed if fits else adapter_up,
        shards,
        replicas if fits else 1,
    )
    others = [swap(block, "tensor", i + 1) for i, block in enumerate(blocks)]
    if fits:
        packets = route(left, pick, pieces, rank, rank_part * own // lanes, shards)
    else:
        packets = route_plain(
            owners, tokens, adapter_down, adapter_up, rank_part, own, shards
        )
    partials = attend(lengths, query_rows, cache_keys, stored_values, packets[0], step_count)
    packets = [packets[0]] + [swap(packets[i], "tensor", i) for i in range(1, shards)]
    attention, keys, values = finish(
        mine,
        others,
        partials,
        key_gain.reshape(1, -1),
        packets,
        rank,
        step_count,
        row_count,
        query_rows.shape[1],
    )
    return tuple(a.reshape(step_count, row_count, -1) for a in (attention, keys, values))


def solution(mesh):
    placed = (
        P(None, ("job", "rollout"), "tensor"),
        P("tensor", None),
        P(("job", "rollout", "tensor"), None),
        P(None, ("job", "rollout")),
        P(),
        P(None, ("job", "rollout"), "tensor"),
        P(("job", "rollout"), None, "tensor"),
        P(("job", "rollout"), None, "tensor"),
        P(("job", "rollout")),
        P("job"),
    )
    return jax.shard_map(
        per_device,
        mesh=mesh,
        in_specs=placed,
        out_specs=(
            P(None, ("job", "rollout"), "tensor"),
            P(None, ("job", "rollout"), "tensor"),
            P(None, ("job", "rollout"), "tensor"),
        ),
        check_vma=False,
    )
```

```python
import functools
import math

import jax
import jax.numpy as jnp
from jax import lax
from jax.experimental import pallas as pl
from jax.experimental.pallas import tpu as pltpu
from jax.sharding import PartitionSpec as P

norm_eps = 1e-06
rope_base = 1000000.0
adapter_scale = 2.0
masked_score = -1e30
lanes = 128
exponent_scale = lanes**-0.5 / math.log(2.0)
f32 = jnp.float32
bf16 = jnp.bfloat16

whole_in_vmem = pl.BlockSpec(memory_space=pltpu.VMEM)
whole_in_smem = pl.BlockSpec(memory_space=pltpu.SMEM)
stays_in_hbm = pl.BlockSpec(memory_space=pltpu.HBM)


def swap(block, axis, offset):
    count = lax.axis_size(axis)
    return lax.ppermute(block, axis, [(s, s ^ offset) for s in range(count)])


def in_hbm(*arrays):
    return tuple(pltpu.with_memory_space_constraint(a, pltpu.HBM) for a in arrays)


def side_by_side(rows_of_blocks):
    r, c = rows_of_blocks.shape
    return rows_of_blocks.reshape(r, c // lanes, lanes).transpose(1, 0, 2).reshape(-1, lanes)


def split_halves(total):
    high = total.astype(bf16)
    return high, (total - high.astype(f32)).astype(bf16)


def frequencies_kernel(out_ref):
    lane = lax.broadcasted_iota(jnp.int32, out_ref.shape, 1)
    spacing = (lane % (lanes // 2)).astype(f32) * (-2.0 / lanes * math.log(rope_base))
    out_ref[...] = jnp.exp(spacing)


def frequencies(beside):
    return pl.pallas_call(
        frequencies_kernel,
        out_shape=jax.ShapeDtypeStruct((8, lanes), f32),
        out_specs=whole_in_vmem,
        compiler_params=pltpu.CompilerParams(vmem_limit_bytes=2**20),
        name="frequencies",
        cost_estimate=beside,
    )()


def pack_kernel(down_ref, up_all_ref, _, out_ref):
    rank, down_rows = down_ref.shape
    rank_part = (out_ref.shape[0] * lanes - down_ref.size) // up_all_ref.shape[1]
    start = pl.multiple_of(lax.axis_index("tensor") * rank_part, rank_part)
    up_ref = up_all_ref.at[pl.ds(start, rank_part), :]
    first = 0
    for c in range(down_rows // lanes):
        out_ref[first : first + rank, :] = down_ref[:, c * lanes : (c + 1) * lanes]
        first += rank
    rest = down_rows % lanes
    if rest:
        half = rank // 2
        tail = down_ref[:, down_rows - rest :]
        out_ref[first : first + half, :] = jnp.concatenate([tail[:half], tail[half:]], axis=1)
        first += half
    for c in range(up_ref.shape[1] // lanes):
        out_ref[first : first + rank_part, :] = up_ref[:, c * lanes : (c + 1) * lanes]
        first += rank_part


def pack(down, up, rank_part, after):
    rows = (down.size + rank_part * up.shape[1]) // lanes
    return pl.pallas_call(
        pack_kernel,
        out_shape=jax.ShapeDtypeStruct((rows, lanes), bf16),
        in_specs=[whole_in_vmem] * 3,
        out_specs=whole_in_vmem,
        compiler_params=pltpu.CompilerParams(vmem_limit_bytes=2 * 2**20),
        name="pack",
        cost_estimate=pl.CostEstimate(flops=0, bytes_accessed=200000, transcendentals=0),
    )(down, up, after)


def project_kernel(step_count, row_count, head_count, shards, replicas, *refs):
    owners_hbm, lengths_hbm, tokens_ref, weight_ref, queries_ref, turns_ref, _ = refs[:7]
    own_ref = refs[7]
    block_refs = refs[8 : 7 + shards]
    left_ref, pick_ref, asked_ref, grouped_ref, cosine_ref, sine_ref, bias_ref = refs[
        7 + shards : 14 + shards
    ]
    owners_ref, lengths_ref, token_buf, regroup, sems = refs[14 + shards :]
    owners_copy = pltpu.make_async_copy(owners_hbm, owners_ref, sems.at[0])
    lengths_copy = pltpu.make_async_copy(lengths_hbm, lengths_ref, sems.at[1])
    owners_copy.start()
    lengths_copy.start()

    shard = lax.axis_index("tensor")
    rows, own = own_ref.shape
    for i in range(shards):
        first = pl.multiple_of((shard ^ i) * own, lanes)
        block = jnp.dot(
            tokens_ref[...], weight_ref[:, pl.ds(first, own)], preferred_element_type=f32
        )
        if i == 0:
            own_ref[...] = block
        else:
            block_refs[i - 1][...] = block.astype(bf16)

    group = queries_ref.shape[1] // (head_count * lanes)
    seen = step_count * group
    for pair in range(step_count // 2):
        for q in range(head_count * group):
            h, g = q // group, q % group
            both = queries_ref[
                pair * 2 * row_count : (pair + 1) * 2 * row_count, q * lanes : (q + 1) * lanes
            ].astype(f32)
            for side in range(2):
                first = h * row_count * seen + (pair * 2 + side) * group + g
                regroup[pl.ds(first, row_count, stride=seen), :] = both[
                    side * row_count : (side + 1) * row_count, :
                ]
            if g % 2:
                for side in range(2):
                    half = slice(side * row_count, (side + 1) * row_count)
                    last = (h * seen + (pair * 2 + side) * group + g + 1) * row_count
                    grouped_ref[last - 2 * row_count : last, :] = jnp.concatenate(
                        [before[half], both[half]], axis=0
                    ).astype(bf16)
            before = both
    asked_ref[...] = regroup[...].astype(bf16)

    owners_copy.wait()
    replica = lax.axis_index("rollout")
    width = token_buf.shape[2]
    down_rows = tokens_ref.shape[1] // replicas
    for k in range(replicas):
        token_buf[k, :, :down_rows] = tokens_ref[:, k * down_rows : (k + 1) * down_rows]
        if down_rows < width:
            token_buf[k, :, down_rows:] = jnp.zeros((rows, width - down_rows), bf16)
    for i in range(replicas):
        place = jnp.int32(0)
        for k in range(1, replicas):
            place = place + jnp.where(owners_ref[k] == replica ^ i, k, 0)
        left_ref[:, i * width : (i + 1) * width] = token_buf[place]
    if replicas > 1:
        for i in range(shards):
            for k in range(replicas):
                picked = jnp.where(owners_ref[shard ^ i] == replica ^ k, 1.0, 0.0)
                row = i * replicas + k
                pick_ref[row : row + 1, :] = jnp.full((1, lanes), picked, f32)

    lengths_copy.wait()
    row = lax.broadcasted_iota(jnp.int32, (rows, lanes), 0)
    lane = lax.broadcasted_iota(jnp.int32, (rows, lanes), 1)
    position = row // row_count
    for b in range(row_count):
        position = position + jnp.where(row % row_count == b, lengths_ref[b], 0)
    angles = position.astype(f32) * turns_ref[:1, :]
    cosine_ref[...] = jnp.cos(angles)
    sine = jnp.sin(angles)
    sine_ref[...] = jnp.where(lane < lanes // 2, -sine, sine)
    slot = lax.broadcasted_iota(jnp.int32, bias_ref.shape, 1)
    whose = lax.broadcasted_iota(jnp.int32, bias_ref.shape, 0)
    length = jnp.zeros(bias_ref.shape, jnp.int32)
    for b in range(row_count):
        length = jnp.where(whose == b, lengths_ref[b], length)
    bias_ref[...] = jnp.where(slot < length, 0.0, masked_score)


def project(
    owners, lengths, tokens, weight, queries, turns, after, step_count, head_count, slots, shards, replicas
):
    rows, depth = tokens.shape
    row_count = rows // step_count
    own = weight.shape[1] // shards
    piece_width = -(-depth // replicas // lanes) * lanes
    seen_rows = rows * queries.shape[1] // lanes
    table = jax.ShapeDtypeStruct((rows, lanes), f32)
    mine, *rest = pl.pallas_call(
        functools.partial(project_kernel, step_count, row_count, head_count, shards, replicas),
        out_shape=[jax.ShapeDtypeStruct((rows, own), f32)]
        + [jax.ShapeDtypeStruct((rows, own), bf16)] * (shards - 1)
        + [
            jax.ShapeDtypeStruct((rows, replicas * piece_width), bf16),
            jax.ShapeDtypeStruct((shards * replicas, lanes), f32),
            jax.ShapeDtypeStruct((seen_rows, lanes), bf16),
            jax.ShapeDtypeStruct((seen_rows, lanes), bf16),
            table,
            table,
            jax.ShapeDtypeStruct((row_count, slots), f32),
        ],
        in_specs=[stays_in_hbm] * 2 + [whole_in_vmem] * 5,
        out_specs=[whole_in_vmem] * (shards + 7),
        scratch_shapes=[
            pltpu.SMEM(owners.shape, jnp.int32),
            pltpu.SMEM(lengths.shape, jnp.int32),
            pltpu.VMEM((replicas, rows, piece_width), bf16),
            pltpu.VMEM((seen_rows, lanes), f32),
            pltpu.SemaphoreType.DMA((2,)),
        ],
        compiler_params=pltpu.CompilerParams(vmem_limit_bytes=6 * 2**20),
        name="project",
        cost_estimate=pl.CostEstimate(
            flops=2 * rows * weight.size, bytes_accessed=2 * weight.size, transcendentals=0
        ),
    )(*in_hbm(owners, lengths), tokens, weight, queries, turns, after)
    return mine, rest[: shards - 1], *rest[shards - 1 :]


def attend_kernel(
    head_count,
    asked_ref,
    keys_ref,
    values_ref,
    bias_ref,
    _,
    total_ref,
    peak_ref,
    sum_ref,
    scores_ref,
    raised,
):
    row_count, slots, _ = keys_ref.shape
    seen = asked_ref.shape[0] // (head_count * row_count)

    for b in range(row_count):
        for h in range(head_count):
            at = (h * row_count + b) * seen
            scores_ref[at : at + seen, :] = lax.dot_general(
                asked_ref[at : at + seen, :],
                keys_ref[b, :, h * lanes : (h + 1) * lanes],
                (((1,), (1,)), ((), ())),
                preferred_element_type=f32,
            )

    places = [
        (
            b,
            h,
            slice((h * row_count + b) * seen, (h * row_count + b + 1) * seen),
            pl.ds(h * row_count * seen + b, seen, stride=row_count),
        )
        for b in range(row_count)
        for h in range(head_count)
    ]
    for b, h, place, out in places:
        score = scores_ref[place, :] + bias_ref[b : b + 1, :]
        peak = jnp.max(score, axis=1, keepdims=True)
        lifted = jnp.exp2((score - peak) * exponent_scale)
        raised[place, :] = lifted.astype(bf16)
        peak_ref[out, :] = jnp.broadcast_to(peak, (seen, lanes))
        sum_ref[out, :] = jnp.broadcast_to(
            jnp.sum(lifted, axis=1, keepdims=True), (seen, lanes)
        )
    for b, h, place, out in places:
        total_ref[out, :] = jnp.dot(
            raised[place, :],
            values_ref[b, :, h * lanes : (h + 1) * lanes],
            preferred_element_type=f32,
        )


def attend(asked, keys, values, bias, after):
    row_count, slots, width = keys.shape
    seen_rows = asked.shape[0]
    seen_table = jax.ShapeDtypeStruct((seen_rows, lanes), f32)
    return pl.pallas_call(
        functools.partial(attend_kernel, width // lanes),
        out_shape=(seen_table,) * 3,
        in_specs=[whole_in_vmem] * 5,
        out_specs=(whole_in_vmem,) * 3,
        scratch_shapes=[
            pltpu.VMEM((seen_rows, slots), f32),
            pltpu.VMEM((seen_rows, slots), bf16),
        ],
        compiler_params=pltpu.CompilerParams(vmem_limit_bytes=8 * 2**20),
        name="attend",
        cost_estimate=pl.CostEstimate(
            flops=4 * seen_rows * slots * lanes,
            bytes_accessed=2 * (keys.size + values.size),
            transcendentals=seen_rows * slots,
        ),
    )(asked, keys, values, bias, after)


def piece_places(replicas):
    order = [0, 1] + list(range(replicas - 1, 1, -1))
    return [order.index(i) for i in range(replicas)]


def route_kernel(replicas, shards, *refs):
    left_ref, pick_ref = refs[:2]
    piece_refs = [refs[2 + place] for place in piece_places(replicas)]
    out_refs = refs[2 + replicas : 2 + replicas + shards]
    (right,) = refs[2 + replicas + shards :]
    up_rows = out_refs[0].shape[0] - left_ref.shape[0]
    rows = left_ref.shape[0]
    rank = right.shape[0]
    width = right.shape[1] // replicas
    half = rank // 2
    rest = (piece_refs[0].shape[0] - up_rows) % rank
    for i in range(replicas):
        first = 0
        for c in range(width // lanes - (1 if rest else 0)):
            right[:, i * width + c * lanes : i * width + (c + 1) * lanes] = piece_refs[i][
                first : first + rank, :
            ]
            first += rank
        if rest:
            both = piece_refs[i][first : first + half, :]
            tail = jnp.concatenate([both[:, : lanes // 2], both[:, lanes // 2 :]], axis=0)
            right[:, (i + 1) * width - lanes : (i + 1) * width] = jnp.concatenate(
                [tail, jnp.zeros((rank, lanes // 2), bf16)], axis=1
            )
            first += half
    lowered = lax.dot_general(
        left_ref[...], right[...], (((1,), (1,)), ((), ())), preferred_element_type=f32
    )
    both = jnp.concatenate(split_halves(lowered), axis=1)
    ups = [piece[piece.shape[0] - up_rows :, :].astype(f32) for piece in piece_refs]
    for i in range(shards):
        out_refs[i][:rows, :] = both
        picked = sum(up * pick_ref[i * replicas + k, :][None, :] for k, up in enumerate(ups))
        out_refs[i][rows:, :] = picked.astype(bf16)


def route(left, pick, pieces, rank, up_rows, shards):
    rows, depth = left.shape
    replicas = len(pieces)
    return pl.pallas_call(
        functools.partial(route_kernel, replicas, shards),
        out_shape=[jax.ShapeDtypeStruct((rows + up_rows, lanes), bf16)] * shards,
        in_specs=[whole_in_vmem] * (2 + replicas),
        out_specs=[whole_in_vmem] * shards,
        scratch_shapes=[pltpu.VMEM((rank, depth), bf16)],
        compiler_params=pltpu.CompilerParams(vmem_limit_bytes=4 * 2**20),
        name="route",
        cost_estimate=pl.CostEstimate(flops=0, bytes_accessed=800000, transcendentals=0),
    )(left, pick, *[pieces[i] for i in piece_places(replicas)])


def route_plain(owners, tokens, down, up, rank_part, own, shards):
    rank = down.shape[1]
    shard = lax.axis_index("tensor")
    first = shard * rank_part
    up_part = lax.dynamic_slice_in_dim(up, first, rank_part, axis=0)
    downs = lax.all_gather(down, "rollout", axis=0, tiled=False)
    ups = lax.all_gather(up_part, "rollout", axis=0, tiled=False)
    down_matrix = jnp.take(downs, owners, axis=0, mode="clip").reshape(-1, rank)
    up_matrix = jnp.take(ups, owners, axis=0, mode="clip").transpose(1, 0, 2)
    up_matrix = up_matrix.reshape(rank_part, -1)
    lowered = jnp.dot(tokens, down_matrix, preferred_element_type=f32)
    both = jnp.concatenate(split_halves(lowered), axis=1)
    packets = []
    for i in range(shards):
        up_block = lax.dynamic_slice_in_dim(up_matrix, (shard ^ i) * own, own, axis=1)
        parts = [both, side_by_side(up_block)]
        packets.append(jnp.concatenate(parts, axis=0))
    return packets


def finish_kernel(step_count, row_count, head_count, shards, *refs):
    gain_ref, base_ref, grouped_ref, total_ref, peak_ref, sum_ref, cosine_ref, sine_ref = refs[:8]
    packet_refs = refs[8 : 8 + shards][::-1]
    sum_refs = refs[8 + shards : 7 + 2 * shards]
    attention_ref, keys_ref, values_ref = refs[7 + 2 * shards : 10 + 2 * shards]
    (up_buf,) = refs[10 + 2 * shards :]
    shard = lax.axis_index("tensor")
    rows = step_count * row_count
    own = base_ref.shape[1]
    blocks = own // lanes
    rank = up_buf.shape[0]
    rank_part = rank // shards
    group = grouped_ref.shape[0] // (head_count * rows)
    seen = step_count * group

    lowered = jnp.zeros((rows, lanes), f32)
    for i in range(shards):
        lowered = lowered + packet_refs[i][:rows, :].astype(f32)
        ups = packet_refs[i][rows:, :].astype(f32)
        at = pl.multiple_of((shard ^ i) * rank_part, rank_part)
        for c in range(blocks):
            up_buf[pl.ds(at, rank_part), c * lanes : (c + 1) * lanes] = ups[
                c * rank_part : (c + 1) * rank_part, :
            ]
    lane = lax.broadcasted_iota(jnp.int32, (rows, lanes), 1)
    lowered = lowered + pltpu.roll(lowered, rank, 1)
    high, low = split_halves(lowered)
    left = jnp.where(lane < rank, high.astype(f32), low.astype(f32)).astype(bf16)
    up = up_buf[...].astype(bf16)
    raised_up = jnp.dot(left, jnp.concatenate([up, up], axis=0), preferred_element_type=f32)
    joined = []
    for c in range(blocks):
        block = base_ref[:, c * lanes : (c + 1) * lanes]
        for partial_ref in sum_refs:
            block = block + partial_ref[:, c * lanes : (c + 1) * lanes].astype(f32)
        joined.append(block + adapter_scale * raised_up[:, c * lanes : (c + 1) * lanes])

    all_rows = row_count * seen
    seen_by = lax.broadcasted_iota(jnp.int32, (all_rows, rows), 0)
    made_by = lax.broadcasted_iota(jnp.int32, (all_rows, rows), 1)
    visible = (seen_by % row_count == made_by % row_count) & (
        made_by // row_count <= seen_by // (row_count * group)
    )
    heads = [(h, slice(h * all_rows, (h + 1) * all_rows)) for h in range(head_count)]
    keys, values, scores, results = [], [], [], []
    for h, _ in heads:
        raw_key = joined[2 * h]
        mean_square = jnp.mean(raw_key * raw_key, axis=1, keepdims=True)
        normed = raw_key * lax.rsqrt(mean_square + norm_eps) * gain_ref[...]
        key = normed * cosine_ref[...] + pltpu.roll(normed, lanes // 2, 1) * sine_ref[...]
        keys.append(key.astype(bf16))
        values.append(joined[2 * h + 1].astype(bf16))
        keys_ref[:, h * lanes : (h + 1) * lanes] = keys[h]
        values_ref[:, h * lanes : (h + 1) * lanes] = values[h]
    for h, mine in heads:
        score = lax.dot_general(
            grouped_ref[mine, :], keys[h], (((1,), (1,)), ((), ())), preferred_element_type=f32
        )
        scores.append(jnp.where(visible, score, masked_score))
    for h, mine in heads:
        old_peak = peak_ref[mine, :]
        peak = jnp.maximum(old_peak, jnp.max(scores[h], axis=1, keepdims=True))
        fade = jnp.exp2((old_peak - peak) * exponent_scale)
        lifted = jnp.exp2((scores[h] - peak[:, :rows]) * exponent_scale)
        denominator = fade * sum_ref[mine, :] + jnp.sum(lifted, axis=1, keepdims=True)
        total = fade * total_ref[mine, :] + jnp.dot(
            lifted.astype(bf16), values[h], preferred_element_type=f32
        )
        results.append(total / denominator)
    for pair in range(step_count // 2):
        for q in range(head_count * group):
            h, g = q // group, q % group
            both = []
            for side in range(2):
                first = ((pair * 2 + side) * group + g) * row_count
                both.append(results[h][first : first + row_count])
            attention_ref[
                pair * 2 * row_count : (pair + 1) * 2 * row_count, q * lanes : (q + 1) * lanes
            ] = jnp.concatenate(both, axis=0).astype(bf16)


def finish(mine, others, partials, gain, packets, rank, step_count, row_count, query_width):
    rows, own = mine.shape
    shards = len(packets)
    head_count = own // (2 * lanes)
    return pl.pallas_call(
        functools.partial(finish_kernel, step_count, row_count, head_count, shards),
        out_shape=(
            jax.ShapeDtypeStruct((rows, query_width), bf16),
            jax.ShapeDtypeStruct((rows, head_count * lanes), bf16),
            jax.ShapeDtypeStruct((rows, head_count * lanes), bf16),
        ),
        in_specs=[whole_in_vmem] * (7 + 2 * shards),
        out_specs=(whole_in_vmem,) * 3,
        scratch_shapes=[
            pltpu.VMEM((rank, own), f32),
        ],
        compiler_params=pltpu.CompilerParams(vmem_limit_bytes=6 * 2**20),
        name="finish",
        cost_estimate=pl.CostEstimate(flops=0, bytes_accessed=1000000, transcendentals=0),
    )(gain, mine, *partials, *packets[::-1], *others)


def per_device(
    normed_tokens,
    key_value_weight,
    adapter_down,
    adapter_up,
    key_gain,
    queries,
    cache_keys,
    stored_values,
    lengths,
    owners,
):
    replicas = lax.axis_size("rollout")
    shards = lax.axis_size("tensor")
    down_rows, rank = adapter_down.shape
    step_count, row_count, depth = normed_tokens.shape
    own = key_value_weight.shape[1] // shards
    rank_part = rank // shards
    rows = step_count * row_count
    tokens = normed_tokens.reshape(rows, depth)
    query_rows = queries.reshape(rows, -1)

    fits = (
        replicas <= 4
        and adapter_up.shape[1] == own
        and down_rows % lanes in (0, lanes // 2)
        and rank == lanes // 2
        and rank_part % 16 == 0
    )
    fetched = 2 * (key_value_weight.size + cache_keys.size + stored_values.size)
    turns = frequencies(
        pl.CostEstimate(flops=1000 * fetched, bytes_accessed=fetched, transcendentals=0)
    )
    if fits:
        packed = pack(adapter_down.T, adapter_up, rank_part, turns)
        pieces = [packed] + [swap(packed, "rollout", i) for i in range(1, replicas)]
    mine, blocks, left, pick, asked, grouped, cosine, sine, bias = project(
        owners,
        lengths,
        tokens,
        key_value_weight,
        query_rows,
        turns,
        packed if fits else adapter_up,
        step_count,
        cache_keys.shape[2] // lanes,
        cache_keys.shape[1],
        shards,
        replicas if fits else 1,
    )
    others = [swap(block, "tensor", i + 1) for i, block in enumerate(blocks)]
    if fits:
        packets = route(left, pick, pieces, rank, rank_part * own // lanes, shards)
    else:
        packets = route_plain(
            owners, tokens, adapter_down, adapter_up, rank_part, own, shards
        )
    total, peak, denominator = attend(asked, cache_keys, stored_values, bias, packets[0])
    packets = [packets[0]] + [swap(packets[i], "tensor", i) for i in range(1, shards)]
    attention, keys, values = finish(
        mine,
        others,
        (grouped, total, peak, denominator, cosine, sine),
        key_gain.reshape(1, -1),
        packets,
        rank,
        step_count,
        row_count,
        query_rows.shape[1],
    )
    return tuple(a.reshape(step_count, row_count, -1) for a in (attention, keys, values))


def solution(mesh):
    placed = (
        P(None, ("job", "rollout"), "tensor"),
        P("tensor", None),
        P(("job", "rollout", "tensor"), None),
        P(None, ("job", "rollout")),
        P(),
        P(None, ("job", "rollout"), "tensor"),
        P(("job", "rollout"), None, "tensor"),
        P(("job", "rollout"), None, "tensor"),
        P(("job", "rollout")),
        P("job"),
    )
    return jax.shard_map(
        per_device,
        mesh=mesh,
        in_specs=placed,
        out_specs=(
            P(None, ("job", "rollout"), "tensor"),
            P(None, ("job", "rollout"), "tensor"),
            P(None, ("job", "rollout"), "tensor"),
        ),
        check_vma=False,
    )
```

```python
import functools
import math

import jax
import jax.numpy as jnp
from jax import lax
from jax.experimental import pallas as pl
from jax.experimental.pallas import tpu as pltpu
from jax.sharding import PartitionSpec as P

norm_eps = 1e-06
rope_base = 1000000.0
adapter_scale = 2.0
masked_score = -1e30
lanes = 128
exponent_scale = lanes**-0.5 / math.log(2.0)
f32 = jnp.float32
bf16 = jnp.bfloat16

whole_in_vmem = pl.BlockSpec(memory_space=pltpu.VMEM)
whole_in_smem = pl.BlockSpec(memory_space=pltpu.SMEM)
stays_in_hbm = pl.BlockSpec(memory_space=pltpu.HBM)


def swap(block, axis, offset):
    count = lax.axis_size(axis)
    return lax.ppermute(block, axis, [(s, s ^ offset) for s in range(count)])


def in_hbm(*arrays):
    return tuple(pltpu.with_memory_space_constraint(a, pltpu.HBM) for a in arrays)


def side_by_side(rows_of_blocks):
    r, c = rows_of_blocks.shape
    return rows_of_blocks.reshape(r, c // lanes, lanes).transpose(1, 0, 2).reshape(-1, lanes)


def split_halves(total):
    high = total.astype(bf16)
    return high, (total - high.astype(f32)).astype(bf16)


def frequencies_kernel(out_ref):
    lane = lax.broadcasted_iota(jnp.int32, out_ref.shape, 1)
    spacing = (lane % (lanes // 2)).astype(f32) * (-2.0 / lanes * math.log(rope_base))
    out_ref[...] = jnp.exp(spacing)


def frequencies(beside):
    return pl.pallas_call(
        frequencies_kernel,
        out_shape=jax.ShapeDtypeStruct((8, lanes), f32),
        out_specs=whole_in_vmem,
        compiler_params=pltpu.CompilerParams(vmem_limit_bytes=2**20),
        name="frequencies",
        cost_estimate=beside,
    )()


def pack_kernel(down_ref, up_all_ref, _, out_ref):
    rank, down_rows = down_ref.shape
    rank_part = (out_ref.shape[0] * lanes - down_ref.size) // up_all_ref.shape[1]
    start = pl.multiple_of(lax.axis_index("tensor") * rank_part, rank_part)
    up_ref = up_all_ref.at[pl.ds(start, rank_part), :]
    first = 0
    for c in range(down_rows // lanes):
        out_ref[first : first + rank, :] = down_ref[:, c * lanes : (c + 1) * lanes]
        first += rank
    rest = down_rows % lanes
    if rest:
        half = rank // 2
        tail = down_ref[:, down_rows - rest :]
        out_ref[first : first + half, :] = jnp.concatenate([tail[:half], tail[half:]], axis=1)
        first += half
    for c in range(up_ref.shape[1] // lanes):
        out_ref[first : first + rank_part, :] = up_ref[:, c * lanes : (c + 1) * lanes]
        first += rank_part


def pack(down, up, rank_part, after):
    rows = (down.size + rank_part * up.shape[1]) // lanes
    return pl.pallas_call(
        pack_kernel,
        out_shape=jax.ShapeDtypeStruct((rows, lanes), bf16),
        in_specs=[whole_in_vmem] * 3,
        out_specs=whole_in_vmem,
        compiler_params=pltpu.CompilerParams(vmem_limit_bytes=2 * 2**20),
        name="pack",
        cost_estimate=pl.CostEstimate(flops=0, bytes_accessed=200000, transcendentals=0),
    )(down, up, after)


def project_kernel(step_count, row_count, head_count, shards, replicas, *refs):
    owners_hbm, lengths_hbm, tokens_ref, weight_ref, queries_ref, turns_ref, _ = refs[:7]
    own_ref = refs[7]
    block_refs = refs[8 : 7 + shards]
    left_ref, pick_ref, asked_ref, grouped_ref, cosine_ref, sine_ref, bias_ref, visible_ref = refs[
        7 + shards : 15 + shards
    ]
    owners_ref, lengths_ref, token_buf, regroup, sems = refs[15 + shards :]
    owners_copy = pltpu.make_async_copy(owners_hbm, owners_ref, sems.at[0])
    lengths_copy = pltpu.make_async_copy(lengths_hbm, lengths_ref, sems.at[1])
    owners_copy.start()
    lengths_copy.start()

    shard = lax.axis_index("tensor")
    rows, own = own_ref.shape
    for i in range(shards):
        first = pl.multiple_of((shard ^ i) * own, lanes)
        block = jnp.dot(
            tokens_ref[...], weight_ref[:, pl.ds(first, own)], preferred_element_type=f32
        )
        if i == 0:
            own_ref[...] = block
        else:
            block_refs[i - 1][...] = block.astype(bf16)

    group = queries_ref.shape[1] // (head_count * lanes)
    seen = step_count * group
    for pair in range(step_count // 2):
        for q in range(head_count * group):
            h, g = q // group, q % group
            both = queries_ref[
                pair * 2 * row_count : (pair + 1) * 2 * row_count, q * lanes : (q + 1) * lanes
            ].astype(f32)
            for side in range(2):
                first = h * row_count * seen + (pair * 2 + side) * group + g
                regroup[pl.ds(first, row_count, stride=seen), :] = both[
                    side * row_count : (side + 1) * row_count, :
                ]
            if g % 2:
                for side in range(2):
                    half = slice(side * row_count, (side + 1) * row_count)
                    last = (h * seen + (pair * 2 + side) * group + g + 1) * row_count
                    grouped_ref[last - 2 * row_count : last, :] = jnp.concatenate(
                        [before[half], both[half]], axis=0
                    ).astype(bf16)
            before = both
    asked_ref[...] = regroup[...].astype(bf16)

    owners_copy.wait()
    replica = lax.axis_index("rollout")
    width = token_buf.shape[2]
    down_rows = tokens_ref.shape[1] // replicas
    for k in range(replicas):
        token_buf[k, :, :down_rows] = tokens_ref[:, k * down_rows : (k + 1) * down_rows]
        if down_rows < width:
            token_buf[k, :, down_rows:] = jnp.zeros((rows, width - down_rows), bf16)
    for i in range(replicas):
        place = jnp.int32(0)
        for k in range(1, replicas):
            place = place + jnp.where(owners_ref[k] == replica ^ i, k, 0)
        left_ref[:, i * width : (i + 1) * width] = token_buf[place]
    if replicas > 1:
        for i in range(shards):
            for k in range(replicas):
                picked = jnp.where(owners_ref[shard ^ i] == replica ^ k, 1.0, 0.0)
                row = i * replicas + k
                pick_ref[row : row + 1, :] = jnp.full((1, lanes), picked, f32)

    lengths_copy.wait()
    row = lax.broadcasted_iota(jnp.int32, (rows, lanes), 0)
    lane = lax.broadcasted_iota(jnp.int32, (rows, lanes), 1)
    position = row // row_count
    for b in range(row_count):
        position = position + jnp.where(row % row_count == b, lengths_ref[b], 0)
    angles = position.astype(f32) * turns_ref[:1, :]
    cosine_ref[...] = jnp.cos(angles)
    sine = jnp.sin(angles)
    sine_ref[...] = jnp.where(lane < lanes // 2, -sine, sine)
    slot = lax.broadcasted_iota(jnp.int32, bias_ref.shape, 1)
    whose = lax.broadcasted_iota(jnp.int32, bias_ref.shape, 0)
    length = jnp.zeros(bias_ref.shape, jnp.int32)
    for b in range(row_count):
        length = jnp.where(whose == b, lengths_ref[b], length)
    bias_ref[...] = jnp.where(slot < length, 0.0, masked_score)
    all_rows = row_count * seen
    seen_by = lax.broadcasted_iota(jnp.int32, (all_rows, rows), 0)
    made_by = lax.broadcasted_iota(jnp.int32, (all_rows, rows), 1)
    visible = (seen_by % row_count == made_by % row_count) & (
        made_by // row_count <= seen_by // (row_count * group)
    )
    visible_ref[...] = jnp.where(visible, 0.0, masked_score)


def project(
    owners, lengths, tokens, weight, queries, turns, after, step_count, head_count, slots, shards, replicas
):
    rows, depth = tokens.shape
    row_count = rows // step_count
    own = weight.shape[1] // shards
    piece_width = -(-depth // replicas // lanes) * lanes
    seen_rows = rows * queries.shape[1] // lanes
    table = jax.ShapeDtypeStruct((rows, lanes), f32)
    mine, *rest = pl.pallas_call(
        functools.partial(project_kernel, step_count, row_count, head_count, shards, replicas),
        out_shape=[jax.ShapeDtypeStruct((rows, own), f32)]
        + [jax.ShapeDtypeStruct((rows, own), bf16)] * (shards - 1)
        + [
            jax.ShapeDtypeStruct((rows, replicas * piece_width), bf16),
            jax.ShapeDtypeStruct((shards * replicas, lanes), f32),
            jax.ShapeDtypeStruct((seen_rows, lanes), bf16),
            jax.ShapeDtypeStruct((seen_rows, lanes), bf16),
            table,
            table,
            jax.ShapeDtypeStruct((row_count, slots), f32),
            jax.ShapeDtypeStruct((seen_rows // head_count, rows), f32),
        ],
        in_specs=[stays_in_hbm] * 2 + [whole_in_vmem] * 5,
        out_specs=[whole_in_vmem] * (shards + 8),
        scratch_shapes=[
            pltpu.SMEM(owners.shape, jnp.int32),
            pltpu.SMEM(lengths.shape, jnp.int32),
            pltpu.VMEM((replicas, rows, piece_width), bf16),
            pltpu.VMEM((seen_rows, lanes), f32),
            pltpu.SemaphoreType.DMA((2,)),
        ],
        compiler_params=pltpu.CompilerParams(vmem_limit_bytes=6 * 2**20),
        name="project",
        cost_estimate=pl.CostEstimate(
            flops=2 * rows * weight.size, bytes_accessed=2 * weight.size, transcendentals=0
        ),
    )(*in_hbm(owners, lengths), tokens, weight, queries, turns, after)
    return mine, rest[: shards - 1], *rest[shards - 1 :]


def attend_kernel(
    head_count,
    asked_ref,
    keys_ref,
    values_ref,
    bias_ref,
    _,
    mine_ref,
    *refs,
):
    other_refs = refs[:-6]
    base_ref, total_ref, peak_ref, sum_ref, scores_ref, raised = refs[-6:]
    base = mine_ref[...]
    for other_ref in other_refs:
        base = base + other_ref[...].astype(f32)
    base_ref[...] = base

    row_count, slots, _ = keys_ref.shape
    seen = asked_ref.shape[0] // (head_count * row_count)

    for b in range(row_count):
        for h in range(head_count):
            at = (h * row_count + b) * seen
            scores_ref[at : at + seen, :] = lax.dot_general(
                asked_ref[at : at + seen, :],
                keys_ref[b, :, h * lanes : (h + 1) * lanes],
                (((1,), (1,)), ((), ())),
                preferred_element_type=f32,
            )

    places = [
        (
            b,
            h,
            slice((h * row_count + b) * seen, (h * row_count + b + 1) * seen),
            pl.ds(h * row_count * seen + b, seen, stride=row_count),
        )
        for b in range(row_count)
        for h in range(head_count)
    ]
    for b, h, place, out in places:
        score = scores_ref[place, :] + bias_ref[b : b + 1, :]
        peak = jnp.max(score, axis=1, keepdims=True)
        lifted = jnp.exp2((score - peak) * exponent_scale)
        raised[place, :] = lifted.astype(bf16)
        peak_ref[out, :] = jnp.broadcast_to(peak, (seen, lanes))
        sum_ref[out, :] = jnp.broadcast_to(
            jnp.sum(lifted, axis=1, keepdims=True), (seen, lanes)
        )
    for b, h, place, out in places:
        total_ref[out, :] = jnp.dot(
            raised[place, :],
            values_ref[b, :, h * lanes : (h + 1) * lanes],
            preferred_element_type=f32,
        )


def attend(asked, keys, values, bias, after, mine, others):
    row_count, slots, width = keys.shape
    seen_rows = asked.shape[0]
    seen_table = jax.ShapeDtypeStruct((seen_rows, lanes), f32)
    return pl.pallas_call(
        functools.partial(attend_kernel, width // lanes),
        out_shape=(jax.ShapeDtypeStruct(mine.shape, f32),) + (seen_table,) * 3,
        in_specs=[whole_in_vmem] * (6 + len(others)),
        out_specs=(whole_in_vmem,) * 4,
        scratch_shapes=[
            pltpu.VMEM((seen_rows, slots), f32),
            pltpu.VMEM((seen_rows, slots), bf16),
        ],
        compiler_params=pltpu.CompilerParams(vmem_limit_bytes=8 * 2**20),
        name="attend",
        cost_estimate=pl.CostEstimate(
            flops=4 * seen_rows * slots * lanes,
            bytes_accessed=2 * (keys.size + values.size),
            transcendentals=seen_rows * slots,
        ),
    )(asked, keys, values, bias, after, mine, *others)


def piece_places(replicas):
    order = [0, 1] + list(range(replicas - 1, 1, -1))
    return [order.index(i) for i in range(replicas)]


def route_kernel(replicas, shards, *refs):
    left_ref, pick_ref = refs[:2]
    piece_refs = [refs[2 + place] for place in piece_places(replicas)]
    out_refs = refs[2 + replicas : 2 + replicas + shards]
    (right,) = refs[2 + replicas + shards :]
    up_rows = out_refs[0].shape[0] - left_ref.shape[0]
    rows = left_ref.shape[0]
    rank = right.shape[0]
    width = right.shape[1] // replicas
    half = rank // 2
    rest = (piece_refs[0].shape[0] - up_rows) % rank
    for i in range(replicas):
        first = 0
        for c in range(width // lanes - (1 if rest else 0)):
            right[:, i * width + c * lanes : i * width + (c + 1) * lanes] = piece_refs[i][
                first : first + rank, :
            ]
            first += rank
        if rest:
            both = piece_refs[i][first : first + half, :]
            tail = jnp.concatenate([both[:, : lanes // 2], both[:, lanes // 2 :]], axis=0)
            right[:, (i + 1) * width - lanes : (i + 1) * width] = jnp.concatenate(
                [tail, jnp.zeros((rank, lanes // 2), bf16)], axis=1
            )
            first += half
    lowered = lax.dot_general(
        left_ref[...], right[...], (((1,), (1,)), ((), ())), preferred_element_type=f32
    )
    both = jnp.concatenate(split_halves(lowered), axis=1)
    ups = [piece[piece.shape[0] - up_rows :, :].astype(f32) for piece in piece_refs]
    for i in range(shards):
        out_refs[i][:rows, :] = both
        picked = sum(up * pick_ref[i * replicas + k, :][None, :] for k, up in enumerate(ups))
        out_refs[i][rows:, :] = picked.astype(bf16)


def route(left, pick, pieces, rank, up_rows, shards):
    rows, depth = left.shape
    replicas = len(pieces)
    return pl.pallas_call(
        functools.partial(route_kernel, replicas, shards),
        out_shape=[jax.ShapeDtypeStruct((rows + up_rows, lanes), bf16)] * shards,
        in_specs=[whole_in_vmem] * (2 + replicas),
        out_specs=[whole_in_vmem] * shards,
        scratch_shapes=[pltpu.VMEM((rank, depth), bf16)],
        compiler_params=pltpu.CompilerParams(vmem_limit_bytes=4 * 2**20),
        name="route",
        cost_estimate=pl.CostEstimate(flops=0, bytes_accessed=800000, transcendentals=0),
    )(left, pick, *[pieces[i] for i in piece_places(replicas)])


def route_plain(owners, tokens, down, up, rank_part, own, shards):
    rank = down.shape[1]
    shard = lax.axis_index("tensor")
    first = shard * rank_part
    up_part = lax.dynamic_slice_in_dim(up, first, rank_part, axis=0)
    downs = lax.all_gather(down, "rollout", axis=0, tiled=False)
    ups = lax.all_gather(up_part, "rollout", axis=0, tiled=False)
    down_matrix = jnp.take(downs, owners, axis=0, mode="clip").reshape(-1, rank)
    up_matrix = jnp.take(ups, owners, axis=0, mode="clip").transpose(1, 0, 2)
    up_matrix = up_matrix.reshape(rank_part, -1)
    lowered = jnp.dot(tokens, down_matrix, preferred_element_type=f32)
    both = jnp.concatenate(split_halves(lowered), axis=1)
    packets = []
    for i in range(shards):
        up_block = lax.dynamic_slice_in_dim(up_matrix, (shard ^ i) * own, own, axis=1)
        parts = [both, side_by_side(up_block)]
        packets.append(jnp.concatenate(parts, axis=0))
    return packets


def finish_kernel(step_count, row_count, head_count, shards, *refs):
    gain_ref, base_ref, grouped_ref, total_ref, peak_ref, sum_ref, cosine_ref, sine_ref = refs[:8]
    packet_refs = refs[8 : 8 + shards][::-1]
    visible_ref, attention_ref, keys_ref, values_ref, up_buf = refs[8 + shards :]
    shard = lax.axis_index("tensor")
    rows = step_count * row_count
    own = base_ref.shape[1]
    blocks = own // lanes
    rank = up_buf.shape[0]
    rank_part = rank // shards
    group = grouped_ref.shape[0] // (head_count * rows)
    seen = step_count * group

    lowered = jnp.zeros((rows, lanes), f32)
    for i in range(shards):
        lowered = lowered + packet_refs[i][:rows, :].astype(f32)
        ups = packet_refs[i][rows:, :].astype(up_buf.dtype)
        at = pl.multiple_of((shard ^ i) * rank_part, rank_part)
        for c in range(blocks):
            up_buf[pl.ds(at, rank_part), c * lanes : (c + 1) * lanes] = ups[
                c * rank_part : (c + 1) * rank_part, :
            ]
    lane = lax.broadcasted_iota(jnp.int32, (rows, lanes), 1)
    lowered = lowered + pltpu.roll(lowered, rank, 1)
    high, low = split_halves(lowered)
    left = jnp.where(lane < rank, high.astype(f32), low.astype(f32)).astype(bf16)
    up = up_buf[...].astype(bf16)
    raised_up = jnp.dot(left, jnp.concatenate([up, up], axis=0), preferred_element_type=f32)
    joined = []
    for c in range(blocks):
        block = base_ref[:, c * lanes : (c + 1) * lanes]
        joined.append(block + adapter_scale * raised_up[:, c * lanes : (c + 1) * lanes])

    all_rows = row_count * seen
    heads = [(h, slice(h * all_rows, (h + 1) * all_rows)) for h in range(head_count)]
    keys, values, scores, results = [], [], [], []
    for h, _ in heads:
        raw_key = joined[2 * h]
        mean_square = jnp.mean(raw_key * raw_key, axis=1, keepdims=True)
        normed = raw_key * lax.rsqrt(mean_square + norm_eps) * gain_ref[...]
        key = normed * cosine_ref[...] + pltpu.roll(normed, lanes // 2, 1) * sine_ref[...]
        keys.append(key.astype(bf16))
        values.append(joined[2 * h + 1].astype(bf16))
        keys_ref[:, h * lanes : (h + 1) * lanes] = keys[h]
        values_ref[:, h * lanes : (h + 1) * lanes] = values[h]
    for h, mine in heads:
        score = lax.dot_general(
            grouped_ref[mine, :], keys[h], (((1,), (1,)), ((), ())), preferred_element_type=f32
        )
        scores.append(score + visible_ref[...])
    for h, mine in heads:
        old_peak = peak_ref[mine, :]
        peak = jnp.maximum(old_peak, jnp.max(scores[h], axis=1, keepdims=True))
        fade = jnp.exp2((old_peak - peak) * exponent_scale)
        lifted = jnp.exp2((scores[h] - peak[:, :rows]) * exponent_scale)
        denominator = fade * sum_ref[mine, :] + jnp.sum(lifted, axis=1, keepdims=True)
        total = fade * total_ref[mine, :] + jnp.dot(
            lifted.astype(bf16), values[h], preferred_element_type=f32
        )
        results.append(total / denominator)
    for pair in range(step_count // 2):
        for q in range(head_count * group):
            h, g = q // group, q % group
            both = []
            for side in range(2):
                first = ((pair * 2 + side) * group + g) * row_count
                both.append(results[h][first : first + row_count])
            attention_ref[
                pair * 2 * row_count : (pair + 1) * 2 * row_count, q * lanes : (q + 1) * lanes
            ] = jnp.concatenate(both, axis=0).astype(bf16)


def finish(base, visible, partials, gain, packets, rank, step_count, row_count, query_width):
    rows, own = base.shape
    shards = len(packets)
    head_count = own // (2 * lanes)
    return pl.pallas_call(
        functools.partial(finish_kernel, step_count, row_count, head_count, shards),
        out_shape=(
            jax.ShapeDtypeStruct((rows, query_width), bf16),
            jax.ShapeDtypeStruct((rows, head_count * lanes), bf16),
            jax.ShapeDtypeStruct((rows, head_count * lanes), bf16),
        ),
        in_specs=[whole_in_vmem] * (9 + shards),
        out_specs=(whole_in_vmem,) * 3,
        scratch_shapes=[
            pltpu.VMEM((rank, own), bf16 if rank // shards % 16 == 0 else f32),
        ],
        compiler_params=pltpu.CompilerParams(vmem_limit_bytes=6 * 2**20),
        name="finish",
        cost_estimate=pl.CostEstimate(flops=0, bytes_accessed=1000000, transcendentals=0),
    )(gain, base, *partials, *packets[::-1], visible)


def per_device(
    normed_tokens,
    key_value_weight,
    adapter_down,
    adapter_up,
    key_gain,
    queries,
    cache_keys,
    stored_values,
    lengths,
    owners,
):
    replicas = lax.axis_size("rollout")
    shards = lax.axis_size("tensor")
    down_rows, rank = adapter_down.shape
    step_count, row_count, depth = normed_tokens.shape
    own = key_value_weight.shape[1] // shards
    rank_part = rank // shards
    rows = step_count * row_count
    tokens = normed_tokens.reshape(rows, depth)
    query_rows = queries.reshape(rows, -1)

    fits = (
        replicas <= 4
        and adapter_up.shape[1] == own
        and down_rows % lanes in (0, lanes // 2)
        and rank == lanes // 2
        and rank_part % 16 == 0
    )
    fetched = 2 * (key_value_weight.size + cache_keys.size + stored_values.size)
    turns = frequencies(
        pl.CostEstimate(flops=1000 * fetched, bytes_accessed=fetched, transcendentals=0)
    )
    if fits:
        packed = pack(adapter_down.T, adapter_up, rank_part, turns)
        pieces = [packed] + [swap(packed, "rollout", i) for i in range(1, replicas)]
    mine, blocks, left, pick, asked, grouped, cosine, sine, bias, visible = project(
        owners,
        lengths,
        tokens,
        key_value_weight,
        query_rows,
        turns,
        packed if fits else adapter_up,
        step_count,
        cache_keys.shape[2] // lanes,
        cache_keys.shape[1],
        shards,
        replicas if fits else 1,
    )
    others = [swap(block, "tensor", i + 1) for i, block in enumerate(blocks)]
    if fits:
        packets = route(left, pick, pieces, rank, rank_part * own // lanes, shards)
    else:
        packets = route_plain(
            owners, tokens, adapter_down, adapter_up, rank_part, own, shards
        )
    base, total, peak, denominator = attend(
        asked, cache_keys, stored_values, bias, packets[0], mine, others
    )
    packets = [packets[0]] + [swap(packets[i], "tensor", i) for i in range(1, shards)]
    attention, keys, values = finish(
        base,
        visible,
        (grouped, total, peak, denominator, cosine, sine),
        key_gain.reshape(1, -1),
        packets,
        rank,
        step_count,
        row_count,
        query_rows.shape[1],
    )
    return tuple(a.reshape(step_count, row_count, -1) for a in (attention, keys, values))


def solution(mesh):
    placed = (
        P(None, ("job", "rollout"), "tensor"),
        P("tensor", None),
        P(("job", "rollout", "tensor"), None),
        P(None, ("job", "rollout")),
        P(),
        P(None, ("job", "rollout"), "tensor"),
        P(("job", "rollout"), None, "tensor"),
        P(("job", "rollout"), None, "tensor"),
        P(("job", "rollout")),
        P("job"),
    )
    return jax.shard_map(
        per_device,
        mesh=mesh,
        in_specs=placed,
        out_specs=(
            P(None, ("job", "rollout"), "tensor"),
            P(None, ("job", "rollout"), "tensor"),
            P(None, ("job", "rollout"), "tensor"),
        ),
        check_vma=False,
    )
```

```python
import functools
import math

import jax
import jax.numpy as jnp
from jax import lax
from jax.experimental import pallas as pl
from jax.experimental.pallas import tpu as pltpu
from jax.sharding import PartitionSpec as P

norm_eps = 1e-06
rope_base = 1000000.0
adapter_scale = 2.0
masked_score = -1e30
lanes = 128
exponent_scale = lanes**-0.5 / math.log(2.0)
f32 = jnp.float32
bf16 = jnp.bfloat16

whole_in_vmem = pl.BlockSpec(memory_space=pltpu.VMEM)
whole_in_smem = pl.BlockSpec(memory_space=pltpu.SMEM)
stays_in_hbm = pl.BlockSpec(memory_space=pltpu.HBM)


def swap(block, axis, offset):
    count = lax.axis_size(axis)
    return lax.ppermute(block, axis, [(s, s ^ offset) for s in range(count)])


def in_hbm(*arrays):
    return tuple(pltpu.with_memory_space_constraint(a, pltpu.HBM) for a in arrays)


def side_by_side(rows_of_blocks):
    r, c = rows_of_blocks.shape
    return rows_of_blocks.reshape(r, c // lanes, lanes).transpose(1, 0, 2).reshape(-1, lanes)


def pack_rows(lowered):
    half = lowered.shape[0] // 2
    return jnp.concatenate([lowered[:half], lowered[half:]], axis=1)


def split_halves(total):
    high = total.astype(bf16)
    return high, (total - high.astype(f32)).astype(bf16)


def frequencies_kernel(out_ref):
    lane = lax.broadcasted_iota(jnp.int32, out_ref.shape, 1)
    spacing = (lane % (lanes // 2)).astype(f32) * (-2.0 / lanes * math.log(rope_base))
    out_ref[...] = jnp.exp(spacing)


def frequencies(beside):
    return pl.pallas_call(
        frequencies_kernel,
        out_shape=jax.ShapeDtypeStruct((8, lanes), f32),
        out_specs=whole_in_vmem,
        compiler_params=pltpu.CompilerParams(vmem_limit_bytes=2**20),
        name="frequencies",
        cost_estimate=beside,
    )()


def pack_kernel(down_ref, up_all_ref, _, out_ref):
    rank, down_rows = down_ref.shape
    rank_part = (out_ref.shape[0] * lanes - down_ref.size) // up_all_ref.shape[1]
    start = pl.multiple_of(lax.axis_index("tensor") * rank_part, rank_part)
    up_ref = up_all_ref.at[pl.ds(start, rank_part), :]
    first = 0
    for c in range(down_rows // lanes):
        out_ref[first : first + rank, :] = down_ref[:, c * lanes : (c + 1) * lanes]
        first += rank
    rest = down_rows % lanes
    if rest:
        half = rank // 2
        tail = down_ref[:, down_rows - rest :]
        out_ref[first : first + half, :] = jnp.concatenate([tail[:half], tail[half:]], axis=1)
        first += half
    for c in range(up_ref.shape[1] // lanes):
        out_ref[first : first + rank_part, :] = up_ref[:, c * lanes : (c + 1) * lanes]
        first += rank_part


def pack(down, up, rank_part, after):
    rows = (down.size + rank_part * up.shape[1]) // lanes
    return pl.pallas_call(
        pack_kernel,
        out_shape=jax.ShapeDtypeStruct((rows, lanes), bf16),
        in_specs=[whole_in_vmem] * 3,
        out_specs=whole_in_vmem,
        compiler_params=pltpu.CompilerParams(vmem_limit_bytes=2 * 2**20),
        name="pack",
        cost_estimate=pl.CostEstimate(flops=0, bytes_accessed=200000, transcendentals=0),
    )(down, up, after)


def project_kernel(step_count, row_count, head_count, shards, replicas, *refs):
    owners_hbm, lengths_hbm, tokens_ref, weight_ref, queries_ref, turns_ref, _ = refs[:7]
    own_ref = refs[7]
    block_refs = refs[8 : 7 + shards]
    left_ref, pick_ref, asked_ref, grouped_ref, cosine_ref, sine_ref, bias_ref, visible_ref = refs[
        7 + shards : 15 + shards
    ]
    owners_ref, lengths_ref, token_buf, regroup, sems = refs[15 + shards :]
    owners_copy = pltpu.make_async_copy(owners_hbm, owners_ref, sems.at[0])
    lengths_copy = pltpu.make_async_copy(lengths_hbm, lengths_ref, sems.at[1])
    owners_copy.start()
    lengths_copy.start()

    shard = lax.axis_index("tensor")
    rows, own = own_ref.shape
    for i in range(shards):
        first = pl.multiple_of((shard ^ i) * own, lanes)
        block = jnp.dot(
            tokens_ref[...], weight_ref[:, pl.ds(first, own)], preferred_element_type=f32
        )
        if i == 0:
            own_ref[...] = block
        else:
            block_refs[i - 1][...] = block.astype(bf16)

    group = queries_ref.shape[1] // (head_count * lanes)
    seen = step_count * group
    for pair in range(step_count // 2):
        for q in range(head_count * group):
            h, g = q // group, q % group
            both = queries_ref[
                pair * 2 * row_count : (pair + 1) * 2 * row_count, q * lanes : (q + 1) * lanes
            ].astype(f32)
            for side in range(2):
                first = h * row_count * seen + (pair * 2 + side) * group + g
                regroup[pl.ds(first, row_count, stride=seen), :] = both[
                    side * row_count : (side + 1) * row_count, :
                ]
            if g % 2:
                for side in range(2):
                    half = slice(side * row_count, (side + 1) * row_count)
                    last = (h * seen + (pair * 2 + side) * group + g + 1) * row_count
                    grouped_ref[last - 2 * row_count : last, :] = jnp.concatenate(
                        [before[half], both[half]], axis=0
                    ).astype(bf16)
            before = both
    asked_ref[...] = regroup[...].astype(bf16)

    owners_copy.wait()
    replica = lax.axis_index("rollout")
    width = token_buf.shape[2]
    down_rows = tokens_ref.shape[1] // replicas
    for k in range(replicas):
        token_buf[k, :, :down_rows] = tokens_ref[:, k * down_rows : (k + 1) * down_rows]
        if down_rows < width:
            token_buf[k, :, down_rows:] = jnp.zeros((rows, width - down_rows), bf16)
    for i in range(replicas):
        place = jnp.int32(0)
        for k in range(1, replicas):
            place = place + jnp.where(owners_ref[k] == replica ^ i, k, 0)
        left_ref[:, i * width : (i + 1) * width] = token_buf[place]
    if replicas > 1:
        for i in range(shards):
            for k in range(replicas):
                picked = jnp.where(owners_ref[shard ^ i] == replica ^ k, 1.0, 0.0)
                row = i * replicas + k
                pick_ref[row : row + 1, :] = jnp.full((1, lanes), picked, f32)

    lengths_copy.wait()
    row = lax.broadcasted_iota(jnp.int32, (rows, lanes), 0)
    lane = lax.broadcasted_iota(jnp.int32, (rows, lanes), 1)
    position = row // row_count
    for b in range(row_count):
        position = position + jnp.where(row % row_count == b, lengths_ref[b], 0)
    angles = position.astype(f32) * turns_ref[:1, :]
    cosine_ref[...] = jnp.cos(angles)
    sine = jnp.sin(angles)
    sine_ref[...] = jnp.where(lane < lanes // 2, -sine, sine)
    slot = lax.broadcasted_iota(jnp.int32, bias_ref.shape, 1)
    whose = lax.broadcasted_iota(jnp.int32, bias_ref.shape, 0)
    length = jnp.zeros(bias_ref.shape, jnp.int32)
    for b in range(row_count):
        length = jnp.where(whose == b, lengths_ref[b], length)
    bias_ref[...] = jnp.where(slot < length, 0.0, masked_score)
    all_rows = row_count * seen
    seen_by = lax.broadcasted_iota(jnp.int32, (all_rows, rows), 0)
    made_by = lax.broadcasted_iota(jnp.int32, (all_rows, rows), 1)
    visible = (seen_by % row_count == made_by % row_count) & (
        made_by // row_count <= seen_by // (row_count * group)
    )
    visible_ref[...] = jnp.where(visible, 0.0, masked_score)


def project(
    owners, lengths, tokens, weight, queries, turns, after, step_count, head_count, slots, shards, replicas
):
    rows, depth = tokens.shape
    row_count = rows // step_count
    own = weight.shape[1] // shards
    piece_width = -(-depth // replicas // lanes) * lanes
    seen_rows = rows * queries.shape[1] // lanes
    table = jax.ShapeDtypeStruct((rows, lanes), f32)
    mine, *rest = pl.pallas_call(
        functools.partial(project_kernel, step_count, row_count, head_count, shards, replicas),
        out_shape=[jax.ShapeDtypeStruct((rows, own), f32)]
        + [jax.ShapeDtypeStruct((rows, own), bf16)] * (shards - 1)
        + [
            jax.ShapeDtypeStruct((rows, replicas * piece_width), bf16),
            jax.ShapeDtypeStruct((shards * replicas, lanes), f32),
            jax.ShapeDtypeStruct((seen_rows, lanes), bf16),
            jax.ShapeDtypeStruct((seen_rows, lanes), bf16),
            table,
            table,
            jax.ShapeDtypeStruct((row_count, slots), f32),
            jax.ShapeDtypeStruct((seen_rows // head_count, rows), f32),
        ],
        in_specs=[stays_in_hbm] * 2 + [whole_in_vmem] * 5,
        out_specs=[whole_in_vmem] * (shards + 8),
        scratch_shapes=[
            pltpu.SMEM(owners.shape, jnp.int32),
            pltpu.SMEM(lengths.shape, jnp.int32),
            pltpu.VMEM((replicas, rows, piece_width), bf16),
            pltpu.VMEM((seen_rows, lanes), f32),
            pltpu.SemaphoreType.DMA((2,)),
        ],
        compiler_params=pltpu.CompilerParams(vmem_limit_bytes=6 * 2**20),
        name="project",
        cost_estimate=pl.CostEstimate(
            flops=2 * rows * weight.size, bytes_accessed=2 * weight.size, transcendentals=0
        ),
    )(*in_hbm(owners, lengths), tokens, weight, queries, turns, after)
    return mine, rest[: shards - 1], *rest[shards - 1 :]


def attend_kernel(
    head_count,
    asked_ref,
    keys_ref,
    values_ref,
    bias_ref,
    _,
    mine_ref,
    *refs,
):
    other_refs = refs[:-6]
    base_ref, total_ref, peak_ref, sum_ref, scores_ref, raised = refs[-6:]
    base = mine_ref[...]
    for other_ref in other_refs:
        base = base + other_ref[...].astype(f32)
    base_ref[...] = base

    row_count, slots, _ = keys_ref.shape
    seen = asked_ref.shape[0] // (head_count * row_count)

    for b in range(row_count):
        for h in range(head_count):
            at = (h * row_count + b) * seen
            scores_ref[at : at + seen, :] = lax.dot_general(
                asked_ref[at : at + seen, :],
                keys_ref[b, :, h * lanes : (h + 1) * lanes],
                (((1,), (1,)), ((), ())),
                preferred_element_type=f32,
            )

    places = [
        (
            b,
            h,
            slice((h * row_count + b) * seen, (h * row_count + b + 1) * seen),
            pl.ds(h * row_count * seen + b, seen, stride=row_count),
        )
        for b in range(row_count)
        for h in range(head_count)
    ]
    for b, h, place, out in places:
        score = scores_ref[place, :] + bias_ref[b : b + 1, :]
        peak = jnp.max(score, axis=1, keepdims=True)
        lifted = jnp.exp2((score - peak) * exponent_scale)
        raised[place, :] = lifted.astype(bf16)
        peak_ref[out, :] = jnp.broadcast_to(peak, (seen, lanes))
        sum_ref[out, :] = jnp.broadcast_to(
            jnp.sum(lifted, axis=1, keepdims=True), (seen, lanes)
        )
    for b, h, place, out in places:
        total_ref[out, :] = jnp.dot(
            raised[place, :],
            values_ref[b, :, h * lanes : (h + 1) * lanes],
            preferred_element_type=f32,
        )


def attend(asked, keys, values, bias, after, mine, others):
    row_count, slots, width = keys.shape
    seen_rows = asked.shape[0]
    seen_table = jax.ShapeDtypeStruct((seen_rows, lanes), f32)
    return pl.pallas_call(
        functools.partial(attend_kernel, width // lanes),
        out_shape=(jax.ShapeDtypeStruct(mine.shape, f32),) + (seen_table,) * 3,
        in_specs=[whole_in_vmem] * (6 + len(others)),
        out_specs=(whole_in_vmem,) * 4,
        scratch_shapes=[
            pltpu.VMEM((seen_rows, slots), f32),
            pltpu.VMEM((seen_rows, slots), bf16),
        ],
        compiler_params=pltpu.CompilerParams(vmem_limit_bytes=8 * 2**20),
        name="attend",
        cost_estimate=pl.CostEstimate(
            flops=4 * seen_rows * slots * lanes,
            bytes_accessed=2 * (keys.size + values.size),
            transcendentals=seen_rows * slots,
        ),
    )(asked, keys, values, bias, after, mine, *others)


def piece_places(replicas):
    order = [0, 1] + list(range(replicas - 1, 1, -1))
    return [order.index(i) for i in range(replicas)]


def route_kernel(replicas, shards, *refs):
    left_ref, pick_ref = refs[:2]
    piece_refs = [refs[2 + place] for place in piece_places(replicas)]
    out_refs = refs[2 + replicas : 2 + replicas + shards]
    (right,) = refs[2 + replicas + shards :]
    up_rows = out_refs[0].shape[0] - left_ref.shape[0] // 2
    rows = left_ref.shape[0]
    rank = right.shape[0]
    width = right.shape[1] // replicas
    half = rank // 2
    rest = (piece_refs[0].shape[0] - up_rows) % rank
    for i in range(replicas):
        first = 0
        for c in range(width // lanes - (1 if rest else 0)):
            right[:, i * width + c * lanes : i * width + (c + 1) * lanes] = piece_refs[i][
                first : first + rank, :
            ]
            first += rank
        if rest:
            both = piece_refs[i][first : first + half, :]
            tail = jnp.concatenate([both[:, : lanes // 2], both[:, lanes // 2 :]], axis=0)
            right[:, (i + 1) * width - lanes : (i + 1) * width] = jnp.concatenate(
                [tail, jnp.zeros((rank, lanes // 2), bf16)], axis=1
            )
            first += half
    lowered = lax.dot_general(
        left_ref[...], right[...], (((1,), (1,)), ((), ())), preferred_element_type=f32
    )
    sent = pack_rows(lowered.astype(bf16))
    ups = [piece[piece.shape[0] - up_rows :, :].astype(f32) for piece in piece_refs]
    for i in range(shards):
        out_refs[i][: rows // 2, :] = sent
        picked = sum(up * pick_ref[i * replicas + k, :][None, :] for k, up in enumerate(ups))
        out_refs[i][rows // 2 :, :] = picked.astype(bf16)


def route(left, pick, pieces, rank, up_rows, shards):
    rows, depth = left.shape
    replicas = len(pieces)
    return pl.pallas_call(
        functools.partial(route_kernel, replicas, shards),
        out_shape=[jax.ShapeDtypeStruct((rows // 2 + up_rows, lanes), bf16)] * shards,
        in_specs=[whole_in_vmem] * (2 + replicas),
        out_specs=[whole_in_vmem] * shards,
        scratch_shapes=[pltpu.VMEM((rank, depth), bf16)],
        compiler_params=pltpu.CompilerParams(vmem_limit_bytes=4 * 2**20),
        name="route",
        cost_estimate=pl.CostEstimate(flops=0, bytes_accessed=800000, transcendentals=0),
    )(left, pick, *[pieces[i] for i in piece_places(replicas)])


def route_plain(owners, tokens, down, up, rank_part, own, shards):
    rank = down.shape[1]
    shard = lax.axis_index("tensor")
    first = shard * rank_part
    up_part = lax.dynamic_slice_in_dim(up, first, rank_part, axis=0)
    downs = lax.all_gather(down, "rollout", axis=0, tiled=False)
    ups = lax.all_gather(up_part, "rollout", axis=0, tiled=False)
    down_matrix = jnp.take(downs, owners, axis=0, mode="clip").reshape(-1, rank)
    up_matrix = jnp.take(ups, owners, axis=0, mode="clip").transpose(1, 0, 2)
    up_matrix = up_matrix.reshape(rank_part, -1)
    lowered = jnp.dot(tokens, down_matrix, preferred_element_type=f32)
    sent = pack_rows(lowered.astype(bf16))
    packets = []
    for i in range(shards):
        up_block = lax.dynamic_slice_in_dim(up_matrix, (shard ^ i) * own, own, axis=1)
        parts = [sent, side_by_side(up_block)]
        packets.append(jnp.concatenate(parts, axis=0))
    return packets


def finish_kernel(step_count, row_count, head_count, shards, *refs):
    gain_ref, base_ref, grouped_ref, total_ref, peak_ref, sum_ref, cosine_ref, sine_ref = refs[:8]
    packet_refs = refs[8 : 8 + shards][::-1]
    visible_ref, attention_ref, keys_ref, values_ref, up_buf = refs[8 + shards :]
    shard = lax.axis_index("tensor")
    rows = step_count * row_count
    own = base_ref.shape[1]
    blocks = own // lanes
    rank = up_buf.shape[0]
    rank_part = rank // shards
    group = grouped_ref.shape[0] // (head_count * rows)
    seen = step_count * group

    half = rows // 2
    packed = jnp.zeros((half, lanes), f32)
    for i in range(shards):
        packed = packed + packet_refs[i][:half, :].astype(f32)
        ups = packet_refs[i][half:, :].astype(up_buf.dtype)
        at = pl.multiple_of((shard ^ i) * rank_part, rank_part)
        for c in range(blocks):
            up_buf[pl.ds(at, rank_part), c * lanes : (c + 1) * lanes] = ups[
                c * rank_part : (c + 1) * rank_part, :
            ]
    turned = pltpu.roll(packed, rank, 1)
    first = lax.broadcasted_iota(jnp.int32, (half, lanes), 1) < rank
    lowered = jnp.concatenate(
        [jnp.where(first, packed, turned), jnp.where(first, turned, packed)], axis=0
    )
    lane = lax.broadcasted_iota(jnp.int32, (rows, lanes), 1)
    high, low = split_halves(lowered)
    left = jnp.where(lane < rank, high.astype(f32), low.astype(f32)).astype(bf16)
    up = up_buf[...].astype(bf16)
    raised_up = jnp.dot(left, jnp.concatenate([up, up], axis=0), preferred_element_type=f32)
    joined = []
    for c in range(blocks):
        block = base_ref[:, c * lanes : (c + 1) * lanes]
        joined.append(block + adapter_scale * raised_up[:, c * lanes : (c + 1) * lanes])

    all_rows = row_count * seen
    heads = [(h, slice(h * all_rows, (h + 1) * all_rows)) for h in range(head_count)]
    keys, values, scores, results = [], [], [], []
    for h, _ in heads:
        raw_key = joined[2 * h]
        mean_square = jnp.mean(raw_key * raw_key, axis=1, keepdims=True)
        normed = raw_key * lax.rsqrt(mean_square + norm_eps) * gain_ref[...]
        key = normed * cosine_ref[...] + pltpu.roll(normed, lanes // 2, 1) * sine_ref[...]
        keys.append(key.astype(bf16))
        values.append(joined[2 * h + 1].astype(bf16))
        keys_ref[:, h * lanes : (h + 1) * lanes] = keys[h]
        values_ref[:, h * lanes : (h + 1) * lanes] = values[h]
    for h, mine in heads:
        score = lax.dot_general(
            grouped_ref[mine, :], keys[h], (((1,), (1,)), ((), ())), preferred_element_type=f32
        )
        scores.append(score + visible_ref[...])
    for h, mine in heads:
        old_peak = peak_ref[mine, :]
        peak = jnp.maximum(old_peak, jnp.max(scores[h], axis=1, keepdims=True))
        fade = jnp.exp2((old_peak - peak) * exponent_scale)
        lifted = jnp.exp2((scores[h] - peak[:, :rows]) * exponent_scale)
        weights, left_over = split_halves(lifted)
        ones = jnp.ones((rows, lanes), bf16)
        denominator = (
            fade * sum_ref[mine, :]
            + jnp.dot(weights, ones, preferred_element_type=f32)
            + jnp.dot(left_over, ones, preferred_element_type=f32)
        )
        total = fade * total_ref[mine, :] + jnp.dot(
            weights, values[h], preferred_element_type=f32
        )
        results.append(total / denominator)
    for pair in range(step_count // 2):
        for q in range(head_count * group):
            h, g = q // group, q % group
            both = []
            for side in range(2):
                first = ((pair * 2 + side) * group + g) * row_count
                both.append(results[h][first : first + row_count])
            attention_ref[
                pair * 2 * row_count : (pair + 1) * 2 * row_count, q * lanes : (q + 1) * lanes
            ] = jnp.concatenate(both, axis=0).astype(bf16)


def finish(base, visible, partials, gain, packets, rank, step_count, row_count, query_width):
    rows, own = base.shape
    shards = len(packets)
    head_count = own // (2 * lanes)
    return pl.pallas_call(
        functools.partial(finish_kernel, step_count, row_count, head_count, shards),
        out_shape=(
            jax.ShapeDtypeStruct((rows, query_width), bf16),
            jax.ShapeDtypeStruct((rows, head_count * lanes), bf16),
            jax.ShapeDtypeStruct((rows, head_count * lanes), bf16),
        ),
        in_specs=[whole_in_vmem] * (9 + shards),
        out_specs=(whole_in_vmem,) * 3,
        scratch_shapes=[
            pltpu.VMEM((rank, own), bf16 if rank // shards % 16 == 0 else f32),
        ],
        compiler_params=pltpu.CompilerParams(vmem_limit_bytes=6 * 2**20),
        name="finish",
        cost_estimate=pl.CostEstimate(flops=0, bytes_accessed=1000000, transcendentals=0),
    )(gain, base, *partials, *packets[::-1], visible)


def per_device(
    normed_tokens,
    key_value_weight,
    adapter_down,
    adapter_up,
    key_gain,
    queries,
    cache_keys,
    stored_values,
    lengths,
    owners,
):
    replicas = lax.axis_size("rollout")
    shards = lax.axis_size("tensor")
    down_rows, rank = adapter_down.shape
    step_count, row_count, depth = normed_tokens.shape
    own = key_value_weight.shape[1] // shards
    rank_part = rank // shards
    rows = step_count * row_count
    tokens = normed_tokens.reshape(rows, depth)
    query_rows = queries.reshape(rows, -1)

    fits = (
        replicas <= 4
        and adapter_up.shape[1] == own
        and down_rows % lanes in (0, lanes // 2)
        and rank == lanes // 2
        and rank_part % 16 == 0
    )
    fetched = 2 * (key_value_weight.size + cache_keys.size + stored_values.size)
    turns = frequencies(
        pl.CostEstimate(flops=1000 * fetched, bytes_accessed=fetched, transcendentals=0)
    )
    if fits:
        packed = pack(adapter_down.T, adapter_up, rank_part, turns)
        pieces = [packed] + [swap(packed, "rollout", i) for i in range(1, replicas)]
    mine, blocks, left, pick, asked, grouped, cosine, sine, bias, visible = project(
        owners,
        lengths,
        tokens,
        key_value_weight,
        query_rows,
        turns,
        packed if fits else adapter_up,
        step_count,
        cache_keys.shape[2] // lanes,
        cache_keys.shape[1],
        shards,
        replicas if fits else 1,
    )
    others = [swap(block, "tensor", i + 1) for i, block in enumerate(blocks)]
    if fits:
        packets = route(left, pick, pieces, rank, rank_part * own // lanes, shards)
    else:
        packets = route_plain(
            owners, tokens, adapter_down, adapter_up, rank_part, own, shards
        )
    base, total, peak, denominator = attend(
        asked, cache_keys, stored_values, bias, packets[0], mine, others
    )
    packets = [packets[0]] + [swap(packets[i], "tensor", i) for i in range(1, shards)]
    attention, keys, values = finish(
        base,
        visible,
        (grouped, total, peak, denominator, cosine, sine),
        key_gain.reshape(1, -1),
        packets,
        rank,
        step_count,
        row_count,
        query_rows.shape[1],
    )
    return tuple(a.reshape(step_count, row_count, -1) for a in (attention, keys, values))


def solution(mesh):
    placed = (
        P(None, ("job", "rollout"), "tensor"),
        P("tensor", None),
        P(("job", "rollout", "tensor"), None),
        P(None, ("job", "rollout")),
        P(),
        P(None, ("job", "rollout"), "tensor"),
        P(("job", "rollout"), None, "tensor"),
        P(("job", "rollout"), None, "tensor"),
        P(("job", "rollout")),
        P("job"),
    )
    return jax.shard_map(
        per_device,
        mesh=mesh,
        in_specs=placed,
        out_specs=(
            P(None, ("job", "rollout"), "tensor"),
            P(None, ("job", "rollout"), "tensor"),
            P(None, ("job", "rollout"), "tensor"),
        ),
        check_vma=False,
    )
```

```python
import functools
import math

import jax
import jax.numpy as jnp
from jax import lax
from jax.experimental import pallas as pl
from jax.experimental.pallas import tpu as pltpu
from jax.sharding import PartitionSpec as P

norm_eps = 1e-06
rope_base = 1000000.0
adapter_scale = 2.0
masked_score = -1e30
lanes = 128
exponent_scale = lanes**-0.5 / math.log(2.0)
f32 = jnp.float32
bf16 = jnp.bfloat16

whole_in_vmem = pl.BlockSpec(memory_space=pltpu.VMEM)
whole_in_smem = pl.BlockSpec(memory_space=pltpu.SMEM)
stays_in_hbm = pl.BlockSpec(memory_space=pltpu.HBM)


def swap(block, axis, offset):
    count = lax.axis_size(axis)
    return lax.ppermute(block, axis, [(s, s ^ offset) for s in range(count)])


def send(block, axis, offset, down):
    count = lax.axis_size(axis)
    pairs = [(s, s ^ offset) for s in range(count)]
    return lax.ppermute(block, axis, [(s, d) for s, d in pairs if (s > d) == down])


def in_hbm(*arrays):
    return tuple(pltpu.with_memory_space_constraint(a, pltpu.HBM) for a in arrays)


def side_by_side(rows_of_blocks):
    r, c = rows_of_blocks.shape
    return rows_of_blocks.reshape(r, c // lanes, lanes).transpose(1, 0, 2).reshape(-1, lanes)


def split_halves(total):
    high = total.astype(bf16)
    return high, (total - high.astype(f32)).astype(bf16)


def frequencies_kernel(out_ref):
    lane = lax.broadcasted_iota(jnp.int32, out_ref.shape, 1)
    spacing = (lane % (lanes // 2)).astype(f32) * (-2.0 / lanes * math.log(rope_base))
    out_ref[...] = jnp.exp(spacing)


def frequencies(beside):
    return pl.pallas_call(
        frequencies_kernel,
        out_shape=jax.ShapeDtypeStruct((8, lanes), f32),
        out_specs=whole_in_vmem,
        compiler_params=pltpu.CompilerParams(vmem_limit_bytes=2**20),
        name="frequencies",
        cost_estimate=beside,
    )()


def pack_kernel(down_ref, up_all_ref, _, out_ref):
    rank, down_rows = down_ref.shape
    rank_part = (out_ref.shape[0] * lanes - down_ref.size) // up_all_ref.shape[1]
    start = pl.multiple_of(lax.axis_index("tensor") * rank_part, rank_part)
    up_ref = up_all_ref.at[pl.ds(start, rank_part), :]
    first = 0
    for c in range(down_rows // lanes):
        out_ref[first : first + rank, :] = down_ref[:, c * lanes : (c + 1) * lanes]
        first += rank
    rest = down_rows % lanes
    if rest:
        half = rank // 2
        tail = down_ref[:, down_rows - rest :]
        out_ref[first : first + half, :] = jnp.concatenate([tail[:half], tail[half:]], axis=1)
        first += half
    for c in range(up_ref.shape[1] // lanes):
        out_ref[first : first + rank_part, :] = up_ref[:, c * lanes : (c + 1) * lanes]
        first += rank_part


def pack(down, up, rank_part, after):
    rows = (down.size + rank_part * up.shape[1]) // lanes
    return pl.pallas_call(
        pack_kernel,
        out_shape=jax.ShapeDtypeStruct((rows, lanes), bf16),
        in_specs=[whole_in_vmem] * 3,
        out_specs=whole_in_vmem,
        compiler_params=pltpu.CompilerParams(vmem_limit_bytes=2 * 2**20),
        name="pack",
        cost_estimate=pl.CostEstimate(flops=0, bytes_accessed=200000, transcendentals=0),
    )(down, up, after)


def project_kernel(step_count, row_count, head_count, shards, replicas, *refs):
    owners_hbm, lengths_hbm, tokens_ref, weight_ref, queries_ref, turns_ref, _ = refs[:7]
    own_ref = refs[7]
    block_refs = refs[8 : 7 + shards]
    left_ref, pick_ref, asked_ref, grouped_ref, cosine_ref, sine_ref, bias_ref, visible_ref = refs[
        7 + shards : 15 + shards
    ]
    owners_ref, lengths_ref, token_buf, regroup, sems = refs[15 + shards :]
    owners_copy = pltpu.make_async_copy(owners_hbm, owners_ref, sems.at[0])
    lengths_copy = pltpu.make_async_copy(lengths_hbm, lengths_ref, sems.at[1])
    owners_copy.start()
    lengths_copy.start()

    shard = lax.axis_index("tensor")
    rows, own = own_ref.shape
    for i in range(shards):
        first = pl.multiple_of((shard ^ i) * own, lanes)
        block = jnp.dot(
            tokens_ref[...], weight_ref[:, pl.ds(first, own)], preferred_element_type=f32
        )
        if i == 0:
            own_ref[...] = block
        else:
            block_refs[i - 1][...] = block.astype(bf16)

    group = queries_ref.shape[1] // (head_count * lanes)
    seen = step_count * group
    for pair in range(step_count // 2):
        for q in range(head_count * group):
            h, g = q // group, q % group
            both = queries_ref[
                pair * 2 * row_count : (pair + 1) * 2 * row_count, q * lanes : (q + 1) * lanes
            ].astype(f32)
            for side in range(2):
                first = h * row_count * seen + (pair * 2 + side) * group + g
                regroup[pl.ds(first, row_count, stride=seen), :] = both[
                    side * row_count : (side + 1) * row_count, :
                ]
            if g % 2:
                for side in range(2):
                    half = slice(side * row_count, (side + 1) * row_count)
                    last = (h * seen + (pair * 2 + side) * group + g + 1) * row_count
                    grouped_ref[last - 2 * row_count : last, :] = jnp.concatenate(
                        [before[half], both[half]], axis=0
                    ).astype(bf16)
            before = both
    asked_ref[...] = regroup[...].astype(bf16)

    owners_copy.wait()
    replica = lax.axis_index("rollout")
    width = token_buf.shape[2]
    down_rows = tokens_ref.shape[1] // replicas
    for k in range(replicas):
        token_buf[k, :, :down_rows] = tokens_ref[:, k * down_rows : (k + 1) * down_rows]
        if down_rows < width:
            token_buf[k, :, down_rows:] = jnp.zeros((rows, width - down_rows), bf16)
    for i in range(replicas):
        place = jnp.int32(0)
        for k in range(1, replicas):
            place = place + jnp.where(owners_ref[k] == replica ^ i, k, 0)
        left_ref[:, i * width : (i + 1) * width] = token_buf[place]
    if replicas > 1:
        for i in range(shards):
            for k in range(replicas):
                picked = jnp.where(owners_ref[shard ^ i] == replica ^ k, 1.0, 0.0)
                row = i * replicas + k
                pick_ref[row : row + 1, :] = jnp.full((1, lanes), picked, f32)

    lengths_copy.wait()
    row = lax.broadcasted_iota(jnp.int32, (rows, lanes), 0)
    lane = lax.broadcasted_iota(jnp.int32, (rows, lanes), 1)
    position = row // row_count
    for b in range(row_count):
        position = position + jnp.where(row % row_count == b, lengths_ref[b], 0)
    angles = position.astype(f32) * turns_ref[:1, :]
    cosine_ref[...] = jnp.cos(angles)
    sine = jnp.sin(angles)
    sine_ref[...] = jnp.where(lane < lanes // 2, -sine, sine)
    slot = lax.broadcasted_iota(jnp.int32, bias_ref.shape, 1)
    whose = lax.broadcasted_iota(jnp.int32, bias_ref.shape, 0)
    length = jnp.zeros(bias_ref.shape, jnp.int32)
    for b in range(row_count):
        length = jnp.where(whose == b, lengths_ref[b], length)
    bias_ref[...] = jnp.where(slot < length, 0.0, masked_score)
    all_rows = row_count * seen
    seen_by = lax.broadcasted_iota(jnp.int32, (all_rows, rows), 0)
    made_by = lax.broadcasted_iota(jnp.int32, (all_rows, rows), 1)
    visible = (seen_by % row_count == made_by % row_count) & (
        made_by // row_count <= seen_by // (row_count * group)
    )
    visible_ref[...] = jnp.where(visible, 0.0, masked_score)


def project(
    owners, lengths, tokens, weight, queries, turns, after, step_count, head_count, slots, shards, replicas
):
    rows, depth = tokens.shape
    row_count = rows // step_count
    own = weight.shape[1] // shards
    piece_width = -(-depth // replicas // lanes) * lanes
    seen_rows = rows * queries.shape[1] // lanes
    table = jax.ShapeDtypeStruct((rows, lanes), f32)
    mine, *rest = pl.pallas_call(
        functools.partial(project_kernel, step_count, row_count, head_count, shards, replicas),
        out_shape=[jax.ShapeDtypeStruct((rows, own), f32)]
        + [jax.ShapeDtypeStruct((rows, own), bf16)] * (shards - 1)
        + [
            jax.ShapeDtypeStruct((rows, replicas * piece_width), bf16),
            jax.ShapeDtypeStruct((shards * replicas, lanes), f32),
            jax.ShapeDtypeStruct((seen_rows, lanes), bf16),
            jax.ShapeDtypeStruct((seen_rows, lanes), bf16),
            table,
            table,
            jax.ShapeDtypeStruct((row_count, slots), f32),
            jax.ShapeDtypeStruct((seen_rows // head_count, rows), f32),
        ],
        in_specs=[stays_in_hbm] * 2 + [whole_in_vmem] * 5,
        out_specs=[whole_in_vmem] * (shards + 8),
        scratch_shapes=[
            pltpu.SMEM(owners.shape, jnp.int32),
            pltpu.SMEM(lengths.shape, jnp.int32),
            pltpu.VMEM((replicas, rows, piece_width), bf16),
            pltpu.VMEM((seen_rows, lanes), f32),
            pltpu.SemaphoreType.DMA((2,)),
        ],
        compiler_params=pltpu.CompilerParams(vmem_limit_bytes=6 * 2**20),
        name="project",
        cost_estimate=pl.CostEstimate(
            flops=2 * rows * weight.size, bytes_accessed=2 * weight.size, transcendentals=0
        ),
    )(*in_hbm(owners, lengths), tokens, weight, queries, turns, after)
    return mine, rest[: shards - 1], *rest[shards - 1 :]


def attend_kernel(
    head_count,
    asked_ref,
    keys_ref,
    values_ref,
    bias_ref,
    _,
    mine_ref,
    *refs,
):
    other_refs = refs[:-6]
    base_ref, total_ref, peak_ref, sum_ref, scores_ref, raised = refs[-6:]
    base = mine_ref[...]
    for other_ref in other_refs:
        base = base + other_ref[...].astype(f32)
    base_ref[...] = base

    row_count, slots, _ = keys_ref.shape
    seen = asked_ref.shape[0] // (head_count * row_count)

    for b in range(row_count):
        for h in range(head_count):
            at = (h * row_count + b) * seen
            scores_ref[at : at + seen, :] = lax.dot_general(
                asked_ref[at : at + seen, :],
                keys_ref[b, :, h * lanes : (h + 1) * lanes],
                (((1,), (1,)), ((), ())),
                preferred_element_type=f32,
            )

    places = [
        (
            b,
            h,
            slice((h * row_count + b) * seen, (h * row_count + b + 1) * seen),
            pl.ds(h * row_count * seen + b, seen, stride=row_count),
        )
        for b in range(row_count)
        for h in range(head_count)
    ]
    for b, h, place, out in places:
        score = scores_ref[place, :] + bias_ref[b : b + 1, :]
        peak = jnp.max(score, axis=1, keepdims=True)
        lifted = jnp.exp2((score - peak) * exponent_scale)
        raised[place, :] = lifted.astype(bf16)
        peak_ref[out, :] = jnp.broadcast_to(peak, (seen, lanes))
        sum_ref[out, :] = jnp.broadcast_to(
            jnp.sum(lifted, axis=1, keepdims=True), (seen, lanes)
        )
    for b, h, place, out in places:
        total_ref[out, :] = jnp.dot(
            raised[place, :],
            values_ref[b, :, h * lanes : (h + 1) * lanes],
            preferred_element_type=f32,
        )


def attend(asked, keys, values, bias, after, mine, others):
    row_count, slots, width = keys.shape
    seen_rows = asked.shape[0]
    seen_table = jax.ShapeDtypeStruct((seen_rows, lanes), f32)
    return pl.pallas_call(
        functools.partial(attend_kernel, width // lanes),
        out_shape=(jax.ShapeDtypeStruct(mine.shape, f32),) + (seen_table,) * 3,
        in_specs=[whole_in_vmem] * (6 + len(others)),
        out_specs=(whole_in_vmem,) * 4,
        scratch_shapes=[
            pltpu.VMEM((seen_rows, slots), f32),
            pltpu.VMEM((seen_rows, slots), bf16),
        ],
        compiler_params=pltpu.CompilerParams(vmem_limit_bytes=8 * 2**20),
        name="attend",
        cost_estimate=pl.CostEstimate(
            flops=4 * seen_rows * slots * lanes,
            bytes_accessed=2 * (keys.size + values.size),
            transcendentals=seen_rows * slots,
        ),
    )(asked, keys, values, bias, after, mine, *others)


def arrival_order(shards):
    far = range(2, shards)
    order = [(i, True) for i in far] + [(i, False) for i in far]
    return order + [(1, None), (0, None)]


def piece_order(replicas):
    return [0, 1] + list(range(replicas - 1, 1, -1))


def route_kernel(replicas, shards, *refs):
    left_ref, pick_ref = refs[:2]
    order = piece_order(replicas)
    piece_refs = [refs[2 + order.index(i)] for i in range(replicas)]
    names = arrival_order(shards)
    out_refs = dict(zip(names, refs[2 + replicas : 2 + replicas + len(names)]))
    (right,) = refs[2 + replicas + len(names) :]
    up_rows = out_refs[0, None].shape[0] - left_ref.shape[0]
    rows = left_ref.shape[0]
    rank = right.shape[0]
    width = right.shape[1] // replicas
    half = rank // 2
    rest = (piece_refs[0].shape[0] - up_rows) % rank
    for i in range(replicas):
        first = 0
        for c in range(width // lanes - (1 if rest else 0)):
            right[:, i * width + c * lanes : i * width + (c + 1) * lanes] = piece_refs[i][
                first : first + rank, :
            ]
            first += rank
        if rest:
            both = piece_refs[i][first : first + half, :]
            tail = jnp.concatenate([both[:, : lanes // 2], both[:, lanes // 2 :]], axis=0)
            right[:, (i + 1) * width - lanes : (i + 1) * width] = jnp.concatenate(
                [tail, jnp.zeros((rank, lanes // 2), bf16)], axis=1
            )
            first += half
    lowered = lax.dot_general(
        left_ref[...], right[...], (((1,), (1,)), ((), ())), preferred_element_type=f32
    )
    both = jnp.concatenate(split_halves(lowered), axis=1)
    ups = [piece[piece.shape[0] - up_rows :, :].astype(f32) for piece in piece_refs]
    for i in range(shards):
        picked = sum(up * pick_ref[i * replicas + k, :][None, :] for k, up in enumerate(ups))
        for (offset, _), out_ref in out_refs.items():
            if offset == i:
                out_ref[:rows, :] = both
                out_ref[rows:, :] = picked.astype(bf16)


def route(left, pick, pieces, rank, up_rows, shards):
    rows, depth = left.shape
    replicas = len(pieces)
    names = arrival_order(shards)
    packets = pl.pallas_call(
        functools.partial(route_kernel, replicas, shards),
        out_shape=[jax.ShapeDtypeStruct((rows + up_rows, lanes), bf16)] * len(names),
        in_specs=[whole_in_vmem] * (2 + replicas),
        out_specs=[whole_in_vmem] * len(names),
        scratch_shapes=[pltpu.VMEM((rank, depth), bf16)],
        compiler_params=pltpu.CompilerParams(vmem_limit_bytes=4 * 2**20),
        name="route",
        cost_estimate=pl.CostEstimate(flops=0, bytes_accessed=800000, transcendentals=0),
    )(left, pick, *[pieces[i] for i in piece_order(replicas)])
    return dict(zip(names, packets))


def route_plain(owners, tokens, down, up, rank_part, own, shards):
    rank = down.shape[1]
    shard = lax.axis_index("tensor")
    first = shard * rank_part
    up_part = lax.dynamic_slice_in_dim(up, first, rank_part, axis=0)
    downs = lax.all_gather(down, "rollout", axis=0, tiled=False)
    ups = lax.all_gather(up_part, "rollout", axis=0, tiled=False)
    down_matrix = jnp.take(downs, owners, axis=0, mode="clip").reshape(-1, rank)
    up_matrix = jnp.take(ups, owners, axis=0, mode="clip").transpose(1, 0, 2)
    up_matrix = up_matrix.reshape(rank_part, -1)
    lowered = jnp.dot(tokens, down_matrix, preferred_element_type=f32)
    both = jnp.concatenate(split_halves(lowered), axis=1)
    packets = []
    for i in range(shards):
        up_block = lax.dynamic_slice_in_dim(up_matrix, (shard ^ i) * own, own, axis=1)
        parts = [both, side_by_side(up_block)]
        packets.append(jnp.concatenate(parts, axis=0))
    return {(i, down): packets[i] for i, down in arrival_order(shards)}


def finish_kernel(step_count, row_count, head_count, shards, *refs):
    gain_ref, base_ref, grouped_ref, total_ref, peak_ref, sum_ref, cosine_ref, sine_ref = refs[:8]
    names = arrival_order(shards)
    parts = dict(zip(names, refs[8 : 8 + len(names)]))
    arrivals = [[ref for (i, _), ref in parts.items() if i == offset] for offset in range(shards)]
    visible_ref = refs[8 + len(names)]
    attention_ref, keys_ref, values_ref, up_buf = refs[9 + len(names) :]
    shard = lax.axis_index("tensor")
    rows = step_count * row_count
    own = base_ref.shape[1]
    blocks = own // lanes
    rank = up_buf.shape[0]
    rank_part = rank // shards
    group = grouped_ref.shape[0] // (head_count * rows)
    seen = step_count * group

    lowered = jnp.zeros((rows, lanes), f32)
    for i in range(shards):
        packet = sum(part[...].astype(f32) for part in arrivals[i])
        lowered = lowered + packet[:rows, :]
        ups = packet[rows:, :].astype(up_buf.dtype)
        at = pl.multiple_of((shard ^ i) * rank_part, rank_part)
        for c in range(blocks):
            up_buf[pl.ds(at, rank_part), c * lanes : (c + 1) * lanes] = ups[
                c * rank_part : (c + 1) * rank_part, :
            ]
    lane = lax.broadcasted_iota(jnp.int32, (rows, lanes), 1)
    lowered = lowered + pltpu.roll(lowered, rank, 1)
    high, low = split_halves(lowered)
    left = jnp.where(lane < rank, high.astype(f32), low.astype(f32)).astype(bf16)
    up = up_buf[...].astype(bf16)
    raised_up = jnp.dot(left, jnp.concatenate([up, up], axis=0), preferred_element_type=f32)
    joined = []
    for c in range(blocks):
        block = base_ref[:, c * lanes : (c + 1) * lanes]
        joined.append(block + adapter_scale * raised_up[:, c * lanes : (c + 1) * lanes])

    all_rows = row_count * seen
    heads = [(h, slice(h * all_rows, (h + 1) * all_rows)) for h in range(head_count)]
    keys, values, scores, results = [], [], [], []
    for h, _ in heads:
        raw_key = joined[2 * h]
        mean_square = jnp.mean(raw_key * raw_key, axis=1, keepdims=True)
        normed = raw_key * lax.rsqrt(mean_square + norm_eps) * gain_ref[...]
        key = normed * cosine_ref[...] + pltpu.roll(normed, lanes // 2, 1) * sine_ref[...]
        keys.append(key.astype(bf16))
        values.append(joined[2 * h + 1].astype(bf16))
        keys_ref[:, h * lanes : (h + 1) * lanes] = keys[h]
        values_ref[:, h * lanes : (h + 1) * lanes] = values[h]
    for h, mine in heads:
        score = lax.dot_general(
            grouped_ref[mine, :], keys[h], (((1,), (1,)), ((), ())), preferred_element_type=f32
        )
        scores.append(score + visible_ref[...])
    for h, mine in heads:
        old_peak = peak_ref[mine, :]
        peak = jnp.maximum(old_peak, jnp.max(scores[h], axis=1, keepdims=True))
        fade = jnp.exp2((old_peak - peak) * exponent_scale)
        lifted = jnp.exp2((scores[h] - peak[:, :rows]) * exponent_scale)
        denominator = fade * sum_ref[mine, :] + jnp.sum(lifted, axis=1, keepdims=True)
        total = fade * total_ref[mine, :] + jnp.dot(
            lifted.astype(bf16), values[h], preferred_element_type=f32
        )
        results.append(total / denominator)
    for pair in range(step_count // 2):
        for q in range(head_count * group):
            h, g = q // group, q % group
            both = []
            for side in range(2):
                first = ((pair * 2 + side) * group + g) * row_count
                both.append(results[h][first : first + row_count])
            attention_ref[
                pair * 2 * row_count : (pair + 1) * 2 * row_count, q * lanes : (q + 1) * lanes
            ] = jnp.concatenate(both, axis=0).astype(bf16)


def finish(base, visible, partials, gain, arrived, shards, rank, step_count, row_count, query_width):
    rows, own = base.shape
    head_count = own // (2 * lanes)
    return pl.pallas_call(
        functools.partial(finish_kernel, step_count, row_count, head_count, shards),
        out_shape=(
            jax.ShapeDtypeStruct((rows, query_width), bf16),
            jax.ShapeDtypeStruct((rows, head_count * lanes), bf16),
            jax.ShapeDtypeStruct((rows, head_count * lanes), bf16),
        ),
        in_specs=[whole_in_vmem] * (7 + 2 * shards),
        out_specs=(whole_in_vmem,) * 3,
        scratch_shapes=[
            pltpu.VMEM((rank, own), bf16 if rank // shards % 16 == 0 else f32),
        ],
        compiler_params=pltpu.CompilerParams(vmem_limit_bytes=6 * 2**20),
        name="finish",
        cost_estimate=pl.CostEstimate(flops=0, bytes_accessed=1000000, transcendentals=0),
    )(gain, base, *partials, *[arrived[name] for name in arrival_order(shards)], visible)


def per_device(
    normed_tokens,
    key_value_weight,
    adapter_down,
    adapter_up,
    key_gain,
    queries,
    cache_keys,
    stored_values,
    lengths,
    owners,
):
    replicas = lax.axis_size("rollout")
    shards = lax.axis_size("tensor")
    down_rows, rank = adapter_down.shape
    step_count, row_count, depth = normed_tokens.shape
    own = key_value_weight.shape[1] // shards
    rank_part = rank // shards
    rows = step_count * row_count
    tokens = normed_tokens.reshape(rows, depth)
    query_rows = queries.reshape(rows, -1)

    fits = (
        replicas <= 4
        and adapter_up.shape[1] == own
        and down_rows % lanes in (0, lanes // 2)
        and rank == lanes // 2
        and rank_part % 16 == 0
    )
    fetched = 2 * (key_value_weight.size + cache_keys.size + stored_values.size)
    turns = frequencies(
        pl.CostEstimate(flops=1000 * fetched, bytes_accessed=fetched, transcendentals=0)
    )
    if fits:
        packed = pack(adapter_down.T, adapter_up, rank_part, turns)
        pieces = [packed] + [swap(packed, "rollout", i) for i in range(1, replicas)]
    mine, blocks, left, pick, asked, grouped, cosine, sine, bias, visible = project(
        owners,
        lengths,
        tokens,
        key_value_weight,
        query_rows,
        turns,
        packed if fits else adapter_up,
        step_count,
        cache_keys.shape[2] // lanes,
        cache_keys.shape[1],
        shards,
        replicas if fits else 1,
    )
    others = [swap(block, "tensor", i + 1) for i, block in enumerate(blocks)]
    if fits:
        packets = route(left, pick, pieces, rank, rank_part * own // lanes, shards)
    else:
        packets = route_plain(
            owners, tokens, adapter_down, adapter_up, rank_part, own, shards
        )
    base, total, peak, denominator = attend(
        asked, cache_keys, stored_values, bias, packets[0, None], mine, others
    )
    arrived = {}
    for (i, down), packet in packets.items():
        if i > 1:
            arrived[i, down] = send(packet, "tensor", i, down)
        else:
            arrived[i, down] = swap(packet, "tensor", i) if i else packet
    attention, keys, values = finish(
        base,
        visible,
        (grouped, total, peak, denominator, cosine, sine),
        key_gain.reshape(1, -1),
        arrived,
        shards,
        rank,
        step_count,
        row_count,
        query_rows.shape[1],
    )
    return tuple(a.reshape(step_count, row_count, -1) for a in (attention, keys, values))


def solution(mesh):
    placed = (
        P(None, ("job", "rollout"), "tensor"),
        P("tensor", None),
        P(("job", "rollout", "tensor"), None),
        P(None, ("job", "rollout")),
        P(),
        P(None, ("job", "rollout"), "tensor"),
        P(("job", "rollout"), None, "tensor"),
        P(("job", "rollout"), None, "tensor"),
        P(("job", "rollout")),
        P("job"),
    )
    return jax.shard_map(
        per_device,
        mesh=mesh,
        in_specs=placed,
        out_specs=(
            P(None, ("job", "rollout"), "tensor"),
            P(None, ("job", "rollout"), "tensor"),
            P(None, ("job", "rollout"), "tensor"),
        ),
        check_vma=False,
    )
```

```python
import functools
import math

import jax
import jax.numpy as jnp
from jax import lax
from jax.experimental import pallas as pl
from jax.experimental.pallas import tpu as pltpu
from jax.sharding import PartitionSpec as P

norm_eps = 1e-06
rope_base = 1000000.0
adapter_scale = 2.0
masked_score = -1e30
lanes = 128
exponent_scale = lanes**-0.5 / math.log(2.0)
f32 = jnp.float32
bf16 = jnp.bfloat16

whole_in_vmem = pl.BlockSpec(memory_space=pltpu.VMEM)
whole_in_smem = pl.BlockSpec(memory_space=pltpu.SMEM)
stays_in_hbm = pl.BlockSpec(memory_space=pltpu.HBM)


def swap(block, axis, offset):
    count = lax.axis_size(axis)
    return lax.ppermute(block, axis, [(s, s ^ offset) for s in range(count)])


def in_hbm(*arrays):
    return tuple(pltpu.with_memory_space_constraint(a, pltpu.HBM) for a in arrays)


def side_by_side(rows_of_blocks):
    r, c = rows_of_blocks.shape
    return rows_of_blocks.reshape(r, c // lanes, lanes).transpose(1, 0, 2).reshape(-1, lanes)


def split_halves(total):
    high = total.astype(bf16)
    return high, (total - high.astype(f32)).astype(bf16)


def frequencies_kernel(out_ref):
    lane = lax.broadcasted_iota(jnp.int32, out_ref.shape, 1)
    spacing = (lane % (lanes // 2)).astype(f32) * (-2.0 / lanes * math.log(rope_base))
    out_ref[...] = jnp.exp(spacing)


def frequencies(beside):
    return pl.pallas_call(
        frequencies_kernel,
        out_shape=jax.ShapeDtypeStruct((8, lanes), f32),
        out_specs=whole_in_vmem,
        compiler_params=pltpu.CompilerParams(vmem_limit_bytes=2**20),
        name="frequencies",
        cost_estimate=beside,
    )()


def pack_kernel(down_ref, up_all_ref, _, out_ref):
    rank, down_rows = down_ref.shape
    rank_part = (out_ref.shape[0] * lanes - down_ref.size) // up_all_ref.shape[1]
    start = pl.multiple_of(lax.axis_index("tensor") * rank_part, rank_part)
    up_ref = up_all_ref.at[pl.ds(start, rank_part), :]
    first = 0
    for c in range(down_rows // lanes):
        out_ref[first : first + rank, :] = down_ref[:, c * lanes : (c + 1) * lanes]
        first += rank
    rest = down_rows % lanes
    if rest:
        half = rank // 2
        tail = down_ref[:, down_rows - rest :]
        out_ref[first : first + half, :] = jnp.concatenate([tail[:half], tail[half:]], axis=1)
        first += half
    for c in range(up_ref.shape[1] // lanes):
        out_ref[first : first + rank_part, :] = up_ref[:, c * lanes : (c + 1) * lanes]
        first += rank_part


def pack(down, up, rank_part, after):
    rows = (down.size + rank_part * up.shape[1]) // lanes
    return pl.pallas_call(
        pack_kernel,
        out_shape=jax.ShapeDtypeStruct((rows, lanes), bf16),
        in_specs=[whole_in_vmem] * 3,
        out_specs=whole_in_vmem,
        compiler_params=pltpu.CompilerParams(vmem_limit_bytes=2 * 2**20),
        name="pack",
        cost_estimate=pl.CostEstimate(flops=0, bytes_accessed=200000, transcendentals=0),
    )(down, up, after)


def project_kernel(step_count, row_count, head_count, shards, replicas, *refs):
    owners_hbm, lengths_hbm, tokens_ref, weight_ref, queries_ref, turns_ref, _ = refs[:7]
    own_ref = refs[7]
    block_refs = refs[8 : 7 + shards]
    left_ref, pick_ref, asked_ref, grouped_ref, cosine_ref, sine_ref, bias_ref, visible_ref = refs[
        7 + shards : 15 + shards
    ]
    owners_ref, lengths_ref, token_buf, regroup, sems = refs[15 + shards :]
    owners_copy = pltpu.make_async_copy(owners_hbm, owners_ref, sems.at[0])
    lengths_copy = pltpu.make_async_copy(lengths_hbm, lengths_ref, sems.at[1])
    owners_copy.start()
    lengths_copy.start()

    shard = lax.axis_index("tensor")
    rows, own = own_ref.shape
    for i in range(shards):
        first = pl.multiple_of((shard ^ i) * own, lanes)
        block = jnp.dot(
            tokens_ref[...], weight_ref[:, pl.ds(first, own)], preferred_element_type=f32
        )
        if i == 0:
            own_ref[...] = block
        else:
            block_refs[i - 1][...] = block.astype(bf16)

    group = queries_ref.shape[1] // (head_count * lanes)
    seen = step_count * group
    for pair in range(step_count // 2):
        for q in range(head_count * group):
            h, g = q // group, q % group
            both = queries_ref[
                pair * 2 * row_count : (pair + 1) * 2 * row_count, q * lanes : (q + 1) * lanes
            ].astype(f32)
            for side in range(2):
                first = h * row_count * seen + (pair * 2 + side) * group + g
                regroup[pl.ds(first, row_count, stride=seen), :] = both[
                    side * row_count : (side + 1) * row_count, :
                ]
            if g % 2:
                for side in range(2):
                    half = slice(side * row_count, (side + 1) * row_count)
                    last = (h * seen + (pair * 2 + side) * group + g + 1) * row_count
                    grouped_ref[last - 2 * row_count : last, :] = jnp.concatenate(
                        [before[half], both[half]], axis=0
                    ).astype(bf16)
            before = both
    asked_ref[...] = regroup[...].astype(bf16)

    owners_copy.wait()
    replica = lax.axis_index("rollout")
    width = token_buf.shape[2]
    down_rows = tokens_ref.shape[1] // replicas
    for k in range(replicas):
        token_buf[k, :, :down_rows] = tokens_ref[:, k * down_rows : (k + 1) * down_rows]
        if down_rows < width:
            token_buf[k, :, down_rows:] = jnp.zeros((rows, width - down_rows), bf16)
    for i in range(replicas):
        place = jnp.int32(0)
        for k in range(1, replicas):
            place = place + jnp.where(owners_ref[k] == replica ^ i, k, 0)
        left_ref[:, i * width : (i + 1) * width] = token_buf[place]
    if replicas > 1:
        for i in range(shards):
            for k in range(replicas):
                picked = jnp.where(owners_ref[shard ^ i] == replica ^ k, 1.0, 0.0)
                row = i * replicas + k
                pick_ref[row : row + 1, :] = jnp.full((1, lanes), picked, f32)

    lengths_copy.wait()
    row = lax.broadcasted_iota(jnp.int32, (rows, lanes), 0)
    lane = lax.broadcasted_iota(jnp.int32, (rows, lanes), 1)
    position = row // row_count
    for b in range(row_count):
        position = position + jnp.where(row % row_count == b, lengths_ref[b], 0)
    angles = position.astype(f32) * turns_ref[:1, :]
    cosine_ref[...] = jnp.cos(angles)
    sine = jnp.sin(angles)
    sine_ref[...] = jnp.where(lane < lanes // 2, -sine, sine)
    slot = lax.broadcasted_iota(jnp.int32, bias_ref.shape, 1)
    whose = lax.broadcasted_iota(jnp.int32, bias_ref.shape, 0)
    length = jnp.zeros(bias_ref.shape, jnp.int32)
    for b in range(row_count):
        length = jnp.where(whose == b, lengths_ref[b], length)
    bias_ref[...] = jnp.where(slot < length, 0.0, masked_score)
    all_rows = row_count * seen
    seen_by = lax.broadcasted_iota(jnp.int32, (all_rows, rows), 0)
    made_by = lax.broadcasted_iota(jnp.int32, (all_rows, rows), 1)
    visible = (seen_by % row_count == made_by % row_count) & (
        made_by // row_count <= seen_by // (row_count * group)
    )
    visible_ref[...] = jnp.where(visible, 0.0, masked_score)


def project(
    owners, lengths, tokens, weight, queries, turns, after, step_count, head_count, slots, shards, replicas
):
    rows, depth = tokens.shape
    row_count = rows // step_count
    own = weight.shape[1] // shards
    piece_width = -(-depth // replicas // lanes) * lanes
    seen_rows = rows * queries.shape[1] // lanes
    table = jax.ShapeDtypeStruct((rows, lanes), f32)
    mine, *rest = pl.pallas_call(
        functools.partial(project_kernel, step_count, row_count, head_count, shards, replicas),
        out_shape=[jax.ShapeDtypeStruct((rows, own), f32)]
        + [jax.ShapeDtypeStruct((rows, own), bf16)] * (shards - 1)
        + [
            jax.ShapeDtypeStruct((rows, replicas * piece_width), bf16),
            jax.ShapeDtypeStruct((shards * replicas, lanes), f32),
            jax.ShapeDtypeStruct((seen_rows, lanes), bf16),
            jax.ShapeDtypeStruct((seen_rows, lanes), bf16),
            table,
            table,
            jax.ShapeDtypeStruct((row_count, slots), f32),
            jax.ShapeDtypeStruct((seen_rows // head_count, rows), f32),
        ],
        in_specs=[stays_in_hbm] * 2 + [whole_in_vmem] * 5,
        out_specs=[whole_in_vmem] * (shards + 8),
        scratch_shapes=[
            pltpu.SMEM(owners.shape, jnp.int32),
            pltpu.SMEM(lengths.shape, jnp.int32),
            pltpu.VMEM((replicas, rows, piece_width), bf16),
            pltpu.VMEM((seen_rows, lanes), f32),
            pltpu.SemaphoreType.DMA((2,)),
        ],
        compiler_params=pltpu.CompilerParams(vmem_limit_bytes=6 * 2**20),
        name="project",
        cost_estimate=pl.CostEstimate(
            flops=2 * rows * weight.size, bytes_accessed=2 * weight.size, transcendentals=0
        ),
    )(*in_hbm(owners, lengths), tokens, weight, queries, turns, after)
    return mine, rest[: shards - 1], *rest[shards - 1 :]


def attend_kernel(
    head_count,
    asked_ref,
    keys_ref,
    values_ref,
    bias_ref,
    _,
    mine_ref,
    *refs,
):
    other_refs = refs[:-6]
    base_ref, total_ref, peak_ref, sum_ref, scores_ref, raised = refs[-6:]
    base = mine_ref[...]
    for other_ref in other_refs:
        base = base + other_ref[...].astype(f32)
    base_ref[...] = base

    row_count, slots, _ = keys_ref.shape
    seen = asked_ref.shape[0] // (head_count * row_count)

    for b in range(row_count):
        for h in range(head_count):
            at = (h * row_count + b) * seen
            scores_ref[at : at + seen, :] = lax.dot_general(
                asked_ref[at : at + seen, :],
                keys_ref[b, :, h * lanes : (h + 1) * lanes],
                (((1,), (1,)), ((), ())),
                preferred_element_type=f32,
            )

    places = [
        (
            b,
            h,
            slice((h * row_count + b) * seen, (h * row_count + b + 1) * seen),
            pl.ds(h * row_count * seen + b, seen, stride=row_count),
        )
        for b in range(row_count)
        for h in range(head_count)
    ]
    for b, h, place, out in places:
        score = scores_ref[place, :] + bias_ref[b : b + 1, :]
        peak = jnp.max(score, axis=1, keepdims=True)
        lifted = jnp.exp2((score - peak) * exponent_scale)
        raised[place, :] = lifted.astype(bf16)
        peak_ref[out, :] = jnp.broadcast_to(peak, (seen, lanes))
        sum_ref[out, :] = jnp.broadcast_to(
            jnp.sum(lifted, axis=1, keepdims=True), (seen, lanes)
        )
    for b, h, place, out in places:
        total_ref[out, :] = jnp.dot(
            raised[place, :],
            values_ref[b, :, h * lanes : (h + 1) * lanes],
            preferred_element_type=f32,
        )


def attend(asked, keys, values, bias, after, mine, others):
    row_count, slots, width = keys.shape
    seen_rows = asked.shape[0]
    seen_table = jax.ShapeDtypeStruct((seen_rows, lanes), f32)
    return pl.pallas_call(
        functools.partial(attend_kernel, width // lanes),
        out_shape=(jax.ShapeDtypeStruct(mine.shape, f32),) + (seen_table,) * 3,
        in_specs=[whole_in_vmem] * (6 + len(others)),
        out_specs=(whole_in_vmem,) * 4,
        scratch_shapes=[
            pltpu.VMEM((seen_rows, slots), f32),
            pltpu.VMEM((seen_rows, slots), bf16),
        ],
        compiler_params=pltpu.CompilerParams(vmem_limit_bytes=8 * 2**20),
        name="attend",
        cost_estimate=pl.CostEstimate(
            flops=4 * seen_rows * slots * lanes,
            bytes_accessed=2 * (keys.size + values.size),
            transcendentals=seen_rows * slots,
        ),
    )(asked, keys, values, bias, after, mine, *others)


def piece_places(replicas):
    order = [0, 1] + list(range(replicas - 1, 1, -1))
    return [order.index(i) for i in range(replicas)]


def route_kernel(replicas, shards, *refs):
    left_ref, pick_ref = refs[:2]
    piece_refs = [refs[2 + place] for place in piece_places(replicas)]
    out_refs = refs[2 + replicas : 2 + replicas + shards]
    (right,) = refs[2 + replicas + shards :]
    up_rows = out_refs[0].shape[0] - left_ref.shape[0]
    rows = left_ref.shape[0]
    rank = right.shape[0]
    width = right.shape[1] // replicas
    half = rank // 2
    rest = (piece_refs[0].shape[0] - up_rows) % rank
    for i in range(replicas):
        first = 0
        for c in range(width // lanes - (1 if rest else 0)):
            right[:, i * width + c * lanes : i * width + (c + 1) * lanes] = piece_refs[i][
                first : first + rank, :
            ]
            first += rank
        if rest:
            both = piece_refs[i][first : first + half, :]
            tail = jnp.concatenate([both[:, : lanes // 2], both[:, lanes // 2 :]], axis=0)
            right[:, (i + 1) * width - lanes : (i + 1) * width] = jnp.concatenate(
                [tail, jnp.zeros((rank, lanes // 2), bf16)], axis=1
            )
            first += half
    lowered = lax.dot_general(
        left_ref[...], right[...], (((1,), (1,)), ((), ())), preferred_element_type=f32
    )
    both = jnp.concatenate(split_halves(lowered), axis=1)
    ups = [piece[piece.shape[0] - up_rows :, :].astype(f32) for piece in piece_refs]
    for i in range(shards):
        out_refs[i][:rows, :] = both
        picked = sum(up * pick_ref[i * replicas + k, :][None, :] for k, up in enumerate(ups))
        out_refs[i][rows:, :] = picked.astype(bf16)


def route(left, pick, pieces, rank, up_rows, shards):
    rows, depth = left.shape
    replicas = len(pieces)
    return pl.pallas_call(
        functools.partial(route_kernel, replicas, shards),
        out_shape=[jax.ShapeDtypeStruct((rows + up_rows, lanes), bf16)] * shards,
        in_specs=[whole_in_vmem] * (2 + replicas),
        out_specs=[whole_in_vmem] * shards,
        scratch_shapes=[pltpu.VMEM((rank, depth), bf16)],
        compiler_params=pltpu.CompilerParams(vmem_limit_bytes=4 * 2**20),
        name="route",
        cost_estimate=pl.CostEstimate(flops=0, bytes_accessed=800000, transcendentals=0),
    )(left, pick, *[pieces[i] for i in piece_places(replicas)])


def route_plain(owners, tokens, down, up, rank_part, own, shards):
    rank = down.shape[1]
    shard = lax.axis_index("tensor")
    first = shard * rank_part
    up_part = lax.dynamic_slice_in_dim(up, first, rank_part, axis=0)
    downs = lax.all_gather(down, "rollout", axis=0, tiled=False)
    ups = lax.all_gather(up_part, "rollout", axis=0, tiled=False)
    down_matrix = jnp.take(downs, owners, axis=0, mode="clip").reshape(-1, rank)
    up_matrix = jnp.take(ups, owners, axis=0, mode="clip").transpose(1, 0, 2)
    up_matrix = up_matrix.reshape(rank_part, -1)
    lowered = jnp.dot(tokens, down_matrix, preferred_element_type=f32)
    both = jnp.concatenate(split_halves(lowered), axis=1)
    packets = []
    for i in range(shards):
        up_block = lax.dynamic_slice_in_dim(up_matrix, (shard ^ i) * own, own, axis=1)
        parts = [both, side_by_side(up_block)]
        packets.append(jnp.concatenate(parts, axis=0))
    return packets


def finish_kernel(step_count, row_count, head_count, shards, *refs):
    gain_ref, base_ref, grouped_ref, total_ref, peak_ref, sum_ref, cosine_ref, sine_ref = refs[:8]
    packet_refs = refs[8 : 8 + shards][::-1]
    visible_ref, attention_hbm, keys_hbm, values_hbm = refs[8 + shards : 12 + shards]
    up_buf, attention_ref, keys_ref, values_ref, new_sems, sems = refs[12 + shards :]
    written = [
        pltpu.make_async_copy(keys_ref, keys_hbm, new_sems.at[0]),
        pltpu.make_async_copy(values_ref, values_hbm, new_sems.at[1]),
    ]
    shard = lax.axis_index("tensor")
    rows = step_count * row_count
    own = base_ref.shape[1]
    blocks = own // lanes
    rank = up_buf.shape[0]
    rank_part = rank // shards
    group = grouped_ref.shape[0] // (head_count * rows)
    seen = step_count * group

    lowered = jnp.zeros((rows, lanes), f32)
    for i in range(shards):
        lowered = lowered + packet_refs[i][:rows, :].astype(f32)
        ups = packet_refs[i][rows:, :].astype(up_buf.dtype)
        at = pl.multiple_of((shard ^ i) * rank_part, rank_part)
        for c in range(blocks):
            up_buf[pl.ds(at, rank_part), c * lanes : (c + 1) * lanes] = ups[
                c * rank_part : (c + 1) * rank_part, :
            ]
    lane = lax.broadcasted_iota(jnp.int32, (rows, lanes), 1)
    lowered = lowered + pltpu.roll(lowered, rank, 1)
    high, low = split_halves(lowered)
    left = jnp.where(lane < rank, high.astype(f32), low.astype(f32)).astype(bf16)
    up = up_buf[...].astype(bf16)
    raised_up = jnp.dot(left, jnp.concatenate([up, up], axis=0), preferred_element_type=f32)
    joined = []
    for c in range(blocks):
        block = base_ref[:, c * lanes : (c + 1) * lanes]
        joined.append(block + adapter_scale * raised_up[:, c * lanes : (c + 1) * lanes])

    all_rows = row_count * seen
    heads = [(h, slice(h * all_rows, (h + 1) * all_rows)) for h in range(head_count)]
    keys, values, scores = [], [], []
    for h, _ in heads:
        raw_key = joined[2 * h]
        mean_square = jnp.mean(raw_key * raw_key, axis=1, keepdims=True)
        normed = raw_key * lax.rsqrt(mean_square + norm_eps) * gain_ref[...]
        key = normed * cosine_ref[...] + pltpu.roll(normed, lanes // 2, 1) * sine_ref[...]
        keys.append(key.astype(bf16))
        values.append(joined[2 * h + 1].astype(bf16))
        keys_ref[:, h * lanes : (h + 1) * lanes] = keys[h]
        values_ref[:, h * lanes : (h + 1) * lanes] = values[h]
    for copy in written:
        copy.start()
    for h, mine in heads:
        score = lax.dot_general(
            grouped_ref[mine, :], keys[h], (((1,), (1,)), ((), ())), preferred_element_type=f32
        )
        scores.append(score + visible_ref[...])
    for h, mine in heads:
        old_peak = peak_ref[mine, :]
        peak = jnp.maximum(old_peak, jnp.max(scores[h], axis=1, keepdims=True))
        fade = jnp.exp2((old_peak - peak) * exponent_scale)
        lifted = jnp.exp2((scores[h] - peak[:, :rows]) * exponent_scale)
        denominator = fade * sum_ref[mine, :] + jnp.sum(lifted, axis=1, keepdims=True)
        total = fade * total_ref[mine, :] + jnp.dot(
            lifted.astype(bf16), values[h], preferred_element_type=f32
        )
        result = total / denominator
        for pair in range(step_count // 2):
            window = slice(pair * 2 * row_count, (pair + 1) * 2 * row_count)
            for g in range(group):
                both = []
                for side in range(2):
                    first = ((pair * 2 + side) * group + g) * row_count
                    both.append(result[first : first + row_count])
                q = h * group + g
                attention_ref[window, q * lanes : (q + 1) * lanes] = jnp.concatenate(
                    both, axis=0
                ).astype(bf16)
            part = attention_ref.shape[1] // (2 * head_count)
            for half in range(2):
                columns = slice((2 * h + half) * part, (2 * h + half + 1) * part)
                copy = pltpu.make_async_copy(
                    attention_ref.at[window, columns],
                    attention_hbm.at[window, columns],
                    sems.at[(h * (step_count // 2) + pair) * 2 + half],
                )
                copy.start()
                written.append(copy)
    for copy in written:
        copy.wait()


def finish(base, visible, partials, gain, packets, rank, step_count, row_count, query_width):
    rows, own = base.shape
    shards = len(packets)
    head_count = own // (2 * lanes)
    return pl.pallas_call(
        functools.partial(finish_kernel, step_count, row_count, head_count, shards),
        out_shape=(
            jax.ShapeDtypeStruct((rows, query_width), bf16),
            jax.ShapeDtypeStruct((rows, head_count * lanes), bf16),
            jax.ShapeDtypeStruct((rows, head_count * lanes), bf16),
        ),
        in_specs=[whole_in_vmem] * (9 + shards),
        out_specs=(stays_in_hbm,) * 3,
        scratch_shapes=[
            pltpu.VMEM((rank, own), bf16 if rank // shards % 16 == 0 else f32),
            pltpu.VMEM((rows, query_width), bf16),
            pltpu.VMEM((rows, head_count * lanes), bf16),
            pltpu.VMEM((rows, head_count * lanes), bf16),
            pltpu.SemaphoreType.DMA((2,)),
            pltpu.SemaphoreType.DMA((2 * head_count * (step_count // 2),)),
        ],
        compiler_params=pltpu.CompilerParams(vmem_limit_bytes=6 * 2**20),
        name="finish",
        cost_estimate=pl.CostEstimate(flops=0, bytes_accessed=1000000, transcendentals=0),
    )(gain, base, *partials, *packets[::-1], visible)


def per_device(
    normed_tokens,
    key_value_weight,
    adapter_down,
    adapter_up,
    key_gain,
    queries,
    cache_keys,
    stored_values,
    lengths,
    owners,
):
    replicas = lax.axis_size("rollout")
    shards = lax.axis_size("tensor")
    down_rows, rank = adapter_down.shape
    step_count, row_count, depth = normed_tokens.shape
    own = key_value_weight.shape[1] // shards
    rank_part = rank // shards
    rows = step_count * row_count
    tokens = normed_tokens.reshape(rows, depth)
    query_rows = queries.reshape(rows, -1)

    fits = (
        replicas <= 4
        and adapter_up.shape[1] == own
        and down_rows % lanes in (0, lanes // 2)
        and rank == lanes // 2
        and rank_part % 16 == 0
    )
    fetched = 2 * (key_value_weight.size + cache_keys.size + stored_values.size)
    turns = frequencies(
        pl.CostEstimate(flops=1000 * fetched, bytes_accessed=fetched, transcendentals=0)
    )
    if fits:
        packed = pack(adapter_down.T, adapter_up, rank_part, turns)
        pieces = [packed] + [swap(packed, "rollout", i) for i in range(1, replicas)]
    mine, blocks, left, pick, asked, grouped, cosine, sine, bias, visible = project(
        owners,
        lengths,
        tokens,
        key_value_weight,
        query_rows,
        turns,
        packed if fits else adapter_up,
        step_count,
        cache_keys.shape[2] // lanes,
        cache_keys.shape[1],
        shards,
        replicas if fits else 1,
    )
    others = [swap(block, "tensor", i + 1) for i, block in enumerate(blocks)]
    if fits:
        packets = route(left, pick, pieces, rank, rank_part * own // lanes, shards)
    else:
        packets = route_plain(
            owners, tokens, adapter_down, adapter_up, rank_part, own, shards
        )
    base, total, peak, denominator = attend(
        asked, cache_keys, stored_values, bias, packets[0], mine, others
    )
    packets = [packets[0]] + [swap(packets[i], "tensor", i) for i in range(1, shards)]
    attention, keys, values = finish(
        base,
        visible,
        (grouped, total, peak, denominator, cosine, sine),
        key_gain.reshape(1, -1),
        packets,
        rank,
        step_count,
        row_count,
        query_rows.shape[1],
    )
    return tuple(a.reshape(step_count, row_count, -1) for a in (attention, keys, values))


def solution(mesh):
    placed = (
        P(None, ("job", "rollout"), "tensor"),
        P("tensor", None),
        P(("job", "rollout", "tensor"), None),
        P(None, ("job", "rollout")),
        P(),
        P(None, ("job", "rollout"), "tensor"),
        P(("job", "rollout"), None, "tensor"),
        P(("job", "rollout"), None, "tensor"),
        P(("job", "rollout")),
        P("job"),
    )
    return jax.shard_map(
        per_device,
        mesh=mesh,
        in_specs=placed,
        out_specs=(
            P(None, ("job", "rollout"), "tensor"),
            P(None, ("job", "rollout"), "tensor"),
            P(None, ("job", "rollout"), "tensor"),
        ),
        check_vma=False,
    )
```

```python
import functools
import math

import jax
import jax.numpy as jnp
from jax import lax
from jax.experimental import pallas as pl
from jax.experimental.pallas import tpu as pltpu
from jax.sharding import PartitionSpec as P

norm_eps = 1e-06
rope_base = 1000000.0
adapter_scale = 2.0
masked_score = -1e30
lanes = 128
exponent_scale = lanes**-0.5 / math.log(2.0)
f32 = jnp.float32
bf16 = jnp.bfloat16

whole_in_vmem = pl.BlockSpec(memory_space=pltpu.VMEM)
whole_in_smem = pl.BlockSpec(memory_space=pltpu.SMEM)
stays_in_hbm = pl.BlockSpec(memory_space=pltpu.HBM)


def swap(block, axis, offset):
    count = lax.axis_size(axis)
    return lax.ppermute(block, axis, [(s, s ^ offset) for s in range(count)])


def in_hbm(*arrays):
    return tuple(pltpu.with_memory_space_constraint(a, pltpu.HBM) for a in arrays)


def side_by_side(rows_of_blocks):
    r, c = rows_of_blocks.shape
    return rows_of_blocks.reshape(r, c // lanes, lanes).transpose(1, 0, 2).reshape(-1, lanes)


def split_halves(total):
    high = total.astype(bf16)
    return high, (total - high.astype(f32)).astype(bf16)


def frequencies_kernel(out_ref):
    lane = lax.broadcasted_iota(jnp.int32, out_ref.shape, 1)
    spacing = (lane % (lanes // 2)).astype(f32) * (-2.0 / lanes * math.log(rope_base))
    out_ref[...] = jnp.exp(spacing)


def frequencies(beside):
    return pl.pallas_call(
        frequencies_kernel,
        out_shape=jax.ShapeDtypeStruct((8, lanes), f32),
        out_specs=whole_in_vmem,
        compiler_params=pltpu.CompilerParams(vmem_limit_bytes=2**20),
        name="frequencies",
        cost_estimate=beside,
    )()


def pack_kernel(down_ref, up_all_ref, _, out_ref):
    rank, down_rows = down_ref.shape
    rank_part = (out_ref.shape[0] * lanes - down_ref.size) // up_all_ref.shape[1]
    start = pl.multiple_of(lax.axis_index("tensor") * rank_part, rank_part)
    up_ref = up_all_ref.at[pl.ds(start, rank_part), :]
    first = 0
    for c in range(down_rows // lanes):
        out_ref[first : first + rank, :] = down_ref[:, c * lanes : (c + 1) * lanes]
        first += rank
    rest = down_rows % lanes
    if rest:
        half = rank // 2
        tail = down_ref[:, down_rows - rest :]
        out_ref[first : first + half, :] = jnp.concatenate([tail[:half], tail[half:]], axis=1)
        first += half
    for c in range(up_ref.shape[1] // lanes):
        out_ref[first : first + rank_part, :] = up_ref[:, c * lanes : (c + 1) * lanes]
        first += rank_part


def pack(down, up, rank_part, after):
    rows = (down.size + rank_part * up.shape[1]) // lanes
    return pl.pallas_call(
        pack_kernel,
        out_shape=jax.ShapeDtypeStruct((rows, lanes), bf16),
        in_specs=[whole_in_vmem] * 3,
        out_specs=whole_in_vmem,
        compiler_params=pltpu.CompilerParams(vmem_limit_bytes=2 * 2**20),
        name="pack",
        cost_estimate=pl.CostEstimate(flops=0, bytes_accessed=200000, transcendentals=0),
    )(down, up, after)


def project_kernel(step_count, row_count, shards, replicas, *refs):
    owners_hbm, lengths_hbm, tokens_ref, weight_ref, turns_ref, _ = refs[:6]
    own_ref = refs[6]
    block_refs = refs[7 : 6 + shards]
    left_ref, pick_ref, cosine_ref, sine_ref, bias_ref = refs[6 + shards : 11 + shards]
    owners_ref, lengths_ref, token_buf, sems = refs[11 + shards :]
    owners_copy = pltpu.make_async_copy(owners_hbm, owners_ref, sems.at[0])
    lengths_copy = pltpu.make_async_copy(lengths_hbm, lengths_ref, sems.at[1])
    owners_copy.start()
    lengths_copy.start()

    shard = lax.axis_index("tensor")
    rows, own = own_ref.shape
    for i in range(shards):
        first = pl.multiple_of((shard ^ i) * own, lanes)
        block = jnp.dot(
            tokens_ref[...], weight_ref[:, pl.ds(first, own)], preferred_element_type=f32
        )
        if i == 0:
            own_ref[...] = block
        else:
            block_refs[i - 1][...] = block.astype(bf16)

    owners_copy.wait()
    replica = lax.axis_index("rollout")
    width = token_buf.shape[2]
    down_rows = tokens_ref.shape[1] // replicas
    for k in range(replicas):
        token_buf[k, :, :down_rows] = tokens_ref[:, k * down_rows : (k + 1) * down_rows]
        if down_rows < width:
            token_buf[k, :, down_rows:] = jnp.zeros((rows, width - down_rows), bf16)
    for i in range(replicas):
        place = jnp.int32(0)
        for k in range(1, replicas):
            place = place + jnp.where(owners_ref[k] == replica ^ i, k, 0)
        left_ref[:, i * width : (i + 1) * width] = token_buf[place]
    if replicas > 1:
        for i in range(shards):
            for k in range(replicas):
                picked = jnp.where(owners_ref[shard ^ i] == replica ^ k, 1.0, 0.0)
                row = i * replicas + k
                pick_ref[row : row + 1, :] = jnp.full((1, lanes), picked, f32)

    lengths_copy.wait()
    row = lax.broadcasted_iota(jnp.int32, (rows, lanes), 0)
    lane = lax.broadcasted_iota(jnp.int32, (rows, lanes), 1)
    position = row // row_count
    for b in range(row_count):
        position = position + jnp.where(row % row_count == b, lengths_ref[b], 0)
    angles = position.astype(f32) * turns_ref[:1, :]
    cosine_ref[...] = jnp.cos(angles)
    sine = jnp.sin(angles)
    sine_ref[...] = jnp.where(lane < lanes // 2, -sine, sine)
    slot = lax.broadcasted_iota(jnp.int32, bias_ref.shape, 1)
    whose = lax.broadcasted_iota(jnp.int32, bias_ref.shape, 0)
    length = jnp.zeros(bias_ref.shape, jnp.int32)
    for b in range(row_count):
        length = jnp.where(whose == b, lengths_ref[b], length)
    bias_ref[...] = jnp.where(slot < length, 0.0, masked_score)


def project(
    owners, lengths, tokens, weight, turns, after, step_count, slots, shards, replicas
):
    rows, depth = tokens.shape
    row_count = rows // step_count
    own = weight.shape[1] // shards
    piece_width = -(-depth // replicas // lanes) * lanes
    table = jax.ShapeDtypeStruct((rows, lanes), f32)
    mine, *rest = pl.pallas_call(
        functools.partial(project_kernel, step_count, row_count, shards, replicas),
        out_shape=[jax.ShapeDtypeStruct((rows, own), f32)]
        + [jax.ShapeDtypeStruct((rows, own), bf16)] * (shards - 1)
        + [
            jax.ShapeDtypeStruct((rows, replicas * piece_width), bf16),
            jax.ShapeDtypeStruct((shards * replicas, lanes), f32),
            table,
            table,
            jax.ShapeDtypeStruct((row_count, slots), f32),
        ],
        in_specs=[stays_in_hbm] * 2 + [whole_in_vmem] * 4,
        out_specs=[whole_in_vmem] * (shards + 5),
        scratch_shapes=[
            pltpu.SMEM(owners.shape, jnp.int32),
            pltpu.SMEM(lengths.shape, jnp.int32),
            pltpu.VMEM((replicas, rows, piece_width), bf16),
            pltpu.SemaphoreType.DMA((2,)),
        ],
        compiler_params=pltpu.CompilerParams(vmem_limit_bytes=6 * 2**20),
        name="project",
        cost_estimate=pl.CostEstimate(
            flops=2 * rows * weight.size, bytes_accessed=2 * weight.size, transcendentals=0
        ),
    )(*in_hbm(owners, lengths), tokens, weight, turns, after)
    return mine, rest[: shards - 1], *rest[shards - 1 :]


def attend_kernel(
    step_count,
    head_count,
    queries_ref,
    keys_ref,
    values_ref,
    bias_ref,
    _,
    grouped_ref,
    total_ref,
    peak_ref,
    sum_ref,
    regroup,
    scores_ref,
    raised,
):
    row_count, slots, _ = keys_ref.shape
    group = queries_ref.shape[1] // (head_count * lanes)
    seen = step_count * group
    for pair in range(step_count // 2):
        for q in range(head_count * group):
            h, g = q // group, q % group
            both = queries_ref[
                pair * 2 * row_count : (pair + 1) * 2 * row_count, q * lanes : (q + 1) * lanes
            ].astype(f32)
            for side in range(2):
                first = h * row_count * seen + (pair * 2 + side) * group + g
                regroup[pl.ds(first, row_count, stride=seen), :] = both[
                    side * row_count : (side + 1) * row_count, :
                ]
            if g % 2:
                for side in range(2):
                    half = slice(side * row_count, (side + 1) * row_count)
                    last = (h * seen + (pair * 2 + side) * group + g + 1) * row_count
                    grouped_ref[last - 2 * row_count : last, :] = jnp.concatenate(
                        [before[half], both[half]], axis=0
                    ).astype(bf16)
            before = both

    for b in range(row_count):
        for h in range(head_count):
            at = (h * row_count + b) * seen
            scores_ref[at : at + seen, :] = lax.dot_general(
                regroup[at : at + seen, :].astype(bf16),
                keys_ref[b, :, h * lanes : (h + 1) * lanes],
                (((1,), (1,)), ((), ())),
                preferred_element_type=f32,
            )

    places = [
        (
            b,
            h,
            slice((h * row_count + b) * seen, (h * row_count + b + 1) * seen),
            pl.ds(h * row_count * seen + b, seen, stride=row_count),
        )
        for b in range(row_count)
        for h in range(head_count)
    ]
    for b, h, place, out in places:
        score = scores_ref[place, :] + bias_ref[b : b + 1, :]
        peak = jnp.max(score, axis=1, keepdims=True)
        lifted = jnp.exp2((score - peak) * exponent_scale)
        raised[place, :] = lifted.astype(bf16)
        peak_ref[out, :] = jnp.broadcast_to(peak, (seen, lanes))
        sum_ref[out, :] = jnp.broadcast_to(
            jnp.sum(lifted, axis=1, keepdims=True), (seen, lanes)
        )
    for b, h, place, out in places:
        total_ref[out, :] = jnp.dot(
            raised[place, :],
            values_ref[b, :, h * lanes : (h + 1) * lanes],
            preferred_element_type=f32,
        )


def attend(queries, keys, values, bias, after, step_count):
    row_count, slots, width = keys.shape
    seen_rows = step_count * row_count * queries.shape[1] // lanes
    seen_table = jax.ShapeDtypeStruct((seen_rows, lanes), f32)
    return pl.pallas_call(
        functools.partial(attend_kernel, step_count, width // lanes),
        out_shape=(jax.ShapeDtypeStruct((seen_rows, lanes), bf16),) + (seen_table,) * 3,
        in_specs=[whole_in_vmem] * 5,
        out_specs=(whole_in_vmem,) * 4,
        scratch_shapes=[
            pltpu.VMEM((seen_rows, lanes), f32),
            pltpu.VMEM((seen_rows, slots), f32),
            pltpu.VMEM((seen_rows, slots), bf16),
        ],
        compiler_params=pltpu.CompilerParams(vmem_limit_bytes=8 * 2**20),
        name="attend",
        cost_estimate=pl.CostEstimate(
            flops=4 * seen_rows * slots * lanes,
            bytes_accessed=2 * (keys.size + values.size),
            transcendentals=seen_rows * slots,
        ),
    )(queries, keys, values, bias, after)


def piece_places(replicas):
    order = [0, 1] + list(range(replicas - 1, 1, -1))
    return [order.index(i) for i in range(replicas)]


def route_kernel(replicas, shards, *refs):
    left_ref, pick_ref = refs[:2]
    piece_refs = [refs[2 + place] for place in piece_places(replicas)]
    out_refs = refs[2 + replicas : 2 + replicas + shards]
    (right,) = refs[2 + replicas + shards :]
    up_rows = out_refs[0].shape[0] - left_ref.shape[0]
    rows = left_ref.shape[0]
    rank = right.shape[0]
    width = right.shape[1] // replicas
    half = rank // 2
    rest = (piece_refs[0].shape[0] - up_rows) % rank
    for i in range(replicas):
        first = 0
        for c in range(width // lanes - (1 if rest else 0)):
            right[:, i * width + c * lanes : i * width + (c + 1) * lanes] = piece_refs[i][
                first : first + rank, :
            ]
            first += rank
        if rest:
            both = piece_refs[i][first : first + half, :]
            tail = jnp.concatenate([both[:, : lanes // 2], both[:, lanes // 2 :]], axis=0)
            right[:, (i + 1) * width - lanes : (i + 1) * width] = jnp.concatenate(
                [tail, jnp.zeros((rank, lanes // 2), bf16)], axis=1
            )
            first += half
    lowered = lax.dot_general(
        left_ref[...], right[...], (((1,), (1,)), ((), ())), preferred_element_type=f32
    )
    both = jnp.concatenate(split_halves(lowered), axis=1)
    ups = [piece[piece.shape[0] - up_rows :, :].astype(f32) for piece in piece_refs]
    for i in range(shards):
        out_refs[i][:rows, :] = both
        picked = sum(up * pick_ref[i * replicas + k, :][None, :] for k, up in enumerate(ups))
        out_refs[i][rows:, :] = picked.astype(bf16)


def route(left, pick, pieces, rank, up_rows, shards):
    rows, depth = left.shape
    replicas = len(pieces)
    return pl.pallas_call(
        functools.partial(route_kernel, replicas, shards),
        out_shape=[jax.ShapeDtypeStruct((rows + up_rows, lanes), bf16)] * shards,
        in_specs=[whole_in_vmem] * (2 + replicas),
        out_specs=[whole_in_vmem] * shards,
        scratch_shapes=[pltpu.VMEM((rank, depth), bf16)],
        compiler_params=pltpu.CompilerParams(vmem_limit_bytes=4 * 2**20),
        name="route",
        cost_estimate=pl.CostEstimate(flops=0, bytes_accessed=800000, transcendentals=0),
    )(left, pick, *[pieces[i] for i in piece_places(replicas)])


def route_plain(owners, tokens, down, up, rank_part, own, shards):
    rank = down.shape[1]
    shard = lax.axis_index("tensor")
    first = shard * rank_part
    up_part = lax.dynamic_slice_in_dim(up, first, rank_part, axis=0)
    downs = lax.all_gather(down, "rollout", axis=0, tiled=False)
    ups = lax.all_gather(up_part, "rollout", axis=0, tiled=False)
    down_matrix = jnp.take(downs, owners, axis=0, mode="clip").reshape(-1, rank)
    up_matrix = jnp.take(ups, owners, axis=0, mode="clip").transpose(1, 0, 2)
    up_matrix = up_matrix.reshape(rank_part, -1)
    lowered = jnp.dot(tokens, down_matrix, preferred_element_type=f32)
    both = jnp.concatenate(split_halves(lowered), axis=1)
    packets = []
    for i in range(shards):
        up_block = lax.dynamic_slice_in_dim(up_matrix, (shard ^ i) * own, own, axis=1)
        parts = [both, side_by_side(up_block)]
        packets.append(jnp.concatenate(parts, axis=0))
    return packets


def finish_kernel(step_count, row_count, head_count, shards, *refs):
    gain_ref, base_ref, grouped_ref, total_ref, peak_ref, sum_ref, cosine_ref, sine_ref = refs[:8]
    packet_refs = refs[8 : 8 + shards][::-1]
    sum_refs = refs[8 + shards : 7 + 2 * shards]
    attention_ref, keys_ref, values_ref = refs[7 + 2 * shards : 10 + 2 * shards]
    (up_buf,) = refs[10 + 2 * shards :]
    shard = lax.axis_index("tensor")
    rows = step_count * row_count
    own = base_ref.shape[1]
    blocks = own // lanes
    rank = up_buf.shape[0]
    rank_part = rank // shards
    group = grouped_ref.shape[0] // (head_count * rows)
    seen = step_count * group

    lowered = jnp.zeros((rows, lanes), f32)
    for i in range(shards):
        lowered = lowered + packet_refs[i][:rows, :].astype(f32)
        ups = packet_refs[i][rows:, :].astype(f32)
        at = pl.multiple_of((shard ^ i) * rank_part, rank_part)
        for c in range(blocks):
            up_buf[pl.ds(at, rank_part), c * lanes : (c + 1) * lanes] = ups[
                c * rank_part : (c + 1) * rank_part, :
            ]
    lane = lax.broadcasted_iota(jnp.int32, (rows, lanes), 1)
    lowered = lowered + pltpu.roll(lowered, rank, 1)
    high, low = split_halves(lowered)
    left = jnp.where(lane < rank, high.astype(f32), low.astype(f32)).astype(bf16)
    up = up_buf[...].astype(bf16)
    raised_up = jnp.dot(left, jnp.concatenate([up, up], axis=0), preferred_element_type=f32)
    joined = []
    for c in range(blocks):
        block = base_ref[:, c * lanes : (c + 1) * lanes]
        for partial_ref in sum_refs:
            block = block + partial_ref[:, c * lanes : (c + 1) * lanes].astype(f32)
        joined.append(block + adapter_scale * raised_up[:, c * lanes : (c + 1) * lanes])

    all_rows = row_count * seen
    seen_by = lax.broadcasted_iota(jnp.int32, (all_rows, rows), 0)
    made_by = lax.broadcasted_iota(jnp.int32, (all_rows, rows), 1)
    visible = (seen_by % row_count == made_by % row_count) & (
        made_by // row_count <= seen_by // (row_count * group)
    )
    heads = [(h, slice(h * all_rows, (h + 1) * all_rows)) for h in range(head_count)]
    keys, values, scores, results = [], [], [], []
    for h, _ in heads:
        raw_key = joined[2 * h]
        mean_square = jnp.mean(raw_key * raw_key, axis=1, keepdims=True)
        normed = raw_key * lax.rsqrt(mean_square + norm_eps) * gain_ref[...]
        key = normed * cosine_ref[...] + pltpu.roll(normed, lanes // 2, 1) * sine_ref[...]
        keys.append(key.astype(bf16))
        values.append(joined[2 * h + 1].astype(bf16))
        keys_ref[:, h * lanes : (h + 1) * lanes] = keys[h]
        values_ref[:, h * lanes : (h + 1) * lanes] = values[h]
    for h, mine in heads:
        score = lax.dot_general(
            grouped_ref[mine, :], keys[h], (((1,), (1,)), ((), ())), preferred_element_type=f32
        )
        scores.append(jnp.where(visible, score, masked_score))
    for h, mine in heads:
        old_peak = peak_ref[mine, :]
        peak = jnp.maximum(old_peak, jnp.max(scores[h], axis=1, keepdims=True))
        fade = jnp.exp2((old_peak - peak) * exponent_scale)
        lifted = jnp.exp2((scores[h] - peak[:, :rows]) * exponent_scale)
        denominator = fade * sum_ref[mine, :] + jnp.sum(lifted, axis=1, keepdims=True)
        total = fade * total_ref[mine, :] + jnp.dot(
            lifted.astype(bf16), values[h], preferred_element_type=f32
        )
        results.append(total / denominator)
    for pair in range(step_count // 2):
        for q in range(head_count * group):
            h, g = q // group, q % group
            both = []
            for side in range(2):
                first = ((pair * 2 + side) * group + g) * row_count
                both.append(results[h][first : first + row_count])
            attention_ref[
                pair * 2 * row_count : (pair + 1) * 2 * row_count, q * lanes : (q + 1) * lanes
            ] = jnp.concatenate(both, axis=0).astype(bf16)


def finish(mine, others, partials, gain, packets, rank, step_count, row_count, query_width):
    rows, own = mine.shape
    shards = len(packets)
    head_count = own // (2 * lanes)
    return pl.pallas_call(
        functools.partial(finish_kernel, step_count, row_count, head_count, shards),
        out_shape=(
            jax.ShapeDtypeStruct((rows, query_width), bf16),
            jax.ShapeDtypeStruct((rows, head_count * lanes), bf16),
            jax.ShapeDtypeStruct((rows, head_count * lanes), bf16),
        ),
        in_specs=[whole_in_vmem] * (7 + 2 * shards),
        out_specs=(whole_in_vmem,) * 3,
        scratch_shapes=[
            pltpu.VMEM((rank, own), f32),
        ],
        compiler_params=pltpu.CompilerParams(vmem_limit_bytes=6 * 2**20),
        name="finish",
        cost_estimate=pl.CostEstimate(flops=0, bytes_accessed=1000000, transcendentals=0),
    )(gain, mine, *partials, *packets[::-1], *others)


def per_device(
    normed_tokens,
    key_value_weight,
    adapter_down,
    adapter_up,
    key_gain,
    queries,
    cache_keys,
    stored_values,
    lengths,
    owners,
):
    replicas = lax.axis_size("rollout")
    shards = lax.axis_size("tensor")
    down_rows, rank = adapter_down.shape
    step_count, row_count, depth = normed_tokens.shape
    own = key_value_weight.shape[1] // shards
    rank_part = rank // shards
    rows = step_count * row_count
    tokens = normed_tokens.reshape(rows, depth)
    query_rows = queries.reshape(rows, -1)

    fits = (
        replicas <= 4
        and adapter_up.shape[1] == own
        and down_rows % lanes in (0, lanes // 2)
        and rank == lanes // 2
        and rank_part % 16 == 0
    )
    fetched = 2 * (key_value_weight.size + cache_keys.size + stored_values.size)
    turns = frequencies(
        pl.CostEstimate(flops=1000 * fetched, bytes_accessed=fetched, transcendentals=0)
    )
    if fits:
        packed = pack(adapter_down.T, adapter_up, rank_part, turns)
        pieces = [packed] + [swap(packed, "rollout", i) for i in range(1, replicas)]
    mine, blocks, left, pick, cosine, sine, bias = project(
        owners,
        lengths,
        tokens,
        key_value_weight,
        turns,
        packed if fits else adapter_up,
        step_count,
        cache_keys.shape[1],
        shards,
        replicas if fits else 1,
    )
    others = [swap(block, "tensor", i + 1) for i, block in enumerate(blocks)]
    if fits:
        packets = route(left, pick, pieces, rank, rank_part * own // lanes, shards)
    else:
        packets = route_plain(
            owners, tokens, adapter_down, adapter_up, rank_part, own, shards
        )
    grouped, total, peak, denominator = attend(
        query_rows, cache_keys, stored_values, bias, packets[0], step_count
    )
    packets = [packets[0]] + [swap(packets[i], "tensor", i) for i in range(1, shards)]
    attention, keys, values = finish(
        mine,
        others,
        (grouped, total, peak, denominator, cosine, sine),
        key_gain.reshape(1, -1),
        packets,
        rank,
        step_count,
        row_count,
        query_rows.shape[1],
    )
    return tuple(a.reshape(step_count, row_count, -1) for a in (attention, keys, values))


def solution(mesh):
    placed = (
        P(None, ("job", "rollout"), "tensor"),
        P("tensor", None),
        P(("job", "rollout", "tensor"), None),
        P(None, ("job", "rollout")),
        P(),
        P(None, ("job", "rollout"), "tensor"),
        P(("job", "rollout"), None, "tensor"),
        P(("job", "rollout"), None, "tensor"),
        P(("job", "rollout")),
        P("job"),
    )
    return jax.shard_map(
        per_device,
        mesh=mesh,
        in_specs=placed,
        out_specs=(
            P(None, ("job", "rollout"), "tensor"),
            P(None, ("job", "rollout"), "tensor"),
            P(None, ("job", "rollout"), "tensor"),
        ),
        check_vma=False,
    )
```

```python
import functools
import math

import jax
import jax.numpy as jnp
from jax import lax
from jax.experimental import pallas as pl
from jax.experimental.pallas import tpu as pltpu
from jax.sharding import PartitionSpec as P

norm_eps = 1e-06
rope_base = 1000000.0
adapter_scale = 2.0
masked_score = -1e30
lanes = 128
exponent_scale = lanes**-0.5 / math.log(2.0)
f32 = jnp.float32
bf16 = jnp.bfloat16

whole_in_vmem = pl.BlockSpec(memory_space=pltpu.VMEM)
whole_in_smem = pl.BlockSpec(memory_space=pltpu.SMEM)
stays_in_hbm = pl.BlockSpec(memory_space=pltpu.HBM)


def swap(block, axis, offset):
    count = lax.axis_size(axis)
    return lax.ppermute(block, axis, [(s, s ^ offset) for s in range(count)])


def in_hbm(*arrays):
    return tuple(pltpu.with_memory_space_constraint(a, pltpu.HBM) for a in arrays)


def side_by_side(rows_of_blocks):
    r, c = rows_of_blocks.shape
    return rows_of_blocks.reshape(r, c // lanes, lanes).transpose(1, 0, 2).reshape(-1, lanes)


def split_halves(total):
    high = total.astype(bf16)
    return high, (total - high.astype(f32)).astype(bf16)


def frequencies_kernel(out_ref):
    lane = lax.broadcasted_iota(jnp.int32, out_ref.shape, 1)
    spacing = (lane % (lanes // 2)).astype(f32) * (-2.0 / lanes * math.log(rope_base))
    out_ref[...] = jnp.exp(spacing)


def frequencies(beside):
    return pl.pallas_call(
        frequencies_kernel,
        out_shape=jax.ShapeDtypeStruct((8, lanes), f32),
        out_specs=whole_in_vmem,
        compiler_params=pltpu.CompilerParams(vmem_limit_bytes=2**20),
        name="frequencies",
        cost_estimate=beside,
    )()


def pack_kernel(down_ref, up_all_ref, _, out_ref):
    rank, down_rows = down_ref.shape
    rank_part = (out_ref.shape[0] * lanes - down_ref.size) // up_all_ref.shape[1]
    start = pl.multiple_of(lax.axis_index("tensor") * rank_part, rank_part)
    up_ref = up_all_ref.at[pl.ds(start, rank_part), :]
    first = 0
    for c in range(down_rows // lanes):
        out_ref[first : first + rank, :] = down_ref[:, c * lanes : (c + 1) * lanes]
        first += rank
    rest = down_rows % lanes
    if rest:
        half = rank // 2
        tail = down_ref[:, down_rows - rest :]
        out_ref[first : first + half, :] = jnp.concatenate([tail[:half], tail[half:]], axis=1)
        first += half
    for c in range(up_ref.shape[1] // lanes):
        out_ref[first : first + rank_part, :] = up_ref[:, c * lanes : (c + 1) * lanes]
        first += rank_part


def pack(down, up, rank_part, after):
    rows = (down.size + rank_part * up.shape[1]) // lanes
    return pl.pallas_call(
        pack_kernel,
        out_shape=jax.ShapeDtypeStruct((rows, lanes), bf16),
        in_specs=[whole_in_vmem] * 3,
        out_specs=whole_in_vmem,
        compiler_params=pltpu.CompilerParams(vmem_limit_bytes=2 * 2**20),
        name="pack",
        cost_estimate=pl.CostEstimate(flops=0, bytes_accessed=200000, transcendentals=0),
    )(down, up, after)


def product(tokens_ref, weight_ref, owner, own):
    columns = pl.ds(pl.multiple_of(owner * own, lanes), own)
    return jnp.dot(tokens_ref[...], weight_ref[:, columns], preferred_element_type=f32)


def project_kernel(step_count, row_count, shards, replicas, *refs):
    owners_hbm, lengths_hbm, tokens_ref, weight_ref, turns_ref, _ = refs[:6]
    block_refs = refs[6 : 5 + shards]
    left_ref, pick_ref, cosine_ref, sine_ref, bias_ref = refs[5 + shards : 10 + shards]
    owners_ref, lengths_ref, token_buf, sems = refs[10 + shards :]
    owners_copy = pltpu.make_async_copy(owners_hbm, owners_ref, sems.at[0])
    lengths_copy = pltpu.make_async_copy(lengths_hbm, lengths_ref, sems.at[1])
    owners_copy.start()
    lengths_copy.start()

    shard = lax.axis_index("tensor")
    rows, own = block_refs[0].shape
    for i in reversed(range(1, shards)):
        block_refs[i - 1][...] = product(tokens_ref, weight_ref, shard ^ i, own).astype(bf16)

    owners_copy.wait()
    replica = lax.axis_index("rollout")
    width = token_buf.shape[2]
    down_rows = tokens_ref.shape[1] // replicas
    for k in range(replicas):
        token_buf[k, :, :down_rows] = tokens_ref[:, k * down_rows : (k + 1) * down_rows]
        if down_rows < width:
            token_buf[k, :, down_rows:] = jnp.zeros((rows, width - down_rows), bf16)
    for i in range(replicas):
        place = jnp.int32(0)
        for k in range(1, replicas):
            place = place + jnp.where(owners_ref[k] == replica ^ i, k, 0)
        left_ref[:, i * width : (i + 1) * width] = token_buf[place]
    if replicas > 1:
        for i in range(shards):
            for k in range(replicas):
                picked = jnp.where(owners_ref[shard ^ i] == replica ^ k, 1.0, 0.0)
                row = i * replicas + k
                pick_ref[row : row + 1, :] = jnp.full((1, lanes), picked, f32)

    lengths_copy.wait()
    row = lax.broadcasted_iota(jnp.int32, (rows, lanes), 0)
    lane = lax.broadcasted_iota(jnp.int32, (rows, lanes), 1)
    position = row // row_count
    for b in range(row_count):
        position = position + jnp.where(row % row_count == b, lengths_ref[b], 0)
    angles = position.astype(f32) * turns_ref[:1, :]
    cosine_ref[...] = jnp.cos(angles)
    sine = jnp.sin(angles)
    sine_ref[...] = jnp.where(lane < lanes // 2, -sine, sine)
    slot = lax.broadcasted_iota(jnp.int32, bias_ref.shape, 1)
    whose = lax.broadcasted_iota(jnp.int32, bias_ref.shape, 0)
    length = jnp.zeros(bias_ref.shape, jnp.int32)
    for b in range(row_count):
        length = jnp.where(whose == b, lengths_ref[b], length)
    bias_ref[...] = jnp.where(slot < length, 0.0, masked_score)


def project(
    owners, lengths, tokens, weight, turns, after, step_count, slots, shards, replicas
):
    rows, depth = tokens.shape
    row_count = rows // step_count
    own = weight.shape[1] // shards
    piece_width = -(-depth // replicas // lanes) * lanes
    table = jax.ShapeDtypeStruct((rows, lanes), f32)
    outs = pl.pallas_call(
        functools.partial(project_kernel, step_count, row_count, shards, replicas),
        out_shape=[jax.ShapeDtypeStruct((rows, own), bf16)] * (shards - 1)
        + [
            jax.ShapeDtypeStruct((rows, replicas * piece_width), bf16),
            jax.ShapeDtypeStruct((shards * replicas, lanes), f32),
            table,
            table,
            jax.ShapeDtypeStruct((row_count, slots), f32),
        ],
        in_specs=[stays_in_hbm] * 2 + [whole_in_vmem] * 4,
        out_specs=[whole_in_vmem] * (shards + 4),
        scratch_shapes=[
            pltpu.SMEM(owners.shape, jnp.int32),
            pltpu.SMEM(lengths.shape, jnp.int32),
            pltpu.VMEM((replicas, rows, piece_width), bf16),
            pltpu.SemaphoreType.DMA((2,)),
        ],
        compiler_params=pltpu.CompilerParams(vmem_limit_bytes=6 * 2**20),
        name="project",
        cost_estimate=pl.CostEstimate(
            flops=2 * rows * weight.size, bytes_accessed=2 * weight.size, transcendentals=0
        ),
    )(*in_hbm(owners, lengths), tokens, weight, turns, after)
    return outs[: shards - 1], *outs[shards - 1 :]


def attend_kernel(
    step_count,
    head_count,
    queries_ref,
    keys_ref,
    values_ref,
    bias_ref,
    _,
    tokens_ref,
    weight_ref,
    own_ref,
    grouped_ref,
    total_ref,
    peak_ref,
    sum_ref,
    regroup,
    scores_ref,
    raised,
):
    own_ref[...] = product(tokens_ref, weight_ref, lax.axis_index("tensor"), own_ref.shape[1])

    row_count, slots, _ = keys_ref.shape
    group = queries_ref.shape[1] // (head_count * lanes)
    seen = step_count * group
    for pair in range(step_count // 2):
        for q in range(head_count * group):
            h, g = q // group, q % group
            both = queries_ref[
                pair * 2 * row_count : (pair + 1) * 2 * row_count, q * lanes : (q + 1) * lanes
            ].astype(f32)
            for side in range(2):
                first = h * row_count * seen + (pair * 2 + side) * group + g
                regroup[pl.ds(first, row_count, stride=seen), :] = both[
                    side * row_count : (side + 1) * row_count, :
                ]
            if g % 2:
                for side in range(2):
                    half = slice(side * row_count, (side + 1) * row_count)
                    last = (h * seen + (pair * 2 + side) * group + g + 1) * row_count
                    grouped_ref[last - 2 * row_count : last, :] = jnp.concatenate(
                        [before[half], both[half]], axis=0
                    ).astype(bf16)
            before = both

    for b in range(row_count):
        for h in range(head_count):
            at = (h * row_count + b) * seen
            scores_ref[at : at + seen, :] = lax.dot_general(
                regroup[at : at + seen, :].astype(bf16),
                keys_ref[b, :, h * lanes : (h + 1) * lanes],
                (((1,), (1,)), ((), ())),
                preferred_element_type=f32,
            )

    places = [
        (
            b,
            h,
            slice((h * row_count + b) * seen, (h * row_count + b + 1) * seen),
            pl.ds(h * row_count * seen + b, seen, stride=row_count),
        )
        for b in range(row_count)
        for h in range(head_count)
    ]
    for b, h, place, out in places:
        score = scores_ref[place, :] + bias_ref[b : b + 1, :]
        peak = jnp.max(score, axis=1, keepdims=True)
        lifted = jnp.exp2((score - peak) * exponent_scale)
        raised[place, :] = lifted.astype(bf16)
        peak_ref[out, :] = jnp.broadcast_to(peak, (seen, lanes))
        sum_ref[out, :] = jnp.broadcast_to(
            jnp.sum(lifted, axis=1, keepdims=True), (seen, lanes)
        )
    for b, h, place, out in places:
        total_ref[out, :] = jnp.dot(
            raised[place, :],
            values_ref[b, :, h * lanes : (h + 1) * lanes],
            preferred_element_type=f32,
        )


def attend(queries, keys, values, bias, after, tokens, weight, own, step_count):
    row_count, slots, width = keys.shape
    seen_rows = step_count * row_count * queries.shape[1] // lanes
    seen_table = jax.ShapeDtypeStruct((seen_rows, lanes), f32)
    return pl.pallas_call(
        functools.partial(attend_kernel, step_count, width // lanes),
        out_shape=(
            jax.ShapeDtypeStruct((tokens.shape[0], own), f32),
            jax.ShapeDtypeStruct((seen_rows, lanes), bf16),
            seen_table,
            seen_table,
            seen_table,
        ),
        in_specs=[whole_in_vmem] * 7,
        out_specs=(whole_in_vmem,) * 5,
        scratch_shapes=[
            pltpu.VMEM((seen_rows, lanes), f32),
            pltpu.VMEM((seen_rows, slots), f32),
            pltpu.VMEM((seen_rows, slots), bf16),
        ],
        compiler_params=pltpu.CompilerParams(vmem_limit_bytes=8 * 2**20),
        name="attend",
        cost_estimate=pl.CostEstimate(
            flops=4 * seen_rows * slots * lanes,
            bytes_accessed=2 * (keys.size + values.size),
            transcendentals=seen_rows * slots,
        ),
    )(queries, keys, values, bias, after, tokens, weight)


def piece_places(replicas):
    order = [0, 1] + list(range(replicas - 1, 1, -1))
    return [order.index(i) for i in range(replicas)]


def route_kernel(replicas, shards, *refs):
    left_ref, pick_ref = refs[:2]
    piece_refs = [refs[2 + place] for place in piece_places(replicas)]
    out_refs = refs[2 + replicas : 2 + replicas + shards]
    (right,) = refs[2 + replicas + shards :]
    up_rows = out_refs[0].shape[0] - left_ref.shape[0]
    rows = left_ref.shape[0]
    rank = right.shape[0]
    width = right.shape[1] // replicas
    half = rank // 2
    rest = (piece_refs[0].shape[0] - up_rows) % rank
    for i in range(replicas):
        first = 0
        for c in range(width // lanes - (1 if rest else 0)):
            right[:, i * width + c * lanes : i * width + (c + 1) * lanes] = piece_refs[i][
                first : first + rank, :
            ]
            first += rank
        if rest:
            both = piece_refs[i][first : first + half, :]
            tail = jnp.concatenate([both[:, : lanes // 2], both[:, lanes // 2 :]], axis=0)
            right[:, (i + 1) * width - lanes : (i + 1) * width] = jnp.concatenate(
                [tail, jnp.zeros((rank, lanes // 2), bf16)], axis=1
            )
            first += half
    lowered = lax.dot_general(
        left_ref[...], right[...], (((1,), (1,)), ((), ())), preferred_element_type=f32
    )
    both = jnp.concatenate(split_halves(lowered), axis=1)
    ups = [piece[piece.shape[0] - up_rows :, :].astype(f32) for piece in piece_refs]
    for i in range(shards):
        out_refs[i][:rows, :] = both
        picked = sum(up * pick_ref[i * replicas + k, :][None, :] for k, up in enumerate(ups))
        out_refs[i][rows:, :] = picked.astype(bf16)


def route(left, pick, pieces, rank, up_rows, shards):
    rows, depth = left.shape
    replicas = len(pieces)
    return pl.pallas_call(
        functools.partial(route_kernel, replicas, shards),
        out_shape=[jax.ShapeDtypeStruct((rows + up_rows, lanes), bf16)] * shards,
        in_specs=[whole_in_vmem] * (2 + replicas),
        out_specs=[whole_in_vmem] * shards,
        scratch_shapes=[pltpu.VMEM((rank, depth), bf16)],
        compiler_params=pltpu.CompilerParams(vmem_limit_bytes=4 * 2**20),
        name="route",
        cost_estimate=pl.CostEstimate(flops=0, bytes_accessed=800000, transcendentals=0),
    )(left, pick, *[pieces[i] for i in piece_places(replicas)])


def route_plain(owners, tokens, down, up, rank_part, own, shards):
    rank = down.shape[1]
    shard = lax.axis_index("tensor")
    first = shard * rank_part
    up_part = lax.dynamic_slice_in_dim(up, first, rank_part, axis=0)
    downs = lax.all_gather(down, "rollout", axis=0, tiled=False)
    ups = lax.all_gather(up_part, "rollout", axis=0, tiled=False)
    down_matrix = jnp.take(downs, owners, axis=0, mode="clip").reshape(-1, rank)
    up_matrix = jnp.take(ups, owners, axis=0, mode="clip").transpose(1, 0, 2)
    up_matrix = up_matrix.reshape(rank_part, -1)
    lowered = jnp.dot(tokens, down_matrix, preferred_element_type=f32)
    both = jnp.concatenate(split_halves(lowered), axis=1)
    packets = []
    for i in range(shards):
        up_block = lax.dynamic_slice_in_dim(up_matrix, (shard ^ i) * own, own, axis=1)
        parts = [both, side_by_side(up_block)]
        packets.append(jnp.concatenate(parts, axis=0))
    return packets


def finish_kernel(step_count, row_count, head_count, shards, *refs):
    gain_ref, base_ref, grouped_ref, total_ref, peak_ref, sum_ref, cosine_ref, sine_ref = refs[:8]
    packet_refs = refs[8 : 8 + shards][::-1]
    sum_refs = refs[8 + shards : 7 + 2 * shards]
    attention_ref, keys_ref, values_ref = refs[7 + 2 * shards : 10 + 2 * shards]
    (up_buf,) = refs[10 + 2 * shards :]
    shard = lax.axis_index("tensor")
    rows = step_count * row_count
    own = base_ref.shape[1]
    blocks = own // lanes
    rank = up_buf.shape[0]
    rank_part = rank // shards
    group = grouped_ref.shape[0] // (head_count * rows)
    seen = step_count * group

    lowered = jnp.zeros((rows, lanes), f32)
    for i in range(shards):
        lowered = lowered + packet_refs[i][:rows, :].astype(f32)
        ups = packet_refs[i][rows:, :].astype(f32)
        at = pl.multiple_of((shard ^ i) * rank_part, rank_part)
        for c in range(blocks):
            up_buf[pl.ds(at, rank_part), c * lanes : (c + 1) * lanes] = ups[
                c * rank_part : (c + 1) * rank_part, :
            ]
    lane = lax.broadcasted_iota(jnp.int32, (rows, lanes), 1)
    lowered = lowered + pltpu.roll(lowered, rank, 1)
    high, low = split_halves(lowered)
    left = jnp.where(lane < rank, high.astype(f32), low.astype(f32)).astype(bf16)
    up = up_buf[...].astype(bf16)
    raised_up = jnp.dot(left, jnp.concatenate([up, up], axis=0), preferred_element_type=f32)
    joined = []
    for c in range(blocks):
        block = base_ref[:, c * lanes : (c + 1) * lanes]
        for partial_ref in sum_refs:
            block = block + partial_ref[:, c * lanes : (c + 1) * lanes].astype(f32)
        joined.append(block + adapter_scale * raised_up[:, c * lanes : (c + 1) * lanes])

    all_rows = row_count * seen
    seen_by = lax.broadcasted_iota(jnp.int32, (all_rows, rows), 0)
    made_by = lax.broadcasted_iota(jnp.int32, (all_rows, rows), 1)
    visible = (seen_by % row_count == made_by % row_count) & (
        made_by // row_count <= seen_by // (row_count * group)
    )
    heads = [(h, slice(h * all_rows, (h + 1) * all_rows)) for h in range(head_count)]
    keys, values, scores, results = [], [], [], []
    for h, _ in heads:
        raw_key = joined[2 * h]
        mean_square = jnp.mean(raw_key * raw_key, axis=1, keepdims=True)
        normed = raw_key * lax.rsqrt(mean_square + norm_eps) * gain_ref[...]
        key = normed * cosine_ref[...] + pltpu.roll(normed, lanes // 2, 1) * sine_ref[...]
        keys.append(key.astype(bf16))
        values.append(joined[2 * h + 1].astype(bf16))
        keys_ref[:, h * lanes : (h + 1) * lanes] = keys[h]
        values_ref[:, h * lanes : (h + 1) * lanes] = values[h]
    for h, mine in heads:
        score = lax.dot_general(
            grouped_ref[mine, :], keys[h], (((1,), (1,)), ((), ())), preferred_element_type=f32
        )
        scores.append(jnp.where(visible, score, masked_score))
    for h, mine in heads:
        old_peak = peak_ref[mine, :]
        peak = jnp.maximum(old_peak, jnp.max(scores[h], axis=1, keepdims=True))
        fade = jnp.exp2((old_peak - peak) * exponent_scale)
        lifted = jnp.exp2((scores[h] - peak[:, :rows]) * exponent_scale)
        denominator = fade * sum_ref[mine, :] + jnp.sum(lifted, axis=1, keepdims=True)
        total = fade * total_ref[mine, :] + jnp.dot(
            lifted.astype(bf16), values[h], preferred_element_type=f32
        )
        results.append(total / denominator)
    for pair in range(step_count // 2):
        for q in range(head_count * group):
            h, g = q // group, q % group
            both = []
            for side in range(2):
                first = ((pair * 2 + side) * group + g) * row_count
                both.append(results[h][first : first + row_count])
            attention_ref[
                pair * 2 * row_count : (pair + 1) * 2 * row_count, q * lanes : (q + 1) * lanes
            ] = jnp.concatenate(both, axis=0).astype(bf16)


def finish(mine, others, partials, gain, packets, rank, step_count, row_count, query_width):
    rows, own = mine.shape
    shards = len(packets)
    head_count = own // (2 * lanes)
    return pl.pallas_call(
        functools.partial(finish_kernel, step_count, row_count, head_count, shards),
        out_shape=(
            jax.ShapeDtypeStruct((rows, query_width), bf16),
            jax.ShapeDtypeStruct((rows, head_count * lanes), bf16),
            jax.ShapeDtypeStruct((rows, head_count * lanes), bf16),
        ),
        in_specs=[whole_in_vmem] * (7 + 2 * shards),
        out_specs=(whole_in_vmem,) * 3,
        scratch_shapes=[
            pltpu.VMEM((rank, own), f32),
        ],
        compiler_params=pltpu.CompilerParams(vmem_limit_bytes=6 * 2**20),
        name="finish",
        cost_estimate=pl.CostEstimate(flops=0, bytes_accessed=1000000, transcendentals=0),
    )(gain, mine, *partials, *packets[::-1], *others[::-1])


def per_device(
    normed_tokens,
    key_value_weight,
    adapter_down,
    adapter_up,
    key_gain,
    queries,
    cache_keys,
    stored_values,
    lengths,
    owners,
):
    replicas = lax.axis_size("rollout")
    shards = lax.axis_size("tensor")
    down_rows, rank = adapter_down.shape
    step_count, row_count, depth = normed_tokens.shape
    own = key_value_weight.shape[1] // shards
    rank_part = rank // shards
    rows = step_count * row_count
    tokens = normed_tokens.reshape(rows, depth)
    query_rows = queries.reshape(rows, -1)

    fits = (
        replicas <= 4
        and adapter_up.shape[1] == own
        and down_rows % lanes in (0, lanes // 2)
        and rank == lanes // 2
        and rank_part % 16 == 0
    )
    fetched = 2 * (key_value_weight.size + cache_keys.size + stored_values.size)
    turns = frequencies(
        pl.CostEstimate(flops=1000 * fetched, bytes_accessed=fetched, transcendentals=0)
    )
    if fits:
        packed = pack(adapter_down.T, adapter_up, rank_part, turns)
        pieces = [packed] + [swap(packed, "rollout", i) for i in range(1, replicas)]
    blocks, left, pick, cosine, sine, bias = project(
        owners,
        lengths,
        tokens,
        key_value_weight,
        turns,
        packed if fits else adapter_up,
        step_count,
        cache_keys.shape[1],
        shards,
        replicas if fits else 1,
    )
    others = [swap(block, "tensor", i + 1) for i, block in enumerate(blocks)]
    if fits:
        packets = route(left, pick, pieces, rank, rank_part * own // lanes, shards)
    else:
        packets = route_plain(
            owners, tokens, adapter_down, adapter_up, rank_part, own, shards
        )
    mine, grouped, total, peak, denominator = attend(
        query_rows,
        cache_keys,
        stored_values,
        bias,
        packets[0],
        tokens,
        key_value_weight,
        own,
        step_count,
    )
    packets = [packets[0]] + [swap(packets[i], "tensor", i) for i in range(1, shards)]
    attention, keys, values = finish(
        mine,
        others,
        (grouped, total, peak, denominator, cosine, sine),
        key_gain.reshape(1, -1),
        packets,
        rank,
        step_count,
        row_count,
        query_rows.shape[1],
    )
    return tuple(a.reshape(step_count, row_count, -1) for a in (attention, keys, values))


def solution(mesh):
    placed = (
        P(None, ("job", "rollout"), "tensor"),
        P("tensor", None),
        P(("job", "rollout", "tensor"), None),
        P(None, ("job", "rollout")),
        P(),
        P(None, ("job", "rollout"), "tensor"),
        P(("job", "rollout"), None, "tensor"),
        P(("job", "rollout"), None, "tensor"),
        P(("job", "rollout")),
        P("job"),
    )
    return jax.shard_map(
        per_device,
        mesh=mesh,
        in_specs=placed,
        out_specs=(
            P(None, ("job", "rollout"), "tensor"),
            P(None, ("job", "rollout"), "tensor"),
            P(None, ("job", "rollout"), "tensor"),
        ),
        check_vma=False,
    )
```

```python
import functools
import math

import jax
import jax.numpy as jnp
from jax import lax
from jax.experimental import pallas as pl
from jax.experimental.pallas import tpu as pltpu
from jax.sharding import PartitionSpec as P

norm_eps = 1e-06
rope_base = 1000000.0
adapter_scale = 2.0
masked_score = -1e30
lanes = 128
exponent_scale = lanes**-0.5 / math.log(2.0)
f32 = jnp.float32
bf16 = jnp.bfloat16

whole_in_vmem = pl.BlockSpec(memory_space=pltpu.VMEM)
whole_in_smem = pl.BlockSpec(memory_space=pltpu.SMEM)
stays_in_hbm = pl.BlockSpec(memory_space=pltpu.HBM)


def swap(block, axis, offset):
    count = lax.axis_size(axis)
    return lax.ppermute(block, axis, [(s, s ^ offset) for s in range(count)])


def in_hbm(*arrays):
    return tuple(pltpu.with_memory_space_constraint(a, pltpu.HBM) for a in arrays)


def side_by_side(rows_of_blocks):
    r, c = rows_of_blocks.shape
    return rows_of_blocks.reshape(r, c // lanes, lanes).transpose(1, 0, 2).reshape(-1, lanes)


def split_halves(total):
    high = total.astype(bf16)
    return high, (total - high.astype(f32)).astype(bf16)


def frequencies_kernel(out_ref):
    lane = lax.broadcasted_iota(jnp.int32, out_ref.shape, 1)
    spacing = (lane % (lanes // 2)).astype(f32) * (-2.0 / lanes * math.log(rope_base))
    out_ref[...] = jnp.exp(spacing)


def frequencies(beside):
    return pl.pallas_call(
        frequencies_kernel,
        out_shape=jax.ShapeDtypeStruct((8, lanes), f32),
        out_specs=whole_in_vmem,
        compiler_params=pltpu.CompilerParams(vmem_limit_bytes=2**20),
        name="frequencies",
        cost_estimate=beside,
    )()


def pack_kernel(down_ref, up_all_ref, _, out_ref):
    rank, down_rows = down_ref.shape
    rank_part = (out_ref.shape[0] * lanes - down_ref.size) // up_all_ref.shape[1]
    start = pl.multiple_of(lax.axis_index("tensor") * rank_part, rank_part)
    up_ref = up_all_ref.at[pl.ds(start, rank_part), :]
    first = 0
    for c in range(down_rows // lanes):
        out_ref[first : first + rank, :] = down_ref[:, c * lanes : (c + 1) * lanes]
        first += rank
    rest = down_rows % lanes
    if rest:
        half = rank // 2
        tail = down_ref[:, down_rows - rest :]
        out_ref[first : first + half, :] = jnp.concatenate([tail[:half], tail[half:]], axis=1)
        first += half
    for c in range(up_ref.shape[1] // lanes):
        out_ref[first : first + rank_part, :] = up_ref[:, c * lanes : (c + 1) * lanes]
        first += rank_part


def pack(down, up, rank_part, after):
    rows = (down.size + rank_part * up.shape[1]) // lanes
    return pl.pallas_call(
        pack_kernel,
        out_shape=jax.ShapeDtypeStruct((rows, lanes), bf16),
        in_specs=[whole_in_vmem] * 3,
        out_specs=whole_in_vmem,
        compiler_params=pltpu.CompilerParams(vmem_limit_bytes=2 * 2**20),
        name="pack",
        cost_estimate=pl.CostEstimate(flops=0, bytes_accessed=200000, transcendentals=0),
    )(down, up, after)


def product(tokens_ref, weight_ref, owner, own):
    columns = pl.ds(pl.multiple_of(owner * own, lanes), own)
    return jnp.dot(tokens_ref[...], weight_ref[:, columns], preferred_element_type=f32)


def project_kernel(step_count, row_count, shards, replicas, *refs):
    owners_hbm, lengths_hbm, tokens_ref, weight_ref, turns_ref, _, _, _ = refs[:8]
    block_refs = refs[8 : 7 + shards]
    left_ref, pick_ref, cosine_ref, sine_ref, bias_ref = refs[7 + shards : 12 + shards]
    owners_ref, lengths_ref, token_buf, sems = refs[12 + shards :]
    owners_copy = pltpu.make_async_copy(owners_hbm, owners_ref, sems.at[0])
    lengths_copy = pltpu.make_async_copy(lengths_hbm, lengths_ref, sems.at[1])
    owners_copy.start()
    lengths_copy.start()

    shard = lax.axis_index("tensor")
    rows, own = block_refs[0].shape
    for i in reversed(range(1, shards)):
        block_refs[i - 1][...] = product(tokens_ref, weight_ref, shard ^ i, own).astype(bf16)

    owners_copy.wait()
    replica = lax.axis_index("rollout")
    width = token_buf.shape[2]
    down_rows = tokens_ref.shape[1] // replicas
    for k in range(replicas):
        token_buf[k, :, :down_rows] = tokens_ref[:, k * down_rows : (k + 1) * down_rows]
        if down_rows < width:
            token_buf[k, :, down_rows:] = jnp.zeros((rows, width - down_rows), bf16)
    for i in range(replicas):
        place = jnp.int32(0)
        for k in range(1, replicas):
            place = place + jnp.where(owners_ref[k] == replica ^ i, k, 0)
        left_ref[:, i * width : (i + 1) * width] = token_buf[place]
    if replicas > 1:
        for i in range(shards):
            for k in range(replicas):
                picked = jnp.where(owners_ref[shard ^ i] == replica ^ k, 1.0, 0.0)
                row = i * replicas + k
                pick_ref[row : row + 1, :] = jnp.full((1, lanes), picked, f32)

    lengths_copy.wait()
    row = lax.broadcasted_iota(jnp.int32, (rows, lanes), 0)
    lane = lax.broadcasted_iota(jnp.int32, (rows, lanes), 1)
    position = row // row_count
    for b in range(row_count):
        position = position + jnp.where(row % row_count == b, lengths_ref[b], 0)
    angles = position.astype(f32) * turns_ref[:1, :]
    cosine_ref[...] = jnp.cos(angles)
    sine = jnp.sin(angles)
    sine_ref[...] = jnp.where(lane < lanes // 2, -sine, sine)
    slot = lax.broadcasted_iota(jnp.int32, bias_ref.shape, 1)
    whose = lax.broadcasted_iota(jnp.int32, bias_ref.shape, 0)
    length = jnp.zeros(bias_ref.shape, jnp.int32)
    for b in range(row_count):
        length = jnp.where(whose == b, lengths_ref[b], length)
    bias_ref[...] = jnp.where(slot < length, 0.0, masked_score)


def project(
    owners, lengths, tokens, weight, turns, after, keys, values, step_count, shards, replicas
):
    rows, depth = tokens.shape
    row_count = rows // step_count
    own = weight.shape[1] // shards
    piece_width = -(-depth // replicas // lanes) * lanes
    table = jax.ShapeDtypeStruct((rows, lanes), f32)
    outs = pl.pallas_call(
        functools.partial(project_kernel, step_count, row_count, shards, replicas),
        out_shape=[jax.ShapeDtypeStruct((rows, own), bf16)] * (shards - 1)
        + [
            jax.ShapeDtypeStruct((rows, replicas * piece_width), bf16),
            jax.ShapeDtypeStruct((shards * replicas, lanes), f32),
            table,
            table,
            jax.ShapeDtypeStruct((row_count, keys.shape[1]), f32),
        ],
        in_specs=[stays_in_hbm] * 2 + [whole_in_vmem] * 6,
        out_specs=[whole_in_vmem] * (shards + 4),
        scratch_shapes=[
            pltpu.SMEM(owners.shape, jnp.int32),
            pltpu.SMEM(lengths.shape, jnp.int32),
            pltpu.VMEM((replicas, rows, piece_width), bf16),
            pltpu.SemaphoreType.DMA((2,)),
        ],
        compiler_params=pltpu.CompilerParams(vmem_limit_bytes=6 * 2**20),
        name="project",
        cost_estimate=pl.CostEstimate(flops=0, bytes_accessed=200000, transcendentals=0),
    )(*in_hbm(owners, lengths), tokens, weight, turns, after, keys, values)
    return outs[: shards - 1], *outs[shards - 1 :]


def attend_kernel(
    step_count,
    head_count,
    queries_ref,
    keys_ref,
    values_ref,
    bias_ref,
    _,
    tokens_ref,
    weight_ref,
    own_ref,
    grouped_ref,
    total_ref,
    peak_ref,
    sum_ref,
    regroup,
    scores_ref,
    raised,
):
    own_ref[...] = product(tokens_ref, weight_ref, lax.axis_index("tensor"), own_ref.shape[1])

    row_count, slots, _ = keys_ref.shape
    group = queries_ref.shape[1] // (head_count * lanes)
    seen = step_count * group
    for pair in range(step_count // 2):
        for q in range(head_count * group):
            h, g = q // group, q % group
            both = queries_ref[
                pair * 2 * row_count : (pair + 1) * 2 * row_count, q * lanes : (q + 1) * lanes
            ].astype(f32)
            for side in range(2):
                first = h * row_count * seen + (pair * 2 + side) * group + g
                regroup[pl.ds(first, row_count, stride=seen), :] = both[
                    side * row_count : (side + 1) * row_count, :
                ]
            if g % 2:
                for side in range(2):
                    half = slice(side * row_count, (side + 1) * row_count)
                    last = (h * seen + (pair * 2 + side) * group + g + 1) * row_count
                    grouped_ref[last - 2 * row_count : last, :] = jnp.concatenate(
                        [before[half], both[half]], axis=0
                    ).astype(bf16)
            before = both

    for b in range(row_count):
        for h in range(head_count):
            at = (h * row_count + b) * seen
            scores_ref[at : at + seen, :] = lax.dot_general(
                regroup[at : at + seen, :].astype(bf16),
                keys_ref[b, :, h * lanes : (h + 1) * lanes],
                (((1,), (1,)), ((), ())),
                preferred_element_type=f32,
            )

    places = [
        (
            b,
            h,
            slice((h * row_count + b) * seen, (h * row_count + b + 1) * seen),
            pl.ds(h * row_count * seen + b, seen, stride=row_count),
        )
        for b in range(row_count)
        for h in range(head_count)
    ]
    for b, h, place, out in places:
        score = scores_ref[place, :] + bias_ref[b : b + 1, :]
        peak = jnp.max(score, axis=1, keepdims=True)
        lifted = jnp.exp2((score - peak) * exponent_scale)
        raised[place, :] = lifted.astype(bf16)
        peak_ref[out, :] = jnp.broadcast_to(peak, (seen, lanes))
        sum_ref[out, :] = jnp.broadcast_to(
            jnp.sum(lifted, axis=1, keepdims=True), (seen, lanes)
        )
    for b, h, place, out in places:
        total_ref[out, :] = jnp.dot(
            raised[place, :],
            values_ref[b, :, h * lanes : (h + 1) * lanes],
            preferred_element_type=f32,
        )


def attend(queries, keys, values, bias, after, tokens, weight, own, step_count):
    row_count, slots, width = keys.shape
    seen_rows = step_count * row_count * queries.shape[1] // lanes
    seen_table = jax.ShapeDtypeStruct((seen_rows, lanes), f32)
    return pl.pallas_call(
        functools.partial(attend_kernel, step_count, width // lanes),
        out_shape=(
            jax.ShapeDtypeStruct((tokens.shape[0], own), f32),
            jax.ShapeDtypeStruct((seen_rows, lanes), bf16),
            seen_table,
            seen_table,
            seen_table,
        ),
        in_specs=[whole_in_vmem] * 7,
        out_specs=(whole_in_vmem,) * 5,
        scratch_shapes=[
            pltpu.VMEM((seen_rows, lanes), f32),
            pltpu.VMEM((seen_rows, slots), f32),
            pltpu.VMEM((seen_rows, slots), bf16),
        ],
        compiler_params=pltpu.CompilerParams(vmem_limit_bytes=8 * 2**20),
        name="attend",
        cost_estimate=pl.CostEstimate(
            flops=4 * seen_rows * slots * lanes,
            bytes_accessed=2 * (keys.size + values.size),
            transcendentals=seen_rows * slots,
        ),
    )(queries, keys, values, bias, after, tokens, weight)


def piece_places(replicas):
    order = [0, 1] + list(range(replicas - 1, 1, -1))
    return [order.index(i) for i in range(replicas)]


def route_kernel(replicas, shards, *refs):
    left_ref, pick_ref = refs[:2]
    piece_refs = [refs[2 + place] for place in piece_places(replicas)]
    out_refs = refs[2 + replicas : 2 + replicas + shards]
    (right,) = refs[2 + replicas + shards :]
    up_rows = out_refs[0].shape[0] - left_ref.shape[0]
    rows = left_ref.shape[0]
    rank = right.shape[0]
    width = right.shape[1] // replicas
    half = rank // 2
    rest = (piece_refs[0].shape[0] - up_rows) % rank
    for i in range(replicas):
        first = 0
        for c in range(width // lanes - (1 if rest else 0)):
            right[:, i * width + c * lanes : i * width + (c + 1) * lanes] = piece_refs[i][
                first : first + rank, :
            ]
            first += rank
        if rest:
            both = piece_refs[i][first : first + half, :]
            tail = jnp.concatenate([both[:, : lanes // 2], both[:, lanes // 2 :]], axis=0)
            right[:, (i + 1) * width - lanes : (i + 1) * width] = jnp.concatenate(
                [tail, jnp.zeros((rank, lanes // 2), bf16)], axis=1
            )
            first += half
    lowered = lax.dot_general(
        left_ref[...], right[...], (((1,), (1,)), ((), ())), preferred_element_type=f32
    )
    both = jnp.concatenate(split_halves(lowered), axis=1)
    ups = [piece[piece.shape[0] - up_rows :, :].astype(f32) for piece in piece_refs]
    for i in range(shards):
        out_refs[i][:rows, :] = both
        picked = sum(up * pick_ref[i * replicas + k, :][None, :] for k, up in enumerate(ups))
        out_refs[i][rows:, :] = picked.astype(bf16)


def route(left, pick, pieces, rank, up_rows, shards):
    rows, depth = left.shape
    replicas = len(pieces)
    return pl.pallas_call(
        functools.partial(route_kernel, replicas, shards),
        out_shape=[jax.ShapeDtypeStruct((rows + up_rows, lanes), bf16)] * shards,
        in_specs=[whole_in_vmem] * (2 + replicas),
        out_specs=[whole_in_vmem] * shards,
        scratch_shapes=[pltpu.VMEM((rank, depth), bf16)],
        compiler_params=pltpu.CompilerParams(vmem_limit_bytes=4 * 2**20),
        name="route",
        cost_estimate=pl.CostEstimate(flops=0, bytes_accessed=800000, transcendentals=0),
    )(left, pick, *[pieces[i] for i in piece_places(replicas)])


def route_plain(owners, tokens, down, up, rank_part, own, shards):
    rank = down.shape[1]
    shard = lax.axis_index("tensor")
    first = shard * rank_part
    up_part = lax.dynamic_slice_in_dim(up, first, rank_part, axis=0)
    downs = lax.all_gather(down, "rollout", axis=0, tiled=False)
    ups = lax.all_gather(up_part, "rollout", axis=0, tiled=False)
    down_matrix = jnp.take(downs, owners, axis=0, mode="clip").reshape(-1, rank)
    up_matrix = jnp.take(ups, owners, axis=0, mode="clip").transpose(1, 0, 2)
    up_matrix = up_matrix.reshape(rank_part, -1)
    lowered = jnp.dot(tokens, down_matrix, preferred_element_type=f32)
    both = jnp.concatenate(split_halves(lowered), axis=1)
    packets = []
    for i in range(shards):
        up_block = lax.dynamic_slice_in_dim(up_matrix, (shard ^ i) * own, own, axis=1)
        parts = [both, side_by_side(up_block)]
        packets.append(jnp.concatenate(parts, axis=0))
    return packets


def finish_kernel(step_count, row_count, head_count, shards, *refs):
    gain_ref, base_ref, grouped_ref, total_ref, peak_ref, sum_ref, cosine_ref, sine_ref = refs[:8]
    packet_refs = refs[8 : 8 + shards][::-1]
    sum_refs = refs[8 + shards : 7 + 2 * shards]
    attention_ref, keys_ref, values_ref = refs[7 + 2 * shards : 10 + 2 * shards]
    (up_buf,) = refs[10 + 2 * shards :]
    shard = lax.axis_index("tensor")
    rows = step_count * row_count
    own = base_ref.shape[1]
    blocks = own // lanes
    rank = up_buf.shape[0]
    rank_part = rank // shards
    group = grouped_ref.shape[0] // (head_count * rows)
    seen = step_count * group

    lowered = jnp.zeros((rows, lanes), f32)
    for i in range(shards):
        lowered = lowered + packet_refs[i][:rows, :].astype(f32)
        ups = packet_refs[i][rows:, :].astype(f32)
        at = pl.multiple_of((shard ^ i) * rank_part, rank_part)
        for c in range(blocks):
            up_buf[pl.ds(at, rank_part), c * lanes : (c + 1) * lanes] = ups[
                c * rank_part : (c + 1) * rank_part, :
            ]
    lane = lax.broadcasted_iota(jnp.int32, (rows, lanes), 1)
    lowered = lowered + pltpu.roll(lowered, rank, 1)
    high, low = split_halves(lowered)
    left = jnp.where(lane < rank, high.astype(f32), low.astype(f32)).astype(bf16)
    up = up_buf[...].astype(bf16)
    raised_up = jnp.dot(left, jnp.concatenate([up, up], axis=0), preferred_element_type=f32)
    joined = []
    for c in range(blocks):
        block = base_ref[:, c * lanes : (c + 1) * lanes]
        for partial_ref in sum_refs:
            block = block + partial_ref[:, c * lanes : (c + 1) * lanes].astype(f32)
        joined.append(block + adapter_scale * raised_up[:, c * lanes : (c + 1) * lanes])

    all_rows = row_count * seen
    seen_by = lax.broadcasted_iota(jnp.int32, (all_rows, rows), 0)
    made_by = lax.broadcasted_iota(jnp.int32, (all_rows, rows), 1)
    visible = (seen_by % row_count == made_by % row_count) & (
        made_by // row_count <= seen_by // (row_count * group)
    )
    heads = [(h, slice(h * all_rows, (h + 1) * all_rows)) for h in range(head_count)]
    keys, values, scores, results = [], [], [], []
    for h, _ in heads:
        raw_key = joined[2 * h]
        mean_square = jnp.mean(raw_key * raw_key, axis=1, keepdims=True)
        normed = raw_key * lax.rsqrt(mean_square + norm_eps) * gain_ref[...]
        key = normed * cosine_ref[...] + pltpu.roll(normed, lanes // 2, 1) * sine_ref[...]
        keys.append(key.astype(bf16))
        values.append(joined[2 * h + 1].astype(bf16))
        keys_ref[:, h * lanes : (h + 1) * lanes] = keys[h]
        values_ref[:, h * lanes : (h + 1) * lanes] = values[h]
    for h, mine in heads:
        score = lax.dot_general(
            grouped_ref[mine, :], keys[h], (((1,), (1,)), ((), ())), preferred_element_type=f32
        )
        scores.append(jnp.where(visible, score, masked_score))
    for h, mine in heads:
        old_peak = peak_ref[mine, :]
        peak = jnp.maximum(old_peak, jnp.max(scores[h], axis=1, keepdims=True))
        fade = jnp.exp2((old_peak - peak) * exponent_scale)
        lifted = jnp.exp2((scores[h] - peak[:, :rows]) * exponent_scale)
        denominator = fade * sum_ref[mine, :] + jnp.sum(lifted, axis=1, keepdims=True)
        total = fade * total_ref[mine, :] + jnp.dot(
            lifted.astype(bf16), values[h], preferred_element_type=f32
        )
        results.append(total / denominator)
    for pair in range(step_count // 2):
        for q in range(head_count * group):
            h, g = q // group, q % group
            both = []
            for side in range(2):
                first = ((pair * 2 + side) * group + g) * row_count
                both.append(results[h][first : first + row_count])
            attention_ref[
                pair * 2 * row_count : (pair + 1) * 2 * row_count, q * lanes : (q + 1) * lanes
            ] = jnp.concatenate(both, axis=0).astype(bf16)


def finish(mine, others, partials, gain, packets, rank, step_count, row_count, query_width):
    rows, own = mine.shape
    shards = len(packets)
    head_count = own // (2 * lanes)
    return pl.pallas_call(
        functools.partial(finish_kernel, step_count, row_count, head_count, shards),
        out_shape=(
            jax.ShapeDtypeStruct((rows, query_width), bf16),
            jax.ShapeDtypeStruct((rows, head_count * lanes), bf16),
            jax.ShapeDtypeStruct((rows, head_count * lanes), bf16),
        ),
        in_specs=[whole_in_vmem] * (7 + 2 * shards),
        out_specs=(whole_in_vmem,) * 3,
        scratch_shapes=[
            pltpu.VMEM((rank, own), f32),
        ],
        compiler_params=pltpu.CompilerParams(vmem_limit_bytes=6 * 2**20),
        name="finish",
        cost_estimate=pl.CostEstimate(flops=0, bytes_accessed=1000000, transcendentals=0),
    )(gain, mine, *partials, *packets[::-1], *others[::-1])


def per_device(
    normed_tokens,
    key_value_weight,
    adapter_down,
    adapter_up,
    key_gain,
    queries,
    cache_keys,
    stored_values,
    lengths,
    owners,
):
    replicas = lax.axis_size("rollout")
    shards = lax.axis_size("tensor")
    down_rows, rank = adapter_down.shape
    step_count, row_count, depth = normed_tokens.shape
    own = key_value_weight.shape[1] // shards
    rank_part = rank // shards
    rows = step_count * row_count
    tokens = normed_tokens.reshape(rows, depth)
    query_rows = queries.reshape(rows, -1)

    fits = (
        replicas <= 4
        and adapter_up.shape[1] == own
        and down_rows % lanes in (0, lanes // 2)
        and rank == lanes // 2
        and rank_part % 16 == 0
    )
    fetched = 2 * (key_value_weight.size + cache_keys.size + stored_values.size)
    turns = frequencies(
        pl.CostEstimate(flops=1000 * fetched, bytes_accessed=fetched, transcendentals=0)
    )
    if fits:
        packed = pack(adapter_down.T, adapter_up, rank_part, turns)
        pieces = [packed] + [swap(packed, "rollout", i) for i in range(1, replicas)]
    blocks, left, pick, cosine, sine, bias = project(
        owners,
        lengths,
        tokens,
        key_value_weight,
        turns,
        packed if fits else adapter_up,
        cache_keys,
        stored_values,
        step_count,
        shards,
        replicas if fits else 1,
    )
    others = [swap(block, "tensor", i + 1) for i, block in enumerate(blocks)]
    if fits:
        packets = route(left, pick, pieces, rank, rank_part * own // lanes, shards)
    else:
        packets = route_plain(
            owners, tokens, adapter_down, adapter_up, rank_part, own, shards
        )
    mine, grouped, total, peak, denominator = attend(
        query_rows,
        cache_keys,
        stored_values,
        bias,
        packets[0],
        tokens,
        key_value_weight,
        own,
        step_count,
    )
    packets = [packets[0]] + [swap(packets[i], "tensor", i) for i in range(1, shards)]
    attention, keys, values = finish(
        mine,
        others,
        (grouped, total, peak, denominator, cosine, sine),
        key_gain.reshape(1, -1),
        packets,
        rank,
        step_count,
        row_count,
        query_rows.shape[1],
    )
    return tuple(a.reshape(step_count, row_count, -1) for a in (attention, keys, values))


def solution(mesh):
    placed = (
        P(None, ("job", "rollout"), "tensor"),
        P("tensor", None),
        P(("job", "rollout", "tensor"), None),
        P(None, ("job", "rollout")),
        P(),
        P(None, ("job", "rollout"), "tensor"),
        P(("job", "rollout"), None, "tensor"),
        P(("job", "rollout"), None, "tensor"),
        P(("job", "rollout")),
        P("job"),
    )
    return jax.shard_map(
        per_device,
        mesh=mesh,
        in_specs=placed,
        out_specs=(
            P(None, ("job", "rollout"), "tensor"),
            P(None, ("job", "rollout"), "tensor"),
            P(None, ("job", "rollout"), "tensor"),
        ),
        check_vma=False,
    )
```

```python
import functools
import math

import jax
import jax.numpy as jnp
from jax import lax
from jax.experimental import pallas as pl
from jax.experimental.pallas import tpu as pltpu
from jax.sharding import PartitionSpec as P

norm_eps = 1e-06
rope_base = 1000000.0
adapter_scale = 2.0
masked_score = -1e30
lanes = 128
exponent_scale = lanes**-0.5 / math.log(2.0)
f32 = jnp.float32
bf16 = jnp.bfloat16

whole_in_vmem = pl.BlockSpec(memory_space=pltpu.VMEM)
whole_in_smem = pl.BlockSpec(memory_space=pltpu.SMEM)
stays_in_hbm = pl.BlockSpec(memory_space=pltpu.HBM)


def swap(block, axis, offset):
    count = lax.axis_size(axis)
    return lax.ppermute(block, axis, [(s, s ^ offset) for s in range(count)])


def in_hbm(*arrays):
    return tuple(pltpu.with_memory_space_constraint(a, pltpu.HBM) for a in arrays)


def side_by_side(rows_of_blocks):
    r, c = rows_of_blocks.shape
    return rows_of_blocks.reshape(r, c // lanes, lanes).transpose(1, 0, 2).reshape(-1, lanes)


def split_halves(total):
    high = total.astype(bf16)
    return high, (total - high.astype(f32)).astype(bf16)


def frequencies_kernel(out_ref):
    lane = lax.broadcasted_iota(jnp.int32, out_ref.shape, 1)
    spacing = (lane % (lanes // 2)).astype(f32) * (-2.0 / lanes * math.log(rope_base))
    out_ref[...] = jnp.exp(spacing)


def frequencies(beside):
    return pl.pallas_call(
        frequencies_kernel,
        out_shape=jax.ShapeDtypeStruct((8, lanes), f32),
        out_specs=whole_in_vmem,
        compiler_params=pltpu.CompilerParams(vmem_limit_bytes=2**20),
        name="frequencies",
        cost_estimate=beside,
    )()


def pack_kernel(down_ref, up_all_ref, _, out_ref):
    rank, down_rows = down_ref.shape
    rank_part = (out_ref.shape[0] * lanes - down_ref.size) // up_all_ref.shape[1]
    start = pl.multiple_of(lax.axis_index("tensor") * rank_part, rank_part)
    up_ref = up_all_ref.at[pl.ds(start, rank_part), :]
    first = 0
    for c in range(down_rows // lanes):
        out_ref[first : first + rank, :] = down_ref[:, c * lanes : (c + 1) * lanes]
        first += rank
    rest = down_rows % lanes
    if rest:
        half = rank // 2
        tail = down_ref[:, down_rows - rest :]
        out_ref[first : first + half, :] = jnp.concatenate([tail[:half], tail[half:]], axis=1)
        first += half
    for c in range(up_ref.shape[1] // lanes):
        out_ref[first : first + rank_part, :] = up_ref[:, c * lanes : (c + 1) * lanes]
        first += rank_part


def pack(down, up, rank_part, after):
    rows = (down.size + rank_part * up.shape[1]) // lanes
    return pl.pallas_call(
        pack_kernel,
        out_shape=jax.ShapeDtypeStruct((rows, lanes), bf16),
        in_specs=[whole_in_vmem] * 3,
        out_specs=whole_in_vmem,
        compiler_params=pltpu.CompilerParams(vmem_limit_bytes=2 * 2**20),
        name="pack",
        cost_estimate=pl.CostEstimate(flops=0, bytes_accessed=200000, transcendentals=0),
    )(down, up, after)


def product(tokens_ref, weight_ref, owner, own):
    columns = pl.ds(pl.multiple_of(owner * own, lanes), own)
    return jnp.dot(tokens_ref[...], weight_ref[:, columns], preferred_element_type=f32)


def project_kernel(step_count, row_count, shards, replicas, *refs):
    owners_hbm, lengths_hbm, tokens_ref, weight_ref, turns_ref, _, _, _ = refs[:8]
    block_refs = refs[8 : 7 + shards]
    left_ref, pick_ref, cosine_ref, sine_ref, bias_ref = refs[7 + shards : 12 + shards]
    owners_ref, lengths_ref, token_buf, sems = refs[12 + shards :]
    owners_copy = pltpu.make_async_copy(owners_hbm, owners_ref, sems.at[0])
    lengths_copy = pltpu.make_async_copy(lengths_hbm, lengths_ref, sems.at[1])
    owners_copy.start()
    lengths_copy.start()

    shard = lax.axis_index("tensor")
    rows, own = block_refs[0].shape
    for i in reversed(range(1, shards)):
        block_refs[i - 1][...] = product(tokens_ref, weight_ref, shard ^ i, own).astype(bf16)

    owners_copy.wait()
    replica = lax.axis_index("rollout")
    width = token_buf.shape[2]
    down_rows = tokens_ref.shape[1] // replicas
    for k in range(replicas):
        token_buf[k, :, :down_rows] = tokens_ref[:, k * down_rows : (k + 1) * down_rows]
        if down_rows < width:
            token_buf[k, :, down_rows:] = jnp.zeros((rows, width - down_rows), bf16)
    for i in range(replicas):
        place = jnp.int32(0)
        for k in range(1, replicas):
            place = place + jnp.where(owners_ref[k] == replica ^ i, k, 0)
        left_ref[:, i * width : (i + 1) * width] = token_buf[place]
    if replicas > 1:
        for i in range(shards):
            for k in range(replicas):
                picked = jnp.where(owners_ref[shard ^ i] == replica ^ k, 1.0, 0.0)
                row = i * replicas + k
                pick_ref[row : row + 1, :] = jnp.full((1, lanes), picked, f32)

    lengths_copy.wait()
    row = lax.broadcasted_iota(jnp.int32, (rows, lanes), 0)
    lane = lax.broadcasted_iota(jnp.int32, (rows, lanes), 1)
    position = row // row_count
    for b in range(row_count):
        position = position + jnp.where(row % row_count == b, lengths_ref[b], 0)
    angles = position.astype(f32) * turns_ref[:1, :]
    cosine_ref[...] = jnp.cos(angles)
    sine = jnp.sin(angles)
    sine_ref[...] = jnp.where(lane < lanes // 2, -sine, sine)
    slot = lax.broadcasted_iota(jnp.int32, bias_ref.shape, 1)
    whose = lax.broadcasted_iota(jnp.int32, bias_ref.shape, 0)
    length = jnp.zeros(bias_ref.shape, jnp.int32)
    for b in range(row_count):
        length = jnp.where(whose == b, lengths_ref[b], length)
    bias_ref[...] = jnp.where(slot < length, 0.0, masked_score)


def project(
    owners, lengths, tokens, weight, turns, after, keys, values, step_count, shards, replicas
):
    rows, depth = tokens.shape
    row_count = rows // step_count
    own = weight.shape[1] // shards
    piece_width = -(-depth // replicas // lanes) * lanes
    table = jax.ShapeDtypeStruct((rows, lanes), f32)
    outs = pl.pallas_call(
        functools.partial(project_kernel, step_count, row_count, shards, replicas),
        out_shape=[jax.ShapeDtypeStruct((rows, own), bf16)] * (shards - 1)
        + [
            jax.ShapeDtypeStruct((rows, replicas * piece_width), bf16),
            jax.ShapeDtypeStruct((shards * replicas, lanes), f32),
            table,
            table,
            jax.ShapeDtypeStruct((row_count, keys.shape[1]), f32),
        ],
        in_specs=[stays_in_hbm] * 2 + [whole_in_vmem] * 6,
        out_specs=[whole_in_vmem] * (shards + 4),
        scratch_shapes=[
            pltpu.SMEM(owners.shape, jnp.int32),
            pltpu.SMEM(lengths.shape, jnp.int32),
            pltpu.VMEM((replicas, rows, piece_width), bf16),
            pltpu.SemaphoreType.DMA((2,)),
        ],
        compiler_params=pltpu.CompilerParams(vmem_limit_bytes=6 * 2**20),
        name="project",
        cost_estimate=pl.CostEstimate(flops=0, bytes_accessed=200000, transcendentals=0),
    )(*in_hbm(owners, lengths), tokens, weight, turns, after, keys, values)
    return outs[: shards - 1], *outs[shards - 1 :]


def attend_kernel(
    step_count,
    head_count,
    queries_ref,
    keys_ref,
    values_ref,
    bias_ref,
    _,
    tokens_ref,
    weight_ref,
    own_ref,
    grouped_ref,
    total_ref,
    peak_ref,
    sum_ref,
    regroup,
    scores_ref,
    raised,
):
    own_ref[...] = product(tokens_ref, weight_ref, lax.axis_index("tensor"), own_ref.shape[1])

    row_count, slots, _ = keys_ref.shape
    group = queries_ref.shape[1] // (head_count * lanes)
    seen = step_count * group
    for pair in range(step_count // 2):
        for q in range(head_count * group):
            h, g = q // group, q % group
            both = queries_ref[
                pair * 2 * row_count : (pair + 1) * 2 * row_count, q * lanes : (q + 1) * lanes
            ].astype(f32)
            for side in range(2):
                first = h * row_count * seen + (pair * 2 + side) * group + g
                regroup[pl.ds(first, row_count, stride=seen), :] = both[
                    side * row_count : (side + 1) * row_count, :
                ]
            if g % 2:
                for side in range(2):
                    half = slice(side * row_count, (side + 1) * row_count)
                    last = (h * seen + (pair * 2 + side) * group + g + 1) * row_count
                    grouped_ref[last - 2 * row_count : last, :] = jnp.concatenate(
                        [before[half], both[half]], axis=0
                    ).astype(bf16)
            before = both

    for b in range(row_count):
        for h in range(head_count):
            at = (h * row_count + b) * seen
            scores_ref[at : at + seen, :] = lax.dot_general(
                regroup[at : at + seen, :].astype(bf16),
                keys_ref[b, :, h * lanes : (h + 1) * lanes],
                (((1,), (1,)), ((), ())),
                preferred_element_type=f32,
            )

    places = [
        (
            b,
            h,
            slice((h * row_count + b) * seen, (h * row_count + b + 1) * seen),
            pl.ds(h * row_count * seen + b, seen, stride=row_count),
        )
        for b in range(row_count)
        for h in range(head_count)
    ]
    for b, h, place, out in places:
        score = scores_ref[place, :] + bias_ref[b : b + 1, :]
        peak = jnp.max(score, axis=1, keepdims=True)
        lifted = jnp.exp2((score - peak) * exponent_scale)
        raised[place, :] = lifted.astype(bf16)
        peak_ref[out, :] = jnp.broadcast_to(peak, (seen, lanes))
        sum_ref[out, :] = jnp.broadcast_to(
            jnp.sum(lifted, axis=1, keepdims=True), (seen, lanes)
        )
    for b, h, place, out in places:
        total_ref[out, :] = jnp.dot(
            raised[place, :],
            values_ref[b, :, h * lanes : (h + 1) * lanes],
            preferred_element_type=f32,
        )


def attend(queries, keys, values, bias, after, tokens, weight, own, step_count):
    row_count, slots, width = keys.shape
    seen_rows = step_count * row_count * queries.shape[1] // lanes
    seen_table = jax.ShapeDtypeStruct((seen_rows, lanes), f32)
    return pl.pallas_call(
        functools.partial(attend_kernel, step_count, width // lanes),
        out_shape=(
            jax.ShapeDtypeStruct((tokens.shape[0], own), f32),
            jax.ShapeDtypeStruct((seen_rows, lanes), bf16),
            seen_table,
            seen_table,
            seen_table,
        ),
        in_specs=[whole_in_vmem] * 7,
        out_specs=(whole_in_vmem,) * 5,
        scratch_shapes=[
            pltpu.VMEM((seen_rows, lanes), f32),
            pltpu.VMEM((seen_rows, slots), f32),
            pltpu.VMEM((seen_rows, slots), bf16),
        ],
        compiler_params=pltpu.CompilerParams(vmem_limit_bytes=8 * 2**20),
        name="attend",
        cost_estimate=pl.CostEstimate(
            flops=4 * seen_rows * slots * lanes,
            bytes_accessed=2 * (keys.size + values.size),
            transcendentals=seen_rows * slots,
        ),
    )(queries, keys, values, bias, after, tokens, weight)


def piece_places(replicas):
    return [0] + list(range(replicas - 1, 0, -1))


def route_kernel(replicas, shards, *refs):
    left_ref, pick_ref = refs[:2]
    piece_refs = [refs[2 + place] for place in piece_places(replicas)]
    out_refs = refs[2 + replicas : 2 + replicas + shards]
    (right,) = refs[2 + replicas + shards :]
    up_rows = out_refs[0].shape[0] - left_ref.shape[0]
    rows = left_ref.shape[0]
    rank = right.shape[0]
    width = right.shape[1] // replicas
    half = rank // 2
    rest = (piece_refs[0].shape[0] - up_rows) % rank
    for i in range(replicas):
        first = 0
        for c in range(width // lanes - (1 if rest else 0)):
            right[:, i * width + c * lanes : i * width + (c + 1) * lanes] = piece_refs[i][
                first : first + rank, :
            ]
            first += rank
        if rest:
            both = piece_refs[i][first : first + half, :]
            tail = jnp.concatenate([both[:, : lanes // 2], both[:, lanes // 2 :]], axis=0)
            right[:, (i + 1) * width - lanes : (i + 1) * width] = jnp.concatenate(
                [tail, jnp.zeros((rank, lanes // 2), bf16)], axis=1
            )
            first += half
    lowered = lax.dot_general(
        left_ref[...], right[...], (((1,), (1,)), ((), ())), preferred_element_type=f32
    )
    both = jnp.concatenate(split_halves(lowered), axis=1)
    ups = [piece[piece.shape[0] - up_rows :, :].astype(f32) for piece in piece_refs]
    for i in range(shards):
        out_refs[i][:rows, :] = both
        picked = sum(up * pick_ref[i * replicas + k, :][None, :] for k, up in enumerate(ups))
        out_refs[i][rows:, :] = picked.astype(bf16)


def route(left, pick, pieces, rank, up_rows, shards):
    rows, depth = left.shape
    replicas = len(pieces)
    return pl.pallas_call(
        functools.partial(route_kernel, replicas, shards),
        out_shape=[jax.ShapeDtypeStruct((rows + up_rows, lanes), bf16)] * shards,
        in_specs=[whole_in_vmem] * (2 + replicas),
        out_specs=[whole_in_vmem] * shards,
        scratch_shapes=[pltpu.VMEM((rank, depth), bf16)],
        compiler_params=pltpu.CompilerParams(vmem_limit_bytes=4 * 2**20),
        name="route",
        cost_estimate=pl.CostEstimate(flops=0, bytes_accessed=800000, transcendentals=0),
    )(left, pick, *[pieces[i] for i in piece_places(replicas)])


def route_plain(owners, tokens, down, up, rank_part, own, shards):
    rank = down.shape[1]
    shard = lax.axis_index("tensor")
    first = shard * rank_part
    up_part = lax.dynamic_slice_in_dim(up, first, rank_part, axis=0)
    downs = lax.all_gather(down, "rollout", axis=0, tiled=False)
    ups = lax.all_gather(up_part, "rollout", axis=0, tiled=False)
    down_matrix = jnp.take(downs, owners, axis=0, mode="clip").reshape(-1, rank)
    up_matrix = jnp.take(ups, owners, axis=0, mode="clip").transpose(1, 0, 2)
    up_matrix = up_matrix.reshape(rank_part, -1)
    lowered = jnp.dot(tokens, down_matrix, preferred_element_type=f32)
    both = jnp.concatenate(split_halves(lowered), axis=1)
    packets = []
    for i in range(shards):
        up_block = lax.dynamic_slice_in_dim(up_matrix, (shard ^ i) * own, own, axis=1)
        parts = [both, side_by_side(up_block)]
        packets.append(jnp.concatenate(parts, axis=0))
    return packets


def finish_kernel(step_count, row_count, head_count, shards, *refs):
    gain_ref, base_ref, grouped_ref, total_ref, peak_ref, sum_ref, cosine_ref, sine_ref = refs[:8]
    packet_refs = refs[8 : 8 + shards][::-1]
    sum_refs = refs[8 + shards : 7 + 2 * shards]
    attention_ref, keys_ref, values_ref = refs[7 + 2 * shards : 10 + 2 * shards]
    (up_buf,) = refs[10 + 2 * shards :]
    shard = lax.axis_index("tensor")
    rows = step_count * row_count
    own = base_ref.shape[1]
    blocks = own // lanes
    rank = up_buf.shape[0]
    rank_part = rank // shards
    group = grouped_ref.shape[0] // (head_count * rows)
    seen = step_count * group

    lowered = jnp.zeros((rows, lanes), f32)
    for i in range(shards):
        lowered = lowered + packet_refs[i][:rows, :].astype(f32)
        ups = packet_refs[i][rows:, :].astype(f32)
        at = pl.multiple_of((shard ^ i) * rank_part, rank_part)
        for c in range(blocks):
            up_buf[pl.ds(at, rank_part), c * lanes : (c + 1) * lanes] = ups[
                c * rank_part : (c + 1) * rank_part, :
            ]
    lane = lax.broadcasted_iota(jnp.int32, (rows, lanes), 1)
    lowered = lowered + pltpu.roll(lowered, rank, 1)
    high, low = split_halves(lowered)
    left = jnp.where(lane < rank, high.astype(f32), low.astype(f32)).astype(bf16)
    up = up_buf[...].astype(bf16)
    raised_up = jnp.dot(left, jnp.concatenate([up, up], axis=0), preferred_element_type=f32)
    joined = []
    for c in range(blocks):
        block = base_ref[:, c * lanes : (c + 1) * lanes]
        for partial_ref in sum_refs:
            block = block + partial_ref[:, c * lanes : (c + 1) * lanes].astype(f32)
        joined.append(block + adapter_scale * raised_up[:, c * lanes : (c + 1) * lanes])

    all_rows = row_count * seen
    seen_by = lax.broadcasted_iota(jnp.int32, (all_rows, rows), 0)
    made_by = lax.broadcasted_iota(jnp.int32, (all_rows, rows), 1)
    visible = (seen_by % row_count == made_by % row_count) & (
        made_by // row_count <= seen_by // (row_count * group)
    )
    heads = [(h, slice(h * all_rows, (h + 1) * all_rows)) for h in range(head_count)]
    keys, values, scores, results = [], [], [], []
    for h, _ in heads:
        raw_key = joined[2 * h]
        mean_square = jnp.mean(raw_key * raw_key, axis=1, keepdims=True)
        normed = raw_key * lax.rsqrt(mean_square + norm_eps) * gain_ref[...]
        key = normed * cosine_ref[...] + pltpu.roll(normed, lanes // 2, 1) * sine_ref[...]
        keys.append(key.astype(bf16))
        values.append(joined[2 * h + 1].astype(bf16))
        keys_ref[:, h * lanes : (h + 1) * lanes] = keys[h]
        values_ref[:, h * lanes : (h + 1) * lanes] = values[h]
    for h, mine in heads:
        score = lax.dot_general(
            grouped_ref[mine, :], keys[h], (((1,), (1,)), ((), ())), preferred_element_type=f32
        )
        scores.append(jnp.where(visible, score, masked_score))
    for h, mine in heads:
        old_peak = peak_ref[mine, :]
        peak = jnp.maximum(old_peak, jnp.max(scores[h], axis=1, keepdims=True))
        fade = jnp.exp2((old_peak - peak) * exponent_scale)
        lifted = jnp.exp2((scores[h] - peak[:, :rows]) * exponent_scale)
        denominator = fade * sum_ref[mine, :] + jnp.sum(lifted, axis=1, keepdims=True)
        total = fade * total_ref[mine, :] + jnp.dot(
            lifted.astype(bf16), values[h], preferred_element_type=f32
        )
        results.append(total / denominator)
    for pair in range(step_count // 2):
        for q in range(head_count * group):
            h, g = q // group, q % group
            both = []
            for side in range(2):
                first = ((pair * 2 + side) * group + g) * row_count
                both.append(results[h][first : first + row_count])
            attention_ref[
                pair * 2 * row_count : (pair + 1) * 2 * row_count, q * lanes : (q + 1) * lanes
            ] = jnp.concatenate(both, axis=0).astype(bf16)


def finish(mine, others, partials, gain, packets, rank, step_count, row_count, query_width):
    rows, own = mine.shape
    shards = len(packets)
    head_count = own // (2 * lanes)
    return pl.pallas_call(
        functools.partial(finish_kernel, step_count, row_count, head_count, shards),
        out_shape=(
            jax.ShapeDtypeStruct((rows, query_width), bf16),
            jax.ShapeDtypeStruct((rows, head_count * lanes), bf16),
            jax.ShapeDtypeStruct((rows, head_count * lanes), bf16),
        ),
        in_specs=[whole_in_vmem] * (7 + 2 * shards),
        out_specs=(whole_in_vmem,) * 3,
        scratch_shapes=[
            pltpu.VMEM((rank, own), f32),
        ],
        compiler_params=pltpu.CompilerParams(vmem_limit_bytes=6 * 2**20),
        name="finish",
        cost_estimate=pl.CostEstimate(flops=0, bytes_accessed=1000000, transcendentals=0),
    )(gain, mine, *partials, *packets[::-1], *others[::-1])


def per_device(
    normed_tokens,
    key_value_weight,
    adapter_down,
    adapter_up,
    key_gain,
    queries,
    cache_keys,
    stored_values,
    lengths,
    owners,
):
    replicas = lax.axis_size("rollout")
    shards = lax.axis_size("tensor")
    down_rows, rank = adapter_down.shape
    step_count, row_count, depth = normed_tokens.shape
    own = key_value_weight.shape[1] // shards
    rank_part = rank // shards
    rows = step_count * row_count
    tokens = normed_tokens.reshape(rows, depth)
    query_rows = queries.reshape(rows, -1)

    fits = (
        replicas <= 4
        and adapter_up.shape[1] == own
        and down_rows % lanes in (0, lanes // 2)
        and rank == lanes // 2
        and rank_part % 16 == 0
    )
    fetched = 2 * (key_value_weight.size + cache_keys.size + stored_values.size)
    turns = frequencies(
        pl.CostEstimate(flops=1000 * fetched, bytes_accessed=fetched, transcendentals=0)
    )
    if fits:
        packed = pack(adapter_down.T, adapter_up, rank_part, turns)
        pieces = [packed] + [swap(packed, "rollout", i) for i in range(1, replicas)]
    blocks, left, pick, cosine, sine, bias = project(
        owners,
        lengths,
        tokens,
        key_value_weight,
        turns,
        packed if fits else adapter_up,
        cache_keys,
        stored_values,
        step_count,
        shards,
        replicas if fits else 1,
    )
    others = [swap(block, "tensor", i + 1) for i, block in enumerate(blocks)]
    if fits:
        packets = route(left, pick, pieces, rank, rank_part * own // lanes, shards)
    else:
        packets = route_plain(
            owners, tokens, adapter_down, adapter_up, rank_part, own, shards
        )
    mine, grouped, total, peak, denominator = attend(
        query_rows,
        cache_keys,
        stored_values,
        bias,
        packets[0],
        tokens,
        key_value_weight,
        own,
        step_count,
    )
    packets = [packets[0]] + [swap(packets[i], "tensor", i) for i in range(1, shards)]
    attention, keys, values = finish(
        mine,
        others,
        (grouped, total, peak, denominator, cosine, sine),
        key_gain.reshape(1, -1),
        packets,
        rank,
        step_count,
        row_count,
        query_rows.shape[1],
    )
    return tuple(a.reshape(step_count, row_count, -1) for a in (attention, keys, values))


def solution(mesh):
    placed = (
        P(None, ("job", "rollout"), "tensor"),
        P("tensor", None),
        P(("job", "rollout", "tensor"), None),
        P(None, ("job", "rollout")),
        P(),
        P(None, ("job", "rollout"), "tensor"),
        P(("job", "rollout"), None, "tensor"),
        P(("job", "rollout"), None, "tensor"),
        P(("job", "rollout")),
        P("job"),
    )
    return jax.shard_map(
        per_device,
        mesh=mesh,
        in_specs=placed,
        out_specs=(
            P(None, ("job", "rollout"), "tensor"),
            P(None, ("job", "rollout"), "tensor"),
            P(None, ("job", "rollout"), "tensor"),
        ),
        check_vma=False,
    )
```

```python
import functools
import math

import jax
import jax.numpy as jnp
from jax import lax
from jax.experimental import pallas as pl
from jax.experimental.pallas import tpu as pltpu
from jax.sharding import PartitionSpec as P

norm_eps = 1e-06
rope_base = 1000000.0
adapter_scale = 2.0
masked_score = -1e30
lanes = 128
exponent_scale = lanes**-0.5 / math.log(2.0)
f32 = jnp.float32
bf16 = jnp.bfloat16

whole_in_vmem = pl.BlockSpec(memory_space=pltpu.VMEM)
whole_in_smem = pl.BlockSpec(memory_space=pltpu.SMEM)
stays_in_hbm = pl.BlockSpec(memory_space=pltpu.HBM)


def swap(block, axis, offset):
    count = lax.axis_size(axis)
    return lax.ppermute(block, axis, [(s, s ^ offset) for s in range(count)])


def in_hbm(*arrays):
    return tuple(pltpu.with_memory_space_constraint(a, pltpu.HBM) for a in arrays)


def side_by_side(rows_of_blocks):
    r, c = rows_of_blocks.shape
    return rows_of_blocks.reshape(r, c // lanes, lanes).transpose(1, 0, 2).reshape(-1, lanes)


def split_halves(total):
    high = total.astype(bf16)
    return high, (total - high.astype(f32)).astype(bf16)


def frequencies_kernel(out_ref):
    lane = lax.broadcasted_iota(jnp.int32, out_ref.shape, 1)
    spacing = (lane % (lanes // 2)).astype(f32) * (-2.0 / lanes * math.log(rope_base))
    out_ref[...] = jnp.exp(spacing)


def frequencies(beside):
    return pl.pallas_call(
        frequencies_kernel,
        out_shape=jax.ShapeDtypeStruct((8, lanes), f32),
        out_specs=whole_in_vmem,
        compiler_params=pltpu.CompilerParams(vmem_limit_bytes=2**20),
        name="frequencies",
        cost_estimate=beside,
    )()


def pack_kernel(down_ref, up_all_ref, _, out_ref):
    rank, down_rows = down_ref.shape
    rank_part = (out_ref.shape[0] * lanes - down_ref.size) // up_all_ref.shape[1]
    start = pl.multiple_of(lax.axis_index("tensor") * rank_part, rank_part)
    up_ref = up_all_ref.at[pl.ds(start, rank_part), :]
    first = 0
    for c in range(down_rows // lanes):
        out_ref[first : first + rank, :] = down_ref[:, c * lanes : (c + 1) * lanes]
        first += rank
    rest = down_rows % lanes
    if rest:
        half = rank // 2
        tail = down_ref[:, down_rows - rest :]
        out_ref[first : first + half, :] = jnp.concatenate([tail[:half], tail[half:]], axis=1)
        first += half
    for c in range(up_ref.shape[1] // lanes):
        out_ref[first : first + rank_part, :] = up_ref[:, c * lanes : (c + 1) * lanes]
        first += rank_part


def pack(down, up, rank_part, after, beside):
    rows = (down.size + rank_part * up.shape[1]) // lanes
    return pl.pallas_call(
        pack_kernel,
        out_shape=jax.ShapeDtypeStruct((rows, lanes), bf16),
        in_specs=[whole_in_vmem] * 3,
        out_specs=whole_in_vmem,
        compiler_params=pltpu.CompilerParams(vmem_limit_bytes=2 * 2**20),
        name="pack",
        cost_estimate=beside,
    )(down, up, after)


def product(tokens_ref, weight_ref, owner, own):
    columns = pl.ds(pl.multiple_of(owner * own, lanes), own)
    return jnp.dot(tokens_ref[...], weight_ref[:, columns], preferred_element_type=f32)


def project_kernel(step_count, row_count, shards, replicas, *refs):
    owners_hbm, lengths_hbm, tokens_ref, weight_ref, turns_ref, _, _, _ = refs[:8]
    block_refs = refs[8 : 7 + shards]
    left_ref, pick_ref, cosine_ref, sine_ref, bias_ref = refs[7 + shards : 12 + shards]
    owners_ref, lengths_ref, token_buf, sems = refs[12 + shards :]
    owners_copy = pltpu.make_async_copy(owners_hbm, owners_ref, sems.at[0])
    lengths_copy = pltpu.make_async_copy(lengths_hbm, lengths_ref, sems.at[1])
    owners_copy.start()
    lengths_copy.start()

    shard = lax.axis_index("tensor")
    rows, own = block_refs[0].shape
    for i in reversed(range(1, shards)):
        block_refs[i - 1][...] = product(tokens_ref, weight_ref, shard ^ i, own).astype(bf16)

    owners_copy.wait()
    replica = lax.axis_index("rollout")
    width = token_buf.shape[2]
    down_rows = tokens_ref.shape[1] // replicas
    for k in range(replicas):
        token_buf[k, :, :down_rows] = tokens_ref[:, k * down_rows : (k + 1) * down_rows]
        if down_rows < width:
            token_buf[k, :, down_rows:] = jnp.zeros((rows, width - down_rows), bf16)
    for i in range(replicas):
        place = jnp.int32(0)
        for k in range(1, replicas):
            place = place + jnp.where(owners_ref[k] == replica ^ i, k, 0)
        left_ref[:, i * width : (i + 1) * width] = token_buf[place]
    if replicas > 1:
        for i in range(shards):
            for k in range(replicas):
                picked = jnp.where(owners_ref[shard ^ i] == replica ^ k, 1.0, 0.0)
                row = i * replicas + k
                pick_ref[row : row + 1, :] = jnp.full((1, lanes), picked, f32)

    lengths_copy.wait()
    row = lax.broadcasted_iota(jnp.int32, (rows, lanes), 0)
    lane = lax.broadcasted_iota(jnp.int32, (rows, lanes), 1)
    position = row // row_count
    for b in range(row_count):
        position = position + jnp.where(row % row_count == b, lengths_ref[b], 0)
    angles = position.astype(f32) * turns_ref[:1, :]
    cosine_ref[...] = jnp.cos(angles)
    sine = jnp.sin(angles)
    sine_ref[...] = jnp.where(lane < lanes // 2, -sine, sine)
    slot = lax.broadcasted_iota(jnp.int32, bias_ref.shape, 1)
    whose = lax.broadcasted_iota(jnp.int32, bias_ref.shape, 0)
    length = jnp.zeros(bias_ref.shape, jnp.int32)
    for b in range(row_count):
        length = jnp.where(whose == b, lengths_ref[b], length)
    bias_ref[...] = jnp.where(slot < length, 0.0, masked_score)


def project(
    owners, lengths, tokens, weight, turns, after, keys, values, step_count, shards, replicas
):
    rows, depth = tokens.shape
    row_count = rows // step_count
    own = weight.shape[1] // shards
    piece_width = -(-depth // replicas // lanes) * lanes
    table = jax.ShapeDtypeStruct((rows, lanes), f32)
    outs = pl.pallas_call(
        functools.partial(project_kernel, step_count, row_count, shards, replicas),
        out_shape=[jax.ShapeDtypeStruct((rows, own), bf16)] * (shards - 1)
        + [
            jax.ShapeDtypeStruct((rows, replicas * piece_width), bf16),
            jax.ShapeDtypeStruct((shards * replicas, lanes), f32),
            table,
            table,
            jax.ShapeDtypeStruct((row_count, keys.shape[1]), f32),
        ],
        in_specs=[stays_in_hbm] * 2 + [whole_in_vmem] * 6,
        out_specs=[whole_in_vmem] * (shards + 4),
        scratch_shapes=[
            pltpu.SMEM(owners.shape, jnp.int32),
            pltpu.SMEM(lengths.shape, jnp.int32),
            pltpu.VMEM((replicas, rows, piece_width), bf16),
            pltpu.SemaphoreType.DMA((2,)),
        ],
        compiler_params=pltpu.CompilerParams(vmem_limit_bytes=6 * 2**20),
        name="project",
        cost_estimate=pl.CostEstimate(flops=0, bytes_accessed=200000, transcendentals=0),
    )(*in_hbm(owners, lengths), tokens, weight, turns, after, keys, values)
    return outs[: shards - 1], *outs[shards - 1 :]


def attend_kernel(
    step_count,
    head_count,
    queries_ref,
    keys_ref,
    values_ref,
    bias_ref,
    _,
    tokens_ref,
    weight_ref,
    own_ref,
    grouped_ref,
    total_ref,
    peak_ref,
    sum_ref,
    regroup,
    scores_ref,
    raised,
):
    own_ref[...] = product(tokens_ref, weight_ref, lax.axis_index("tensor"), own_ref.shape[1])

    row_count, slots, _ = keys_ref.shape
    group = queries_ref.shape[1] // (head_count * lanes)
    seen = step_count * group
    for pair in range(step_count // 2):
        for q in range(head_count * group):
            h, g = q // group, q % group
            both = queries_ref[
                pair * 2 * row_count : (pair + 1) * 2 * row_count, q * lanes : (q + 1) * lanes
            ].astype(f32)
            for side in range(2):
                first = h * row_count * seen + (pair * 2 + side) * group + g
                regroup[pl.ds(first, row_count, stride=seen), :] = both[
                    side * row_count : (side + 1) * row_count, :
                ]
            if g % 2:
                for side in range(2):
                    half = slice(side * row_count, (side + 1) * row_count)
                    last = (h * seen + (pair * 2 + side) * group + g + 1) * row_count
                    grouped_ref[last - 2 * row_count : last, :] = jnp.concatenate(
                        [before[half], both[half]], axis=0
                    ).astype(bf16)
            before = both

    for b in range(row_count):
        for h in range(head_count):
            at = (h * row_count + b) * seen
            scores_ref[at : at + seen, :] = lax.dot_general(
                regroup[at : at + seen, :].astype(bf16),
                keys_ref[b, :, h * lanes : (h + 1) * lanes],
                (((1,), (1,)), ((), ())),
                preferred_element_type=f32,
            )

    places = [
        (
            b,
            h,
            slice((h * row_count + b) * seen, (h * row_count + b + 1) * seen),
            pl.ds(h * row_count * seen + b, seen, stride=row_count),
        )
        for b in range(row_count)
        for h in range(head_count)
    ]
    for b, h, place, out in places:
        score = scores_ref[place, :] + bias_ref[b : b + 1, :]
        peak = jnp.max(score, axis=1, keepdims=True)
        lifted = jnp.exp2((score - peak) * exponent_scale)
        raised[place, :] = lifted.astype(bf16)
        peak_ref[out, :] = jnp.broadcast_to(peak, (seen, lanes))
        sum_ref[out, :] = jnp.broadcast_to(
            jnp.sum(lifted, axis=1, keepdims=True), (seen, lanes)
        )
    for b, h, place, out in places:
        total_ref[out, :] = jnp.dot(
            raised[place, :],
            values_ref[b, :, h * lanes : (h + 1) * lanes],
            preferred_element_type=f32,
        )


def attend(queries, keys, values, bias, after, tokens, weight, own, step_count):
    row_count, slots, width = keys.shape
    seen_rows = step_count * row_count * queries.shape[1] // lanes
    seen_table = jax.ShapeDtypeStruct((seen_rows, lanes), f32)
    return pl.pallas_call(
        functools.partial(attend_kernel, step_count, width // lanes),
        out_shape=(
            jax.ShapeDtypeStruct((tokens.shape[0], own), f32),
            jax.ShapeDtypeStruct((seen_rows, lanes), bf16),
            seen_table,
            seen_table,
            seen_table,
        ),
        in_specs=[whole_in_vmem] * 7,
        out_specs=(whole_in_vmem,) * 5,
        scratch_shapes=[
            pltpu.VMEM((seen_rows, lanes), f32),
            pltpu.VMEM((seen_rows, slots), f32),
            pltpu.VMEM((seen_rows, slots), bf16),
        ],
        compiler_params=pltpu.CompilerParams(vmem_limit_bytes=8 * 2**20),
        name="attend",
        cost_estimate=pl.CostEstimate(
            flops=4 * seen_rows * slots * lanes,
            bytes_accessed=2 * (keys.size + values.size),
            transcendentals=seen_rows * slots,
        ),
    )(queries, keys, values, bias, after, tokens, weight)


def piece_places(replicas):
    order = [0, 1] + list(range(replicas - 1, 1, -1))
    return [order.index(i) for i in range(replicas)]


def route_kernel(replicas, shards, *refs):
    left_ref, pick_ref = refs[:2]
    piece_refs = [refs[2 + place] for place in piece_places(replicas)]
    out_refs = refs[2 + replicas : 2 + replicas + shards]
    (right,) = refs[2 + replicas + shards :]
    up_rows = out_refs[0].shape[0] - left_ref.shape[0]
    rows = left_ref.shape[0]
    rank = right.shape[0]
    width = right.shape[1] // replicas
    half = rank // 2
    rest = (piece_refs[0].shape[0] - up_rows) % rank
    for i in range(replicas):
        first = 0
        for c in range(width // lanes - (1 if rest else 0)):
            right[:, i * width + c * lanes : i * width + (c + 1) * lanes] = piece_refs[i][
                first : first + rank, :
            ]
            first += rank
        if rest:
            both = piece_refs[i][first : first + half, :]
            tail = jnp.concatenate([both[:, : lanes // 2], both[:, lanes // 2 :]], axis=0)
            right[:, (i + 1) * width - lanes : (i + 1) * width] = jnp.concatenate(
                [tail, jnp.zeros((rank, lanes // 2), bf16)], axis=1
            )
            first += half
    lowered = lax.dot_general(
        left_ref[...], right[...], (((1,), (1,)), ((), ())), preferred_element_type=f32
    )
    both = jnp.concatenate(split_halves(lowered), axis=1)
    ups = [piece[piece.shape[0] - up_rows :, :].astype(f32) for piece in piece_refs]
    for i in range(shards):
        out_refs[i][:rows, :] = both
        picked = sum(up * pick_ref[i * replicas + k, :][None, :] for k, up in enumerate(ups))
        out_refs[i][rows:, :] = picked.astype(bf16)


def route(left, pick, pieces, rank, up_rows, shards):
    rows, depth = left.shape
    replicas = len(pieces)
    return pl.pallas_call(
        functools.partial(route_kernel, replicas, shards),
        out_shape=[jax.ShapeDtypeStruct((rows + up_rows, lanes), bf16)] * shards,
        in_specs=[whole_in_vmem] * (2 + replicas),
        out_specs=[whole_in_vmem] * shards,
        scratch_shapes=[pltpu.VMEM((rank, depth), bf16)],
        compiler_params=pltpu.CompilerParams(vmem_limit_bytes=4 * 2**20),
        name="route",
        cost_estimate=pl.CostEstimate(flops=0, bytes_accessed=800000, transcendentals=0),
    )(left, pick, *[pieces[i] for i in piece_places(replicas)])


def route_plain(owners, tokens, down, up, rank_part, own, shards):
    rank = down.shape[1]
    shard = lax.axis_index("tensor")
    first = shard * rank_part
    up_part = lax.dynamic_slice_in_dim(up, first, rank_part, axis=0)
    downs = lax.all_gather(down, "rollout", axis=0, tiled=False)
    ups = lax.all_gather(up_part, "rollout", axis=0, tiled=False)
    down_matrix = jnp.take(downs, owners, axis=0, mode="clip").reshape(-1, rank)
    up_matrix = jnp.take(ups, owners, axis=0, mode="clip").transpose(1, 0, 2)
    up_matrix = up_matrix.reshape(rank_part, -1)
    lowered = jnp.dot(tokens, down_matrix, preferred_element_type=f32)
    both = jnp.concatenate(split_halves(lowered), axis=1)
    packets = []
    for i in range(shards):
        up_block = lax.dynamic_slice_in_dim(up_matrix, (shard ^ i) * own, own, axis=1)
        parts = [both, side_by_side(up_block)]
        packets.append(jnp.concatenate(parts, axis=0))
    return packets


def finish_kernel(step_count, row_count, head_count, shards, *refs):
    gain_ref, base_ref, grouped_ref, total_ref, peak_ref, sum_ref, cosine_ref, sine_ref = refs[:8]
    packet_refs = refs[8 : 8 + shards][::-1]
    sum_refs = refs[8 + shards : 7 + 2 * shards]
    attention_ref, keys_ref, values_ref = refs[7 + 2 * shards : 10 + 2 * shards]
    (up_buf,) = refs[10 + 2 * shards :]
    shard = lax.axis_index("tensor")
    rows = step_count * row_count
    own = base_ref.shape[1]
    blocks = own // lanes
    rank = up_buf.shape[0]
    rank_part = rank // shards
    group = grouped_ref.shape[0] // (head_count * rows)
    seen = step_count * group

    lowered = jnp.zeros((rows, lanes), f32)
    for i in range(shards):
        lowered = lowered + packet_refs[i][:rows, :].astype(f32)
        ups = packet_refs[i][rows:, :].astype(f32)
        at = pl.multiple_of((shard ^ i) * rank_part, rank_part)
        for c in range(blocks):
            up_buf[pl.ds(at, rank_part), c * lanes : (c + 1) * lanes] = ups[
                c * rank_part : (c + 1) * rank_part, :
            ]
    lane = lax.broadcasted_iota(jnp.int32, (rows, lanes), 1)
    lowered = lowered + pltpu.roll(lowered, rank, 1)
    high, low = split_halves(lowered)
    left = jnp.where(lane < rank, high.astype(f32), low.astype(f32)).astype(bf16)
    up = up_buf[...].astype(bf16)
    raised_up = jnp.dot(left, jnp.concatenate([up, up], axis=0), preferred_element_type=f32)
    joined = []
    for c in range(blocks):
        block = base_ref[:, c * lanes : (c + 1) * lanes]
        for partial_ref in sum_refs:
            block = block + partial_ref[:, c * lanes : (c + 1) * lanes].astype(f32)
        joined.append(block + adapter_scale * raised_up[:, c * lanes : (c + 1) * lanes])

    all_rows = row_count * seen
    seen_by = lax.broadcasted_iota(jnp.int32, (all_rows, rows), 0)
    made_by = lax.broadcasted_iota(jnp.int32, (all_rows, rows), 1)
    visible = (seen_by % row_count == made_by % row_count) & (
        made_by // row_count <= seen_by // (row_count * group)
    )
    heads = [(h, slice(h * all_rows, (h + 1) * all_rows)) for h in range(head_count)]
    keys, values, scores, results = [], [], [], []
    for h, _ in heads:
        raw_key = joined[2 * h]
        mean_square = jnp.mean(raw_key * raw_key, axis=1, keepdims=True)
        normed = raw_key * lax.rsqrt(mean_square + norm_eps) * gain_ref[...]
        key = normed * cosine_ref[...] + pltpu.roll(normed, lanes // 2, 1) * sine_ref[...]
        keys.append(key.astype(bf16))
        values.append(joined[2 * h + 1].astype(bf16))
        keys_ref[:, h * lanes : (h + 1) * lanes] = keys[h]
        values_ref[:, h * lanes : (h + 1) * lanes] = values[h]
    for h, mine in heads:
        score = lax.dot_general(
            grouped_ref[mine, :], keys[h], (((1,), (1,)), ((), ())), preferred_element_type=f32
        )
        scores.append(jnp.where(visible, score, masked_score))
    for h, mine in heads:
        old_peak = peak_ref[mine, :]
        peak = jnp.maximum(old_peak, jnp.max(scores[h], axis=1, keepdims=True))
        fade = jnp.exp2((old_peak - peak) * exponent_scale)
        lifted = jnp.exp2((scores[h] - peak[:, :rows]) * exponent_scale)
        denominator = fade * sum_ref[mine, :] + jnp.sum(lifted, axis=1, keepdims=True)
        total = fade * total_ref[mine, :] + jnp.dot(
            lifted.astype(bf16), values[h], preferred_element_type=f32
        )
        results.append(total / denominator)
    for pair in range(step_count // 2):
        for q in range(head_count * group):
            h, g = q // group, q % group
            both = []
            for side in range(2):
                first = ((pair * 2 + side) * group + g) * row_count
                both.append(results[h][first : first + row_count])
            attention_ref[
                pair * 2 * row_count : (pair + 1) * 2 * row_count, q * lanes : (q + 1) * lanes
            ] = jnp.concatenate(both, axis=0).astype(bf16)


def finish(mine, others, partials, gain, packets, rank, step_count, row_count, query_width):
    rows, own = mine.shape
    shards = len(packets)
    head_count = own // (2 * lanes)
    return pl.pallas_call(
        functools.partial(finish_kernel, step_count, row_count, head_count, shards),
        out_shape=(
            jax.ShapeDtypeStruct((rows, query_width), bf16),
            jax.ShapeDtypeStruct((rows, head_count * lanes), bf16),
            jax.ShapeDtypeStruct((rows, head_count * lanes), bf16),
        ),
        in_specs=[whole_in_vmem] * (7 + 2 * shards),
        out_specs=(whole_in_vmem,) * 3,
        scratch_shapes=[
            pltpu.VMEM((rank, own), f32),
        ],
        compiler_params=pltpu.CompilerParams(vmem_limit_bytes=6 * 2**20),
        name="finish",
        cost_estimate=pl.CostEstimate(flops=0, bytes_accessed=1000000, transcendentals=0),
    )(gain, mine, *partials, *packets[::-1], *others[::-1])


def per_device(
    normed_tokens,
    key_value_weight,
    adapter_down,
    adapter_up,
    key_gain,
    queries,
    cache_keys,
    stored_values,
    lengths,
    owners,
):
    replicas = lax.axis_size("rollout")
    shards = lax.axis_size("tensor")
    down_rows, rank = adapter_down.shape
    step_count, row_count, depth = normed_tokens.shape
    own = key_value_weight.shape[1] // shards
    rank_part = rank // shards
    rows = step_count * row_count
    tokens = normed_tokens.reshape(rows, depth)
    query_rows = queries.reshape(rows, -1)

    fits = (
        replicas <= 4
        and adapter_up.shape[1] == own
        and down_rows % lanes in (0, lanes // 2)
        and rank == lanes // 2
        and rank_part % 16 == 0
    )
    pieces_size = 2 * (adapter_down.size + adapter_up.size)
    fetched = 2 * (key_value_weight.size + cache_keys.size + stored_values.size)
    turns = frequencies(
        pl.CostEstimate(flops=10000 * pieces_size, bytes_accessed=10 * pieces_size, transcendentals=0)
    )
    beside = pl.CostEstimate(flops=1000 * fetched, bytes_accessed=fetched, transcendentals=0)
    if fits:
        packed = pack(adapter_down.T, adapter_up, rank_part, turns, beside)
        pieces = [packed] + [swap(packed, "rollout", i) for i in range(1, replicas)]
    blocks, left, pick, cosine, sine, bias = project(
        owners,
        lengths,
        tokens,
        key_value_weight,
        turns,
        packed if fits else adapter_up,
        cache_keys,
        stored_values,
        step_count,
        shards,
        replicas if fits else 1,
    )
    others = [swap(block, "tensor", i + 1) for i, block in enumerate(blocks)]
    if fits:
        packets = route(left, pick, pieces, rank, rank_part * own // lanes, shards)
    else:
        packets = route_plain(
            owners, tokens, adapter_down, adapter_up, rank_part, own, shards
        )
    mine, grouped, total, peak, denominator = attend(
        query_rows,
        cache_keys,
        stored_values,
        bias,
        packets[0],
        tokens,
        key_value_weight,
        own,
        step_count,
    )
    packets = [packets[0]] + [swap(packets[i], "tensor", i) for i in range(1, shards)]
    attention, keys, values = finish(
        mine,
        others,
        (grouped, total, peak, denominator, cosine, sine),
        key_gain.reshape(1, -1),
        packets,
        rank,
        step_count,
        row_count,
        query_rows.shape[1],
    )
    return tuple(a.reshape(step_count, row_count, -1) for a in (attention, keys, values))


def solution(mesh):
    placed = (
        P(None, ("job", "rollout"), "tensor"),
        P("tensor", None),
        P(("job", "rollout", "tensor"), None),
        P(None, ("job", "rollout")),
        P(),
        P(None, ("job", "rollout"), "tensor"),
        P(("job", "rollout"), None, "tensor"),
        P(("job", "rollout"), None, "tensor"),
        P(("job", "rollout")),
        P("job"),
    )
    return jax.shard_map(
        per_device,
        mesh=mesh,
        in_specs=placed,
        out_specs=(
            P(None, ("job", "rollout"), "tensor"),
            P(None, ("job", "rollout"), "tensor"),
            P(None, ("job", "rollout"), "tensor"),
        ),
        check_vma=False,
    )
```

```python
import functools
import math

import jax
import jax.numpy as jnp
from jax import lax
from jax.experimental import pallas as pl
from jax.experimental.pallas import tpu as pltpu
from jax.sharding import PartitionSpec as P

norm_eps = 1e-06
rope_base = 1000000.0
adapter_scale = 2.0
masked_score = -1e30
lanes = 128
exponent_scale = lanes**-0.5 / math.log(2.0)
f32 = jnp.float32
bf16 = jnp.bfloat16

whole_in_vmem = pl.BlockSpec(memory_space=pltpu.VMEM)
whole_in_smem = pl.BlockSpec(memory_space=pltpu.SMEM)
stays_in_hbm = pl.BlockSpec(memory_space=pltpu.HBM)


def swap(block, axis, offset):
    count = lax.axis_size(axis)
    return lax.ppermute(block, axis, [(s, s ^ offset) for s in range(count)])


def in_hbm(*arrays):
    return tuple(pltpu.with_memory_space_constraint(a, pltpu.HBM) for a in arrays)


def side_by_side(rows_of_blocks):
    r, c = rows_of_blocks.shape
    return rows_of_blocks.reshape(r, c // lanes, lanes).transpose(1, 0, 2).reshape(-1, lanes)


def split_halves(total):
    high = total.astype(bf16)
    return high, (total - high.astype(f32)).astype(bf16)


def frequencies_kernel(out_ref):
    lane = lax.broadcasted_iota(jnp.int32, out_ref.shape, 1)
    spacing = (lane % (lanes // 2)).astype(f32) * (-2.0 / lanes * math.log(rope_base))
    out_ref[...] = jnp.exp(spacing)


def frequencies(beside):
    return pl.pallas_call(
        frequencies_kernel,
        out_shape=jax.ShapeDtypeStruct((8, lanes), f32),
        out_specs=whole_in_vmem,
        compiler_params=pltpu.CompilerParams(vmem_limit_bytes=2**20),
        name="frequencies",
        cost_estimate=beside,
    )()


def pack_kernel(down_ref, up_all_ref, _, out_ref):
    rank, down_rows = down_ref.shape
    rank_part = (out_ref.shape[0] * lanes - down_ref.size) // up_all_ref.shape[1]
    start = pl.multiple_of(lax.axis_index("tensor") * rank_part, rank_part)
    up_ref = up_all_ref.at[pl.ds(start, rank_part), :]
    first = 0
    for c in range(down_rows // lanes):
        out_ref[first : first + rank, :] = down_ref[:, c * lanes : (c + 1) * lanes]
        first += rank
    rest = down_rows % lanes
    if rest:
        half = rank // 2
        tail = down_ref[:, down_rows - rest :]
        out_ref[first : first + half, :] = jnp.concatenate([tail[:half], tail[half:]], axis=1)
        first += half
    for c in range(up_ref.shape[1] // lanes):
        out_ref[first : first + rank_part, :] = up_ref[:, c * lanes : (c + 1) * lanes]
        first += rank_part


def pack(down, up, rank_part, after):
    rows = (down.size + rank_part * up.shape[1]) // lanes
    return pl.pallas_call(
        pack_kernel,
        out_shape=jax.ShapeDtypeStruct((rows, lanes), bf16),
        in_specs=[whole_in_vmem] * 3,
        out_specs=whole_in_vmem,
        compiler_params=pltpu.CompilerParams(vmem_limit_bytes=2 * 2**20),
        name="pack",
        cost_estimate=pl.CostEstimate(flops=0, bytes_accessed=200000, transcendentals=0),
    )(down, up, after)


def product(tokens_ref, weight_ref, owner, own):
    columns = pl.ds(pl.multiple_of(owner * own, lanes), own)
    return jnp.dot(tokens_ref[...], weight_ref[:, columns], preferred_element_type=f32)


def project_kernel(step_count, row_count, shards, replicas, *refs):
    owners_hbm, lengths_hbm, tokens_ref, weight_ref, turns_ref, _, _, _ = refs[:8]
    block_refs = refs[8 : 7 + shards]
    left_ref, pick_ref, cosine_ref, sine_ref, bias_ref = refs[7 + shards : 12 + shards]
    owners_ref, lengths_ref, token_buf, sems = refs[12 + shards :]
    owners_copy = pltpu.make_async_copy(owners_hbm, owners_ref, sems.at[0])
    lengths_copy = pltpu.make_async_copy(lengths_hbm, lengths_ref, sems.at[1])
    owners_copy.start()
    lengths_copy.start()

    shard = lax.axis_index("tensor")
    rows, own = block_refs[0].shape
    for i in reversed(range(1, shards)):
        block_refs[i - 1][...] = product(tokens_ref, weight_ref, shard ^ i, own).astype(bf16)

    owners_copy.wait()
    replica = lax.axis_index("rollout")
    width = token_buf.shape[2]
    down_rows = tokens_ref.shape[1] // replicas
    for k in range(replicas):
        token_buf[k, :, :down_rows] = tokens_ref[:, k * down_rows : (k + 1) * down_rows]
        if down_rows < width:
            token_buf[k, :, down_rows:] = jnp.zeros((rows, width - down_rows), bf16)
    for i in range(replicas):
        place = jnp.int32(0)
        for k in range(1, replicas):
            place = place + jnp.where(owners_ref[k] == replica ^ i, k, 0)
        left_ref[:, i * width : (i + 1) * width] = token_buf[place]
    if replicas > 1:
        for i in range(shards):
            for k in range(replicas):
                picked = jnp.where(owners_ref[shard ^ i] == replica ^ k, 1.0, 0.0)
                row = i * replicas + k
                pick_ref[row : row + 1, :] = jnp.full((1, lanes), picked, f32)

    lengths_copy.wait()
    row = lax.broadcasted_iota(jnp.int32, (rows, lanes), 0)
    lane = lax.broadcasted_iota(jnp.int32, (rows, lanes), 1)
    position = row // row_count
    for b in range(row_count):
        position = position + jnp.where(row % row_count == b, lengths_ref[b], 0)
    angles = position.astype(f32) * turns_ref[:1, :]
    cosine_ref[...] = jnp.cos(angles)
    sine = jnp.sin(angles)
    sine_ref[...] = jnp.where(lane < lanes // 2, -sine, sine)
    slot = lax.broadcasted_iota(jnp.int32, bias_ref.shape, 1)
    whose = lax.broadcasted_iota(jnp.int32, bias_ref.shape, 0)
    length = jnp.zeros(bias_ref.shape, jnp.int32)
    for b in range(row_count):
        length = jnp.where(whose == b, lengths_ref[b], length)
    bias_ref[...] = jnp.where(slot < length, 0.0, masked_score)


def project(
    owners, lengths, tokens, weight, turns, after, keys, values, step_count, shards, replicas
):
    rows, depth = tokens.shape
    row_count = rows // step_count
    own = weight.shape[1] // shards
    piece_width = -(-depth // replicas // lanes) * lanes
    table = jax.ShapeDtypeStruct((rows, lanes), f32)
    outs = pl.pallas_call(
        functools.partial(project_kernel, step_count, row_count, shards, replicas),
        out_shape=[jax.ShapeDtypeStruct((rows, own), bf16)] * (shards - 1)
        + [
            jax.ShapeDtypeStruct((rows, replicas * piece_width), bf16),
            jax.ShapeDtypeStruct((shards * replicas, lanes), f32),
            table,
            table,
            jax.ShapeDtypeStruct((row_count, keys.shape[1]), f32),
        ],
        in_specs=[stays_in_hbm] * 2 + [whole_in_vmem] * 6,
        out_specs=[whole_in_vmem] * (shards + 4),
        scratch_shapes=[
            pltpu.SMEM(owners.shape, jnp.int32),
            pltpu.SMEM(lengths.shape, jnp.int32),
            pltpu.VMEM((replicas, rows, piece_width), bf16),
            pltpu.SemaphoreType.DMA((2,)),
        ],
        compiler_params=pltpu.CompilerParams(vmem_limit_bytes=6 * 2**20),
        name="project",
        cost_estimate=pl.CostEstimate(flops=0, bytes_accessed=200000, transcendentals=0),
    )(*in_hbm(owners, lengths), tokens, weight, turns, after, keys, values)
    return outs[: shards - 1], *outs[shards - 1 :]


def attend_kernel(
    step_count,
    head_count,
    queries_ref,
    keys_ref,
    values_ref,
    bias_ref,
    _,
    tokens_ref,
    weight_ref,
    own_ref,
    grouped_ref,
    total_ref,
    peak_ref,
    sum_ref,
    regroup,
    scores_ref,
    raised,
):
    own_ref[...] = product(tokens_ref, weight_ref, lax.axis_index("tensor"), own_ref.shape[1])

    row_count, slots, _ = keys_ref.shape
    group = queries_ref.shape[1] // (head_count * lanes)
    seen = step_count * group
    for pair in range(step_count // 2):
        for q in range(head_count * group):
            h, g = q // group, q % group
            both = queries_ref[
                pair * 2 * row_count : (pair + 1) * 2 * row_count, q * lanes : (q + 1) * lanes
            ].astype(f32)
            for side in range(2):
                first = h * row_count * seen + (pair * 2 + side) * group + g
                regroup[pl.ds(first, row_count, stride=seen), :] = both[
                    side * row_count : (side + 1) * row_count, :
                ]
            if g % 2:
                for side in range(2):
                    half = slice(side * row_count, (side + 1) * row_count)
                    last = (h * seen + (pair * 2 + side) * group + g + 1) * row_count
                    grouped_ref[last - 2 * row_count : last, :] = jnp.concatenate(
                        [before[half], both[half]], axis=0
                    ).astype(bf16)
            before = both

    for b in range(row_count):
        for h in range(head_count):
            at = (h * row_count + b) * seen
            scores_ref[at : at + seen, :] = lax.dot_general(
                regroup[at : at + seen, :].astype(bf16),
                keys_ref[b, :, h * lanes : (h + 1) * lanes],
                (((1,), (1,)), ((), ())),
                preferred_element_type=f32,
            )

    places = [
        (
            b,
            h,
            slice((h * row_count + b) * seen, (h * row_count + b + 1) * seen),
            pl.ds(h * row_count * seen + b, seen, stride=row_count),
        )
        for b in range(row_count)
        for h in range(head_count)
    ]
    for b, h, place, out in places:
        score = scores_ref[place, :] + bias_ref[b : b + 1, :]
        peak = jnp.max(score, axis=1, keepdims=True)
        lifted = jnp.exp2((score - peak) * exponent_scale)
        raised[place, :] = lifted.astype(bf16)
        peak_ref[out, :] = jnp.broadcast_to(peak, (seen, lanes))
        sum_ref[out, :] = jnp.broadcast_to(
            jnp.sum(lifted, axis=1, keepdims=True), (seen, lanes)
        )
    for b, h, place, out in places:
        total_ref[out, :] = jnp.dot(
            raised[place, :],
            values_ref[b, :, h * lanes : (h + 1) * lanes],
            preferred_element_type=f32,
        )


def attend(queries, keys, values, bias, after, tokens, weight, own, step_count):
    row_count, slots, width = keys.shape
    seen_rows = step_count * row_count * queries.shape[1] // lanes
    seen_table = jax.ShapeDtypeStruct((seen_rows, lanes), f32)
    return pl.pallas_call(
        functools.partial(attend_kernel, step_count, width // lanes),
        out_shape=(
            jax.ShapeDtypeStruct((tokens.shape[0], own), f32),
            jax.ShapeDtypeStruct((seen_rows, lanes), bf16),
            seen_table,
            seen_table,
            seen_table,
        ),
        in_specs=[whole_in_vmem] * 7,
        out_specs=(whole_in_vmem,) * 5,
        scratch_shapes=[
            pltpu.VMEM((seen_rows, lanes), f32),
            pltpu.VMEM((seen_rows, slots), f32),
            pltpu.VMEM((seen_rows, slots), bf16),
        ],
        compiler_params=pltpu.CompilerParams(vmem_limit_bytes=8 * 2**20),
        name="attend",
        cost_estimate=pl.CostEstimate(
            flops=4 * seen_rows * slots * lanes,
            bytes_accessed=2 * (keys.size + values.size),
            transcendentals=seen_rows * slots,
        ),
    )(queries, keys, values, bias, after, tokens, weight)


def piece_places(replicas):
    order = [0, 1] + list(range(replicas - 1, 1, -1))
    return [order.index(i) for i in range(replicas)]


def route_kernel(replicas, shards, *refs):
    left_ref, pick_ref = refs[:2]
    piece_refs = [refs[2 + place] for place in piece_places(replicas)]
    out_refs = refs[2 + replicas : 2 + replicas + shards]
    (right,) = refs[2 + replicas + shards :]
    up_rows = out_refs[0].shape[0] - left_ref.shape[0]
    rows = left_ref.shape[0]
    rank = right.shape[0]
    width = right.shape[1] // replicas
    half = rank // 2
    rest = (piece_refs[0].shape[0] - up_rows) % rank
    for i in range(replicas):
        first = 0
        for c in range(width // lanes - (1 if rest else 0)):
            right[:, i * width + c * lanes : i * width + (c + 1) * lanes] = piece_refs[i][
                first : first + rank, :
            ]
            first += rank
        if rest:
            both = piece_refs[i][first : first + half, :]
            tail = jnp.concatenate([both[:, : lanes // 2], both[:, lanes // 2 :]], axis=0)
            right[:, (i + 1) * width - lanes : (i + 1) * width] = jnp.concatenate(
                [tail, jnp.zeros((rank, lanes // 2), bf16)], axis=1
            )
            first += half
    lowered = lax.dot_general(
        left_ref[...], right[...], (((1,), (1,)), ((), ())), preferred_element_type=f32
    )
    both = jnp.concatenate(split_halves(lowered), axis=1)
    ups = [piece[piece.shape[0] - up_rows :, :].astype(f32) for piece in piece_refs]
    for i in range(shards):
        out_refs[i][:rows, :] = both
        picked = sum(up * pick_ref[i * replicas + k, :][None, :] for k, up in enumerate(ups))
        out_refs[i][rows:, :] = picked.astype(bf16)


def route(left, pick, pieces, rank, up_rows, shards):
    rows, depth = left.shape
    replicas = len(pieces)
    return pl.pallas_call(
        functools.partial(route_kernel, replicas, shards),
        out_shape=[jax.ShapeDtypeStruct((rows + up_rows, lanes), bf16)] * shards,
        in_specs=[whole_in_vmem] * (2 + replicas),
        out_specs=[whole_in_vmem] * shards,
        scratch_shapes=[pltpu.VMEM((rank, depth), bf16)],
        compiler_params=pltpu.CompilerParams(vmem_limit_bytes=4 * 2**20),
        name="route",
        cost_estimate=pl.CostEstimate(flops=0, bytes_accessed=800000, transcendentals=0),
    )(left, pick, *[pieces[i] for i in piece_places(replicas)])


def route_plain(owners, tokens, down, up, rank_part, own, shards):
    rank = down.shape[1]
    shard = lax.axis_index("tensor")
    first = shard * rank_part
    up_part = lax.dynamic_slice_in_dim(up, first, rank_part, axis=0)
    downs = lax.all_gather(down, "rollout", axis=0, tiled=False)
    ups = lax.all_gather(up_part, "rollout", axis=0, tiled=False)
    down_matrix = jnp.take(downs, owners, axis=0, mode="clip").reshape(-1, rank)
    up_matrix = jnp.take(ups, owners, axis=0, mode="clip").transpose(1, 0, 2)
    up_matrix = up_matrix.reshape(rank_part, -1)
    lowered = jnp.dot(tokens, down_matrix, preferred_element_type=f32)
    both = jnp.concatenate(split_halves(lowered), axis=1)
    packets = []
    for i in range(shards):
        up_block = lax.dynamic_slice_in_dim(up_matrix, (shard ^ i) * own, own, axis=1)
        parts = [both, side_by_side(up_block)]
        packets.append(jnp.concatenate(parts, axis=0))
    return packets


def finish_kernel(step_count, row_count, head_count, shards, *refs):
    gain_ref, base_ref, grouped_ref, total_ref, peak_ref, sum_ref, cosine_ref, sine_ref = refs[:8]
    packet_refs = refs[8 : 8 + shards][::-1]
    sum_refs = refs[8 + shards : 7 + 2 * shards]
    attention_ref, keys_ref, values_ref = refs[7 + 2 * shards : 10 + 2 * shards]
    (up_buf,) = refs[10 + 2 * shards :]
    shard = lax.axis_index("tensor")
    rows = step_count * row_count
    own = base_ref.shape[1]
    blocks = own // lanes
    rank = up_buf.shape[0]
    rank_part = rank // shards
    group = grouped_ref.shape[0] // (head_count * rows)
    seen = step_count * group

    lowered = jnp.zeros((rows, lanes), f32)
    for i in range(shards):
        lowered = lowered + packet_refs[i][:rows, :].astype(f32)
        ups = packet_refs[i][rows:, :].astype(f32)
        at = pl.multiple_of((shard ^ i) * rank_part, rank_part)
        for c in range(blocks):
            up_buf[pl.ds(at, rank_part), c * lanes : (c + 1) * lanes] = ups[
                c * rank_part : (c + 1) * rank_part, :
            ]
    lane = lax.broadcasted_iota(jnp.int32, (rows, lanes), 1)
    lowered = lowered + pltpu.roll(lowered, rank, 1)
    high, low = split_halves(lowered)
    left = jnp.where(lane < rank, high.astype(f32), low.astype(f32)).astype(bf16)
    up = up_buf[...].astype(bf16)
    raised_up = jnp.dot(left, jnp.concatenate([up, up], axis=0), preferred_element_type=f32)
    joined = []
    for c in range(blocks):
        block = base_ref[:, c * lanes : (c + 1) * lanes]
        for partial_ref in sum_refs:
            block = block + partial_ref[:, c * lanes : (c + 1) * lanes].astype(f32)
        joined.append(block + adapter_scale * raised_up[:, c * lanes : (c + 1) * lanes])

    all_rows = row_count * seen
    seen_by = lax.broadcasted_iota(jnp.int32, (all_rows, rows), 0)
    made_by = lax.broadcasted_iota(jnp.int32, (all_rows, rows), 1)
    visible = (seen_by % row_count == made_by % row_count) & (
        made_by // row_count <= seen_by // (row_count * group)
    )
    heads = [(h, slice(h * all_rows, (h + 1) * all_rows)) for h in range(head_count)]
    keys, values, scores, results = [], [], [], []
    for h, _ in heads:
        raw_key = joined[2 * h]
        mean_square = jnp.mean(raw_key * raw_key, axis=1, keepdims=True)
        normed = raw_key * lax.rsqrt(mean_square + norm_eps) * gain_ref[...]
        key = normed * cosine_ref[...] + pltpu.roll(normed, lanes // 2, 1) * sine_ref[...]
        keys.append(key.astype(bf16))
        values.append(joined[2 * h + 1].astype(bf16))
        keys_ref[:, h * lanes : (h + 1) * lanes] = keys[h]
        values_ref[:, h * lanes : (h + 1) * lanes] = values[h]
    for h, mine in heads:
        score = lax.dot_general(
            grouped_ref[mine, :], keys[h], (((1,), (1,)), ((), ())), preferred_element_type=f32
        )
        scores.append(jnp.where(visible, score, masked_score))
    for h, mine in heads:
        old_peak = peak_ref[mine, :]
        peak = jnp.maximum(old_peak, jnp.max(scores[h], axis=1, keepdims=True))
        fade = jnp.exp2((old_peak - peak) * exponent_scale)
        lifted = jnp.exp2((scores[h] - peak[:, :rows]) * exponent_scale)
        denominator = fade * sum_ref[mine, :] + jnp.sum(lifted, axis=1, keepdims=True)
        total = fade * total_ref[mine, :] + jnp.dot(
            lifted.astype(bf16), values[h], preferred_element_type=f32
        )
        results.append(total / denominator)
    for pair in range(step_count // 2):
        for q in range(head_count * group):
            h, g = q // group, q % group
            both = []
            for side in range(2):
                first = ((pair * 2 + side) * group + g) * row_count
                both.append(results[h][first : first + row_count])
            attention_ref[
                pair * 2 * row_count : (pair + 1) * 2 * row_count, q * lanes : (q + 1) * lanes
            ] = jnp.concatenate(both, axis=0).astype(bf16)


def finish(mine, others, partials, gain, packets, rank, step_count, row_count, query_width):
    rows, own = mine.shape
    shards = len(packets)
    head_count = own // (2 * lanes)
    return pl.pallas_call(
        functools.partial(finish_kernel, step_count, row_count, head_count, shards),
        out_shape=(
            jax.ShapeDtypeStruct((rows, query_width), bf16),
            jax.ShapeDtypeStruct((rows, head_count * lanes), bf16),
            jax.ShapeDtypeStruct((rows, head_count * lanes), bf16),
        ),
        in_specs=[whole_in_vmem] * (7 + 2 * shards),
        out_specs=(whole_in_vmem,) * 3,
        scratch_shapes=[
            pltpu.VMEM((rank, own), f32),
        ],
        compiler_params=pltpu.CompilerParams(vmem_limit_bytes=6 * 2**20),
        name="finish",
        cost_estimate=pl.CostEstimate(flops=0, bytes_accessed=1000000, transcendentals=0),
    )(gain, mine, *partials, *packets[::-1], *others[1:], *others[:1])


def per_device(
    normed_tokens,
    key_value_weight,
    adapter_down,
    adapter_up,
    key_gain,
    queries,
    cache_keys,
    stored_values,
    lengths,
    owners,
):
    replicas = lax.axis_size("rollout")
    shards = lax.axis_size("tensor")
    down_rows, rank = adapter_down.shape
    step_count, row_count, depth = normed_tokens.shape
    own = key_value_weight.shape[1] // shards
    rank_part = rank // shards
    rows = step_count * row_count
    tokens = normed_tokens.reshape(rows, depth)
    query_rows = queries.reshape(rows, -1)

    fits = (
        replicas <= 4
        and adapter_up.shape[1] == own
        and down_rows % lanes in (0, lanes // 2)
        and rank == lanes // 2
        and rank_part % 16 == 0
    )
    fetched = 2 * (key_value_weight.size + cache_keys.size + stored_values.size)
    turns = frequencies(
        pl.CostEstimate(flops=1000 * fetched, bytes_accessed=fetched, transcendentals=0)
    )
    if fits:
        packed = pack(adapter_down.T, adapter_up, rank_part, turns)
        pieces = [packed] + [swap(packed, "rollout", i) for i in range(1, replicas)]
    blocks, left, pick, cosine, sine, bias = project(
        owners,
        lengths,
        tokens,
        key_value_weight,
        turns,
        packed if fits else adapter_up,
        cache_keys,
        stored_values,
        step_count,
        shards,
        replicas if fits else 1,
    )
    others = [swap(block, "tensor", i + 1) for i, block in enumerate(blocks)]
    if fits:
        packets = route(left, pick, pieces, rank, rank_part * own // lanes, shards)
    else:
        packets = route_plain(
            owners, tokens, adapter_down, adapter_up, rank_part, own, shards
        )
    mine, grouped, total, peak, denominator = attend(
        query_rows,
        cache_keys,
        stored_values,
        bias,
        packets[0],
        tokens,
        key_value_weight,
        own,
        step_count,
    )
    packets = [packets[0]] + [swap(packets[i], "tensor", i) for i in range(1, shards)]
    attention, keys, values = finish(
        mine,
        others,
        (grouped, total, peak, denominator, cosine, sine),
        key_gain.reshape(1, -1),
        packets,
        rank,
        step_count,
        row_count,
        query_rows.shape[1],
    )
    return tuple(a.reshape(step_count, row_count, -1) for a in (attention, keys, values))


def solution(mesh):
    placed = (
        P(None, ("job", "rollout"), "tensor"),
        P("tensor", None),
        P(("job", "rollout", "tensor"), None),
        P(None, ("job", "rollout")),
        P(),
        P(None, ("job", "rollout"), "tensor"),
        P(("job", "rollout"), None, "tensor"),
        P(("job", "rollout"), None, "tensor"),
        P(("job", "rollout")),
        P("job"),
    )
    return jax.shard_map(
        per_device,
        mesh=mesh,
        in_specs=placed,
        out_specs=(
            P(None, ("job", "rollout"), "tensor"),
            P(None, ("job", "rollout"), "tensor"),
            P(None, ("job", "rollout"), "tensor"),
        ),
        check_vma=False,
    )
```
